32 devices in a mesh: dp: 8 (over y, x, core), tensor: 4 (over z).
Axes of the slice: x: 2, y: 2, z: 4, core: 2. Of those that a mesh axis runs over, the one named last changes fastest.
Arguments:
- tokens: bfloat16 [4096, 2048], P('dp', 'tensor'), may hold values from -6 to 6
- series_ids: int32 [4096], replicated, may hold values from 0 to 7, never falling along the last dimension, each value on 1 to 2560 neighbouring positions
- offsets: int32 [4096], P('dp'), may hold values from 0 to 65535
- norm_gain: float32 [2048], replicated, may hold values from 0.5 to 1.5
- mlp_gain: float32 [2048], replicated, may hold values from 0.5 to 1.5
- w_query: bfloat16 [2048, 2048], P(None, 'tensor')
- w_key: bfloat16 [2048, 2048], P(None, 'tensor')
- w_value: bfloat16 [2048, 2048], P(None, 'tensor'), may hold values from -0.125 to 0.125
- w_out: bfloat16 [2048, 2048], P('tensor'), may hold values from -0.125 to 0.125
- w_gate: bfloat16 [2048, 8192], P(None, 'tensor'), may hold values from -0.125 to 0.125
- w_up: bfloat16 [2048, 8192], P(None, 'tensor'), may hold values from -0.125 to 0.125
- w_down: bfloat16 [8192, 2048], P('tensor'), may hold values from -0.0625 to 0.0625
- projector: bfloat16 [2048, 512], replicated, may hold values from -0.125 to 0.125
- student_in: bfloat16 [4096, 512], P('dp'), may hold values from -6 to 6
- s_gate: bfloat16 [512, 2048], P(None, 'tensor'), may hold values from -0.25 to 0.25
- s_up: bfloat16 [512, 2048], P(None, 'tensor'), may hold values from -0.25 to 0.25
- s_down: bfloat16 [2048, 512], P('tensor'), may hold values from -0.125 to 0.125
Outputs:
- teacher_out: bfloat16 [4096, 2048], P('dp', 'tensor')
- grad_gate: float32 [512, 2048], P(None, 'tensor')
- grad_up: float32 [512, 2048], P(None, 'tensor')
- grad_down: float32 [2048, 512], P('tensor')
- error: float32 [], replicated
The draws below stay inside these ranges and needn't reach their ends.
Inputs may be any that keep to these rules, and one draw needn't show every extreme that they name: `series_ids`: ids never fall along the window; each series covers 1 to 2560 consecutive rows, one series exactly that many.
All inputs are finite; a program needn't handle non-finite values.
Results may differ from the reference program's by a relative error of at most 0.025.
Values may be sent and summed in bfloat16 or wider, within the bound.
No kernel may reach another device: no remote copies, remote signals or barrier semaphores. Data moves between devices by JAX's collectives and lax.ppermute only.
A program may use at most 128 MiB of HBM per device.

```python
import math
import jax
import jax.numpy as jnp
import numpy as np
from jax import lax

D = 2048
HEADS = 16
HD = 128
FF = 8192
SD = 512
SFF = 2048
SERIES = 8
TOKENS = 4096


def shared_base(key):
    return jax.random.normal(key, (D, D), jnp.float32)


def draw_w_query(key, part):
    base = shared_base(key)
    return (base * D ** (-0.5)).astype(jnp.bfloat16)


def draw_w_key(key, part):
    key = jax.random.fold_in(key, 12)
    fresh = jax.random.normal(key, (D, D), jnp.float32)
    return (fresh * D ** (-0.5)).astype(jnp.bfloat16)


def with_ends(entries, own_key, smallest, top_value):
    longest = entries.shape.index(max(entries.shape))
    spots = []
    for shift in (0, 1):
        where = [jax.random.randint(jax.random.fold_in(own_key, axis), (), 0, length) for axis, length in enumerate(entries.shape)]
        where[longest] = (where[longest] + shift) % entries.shape[longest]
        spots.append(tuple(where))
    return entries.at[spots[0]].set(smallest).at[spots[1]].set(top_value)


def block_levels(rng, extent, split, low, high):
    level = 1.0
    for axis_at, blocks in split:
        heights = jax.random.uniform(jax.random.fold_in(jax.random.fold_in(rng, 6), axis_at), (blocks,), jnp.float32, low / len(split), high / len(split))
        level = level * jnp.repeat(jnp.exp(heights), extent[axis_at] // blocks).reshape((-1,) + (1,) * (len(extent) - 1 - axis_at))
    return level


def length_profile(number_of, total, most, slope):
    loads = [(1 << 20) // math.isqrt(rank ** slope) + 1 for rank in range(2, number_of + 1)]
    spare, holding = total - most - (number_of - 1), [1] * (number_of - 1)
    while spare > 0:
        movable = [i for i in range(number_of - 1) if holding[i] < most]
        pool, budget = sum([loads[i] for i in movable]), spare
        for i in movable:
            more = min(most - holding[i], max(1, budget * loads[i] // pool), spare)
            holding[i] = holding[i] + more
            spare = spare - more
    return np.array([most] + holding)


def uneven_parts(stream_key, number_of, total, most, slope):
    if number_of == 2:
        one = jax.random.randint(stream_key, (), max(1, total - most), min(most, total - 1) + 1)
        return jnp.stack([one, total - one])
    tallies = jnp.asarray(length_profile(number_of, total, most, slope), jnp.int32)
    pairs = (number_of - 1) // 2
    giver, sink = tallies[1:1 + 2 * pairs:2], tallies[2:2 + 2 * pairs:2]
    slack = jnp.minimum(giver - 1, most - sink)
    moved = jax.random.randint(jax.random.fold_in(stream_key, 1), (pairs,), 0, 1 << 20) % (slack + 1)
    tallies = tallies.at[1:1 + 2 * pairs:2].set(giver - moved).at[2:2 + 2 * pairs:2].set(sink + moved)
    return tallies[jax.random.permutation(jax.random.fold_in(stream_key, 2), number_of)]


def scatter_about(own_key, dims, spread, limit, cuts=(), kind=jnp.bfloat16):
    values = spread * jax.random.normal(own_key, dims, jnp.float32)
    if cuts:
        values = values * block_levels(own_key, dims, cuts, -0.22, 0.18)
    return jnp.clip(values, -limit, limit).astype(kind)


def setup_inputs(seed: int = 0) -> dict:
    arg_keys = jax.random.split(jax.random.key(seed), 18)
    tokens = scatter_about(arg_keys[0], (TOKENS, D), 1.0, 6.0, ((0, 8), (1, 4)))
    series_ids = jnp.searchsorted(jnp.cumsum(uneven_parts(arg_keys[1], SERIES, TOKENS, 5 * TOKENS // 8, 1)), jnp.arange(TOKENS), side="right").astype(jnp.int32)
    offsets = with_ends(jax.random.randint(arg_keys[2], (TOKENS,), 0, 65536), jax.random.fold_in(arg_keys[2], 1), 0, 65535).astype(jnp.int32)
    norm_gain = jnp.clip(1.0 + 0.1 * jax.random.normal(arg_keys[3], (D,), jnp.float32), 0.5, 1.5)
    mlp_gain = jnp.clip(1.0 + 0.1 * jax.random.normal(arg_keys[4], (D,), jnp.float32), 0.5, 1.5)
    w_query = draw_w_query(jax.random.fold_in(arg_keys[17], 71), 0)
    w_key = draw_w_key(jax.random.fold_in(arg_keys[17], 71), 0)
    w_value = scatter_about(arg_keys[7], (D, D), D ** -0.5, 0.125, ((1, 4),))
    w_out = scatter_about(arg_keys[8], (D, D), D ** -0.5, 0.125, ((0, 4),))
    w_gate = scatter_about(arg_keys[9], (D, FF), D ** -0.5, 0.125, ((1, 4),))
    w_up = scatter_about(arg_keys[10], (D, FF), D ** -0.5, 0.125, ((1, 4),))
    w_down = scatter_about(arg_keys[11], (FF, D), FF ** -0.5, 0.0625, ((0, 4),))
    projector = scatter_about(arg_keys[12], (D, SD), D ** -0.5, 0.125)
    student_in = scatter_about(arg_keys[13], (TOKENS, SD), 1.0, 6.0, ((0, 8),))
    s_gate = scatter_about(arg_keys[14], (SD, SFF), SD ** -0.5, 0.25, ((1, 4),))
    s_up = scatter_about(arg_keys[15], (SD, SFF), SD ** -0.5, 0.25, ((1, 4),))
    s_down = scatter_about(arg_keys[16], (SFF, SD), SFF ** -0.5, 0.125, ((0, 4),))
    return {"tokens": tokens, "series_ids": series_ids, "offsets": offsets, "norm_gain": norm_gain, "mlp_gain": mlp_gain, "w_query": w_query, "w_key": w_key, "w_value": w_value, "w_out": w_out, "w_gate": w_gate, "w_up": w_up, "w_down": w_down, "projector": projector, "student_in": student_in, "s_gate": s_gate, "s_up": s_up, "s_down": s_down}


def rms_scale(values):
    return values * lax.rsqrt(lax.optimization_barrier(jnp.mean(values * values, axis=-1, keepdims=True)) + 1e-05)

def frequencies(head_dim):
    indices = jnp.arange(head_dim // 2).astype(jnp.float32)
    return jnp.exp(-jnp.log(500000.0) * 2.0 * indices / head_dim)

def rotary(inputs, angles):
    half_dim = inputs.shape[-1] // 2
    cosine = jnp.cos(angles)
    sine = jnp.sin(angles)
    first_half = inputs[..., :half_dim]
    second_half = inputs[..., half_dim:]
    return jnp.concatenate([first_half * cosine - second_half * sine, first_half * sine + second_half * cosine], axis=-1)

def reference(tokens, series_ids, offsets, norm_gain, mlp_gain, w_query, w_key, w_value, w_out, w_gate, w_up, w_down, projector, student_in, s_gate, s_up, s_down):
    tokens_full = tokens.astype(jnp.float32)
    normed = (rms_scale(tokens_full) * norm_gain).astype(jnp.bfloat16)
    angles = offsets.astype(jnp.float32)[:, None, None] * frequencies(HD)[None, None, :]
    queries = rotary(jnp.dot(normed, w_query, preferred_element_type=jnp.float32).reshape(TOKENS, HEADS, HD), angles).astype(jnp.bfloat16)
    keys_rot = rotary(jnp.dot(normed, w_key, preferred_element_type=jnp.float32).reshape(TOKENS, HEADS, HD), angles).astype(jnp.bfloat16)
    values_all = jnp.dot(normed, w_value, preferred_element_type=jnp.float32).astype(jnp.bfloat16).reshape(TOKENS, HEADS, HD)
    position = jnp.arange(TOKENS, dtype=jnp.int32)
    allowed = (position[None, :] <= position[:, None]) & (series_ids[None, :] == series_ids[:, None])
    factor = HD ** (-0.5)

    def one_head(head_index):
        query_head = lax.dynamic_index_in_dim(queries, head_index, 1, keepdims=False)
        key_head = lax.dynamic_index_in_dim(keys_rot, head_index, 1, keepdims=False)
        value_head = lax.dynamic_index_in_dim(values_all, head_index, 1, keepdims=False)
        scores = jnp.dot(query_head, key_head.T, preferred_element_type=jnp.float32) * factor
        scores = jnp.where(allowed, scores, -1e+30)
        peak = lax.optimization_barrier(jnp.max(scores, axis=1, keepdims=True))
        weights = jnp.where(allowed, jnp.exp(scores - peak), 0.0)
        denom = lax.optimization_barrier(jnp.sum(weights, axis=1, keepdims=True))
        result = jnp.dot(weights.astype(jnp.bfloat16), value_head, preferred_element_type=jnp.float32) / denom
        return result.astype(jnp.bfloat16)
    heads_out = lax.map(one_head, jnp.arange(HEADS, dtype=jnp.int32))
    attended = jnp.transpose(heads_out, (1, 0, 2)).reshape(TOKENS, D)
    mixed = (tokens_full + jnp.dot(attended, w_out, preferred_element_type=jnp.float32)).astype(jnp.bfloat16)
    normed_two = (rms_scale(mixed.astype(jnp.float32)) * mlp_gain).astype(jnp.bfloat16)
    gate_out = jnp.dot(normed_two, w_gate, preferred_element_type=jnp.float32)
    up_out = jnp.dot(normed_two, w_up, preferred_element_type=jnp.float32)
    hidden = (jax.nn.silu(gate_out) * up_out).astype(jnp.bfloat16)
    teacher_out = (mixed.astype(jnp.float32) + jnp.dot(hidden, w_down, preferred_element_type=jnp.float32)).astype(jnp.bfloat16)
    target = jnp.dot(teacher_out, projector, preferred_element_type=jnp.float32)
    student_full = student_in.astype(jnp.float32)
    student_normed = rms_scale(student_full).astype(jnp.bfloat16)
    s_gate_out = jnp.dot(student_normed, s_gate, preferred_element_type=jnp.float32)
    s_up_out = jnp.dot(student_normed, s_up, preferred_element_type=jnp.float32)
    sigmoid_gate = jax.nn.sigmoid(s_gate_out)
    s_hidden = (s_gate_out * sigmoid_gate * s_up_out).astype(jnp.bfloat16)
    predicted = student_full + jnp.dot(s_hidden, s_down, preferred_element_type=jnp.float32)
    difference = predicted - target
    error = jnp.mean(difference * difference)
    scaled = (difference * TOKENS ** (-0.5)).astype(jnp.bfloat16)
    grad_down = jnp.dot(s_hidden.T, scaled, preferred_element_type=jnp.float32)
    grad_hidden = jnp.dot(scaled, s_down.T, preferred_element_type=jnp.float32)
    grad_up_in = (grad_hidden * s_gate_out * sigmoid_gate).astype(jnp.bfloat16)
    grad_gate_in = (grad_hidden * s_up_out * sigmoid_gate * (1.0 + s_gate_out * (1.0 - sigmoid_gate))).astype(jnp.bfloat16)
    grad_gate = jnp.dot(student_normed.T, grad_gate_in, preferred_element_type=jnp.float32)
    grad_up = jnp.dot(student_normed.T, grad_up_in, preferred_element_type=jnp.float32)
    return (teacher_out, grad_gate, grad_up, grad_down, error)
```

```python
import functools
import math

import jax
import jax.numpy as jnp
from jax import lax
from jax.experimental import pallas as pl
from jax.experimental.pallas import tpu as pltpu
from jax.sharding import PartitionSpec as P

HD = 128
COLS = 256
F32 = jnp.float32
BF16 = jnp.bfloat16
VMEM_LIMIT = 56 * 1024 * 1024


def rms_scale(values):
    return values * lax.rsqrt(jnp.mean(values * values, axis=-1, keepdims=True) + 1e-05)


def frequencies(head_dim):
    indices = jnp.arange(head_dim // 2).astype(F32)
    return jnp.exp(-jnp.log(500000.0) * 2.0 * indices / head_dim)


def dot(a, b):
    return jnp.dot(a, b, preferred_element_type=F32)


def ring_gather(block, axis):
    size = lax.axis_size(axis)
    perm = [(i, (i + 1) % size) for i in range(size)]
    blocks = [block]
    for _ in range(size - 1):
        blocks.append(lax.ppermute(blocks[-1], axis, perm))
    return blocks


def qkv_kernel(src_ref, *refs, ring, heads, split):
    blocks = refs[:ring]
    gain_ref, cos_ref, sin_ref, wq_ref, wk_ref, wv_ref, out_ref, tok_ref, normed = refs[ring:]
    step = pl.program_id(0)
    cols = wq_ref.shape[1]
    tiles = heads * HD // cols
    rows, width = blocks[0].shape
    depth = gain_ref.shape[1]

    @pl.when(step == 0)
    def _():
        total = jnp.zeros((rows, 1), F32)
        for block in blocks:
            part = block[...].astype(F32)
            total += jnp.sum(part * part, axis=1, keepdims=True)
        scale = lax.rsqrt(total / depth + 1e-05)
        for s, block in enumerate(blocks):
            at = pl.ds(pl.multiple_of(src_ref[s] * width, 128), width)
            part = block[...]
            tok_ref[:, at] = part
            normed[:, at] = (part.astype(F32) * scale * gain_ref[:, at]).astype(BF16)

    def emit(w_ref, rotate):
        result = dot(normed[...], w_ref[...])
        piece = rows // split
        for h in range(cols // HD):
            head = result[:, h * HD : (h + 1) * HD]
            if rotate:
                head = head * cos_ref[...] + pltpu.roll(head, HD // 2, 1) * sin_ref[...]
            head = head.astype(BF16)
            for p in range(split):
                out_ref[h * split + p, 0] = head[p * piece : (p + 1) * piece]

    @pl.when(step < tiles)
    def _():
        emit(wq_ref, True)

    @pl.when((step >= tiles) & (step < 2 * tiles))
    def _():
        emit(wk_ref, True)

    @pl.when(step >= 2 * tiles)
    def _():
        emit(wv_ref, False)


def qkv_call(src, blocks, gain, cosine, sine, w_query, w_key, w_value, split):
    rows, width = blocks[0].shape
    ring = len(blocks)
    depth, out_cols = w_query.shape
    heads = out_cols // HD
    cols = min(COLS, out_cols)
    tiles = out_cols // cols
    whole = lambda shape: pl.BlockSpec(shape, lambda j, src: (0,) * len(shape))
    weight = lambda k: pl.BlockSpec(
        (depth, cols), lambda j, src: (0, jnp.clip(j - k * tiles, 0, tiles - 1))
    )
    per_step = cols // HD * split
    return pl.pallas_call(
        functools.partial(qkv_kernel, ring=ring, heads=heads, split=split),
        out_shape=(
            jax.ShapeDtypeStruct((heads * split, 3, rows // split, HD), BF16),
            jax.ShapeDtypeStruct((rows, depth), BF16),
        ),
        grid_spec=pltpu.PrefetchScalarGridSpec(
            num_scalar_prefetch=1,
            grid=(3 * tiles,),
            in_specs=[whole((rows, width))] * ring
            + [whole((1, depth)), whole((rows, HD)), whole((rows, HD))]
            + [weight(0), weight(1), weight(2)],
            out_specs=(
                pl.BlockSpec(
                    (per_step, 1, rows // split, HD), lambda j, src: (j % tiles, j // tiles, 0, 0)
                ),
                whole((rows, depth)),
            ),
            scratch_shapes=[pltpu.VMEM((rows, depth), BF16)],
        ),
        compiler_params=pltpu.CompilerParams(vmem_limit_bytes=VMEM_LIMIT),
        cost_estimate=pl.CostEstimate(
            flops=6 * rows * depth * out_cols,
            bytes_accessed=6 * depth * out_cols,
            transcendentals=0,
        ),
        name="qkv",
    )(src, *blocks, gain, cosine, sine, w_query, w_key, w_value)


def attention_kernel(info_ref, qkv_ref, other_ref, start_ref, out_ref, *, factor):
    block = pl.program_id(0)
    count = info_ref.shape[0] - 1
    part = info_ref[count]
    half = out_ref.shape[1]
    span = 2 * half
    query = qkv_ref[block, 0]
    start = start_ref[0]
    row = block * span + part * half + lax.broadcasted_iota(jnp.int32, (half, 1), 0)
    lane = lax.broadcasted_iota(jnp.int32, (1, span), 1)
    place = jnp.where(lane < half, lane + part * half, lane - part * half)

    def body(at, carry):
        peak, denom, accum = carry
        keys = jnp.concatenate([qkv_ref[at, 1], other_ref[at, 0]], axis=0)
        values = jnp.concatenate([qkv_ref[at, 2], other_ref[at, 1]], axis=0)
        scores = (
            lax.dot_general(query, keys, (((1,), (1,)), ((), ())), preferred_element_type=F32)
            * factor
        )
        column = place + at * span
        allowed = (column >= start) & (column <= row)
        scores = jnp.where(allowed, scores, -1e30)
        new_peak = jnp.maximum(peak, jnp.max(scores, axis=1, keepdims=True))
        weights = jnp.where(allowed, jnp.exp2(scores - new_peak), 0.0)
        keep = jnp.exp2(peak - new_peak)
        denom = denom * keep + jnp.sum(weights, axis=1, keepdims=True)
        accum = accum * keep + dot(weights.astype(BF16), values)
        return new_peak, denom, accum

    first = (
        jnp.full((half, 1), -1e30, F32),
        jnp.zeros((half, 1), F32),
        jnp.zeros((half, HD), F32),
    )
    _, denom, accum = lax.fori_loop(info_ref[block], block + 1, body, first)
    out_ref[0] = (accum / denom).astype(BF16)


def attention_call(info, qkv, other, start):
    count, _, half, _ = qkv.shape
    whole = lambda a: pl.BlockSpec(a.shape, lambda b, info: (0,) * a.ndim)
    return pl.pallas_call(
        functools.partial(attention_kernel, factor=HD ** (-0.5) * math.log2(math.e)),
        out_shape=jax.ShapeDtypeStruct((count, half, HD), BF16),
        grid_spec=pltpu.PrefetchScalarGridSpec(
            num_scalar_prefetch=1,
            grid=(count,),
            in_specs=[
                whole(qkv),
                whole(other),
                pl.BlockSpec((1, half, 1), lambda b, info: (b, 0, 0)),
            ],
            out_specs=pl.BlockSpec((1, half, HD), lambda b, info: (b, 0, 0)),
        ),
        compiler_params=pltpu.CompilerParams(vmem_limit_bytes=VMEM_LIMIT),
        cost_estimate=pl.CostEstimate(
            flops=4 * count * half * count * half * HD,
            bytes_accessed=6 * count * half * HD * 2,
            transcendentals=count * half * count * half,
        ),
        name="attention",
    )(info, qkv, other, start)


def middle_kernel(where_ref, *refs, ring, split):
    parts = refs[:ring]
    (
        tok_ref,
        w_out_ref,
        gain_ref,
        gate_ref,
        up_ref,
        wp_ref,
        proj_ref,
        student_ref,
        hidden_ref,
        own_ref,
        diff_ref,
        attended,
        mixed,
        total,
    ) = refs[ring:]
    step = pl.program_id(0)
    rows, depth = mixed.shape
    tiles = depth // COLS
    width = own_ref.shape[1]

    @pl.when(step == 0)
    def _():
        piece = rows // split
        for s, part in enumerate(parts):
            heads = part.shape[0] // split
            for h in range(heads):
                for p in range(split):
                    at = (s * heads + h) * HD
                    attended[p * piece : (p + 1) * piece, at : at + HD] = part[h * split + p]

    @pl.when(step < tiles)
    def _():
        at = pl.ds(pl.multiple_of(step * COLS, COLS), COLS)
        weight = w_out_ref[0].reshape(depth, COLS)
        result = tok_ref[...].astype(F32) + dot(attended[...], weight)
        mixed[:, at] = result.astype(BF16)

    @pl.when(step == tiles)
    def _():
        values = mixed[...].astype(F32)
        attended[...] = (rms_scale(values) * gain_ref[...]).astype(BF16)
        own = mixed[:, pl.ds(pl.multiple_of(where_ref[0] * width, 128), width)]
        own_ref[...] = own
        total[...] = student_ref[...] - dot(own, proj_ref[...])

    @pl.when(step >= tiles)
    def _():
        gate = dot(attended[...], gate_ref[...])
        up = dot(attended[...], up_ref[...])
        hidden = (gate * jax.nn.sigmoid(gate) * up).astype(BF16)
        hidden_ref[...] = hidden
        total[...] -= dot(hidden, wp_ref[...])

    @pl.when(step == pl.num_programs(0) - 1)
    def _():
        diff_ref[...] = total[...].astype(BF16)


def middle_call(where, parts, tok, w_out, gain, w_gate, w_up, wp, projector, student, split):
    rows, depth = tok.shape
    ring = len(parts)
    units = w_gate.shape[1]
    out_tiles, unit_tiles = depth // COLS, units // COLS
    width = depth // ring
    sd = projector.shape[1]
    whole = lambda shape: pl.BlockSpec(shape, lambda j, w: (0,) * len(shape))
    early = lambda j: jnp.minimum(j, out_tiles - 1)
    late = lambda j: jnp.maximum(j - out_tiles, 0)
    return pl.pallas_call(
        functools.partial(middle_kernel, ring=ring, split=split),
        out_shape=(
            jax.ShapeDtypeStruct((rows, units), BF16),
            jax.ShapeDtypeStruct((rows, width), BF16),
            jax.ShapeDtypeStruct((rows, sd), BF16),
        ),
        grid_spec=pltpu.PrefetchScalarGridSpec(
            num_scalar_prefetch=1,
            grid=(out_tiles + unit_tiles,),
            in_specs=[whole(parts[0].shape)] * ring
            + [
                pl.BlockSpec((rows, COLS), lambda j, w: (0, early(j))),
                pl.BlockSpec((1,) + w_out.shape[1:], lambda j, w: (early(j), 0, 0, 0)),
                whole((1, depth)),
                pl.BlockSpec((depth, COLS), lambda j, w: (0, late(j))),
                pl.BlockSpec((depth, COLS), lambda j, w: (0, late(j))),
                pl.BlockSpec((COLS, sd), lambda j, w: (late(j), 0)),
                pl.BlockSpec((width, sd), lambda j, w: (w[0], 0)),
                whole((rows, sd)),
            ],
            out_specs=(
                pl.BlockSpec((rows, COLS), lambda j, w: (0, late(j))),
                whole((rows, width)),
                whole((rows, sd)),
            ),
            scratch_shapes=[
                pltpu.VMEM((rows, depth), BF16),
                pltpu.VMEM((rows, depth), BF16),
                pltpu.VMEM((rows, sd), F32),
            ],
        ),
        compiler_params=pltpu.CompilerParams(vmem_limit_bytes=VMEM_LIMIT),
        cost_estimate=pl.CostEstimate(
            flops=2 * rows * depth * (depth + 2 * units) + 2 * rows * sd * (units + width),
            bytes_accessed=2 * depth * (depth + 2 * units),
            transcendentals=rows * units,
        ),
        name="middle",
    )(where, *parts, tok, w_out, gain, w_gate, w_up, wp, projector, student)


def down_kernel(hidden_ref, weight_ref, out_ref):
    out_ref[0] = dot(hidden_ref[...], weight_ref[...]).astype(BF16)


def down_call(hidden, w_down, ring):
    rows, units = hidden.shape
    depth = w_down.shape[1]
    width = depth // ring
    cols = min(COLS, width)
    per = width // cols
    return pl.pallas_call(
        down_kernel,
        out_shape=jax.ShapeDtypeStruct((ring, rows, width), BF16),
        grid=(depth // cols,),
        in_specs=[
            pl.BlockSpec((rows, units), lambda j: (0, 0)),
            pl.BlockSpec((units, cols), lambda j: (0, j)),
        ],
        out_specs=pl.BlockSpec((1, rows, cols), lambda j: (j // per, 0, j % per)),
        compiler_params=pltpu.CompilerParams(vmem_limit_bytes=VMEM_LIMIT),
        cost_estimate=pl.CostEstimate(
            flops=2 * rows * units * depth, bytes_accessed=2 * units * depth, transcendentals=0
        ),
        name="down",
    )(hidden, w_down)


def grad_sum(flat):
    size = lax.axis_size("dp")
    rows, cols = flat.shape
    me = lax.axis_index("dp")
    core = me % 2
    swap = [(i, i ^ 1) for i in range(size)]
    halves = flat.reshape(2, rows // 2, cols)
    theirs = lax.ppermute(
        lax.dynamic_index_in_dim(halves, 1 - core, 0, False).astype(BF16), "dp", swap
    )
    mine = lax.dynamic_index_in_dim(halves, core, 0, False) + theirs.astype(F32)
    chips = size // 2
    groups = [[2 * c + k for c in range(chips)] for k in range(2)]
    shares = mine.astype(BF16).reshape(chips, rows // size, cols)
    got = lax.all_to_all(shares, "dp", 0, 0, axis_index_groups=groups)
    own = jnp.sum(got.astype(F32), axis=0).astype(BF16)
    chip = me // 2
    slots = jnp.zeros((chips, rows // size, cols), BF16)
    slots = lax.dynamic_update_index_in_dim(slots, own, chip, 0)
    for flip in range(1, chips):
        piece = lax.ppermute(own, "dp", [(i, i ^ (2 * flip)) for i in range(size)])
        slots = lax.dynamic_update_index_in_dim(slots, piece, chip ^ flip, 0)
    half = slots.reshape(rows // 2, cols)
    other = lax.ppermute(half, "dp", swap)
    low = jnp.where(core == 0, half, other)
    high = jnp.where(core == 0, other, half)
    return jnp.concatenate([low, high], axis=0).astype(F32)


def dense_attention(qkv, series_ids, first_row, split):
    share, _, piece, _ = qkv.shape
    heads = share // split
    mine = qkv.reshape(heads, split, 3, piece, HD).transpose(2, 0, 1, 3, 4)
    mine = mine.reshape(3, heads, split * piece, HD)
    rows = split * piece
    keys, values = lax.all_gather(mine[1:], "dp", axis=2, tiled=True)
    column = jnp.arange(keys.shape[1], dtype=jnp.int32)
    row = first_row + jnp.arange(rows, dtype=jnp.int32)
    own_series = lax.dynamic_slice_in_dim(series_ids, first_row, rows, 0)
    allowed = (column[None, :] <= row[:, None]) & (series_ids[None, :] == own_series[:, None])
    scores = jnp.einsum("hqd,hkd->hqk", mine[0], keys, preferred_element_type=F32) * HD ** (-0.5)
    scores = jnp.where(allowed[None], scores, -1e30)
    weights = jnp.where(allowed[None], jnp.exp(scores - jnp.max(scores, 2, keepdims=True)), 0.0)
    denom = jnp.sum(weights, axis=2, keepdims=True)
    mixed = jnp.einsum("hqk,hkd->hqd", weights.astype(BF16), values, preferred_element_type=F32)
    return (mixed / denom).astype(BF16).reshape(share, piece, HD)


def local(
    tokens,
    series_ids,
    offsets,
    norm_gain,
    mlp_gain,
    w_query,
    w_key,
    w_value,
    w_out,
    w_gate,
    w_up,
    w_down,
    projector,
    student_in,
    s_gate,
    s_up,
    s_down,
):
    rows = tokens.shape[0]
    heads = w_query.shape[1] // HD
    depth = w_query.shape[0]
    dp, ring = lax.axis_size("dp"), lax.axis_size("tensor")
    here, level = lax.axis_index("dp"), lax.axis_index("tensor")
    total_rows = rows * dp
    spread = dp == 2 * heads
    split = dp // heads if spread else 1

    token_blocks = ring_gather(tokens, "tensor")
    source = (level - jnp.arange(ring, dtype=jnp.int32)) % ring

    angles = offsets.astype(F32)[:, None] * frequencies(HD)[None, :]
    cosine, sine = jnp.cos(angles), jnp.sin(angles)
    cosine = jnp.concatenate([cosine, cosine], axis=1)
    sine = jnp.concatenate([-sine, sine], axis=1)
    student_full = student_in.astype(F32)
    student_normed = rms_scale(student_full).astype(BF16)
    s_gate_out = dot(student_normed, s_gate)
    s_up_out = dot(student_normed, s_up)
    sigmoid_gate = jax.nn.sigmoid(s_gate_out)
    s_hidden = (s_gate_out * sigmoid_gate * s_up_out).astype(BF16)
    student_part = dot(s_hidden, s_down)
    projected = dot(w_down, projector).astype(BF16)

    qkv, tok_full = qkv_call(
        source,
        token_blocks,
        norm_gain[None, :],
        cosine,
        sine,
        w_query,
        w_key,
        w_value,
        split,
    )

    slice_cols = depth // dp
    w_slice = lax.dynamic_slice_in_dim(w_out, here * slice_cols, slice_cols, 1)
    w_slice, _ = lax.optimization_barrier((w_slice, token_blocks[-1]))
    w_ring = jnp.stack(ring_gather(w_slice, "tensor"))
    w_all = lax.all_gather(w_ring, "dp", axis=0, tiled=False)
    if slice_cols != COLS:
        w_all = w_all.transpose(1, 2, 0, 3).reshape(ring, depth // ring, depth // COLS, COLS)
        w_all = w_all.transpose(2, 0, 1, 3)

    if spread:
        qkv = lax.all_to_all(qkv, "dp", 0, 0)
        other = lax.ppermute(qkv[:, 1:], "dp", [(i, i ^ 1) for i in range(dp)])
        below = jnp.sum(
            series_ids[None, :] < jnp.arange(8, dtype=jnp.int32)[:, None], axis=1, dtype=jnp.int32
        )
        mine = lax.dynamic_index_in_dim(
            series_ids.reshape(dp, 2, rows // 2), here % 2, 1, keepdims=False
        )
        start = jnp.sum(
            jnp.where(mine[:, :, None] == jnp.arange(8, dtype=jnp.int32), below, 0), axis=2
        )
        info = jnp.concatenate([start[:, 0] // rows, (here % 2)[None].astype(jnp.int32)])
        attended = attention_call(info, qkv, other, start[:, :, None])
        attended = lax.all_to_all(attended, "dp", 0, 0)
    else:
        attended = dense_attention(qkv, series_ids, here * rows, split)

    parts = ring_gather(attended, "tensor")
    hidden, mixed_own, diff_part = middle_call(
        level.astype(jnp.int32)[None],
        parts,
        tok_full,
        w_all,
        mlp_gain[None, :],
        w_gate,
        w_up,
        projected,
        projector,
        student_part,
        split,
    )

    sd = student_in.shape[1]
    piece = rows // ring
    pieces = lax.all_to_all(diff_part.reshape(ring, piece, sd), "tensor", 0, 0)
    own_student = lax.dynamic_slice_in_dim(student_in, level * piece, piece, 0).astype(F32)
    difference = own_student + jnp.sum(pieces.astype(F32), axis=0)
    scaled_own = (difference * total_rows ** (-0.5)).astype(BF16)
    scaled_slots = jnp.zeros((ring, piece, sd), BF16)
    for s, block in enumerate(ring_gather(scaled_own, "tensor")):
        scaled_slots = lax.dynamic_update_index_in_dim(scaled_slots, block, source[s], 0)
    scaled = scaled_slots.reshape(rows, sd)

    mlp_part = down_call(hidden, w_down, ring)
    mlp_own = lax.psum_scatter(mlp_part, "tensor", scatter_dimension=0, tiled=False).astype(F32)
    teacher_out = (mixed_own.astype(F32) + mlp_own).astype(BF16)

    grad_down = jnp.einsum("rk,rc->kc", s_hidden, scaled, preferred_element_type=F32)
    grad_hidden = jnp.einsum("rc,kc->rk", scaled, s_down, preferred_element_type=F32)
    grad_up_in = (grad_hidden * s_gate_out * sigmoid_gate).astype(BF16)
    grad_gate_in = (
        grad_hidden * s_up_out * sigmoid_gate * (1.0 + s_gate_out * (1.0 - sigmoid_gate))
    ).astype(BF16)
    grad_gate = jnp.einsum("rc,rk->ck", student_normed, grad_gate_in, preferred_element_type=F32)
    grad_up = jnp.einsum("rc,rk->ck", student_normed, grad_up_in, preferred_element_type=F32)

    wide = scaled.astype(F32)
    error = jnp.full((8, 128), jnp.sum(wide * wide), F32)
    bit = 1
    while bit < dp:
        error = error + lax.ppermute(error, "dp", [(i, i ^ bit) for i in range(dp)])
        bit *= 2
    error = error[0, 0] / sd

    units = s_gate.shape[1]
    flat = jnp.concatenate(
        [grad_gate.reshape(-1, sd), grad_up.reshape(-1, sd), grad_down.reshape(-1, sd)], axis=0
    )
    flat = grad_sum(flat)
    third = flat.shape[0] // 3
    return (
        teacher_out,
        flat[:third].reshape(sd, units),
        flat[third : 2 * third].reshape(sd, units),
        flat[2 * third :].reshape(units, sd),
        error,
    )


def solution(mesh):
    in_specs = (
        P("dp", "tensor"),
        P(),
        P("dp"),
        P(),
        P(),
        P(None, "tensor"),
        P(None, "tensor"),
        P(None, "tensor"),
        P("tensor", None),
        P(None, "tensor"),
        P(None, "tensor"),
        P("tensor", None),
        P(),
        P("dp", None),
        P(None, "tensor"),
        P(None, "tensor"),
        P("tensor", None),
    )
    out_specs = (P("dp", "tensor"), P(None, "tensor"), P(None, "tensor"), P("tensor", None), P())
    return jax.shard_map(local, mesh=mesh, in_specs=in_specs, out_specs=out_specs, check_vma=False)
```

```python
import functools
import math

import jax
import jax.numpy as jnp
from jax import lax
from jax.experimental import pallas as pl
from jax.experimental.pallas import tpu as pltpu
from jax.sharding import PartitionSpec as P

HD = 128
COLS = 256
NOTE = 16
SERIES = 8
F32 = jnp.float32
BF16 = jnp.bfloat16
MIB = 1024 * 1024


def rms_scale(values):
    return values * lax.rsqrt(jnp.mean(values * values, axis=-1, keepdims=True) + 1e-05)


def frequencies(head_dim):
    indices = jnp.arange(head_dim // 2).astype(jnp.float32)
    return jnp.exp(-jnp.log(500000.0) * 2.0 * indices / head_dim)


def rotary(inputs, angles):
    half_dim = inputs.shape[-1] // 2
    cosine = jnp.cos(angles)
    sine = jnp.sin(angles)
    first_half = inputs[..., :half_dim]
    second_half = inputs[..., half_dim:]
    return jnp.concatenate(
        [first_half * cosine - second_half * sine, first_half * sine + second_half * cosine],
        axis=-1,
    )


def general(
    tokens,
    series_ids,
    offsets,
    norm_gain,
    mlp_gain,
    w_query,
    w_key,
    w_value,
    w_out,
    w_gate,
    w_up,
    w_down,
    projector,
    student_in,
    s_gate,
    s_up,
    s_down,
):
    row_count = tokens.shape[0]
    heads_dev = w_query.shape[1] // HD
    first_row = lax.axis_index("dp") * row_count
    tokens_full = lax.all_gather(tokens, "tensor", axis=1, tiled=True).astype(jnp.float32)
    normed = (rms_scale(tokens_full) * norm_gain).astype(jnp.bfloat16)
    angles = offsets.astype(jnp.float32)[:, None, None] * frequencies(HD)[None, None, :]
    queries = rotary(
        jnp.dot(normed, w_query, preferred_element_type=jnp.float32).reshape(
            row_count, heads_dev, HD
        ),
        angles,
    ).astype(jnp.bfloat16)
    keys_rot = rotary(
        jnp.dot(normed, w_key, preferred_element_type=jnp.float32).reshape(
            row_count, heads_dev, HD
        ),
        angles,
    ).astype(jnp.bfloat16)
    values_mine = jnp.dot(normed, w_value, preferred_element_type=jnp.float32).astype(jnp.bfloat16)
    keys_flat = keys_rot.reshape(row_count, heads_dev * HD)
    query_pos = first_row + jnp.arange(row_count, dtype=jnp.int32)
    query_series = lax.dynamic_slice_in_dim(series_ids, first_row, row_count, 0)
    factor = HD ** (-0.5)
    peak = jnp.full((row_count, heads_dev), -1e30, jnp.float32)
    key_block = lax.all_gather(keys_flat, "dp", axis=0, tiled=True)
    value_block = lax.all_gather(values_mine, "dp", axis=0, tiled=True)
    count = key_block.shape[0]
    key_pos = jnp.arange(count, dtype=jnp.int32)
    allowed = (
        (key_pos[None, :] >= 0)
        & (key_pos[None, :] <= query_pos[:, None])
        & (series_ids[None, :] == query_series[:, None])
    )
    scores = (
        jnp.einsum(
            "qhd,khd->qhk",
            queries,
            key_block.reshape(count, heads_dev, HD),
            preferred_element_type=jnp.float32,
        )
        * factor
    )
    scores = jnp.where(allowed[:, None, :], scores, -1e30)
    new_peak = jnp.maximum(peak, jnp.max(scores, axis=2))
    weights = jnp.where(allowed[:, None, :], jnp.exp(scores - new_peak[:, :, None]), 0.0)
    denom = jnp.sum(weights, axis=2)
    accum = jnp.einsum(
        "qhk,khd->qhd",
        weights.astype(jnp.bfloat16),
        value_block.reshape(count, heads_dev, HD),
        preferred_element_type=jnp.float32,
    )
    peak, denom, accum = (new_peak, denom, accum)
    attended = (accum / denom[:, :, None]).astype(jnp.bfloat16).reshape(row_count, heads_dev * HD)
    partial_out = jnp.dot(attended, w_out, preferred_element_type=jnp.float32)
    own_sum = lax.psum_scatter(
        partial_out.astype(jnp.bfloat16), "tensor", scatter_dimension=1, tiled=True
    ).astype(jnp.float32)
    mixed_own = (tokens.astype(jnp.float32) + own_sum).astype(jnp.bfloat16)
    mixed = lax.all_gather(mixed_own, "tensor", axis=1, tiled=True)
    normed_two = (rms_scale(mixed.astype(jnp.float32)) * mlp_gain).astype(jnp.bfloat16)
    gate_out = jnp.dot(normed_two, w_gate, preferred_element_type=jnp.float32)
    up_out = jnp.dot(normed_two, w_up, preferred_element_type=jnp.float32)
    hidden = (jax.nn.silu(gate_out) * up_out).astype(jnp.bfloat16)
    mlp_part = jnp.dot(hidden, w_down, preferred_element_type=jnp.float32)
    mlp_own = lax.psum_scatter(
        mlp_part.astype(jnp.bfloat16), "tensor", scatter_dimension=1, tiled=True
    ).astype(jnp.float32)
    teacher_out = (mixed_own.astype(jnp.float32) + mlp_own).astype(jnp.bfloat16)
    student_full = student_in.astype(jnp.float32)
    student_normed = rms_scale(student_full).astype(jnp.bfloat16)
    s_gate_out = jnp.dot(student_normed, s_gate, preferred_element_type=jnp.float32)
    s_up_out = jnp.dot(student_normed, s_up, preferred_element_type=jnp.float32)
    sigmoid_gate = jax.nn.sigmoid(s_gate_out)
    s_hidden = (s_gate_out * sigmoid_gate * s_up_out).astype(jnp.bfloat16)
    student_part = jnp.dot(s_hidden, s_down, preferred_element_type=jnp.float32)
    teacher_full = lax.all_gather(teacher_out, "tensor", axis=1, tiled=True)
    target = jnp.dot(teacher_full, projector, preferred_element_type=jnp.float32)
    student_summed = lax.psum(student_part.astype(jnp.bfloat16), "tensor").astype(jnp.float32)
    difference = student_full + student_summed - target
    total_rows = row_count * lax.axis_size("dp")
    scaled = (difference * total_rows ** (-0.5)).astype(jnp.bfloat16)
    grad_down_part = jnp.einsum("rk,rc->kc", s_hidden, scaled, preferred_element_type=jnp.float32)
    grad_hidden = jnp.einsum("rc,kc->rk", scaled, s_down, preferred_element_type=jnp.float32)
    grad_up_in = (grad_hidden * s_gate_out * sigmoid_gate).astype(jnp.bfloat16)
    grad_gate_in = (
        grad_hidden * s_up_out * sigmoid_gate * (1.0 + s_gate_out * (1.0 - sigmoid_gate))
    ).astype(jnp.bfloat16)
    grad_gate_part = jnp.einsum(
        "rc,rk->ck", student_normed, grad_gate_in, preferred_element_type=jnp.float32
    )
    grad_up_part = jnp.einsum(
        "rc,rk->ck", student_normed, grad_up_in, preferred_element_type=jnp.float32
    )
    square_sum = jnp.sum(difference * difference)
    grad_gate, grad_up, grad_down, square_total = (
        lax.psum(grad_gate_part.astype(jnp.bfloat16), "dp").astype(jnp.float32),
        lax.psum(grad_up_part.astype(jnp.bfloat16), "dp").astype(jnp.float32),
        lax.psum(grad_down_part.astype(jnp.bfloat16), "dp").astype(jnp.float32),
        lax.psum(square_sum.astype(jnp.bfloat16), "dp").astype(jnp.float32),
    )
    error = square_total / (total_rows * difference.shape[1])
    return (teacher_out, grad_gate, grad_up, grad_down, error)


def dot(a, b):
    return jnp.dot(a, b, preferred_element_type=F32)


def dot_over(a, b, dims):
    return lax.dot_general(a, b, ((dims[:1], dims[1:]), ((), ())), preferred_element_type=F32)


def params(limit):
    return pltpu.CompilerParams(vmem_limit_bytes=limit * MIB)


def whole(shape):
    return pl.BlockSpec(shape, lambda *_: (0,) * len(shape))


def cost(flops, moved, transcendentals=0):
    return pl.CostEstimate(
        flops=int(flops), bytes_accessed=int(moved), transcendentals=int(transcendentals)
    )


def rotate(head, cos_ref, sin_ref):
    return head * cos_ref[...] + pltpu.roll(head, HD // 2, 1) * sin_ref[...]


def kv_kernel(info_ref, *refs, ring, heads):
    blocks = [refs[:ring], refs[ring : 2 * ring]]
    gain_ref, cos_ref, sin_ref, wk_ref, wv_ref = refs[2 * ring : 2 * ring + 5]
    outs = refs[2 * ring + 5 : 2 * ring + 5 + heads]
    tok_ref, normed, made = refs[2 * ring + 5 + heads :]
    step = pl.program_id(0)
    half, width = blocks[0][0].shape
    depth = gain_ref.shape[1]

    @pl.when(step == 0)
    def _():
        for k in range(2):
            mine = slice(k * half, (k + 1) * half)
            total = jnp.zeros((half, 1), F32)
            for block in blocks[k]:
                part = block[...].astype(F32)
                total += jnp.sum(part * part, axis=1, keepdims=True)
            scale = lax.rsqrt(total / depth + 1e-05)
            for s, block in enumerate(blocks[k]):
                at = pl.ds(pl.multiple_of(info_ref[s] * width, 128), width)
                part = block[...]
                tok_ref[mine, at] = part
                normed[mine, at] = (part.astype(F32) * scale * gain_ref[:, at]).astype(BF16)
        result = dot(normed[...], wk_ref[...])
        for h in range(heads):
            head = rotate(result[:, h * HD : (h + 1) * HD], cos_ref, sin_ref)
            made[h, 0] = head.astype(BF16)

    @pl.when(step == 1)
    def _():
        result = dot(normed[...], wv_ref[...])
        for h in range(heads):
            made[h, 1] = result[:, h * HD : (h + 1) * HD].astype(BF16)
        for f in range(heads):
            outs[f][...] = made[info_ref[ring] ^ f]


def kv_call(info, blocks, gain, cosine, sine, w_key, w_value):
    half, width = blocks[0][0].shape
    rows, ring = 2 * half, len(blocks[0])
    depth, out_cols = w_key.shape
    heads = out_cols // HD
    result = pl.pallas_call(
        functools.partial(kv_kernel, ring=ring, heads=heads),
        out_shape=[jax.ShapeDtypeStruct((2, rows, HD), BF16)] * heads
        + [jax.ShapeDtypeStruct((rows, depth), BF16)] * 2,
        grid_spec=pltpu.PrefetchScalarGridSpec(
            num_scalar_prefetch=1,
            grid=(2,),
            in_specs=[whole((half, width))] * (2 * ring)
            + [whole((1, depth)), whole((rows, HD)), whole((rows, HD))]
            + [whole((depth, out_cols))] * 2,
            out_specs=[whole((2, rows, HD))] * heads + [whole((rows, depth))] * 2,
            scratch_shapes=[pltpu.VMEM((heads, 2, rows, HD), BF16)],
        ),
        compiler_params=params(36),
        cost_estimate=cost(4 * rows * depth * out_cols, 4 * depth * out_cols),
        name="keys_values",
    )(info, *blocks[0], *blocks[1], gain, cosine, sine, w_key, w_value)
    return result[:heads], result[heads], result[heads + 1]


def query_kernel(info_ref, normed_ref, cos_ref, sin_ref, wq_ref, *refs, heads):
    outs, made = refs[:heads], refs[heads]
    result = dot(normed_ref[...], wq_ref[...])
    for h in range(heads):
        head = rotate(result[:, h * HD : (h + 1) * HD], cos_ref, sin_ref)
        made[h] = head.astype(BF16)
    for f in range(heads):
        outs[f][...] = made[info_ref[info_ref.shape[0] - 1] ^ f]


def query_call(info, normed, cosine, sine, w_query):
    rows, depth = normed.shape
    out_cols = w_query.shape[1]
    heads = out_cols // HD
    return pl.pallas_call(
        functools.partial(query_kernel, heads=heads),
        out_shape=[jax.ShapeDtypeStruct((rows, HD), BF16)] * heads,
        grid_spec=pltpu.PrefetchScalarGridSpec(
            num_scalar_prefetch=1,
            grid=(1,),
            in_specs=[
                whole((rows, depth)),
                whole((rows, HD)),
                whole((rows, HD)),
                whole((depth, out_cols)),
            ],
            out_specs=[whole((rows, HD))] * heads,
            scratch_shapes=[pltpu.VMEM((heads, rows, HD), BF16)],
        ),
        compiler_params=params(24),
        cost_estimate=cost(2 * rows * depth * out_cols, 2 * depth * out_cols),
        name="queries",
    )(info, normed, cosine, sine, w_query)


def attention_kernel(info_ref, *refs, chips):
    queries, own, other = refs[:chips], refs[chips : 2 * chips], refs[2 * chips : 3 * chips]
    outs = refs[3 * chips : 4 * chips]
    keys_all, values_all = refs[4 * chips :]
    chip, core = info_ref[SERIES], info_ref[SERIES + 1]
    half = outs[0].shape[1]
    span = 2 * half
    for f in range(chips):
        for source, side in ((own[f], core), (other[f], 1 - core)):
            at = pl.ds(pl.multiple_of(side * half, half), half)
            for odd, index in ((0, side), (1, 1 - side)):
                block = 2 * (chip ^ f) + odd
                keys_all[block, at, :] = source[0, index]
                values_all[block, :, at] = source[1, index].T

    def first_of(row):
        found = jnp.int32(0)
        for s in range(SERIES):
            edge = info_ref[s]
            found = jnp.where(edge <= row, jnp.maximum(found, edge), found)
        return found

    for f in range(chips):
        even = 2 * (chip ^ f)
        first_row = even * span + core * half
        last_row = first_row + span + half - 1
        query = jnp.concatenate([queries[f][core], queries[f][1 - core]], axis=0)
        place = lax.broadcasted_iota(jnp.int32, (1, span), 1)
        row = first_row + place + jnp.where(place < half, 0, half)
        start = jnp.zeros((1, span), jnp.int32)
        for s in range(SERIES):
            edge = info_ref[s]
            start = jnp.where(edge <= row, jnp.maximum(start, edge), start)
        lane = lax.broadcasted_iota(jnp.int32, (span, 1), 0)

        def body(at, carry, masked, query=query, row=row, start=start, lane=lane):
            peak, denom, accum = carry
            scores = dot_over(keys_all[at], query, (1, 1))
            if masked:
                column = lane + at * span
                allowed = (column >= start) & (column <= row)
                scores = jnp.where(allowed, scores, -1e30)
            new_peak = jnp.maximum(peak, jnp.max(scores, axis=0, keepdims=True))
            weights = jnp.exp2(scores - new_peak)
            if masked:
                weights = jnp.where(allowed, weights, 0.0)
            keep = jnp.exp2(peak - new_peak)
            denom = denom * keep + jnp.sum(weights, axis=0, keepdims=True)
            accum = accum * keep + dot(values_all[at], weights.astype(BF16))
            return new_peak, denom, accum

        begin = first_of(first_row) // span
        full = jnp.minimum(even, (first_of(last_row) + span - 1) // span)
        carry = (
            jnp.full((1, span), -1e30, F32),
            jnp.zeros((1, span), F32),
            jnp.zeros((HD, span), F32),
        )
        carry = lax.fori_loop(begin, full, functools.partial(body, masked=True), carry)
        carry = lax.fori_loop(full, even, functools.partial(body, masked=False), carry)
        peak, denom, accum = body(even, carry, masked=True)
        outs[f][core] = (accum[:, :half] / denom[:, :half]).T.astype(BF16)
        carry = (peak[:, half:], denom[:, half:], accum[:, half:])
        _, denom, accum = body(
            even + 1, carry, True, query[half:], row[:, half:], start[:, half:], lane
        )
        outs[f][1 - core] = (accum / denom).T.astype(BF16)


def attention_call(info, queries, own, other):
    chips = len(queries)
    _, half, _ = queries[0].shape
    return pl.pallas_call(
        functools.partial(attention_kernel, chips=chips),
        out_shape=[jax.ShapeDtypeStruct((2, half, HD), BF16)] * chips,
        grid_spec=pltpu.PrefetchScalarGridSpec(
            num_scalar_prefetch=1,
            grid=(1,),
            in_specs=[whole((2, half, HD))] * chips + [whole((2, 2, half, HD))] * (2 * chips),
            out_specs=[whole((2, half, HD))] * chips,
            scratch_shapes=[
                pltpu.VMEM((2 * chips, 2 * half, HD), BF16),
                pltpu.VMEM((2 * chips, HD, 2 * half), BF16),
            ],
        ),
        compiler_params=params(30),
        cost_estimate=cost(
            4 * chips * half * 4 * chips * half * HD,
            12 * chips * half * HD * 2,
            2 * chips * half * 4 * chips * half // 2,
        ),
        name="attention",
    )(info, *queries, *own, *other)


def middle_kernel(info_ref, *refs, ring, chips):
    parts = [refs[:ring], refs[ring : 2 * ring]]
    refs = refs[2 * ring :]
    tok_ref, w_own_ref = refs[:2]
    near_refs, far_refs = refs[2:4], refs[4:6]
    gain_ref, gate_ref, up_ref, wp_ref, proj_ref, student_ref = refs[6:12]
    hidden_ref, own_ref = refs[12:14]
    pieces = refs[14 : 14 + ring]
    attended, mixed, total = refs[14 + ring :]
    step = pl.program_id(0)
    level, chip, core = info_ref[0], info_ref[1], info_ref[2]
    rows, depth = mixed.shape
    half = rows // 2
    width = own_ref.shape[1]

    @pl.when(step == 0)
    def _():
        for k in range(2):
            for s, part in enumerate(parts[k]):
                for i in range(part.shape[0]):
                    at = s * width + (chip ^ (k * part.shape[0] + i)) * HD
                    at = pl.ds(pl.multiple_of(at, HD), HD)
                    attended[:half, at] = part[i, 0]
                    attended[half:, at] = part[i, 1]

    @pl.when(step < chips)
    def _():
        for w_refs, side in ((near_refs, core), (far_refs, 1 - core)):
            here = pl.ds(pl.multiple_of(side * COLS, COLS), COLS)
            result = tok_ref[:, here].astype(F32) + dot(attended[:, :width], w_own_ref[:, here])
            done = width
            for w_ref in w_refs:
                some = w_ref.shape[1] * width
                weight = w_ref[0].reshape(some, COLS)
                result += dot(attended[:, done : done + some], weight)
                done += some
            at = pl.ds(pl.multiple_of((2 * step + side) * COLS, COLS), COLS)
            mixed[:, at] = result.astype(BF16)

    @pl.when(step == chips)
    def _():
        values = mixed[...].astype(F32)
        attended[...] = (rms_scale(values) * gain_ref[...]).astype(BF16)
        own = mixed[:, pl.ds(pl.multiple_of(level * width, 128), width)]
        own_ref[...] = own
        total[...] = student_ref[...] - dot(own, proj_ref[...])

    @pl.when(step >= chips)
    def _():
        gate = dot(attended[...], gate_ref[...])
        up = dot(attended[...], up_ref[...])
        hidden = (gate * jax.nn.sigmoid(gate) * up).astype(BF16)
        hidden_ref[...] = hidden
        total[...] -= dot(hidden, wp_ref[...])

    @pl.when(step == pl.num_programs(0) - 1)
    def _():
        size = rows // ring
        for s in range(ring):
            at = pl.ds(pl.multiple_of((level + s) % ring * size, size), size)
            pieces[s][...] = total[at, :].astype(BF16)


def middle_call(info, parts, tok, w_out, near, far, gain, w_gate, w_up, wp, projector, student):
    rows, depth = tok.shape
    ring, chips = len(parts[0]), near[0].shape[0]
    units = w_gate.shape[1]
    wide = 2 * COLS
    width = depth // ring
    sd = projector.shape[1]
    early = lambda j: jnp.minimum(j, chips - 1)
    late = lambda j: jnp.maximum(j - chips, 0)
    gathered = [
        pl.BlockSpec((1,) + a.shape[1:], lambda j, info: (early(j) ^ info[1], 0, 0, 0))
        for a in near
    ]
    result = pl.pallas_call(
        functools.partial(middle_kernel, ring=ring, chips=chips),
        out_shape=[
            jax.ShapeDtypeStruct((rows, units), BF16),
            jax.ShapeDtypeStruct((rows, width), BF16),
        ]
        + [jax.ShapeDtypeStruct((rows // ring, sd), BF16)] * ring,
        grid_spec=pltpu.PrefetchScalarGridSpec(
            num_scalar_prefetch=1,
            grid=(chips + units // wide,),
            in_specs=[whole(parts[0][0].shape)] * (2 * ring)
            + [
                pl.BlockSpec((rows, wide), lambda j, info: (0, early(j))),
                pl.BlockSpec((width, wide), lambda j, info: (0, early(j))),
                *gathered,
                *gathered,
                whole((1, depth)),
                pl.BlockSpec((depth, wide), lambda j, info: (0, late(j))),
                pl.BlockSpec((depth, wide), lambda j, info: (0, late(j))),
                pl.BlockSpec((wide, sd), lambda j, info: (late(j), 0)),
                pl.BlockSpec((width, sd), lambda j, info: (info[0], 0)),
                whole((rows, sd)),
            ],
            out_specs=[
                pl.BlockSpec((rows, wide), lambda j, info: (0, late(j))),
                whole((rows, width)),
            ]
            + [whole((rows // ring, sd))] * ring,
            scratch_shapes=[
                pltpu.VMEM((rows, depth), BF16),
                pltpu.VMEM((rows, depth), BF16),
                pltpu.VMEM((rows, sd), F32),
            ],
        ),
        compiler_params=params(44),
        cost_estimate=cost(
            2 * rows * depth * (depth + 2 * units) + 2 * rows * sd * (units + width),
            2 * depth * (depth + 2 * units),
            rows * units,
        ),
        name="middle",
    )(
        info,
        *parts[0],
        *parts[1],
        tok,
        w_out,
        *near,
        *far,
        gain,
        w_gate,
        w_up,
        wp,
        projector,
        student,
    )
    return result[0], result[1], result[2:]


def down_kernel(level_ref, hidden_ref, weight_ref, out_ref):
    out_ref[0] = dot(hidden_ref[...], weight_ref[...]).astype(BF16)


def down_call(level, hidden, w_down, ring):
    rows, units = hidden.shape
    depth = w_down.shape[1]
    width = depth // ring
    return pl.pallas_call(
        down_kernel,
        out_shape=jax.ShapeDtypeStruct((ring, rows, width), BF16),
        grid_spec=pltpu.PrefetchScalarGridSpec(
            num_scalar_prefetch=1,
            grid=(ring,),
            in_specs=[
                whole((rows, units)),
                pl.BlockSpec(
                    (units, width), lambda j, level: (0, (level[0] + 2 * ring - 1 - j) % ring)
                ),
            ],
            out_specs=pl.BlockSpec((1, rows, width), lambda j, level: (j, 0, 0)),
        ),
        compiler_params=params(24),
        cost_estimate=cost(2 * rows * units * depth, 2 * units * depth),
        name="down",
    )(level, hidden, w_down)


def grads_kernel(info_ref, *refs, ring, chips):
    pieces = refs[:ring]
    normed_ref, hidden_ref, s_down_ref, up_ref, gate_ref = refs[ring : ring + 5]
    keep_ref, give_ref, scaled, grads = refs[ring + 5 :]
    chip, core = info_ref[ring], info_ref[ring + 1]
    size, sd = pieces[0].shape
    for s in range(ring):
        scaled[pl.ds(pl.multiple_of(info_ref[s] * size, size), size), :] = pieces[s][...]
    value = scaled[...]
    wide = value.astype(F32)
    error = jnp.sum(wide * wide)
    grad_hidden = dot_over(value, s_down_ref[...], (1, 1))
    grads[0] = dot_over(normed_ref[...], (grad_hidden * gate_ref[...]).astype(BF16), (0, 0))
    grads[1] = dot_over(normed_ref[...], (grad_hidden * up_ref[...]).astype(BF16), (0, 0))
    grads[2] = dot_over(hidden_ref[...], value, (0, 0))
    share = grads.shape[1] // (2 * chips)
    for f in range(chips):
        for k in range(3):
            for part, ref in ((core, keep_ref), (1 - core, give_ref)):
                at = pl.multiple_of((part * chips + (chip ^ f)) * share, share)
                ref[f, k * share : (k + 1) * share] = grads[k, pl.ds(at, share), :].astype(
                    ref.dtype
                )
        for ref in (keep_ref, give_ref):
            ref[f, 3 * share :] = jnp.full((NOTE, sd), error, F32).astype(ref.dtype)


def grads_call(info, pieces, normed, hidden, s_down, up, gate, chips):
    ring = len(pieces)
    rows, sd = normed.shape
    units = hidden.shape[1]
    share = 3 * sd // (2 * chips) + NOTE
    operands = [*pieces, normed, hidden, s_down, up, gate]
    return pl.pallas_call(
        functools.partial(grads_kernel, ring=ring, chips=chips),
        out_shape=(
            jax.ShapeDtypeStruct((chips, share, units), F32),
            jax.ShapeDtypeStruct((chips, share, units), BF16),
        ),
        grid_spec=pltpu.PrefetchScalarGridSpec(
            num_scalar_prefetch=1,
            grid=(1,),
            in_specs=[whole(a.shape) for a in operands],
            out_specs=(whole((chips, share, units)), whole((chips, share, units))),
            scratch_shapes=[pltpu.VMEM((rows, sd), BF16), pltpu.VMEM((3, sd, units), F32)],
        ),
        compiler_params=params(24),
        cost_estimate=cost(8 * rows * sd * units, 20 * sd * units),
        name="grads",
    )(info, *operands)


def pair_kernel(keep_ref, theirs_ref, *outs):
    for f, out in enumerate(outs):
        out[...] = (keep_ref[f] + theirs_ref[f].astype(F32)).astype(out.dtype)


def pair_call(keep, theirs):
    chips, share, sd = keep.shape
    return pl.pallas_call(
        pair_kernel,
        out_shape=[jax.ShapeDtypeStruct((share, sd), BF16)] * chips,
        compiler_params=params(16),
        cost_estimate=cost(keep.size, 8 * keep.size),
        name="pair",
    )(keep, theirs)


def finish_kernel(info_ref, *refs, chips):
    mine, others = refs[:chips], refs[chips : 2 * chips]
    outs = refs[2 * chips : 2 * chips + 3]
    notes = refs[2 * chips + 3]
    chip, core = info_ref[0], info_ref[1]
    share = (mine[0].shape[0] - NOTE) // 3
    for f in range(chips):
        for part, ref in ((core, mine[f]), (1 - core, others[f])):
            index = part * chips + (chip ^ f)
            at = pl.ds(pl.multiple_of(index * share, share), share)
            for k in range(3):
                outs[k][at, :] = ref[k * share : (k + 1) * share].astype(F32)
            notes[index] = ref[3 * share :, :HD].astype(F32)


def finish_call(info, mine, others):
    chips = len(mine)
    share, sd = mine[0].shape
    rows = (share - NOTE) // 3 * 2 * chips
    return pl.pallas_call(
        functools.partial(finish_kernel, chips=chips),
        out_shape=[jax.ShapeDtypeStruct((rows, sd), F32)] * 3
        + [jax.ShapeDtypeStruct((2 * chips, NOTE, HD), F32)],
        grid_spec=pltpu.PrefetchScalarGridSpec(
            num_scalar_prefetch=1,
            grid=(1,),
            in_specs=[whole((share, sd))] * (2 * chips),
            out_specs=[whole((rows, sd))] * 3 + [whole((2 * chips, NOTE, HD))],
        ),
        compiler_params=params(20),
        cost_estimate=cost(rows * sd, 12 * rows * sd),
        name="finish",
    )(info, *mine, *others)


def step_on(block, axis):
    size = lax.axis_size(axis)
    return lax.ppermute(block, axis, [(i, (i + 1) % size) for i in range(size)])


def ring_gather(block, axis, steps=None):
    blocks = [block]
    for _ in range(lax.axis_size(axis) - 1 if steps is None else steps):
        blocks.append(step_on(blocks[-1], axis))
    return blocks


def shifted(pieces, axis):
    size = lax.axis_size(axis)
    moved = [
        lax.ppermute(pieces[s], axis, [(i, (i + s) % size) for i in range(size)])
        for s in range(1, size)
    ]
    return [pieces[0], *moved]


def flipped(pieces):
    size = lax.axis_size("dp")
    moved = [
        lax.ppermute(pieces[f], "dp", [(i, i ^ (2 * f)) for i in range(size)])
        for f in range(1, len(pieces))
    ]
    return [pieces[0], *moved]


def swapped(value):
    size = lax.axis_size("dp")
    return lax.ppermute(value, "dp", [(i, i ^ 1) for i in range(size)])


def after(value, *others):
    return lax.optimization_barrier((value, *others))[0]


def paired(
    tokens,
    series_ids,
    offsets,
    norm_gain,
    mlp_gain,
    w_query,
    w_key,
    w_value,
    w_out,
    w_gate,
    w_up,
    w_down,
    projector,
    student_in,
    s_gate,
    s_up,
    s_down,
):
    rows = tokens.shape[0]
    depth, sd = w_query.shape[0], student_in.shape[1]
    dp, ring = lax.axis_size("dp"), lax.axis_size("tensor")
    here, level = lax.axis_index("dp"), lax.axis_index("tensor")
    chips, half = dp // 2, rows // 2
    chip, core = here // 2, here % 2
    total_rows = rows * dp
    number = lambda *values: jnp.stack([jnp.asarray(v, jnp.int32) for v in values])
    source = [(level - s) % ring for s in range(ring)]

    def deal(value):
        parts = value.reshape((2, half) + value.shape[1:])
        kept = lax.dynamic_index_in_dim(parts, core, 0, False)
        return kept, swapped(lax.dynamic_index_in_dim(parts, 1 - core, 0, False))

    token_chunks = deal(tokens)
    token_rings = [ring_gather(chunk, "tensor") for chunk in token_chunks]
    student_chunks = deal(student_in)
    offset_chunks = deal(offsets.astype(F32))

    angles = jnp.concatenate(offset_chunks)[:, None] * frequencies(HD)[None, :]
    cosine, sine = jnp.cos(angles), jnp.sin(angles)
    cosine = jnp.concatenate([cosine, cosine], axis=1)
    sine = jnp.concatenate([-sine, sine], axis=1)
    factor = HD ** (-0.5) * math.log2(math.e)
    student_full = jnp.concatenate(student_chunks, axis=0).astype(F32)
    student_normed = rms_scale(student_full).astype(BF16)
    s_gate_out = dot(student_normed, s_gate)
    s_up_out = dot(student_normed, s_up)
    sigmoid_gate = jax.nn.sigmoid(s_gate_out)
    up_slope = s_gate_out * sigmoid_gate
    gate_slope = s_up_out * sigmoid_gate * (1.0 + s_gate_out * (1.0 - sigmoid_gate))
    s_hidden = (up_slope * s_up_out).astype(BF16)
    student_part = dot(s_hidden, s_down)
    projected = dot(w_down, projector).astype(BF16)
    below = jnp.sum(
        series_ids[None, :] < jnp.arange(SERIES, dtype=jnp.int32)[:, None], axis=1, dtype=jnp.int32
    )

    early = (projected, student_part, s_hidden, up_slope, gate_slope, student_normed)
    info = after(number(*source, chip), *early)
    made, tok_full, normed = kv_call(
        info, token_rings, norm_gain[None, :], cosine, sine, w_key, w_value
    )
    own_kv = flipped(made)
    queries = query_call(info, normed, cosine * factor, sine * factor, w_query)
    own_kv = lax.optimization_barrier((*own_kv, queries[0]))[:chips]
    other_kv = [swapped(a) for a in own_kv]

    slice_cols = depth // dp
    w_slice = lax.dynamic_slice_in_dim(w_out, here * slice_cols, slice_cols, 1)
    w_slice = after(w_slice, queries[0])
    w_others = shifted([w_slice] * ring, "tensor")[1:]
    queries = flipped(queries)

    pairs = lambda a: a.reshape(a.shape[:-2] + (2, half, HD))
    w_first = after(w_others[0], *queries, *other_kv)
    near_first = flipped([w_first] * chips)
    attention_info = jnp.concatenate([below, number(chip, core)])
    made = attention_call(
        attention_info,
        [pairs(a) for a in queries],
        [pairs(a) for a in own_kv],
        [pairs(a) for a in other_kv],
    )
    held = lax.optimization_barrier((*made, *w_others[1:], *near_first))
    made, w_rest = held[:chips], jnp.stack(held[chips : chips + ring - 2])
    attended = flipped(made)
    parts = [
        ring_gather(jnp.stack(attended[k : k + chips // 2]), "tensor") for k in (0, chips // 2)
    ]
    w_rest = after(w_rest, *attended)
    near_rest = flipped([w_rest] * chips)
    near_rest = lax.optimization_barrier((*near_rest, *parts[0], *parts[1][:-1]))[:chips]
    near = (jnp.stack(near_first)[:, None], jnp.stack(near_rest))
    far = [swapped(after(a, *attended)) for a in near]

    hidden, mixed_own, pieces = middle_call(
        number(level, chip, core),
        parts,
        tok_full,
        w_out,
        near,
        far,
        mlp_gain[None, :],
        w_gate,
        w_up,
        projected,
        projector,
        student_part,
    )

    size = rows // ring
    own = lax.dynamic_slice_in_dim(student_full, level * size, size, 0)
    difference = own + sum(piece.astype(F32) for piece in shifted(pieces, "tensor"))
    own = (difference * total_rows ** (-0.5)).astype(BF16)
    scaled = shifted([own] * ring, "tensor")

    mlp_part = down_call(level.astype(jnp.int32)[None], hidden, w_down, ring)
    mlp_part = after(mlp_part, *scaled)
    mlp_own = mlp_part[0]
    for s in range(1, ring):
        mlp_own = step_on(mlp_own, "tensor").astype(F32) + mlp_part[s].astype(F32)
        mlp_own = mlp_own.astype(BF16) if s < ring - 1 else mlp_own

    keep, give = grads_call(
        number(*source, chip, core),
        scaled,
        student_normed,
        s_hidden,
        s_down,
        up_slope,
        gate_slope,
        chips,
    )
    shares = flipped(pair_call(keep, swapped(give)))
    own = sum(share.astype(F32) for share in shares).astype(BF16)
    mine = flipped([own] * chips)
    others = [swapped(share) for share in mine]
    mlp_own = after(mlp_own, *others)
    teacher = (mixed_own.astype(F32) + mlp_own).astype(BF16)
    back = swapped(teacher[half:])
    teacher_out = jnp.where(
        core == 0,
        jnp.concatenate([teacher[:half], back], axis=0),
        jnp.concatenate([back, teacher[:half]], axis=0),
    )

    grad_gate, grad_up, grad_down, notes = finish_call(number(chip, core), mine, others)
    return teacher_out, grad_gate, grad_up, grad_down, notes[0, 0, 0] / sd


def local(*args):
    rows, w_query, s_gate = args[0].shape[0], args[5], args[14]
    dp, ring = lax.axis_size("dp"), lax.axis_size("tensor")
    heads = w_query.shape[1] // HD
    fits = (
        dp == 2 * heads
        and heads > 1
        and heads & (heads - 1) == 0
        and w_query.shape[0] == dp * COLS
        and s_gate.shape[0] == s_gate.shape[1]
        and rows % (32 * ring) == 0
    )
    return paired(*args) if fits else general(*args)


def solution(mesh):
    in_specs = (
        P("dp", "tensor"),
        P(),
        P("dp"),
        P(),
        P(),
        P(None, "tensor"),
        P(None, "tensor"),
        P(None, "tensor"),
        P("tensor", None),
        P(None, "tensor"),
        P(None, "tensor"),
        P("tensor", None),
        P(),
        P("dp", None),
        P(None, "tensor"),
        P(None, "tensor"),
        P("tensor", None),
    )
    out_specs = (P("dp", "tensor"), P(None, "tensor"), P(None, "tensor"), P("tensor", None), P())
    return jax.shard_map(local, mesh=mesh, in_specs=in_specs, out_specs=out_specs, check_vma=False)
```

```python
import functools
import math

import jax
import jax.numpy as jnp
from jax import lax
from jax.experimental import pallas as pl
from jax.experimental.pallas import tpu as pltpu
from jax.sharding import PartitionSpec as P

HD = 128
COLS = 256
NOTE = 16
SERIES = 8
F32 = jnp.float32
BF16 = jnp.bfloat16
MIB = 1024 * 1024


def rms_scale(values):
    return values * lax.rsqrt(jnp.mean(values * values, axis=-1, keepdims=True) + 1e-05)


def frequencies(head_dim):
    indices = jnp.arange(head_dim // 2).astype(jnp.float32)
    return jnp.exp(-jnp.log(500000.0) * 2.0 * indices / head_dim)


def rotary(inputs, angles):
    half_dim = inputs.shape[-1] // 2
    cosine = jnp.cos(angles)
    sine = jnp.sin(angles)
    first_half = inputs[..., :half_dim]
    second_half = inputs[..., half_dim:]
    return jnp.concatenate(
        [first_half * cosine - second_half * sine, first_half * sine + second_half * cosine],
        axis=-1,
    )


def general(
    tokens,
    series_ids,
    offsets,
    norm_gain,
    mlp_gain,
    w_query,
    w_key,
    w_value,
    w_out,
    w_gate,
    w_up,
    w_down,
    projector,
    student_in,
    s_gate,
    s_up,
    s_down,
):
    row_count = tokens.shape[0]
    heads_dev = w_query.shape[1] // HD
    first_row = lax.axis_index("dp") * row_count
    tokens_full = lax.all_gather(tokens, "tensor", axis=1, tiled=True).astype(jnp.float32)
    normed = (rms_scale(tokens_full) * norm_gain).astype(jnp.bfloat16)
    angles = offsets.astype(jnp.float32)[:, None, None] * frequencies(HD)[None, None, :]
    queries = rotary(
        jnp.dot(normed, w_query, preferred_element_type=jnp.float32).reshape(
            row_count, heads_dev, HD
        ),
        angles,
    ).astype(jnp.bfloat16)
    keys_rot = rotary(
        jnp.dot(normed, w_key, preferred_element_type=jnp.float32).reshape(
            row_count, heads_dev, HD
        ),
        angles,
    ).astype(jnp.bfloat16)
    values_mine = jnp.dot(normed, w_value, preferred_element_type=jnp.float32).astype(jnp.bfloat16)
    keys_flat = keys_rot.reshape(row_count, heads_dev * HD)
    query_pos = first_row + jnp.arange(row_count, dtype=jnp.int32)
    query_series = lax.dynamic_slice_in_dim(series_ids, first_row, row_count, 0)
    factor = HD ** (-0.5)
    peak = jnp.full((row_count, heads_dev), -1e30, jnp.float32)
    key_block = lax.all_gather(keys_flat, "dp", axis=0, tiled=True)
    value_block = lax.all_gather(values_mine, "dp", axis=0, tiled=True)
    count = key_block.shape[0]
    key_pos = jnp.arange(count, dtype=jnp.int32)
    allowed = (
        (key_pos[None, :] >= 0)
        & (key_pos[None, :] <= query_pos[:, None])
        & (series_ids[None, :] == query_series[:, None])
    )
    scores = (
        jnp.einsum(
            "qhd,khd->qhk",
            queries,
            key_block.reshape(count, heads_dev, HD),
            preferred_element_type=jnp.float32,
        )
        * factor
    )
    scores = jnp.where(allowed[:, None, :], scores, -1e30)
    new_peak = jnp.maximum(peak, jnp.max(scores, axis=2))
    weights = jnp.where(allowed[:, None, :], jnp.exp(scores - new_peak[:, :, None]), 0.0)
    denom = jnp.sum(weights, axis=2)
    accum = jnp.einsum(
        "qhk,khd->qhd",
        weights.astype(jnp.bfloat16),
        value_block.reshape(count, heads_dev, HD),
        preferred_element_type=jnp.float32,
    )
    peak, denom, accum = (new_peak, denom, accum)
    attended = (accum / denom[:, :, None]).astype(jnp.bfloat16).reshape(row_count, heads_dev * HD)
    partial_out = jnp.dot(attended, w_out, preferred_element_type=jnp.float32)
    own_sum = lax.psum_scatter(
        partial_out.astype(jnp.bfloat16), "tensor", scatter_dimension=1, tiled=True
    ).astype(jnp.float32)
    mixed_own = (tokens.astype(jnp.float32) + own_sum).astype(jnp.bfloat16)
    mixed = lax.all_gather(mixed_own, "tensor", axis=1, tiled=True)
    normed_two = (rms_scale(mixed.astype(jnp.float32)) * mlp_gain).astype(jnp.bfloat16)
    gate_out = jnp.dot(normed_two, w_gate, preferred_element_type=jnp.float32)
    up_out = jnp.dot(normed_two, w_up, preferred_element_type=jnp.float32)
    hidden = (jax.nn.silu(gate_out) * up_out).astype(jnp.bfloat16)
    mlp_part = jnp.dot(hidden, w_down, preferred_element_type=jnp.float32)
    mlp_own = lax.psum_scatter(
        mlp_part.astype(jnp.bfloat16), "tensor", scatter_dimension=1, tiled=True
    ).astype(jnp.float32)
    teacher_out = (mixed_own.astype(jnp.float32) + mlp_own).astype(jnp.bfloat16)
    student_full = student_in.astype(jnp.float32)
    student_normed = rms_scale(student_full).astype(jnp.bfloat16)
    s_gate_out = jnp.dot(student_normed, s_gate, preferred_element_type=jnp.float32)
    s_up_out = jnp.dot(student_normed, s_up, preferred_element_type=jnp.float32)
    sigmoid_gate = jax.nn.sigmoid(s_gate_out)
    s_hidden = (s_gate_out * sigmoid_gate * s_up_out).astype(jnp.bfloat16)
    student_part = jnp.dot(s_hidden, s_down, preferred_element_type=jnp.float32)
    teacher_full = lax.all_gather(teacher_out, "tensor", axis=1, tiled=True)
    target = jnp.dot(teacher_full, projector, preferred_element_type=jnp.float32)
    student_summed = lax.psum(student_part.astype(jnp.bfloat16), "tensor").astype(jnp.float32)
    difference = student_full + student_summed - target
    total_rows = row_count * lax.axis_size("dp")
    scaled = (difference * total_rows ** (-0.5)).astype(jnp.bfloat16)
    grad_down_part = jnp.einsum("rk,rc->kc", s_hidden, scaled, preferred_element_type=jnp.float32)
    grad_hidden = jnp.einsum("rc,kc->rk", scaled, s_down, preferred_element_type=jnp.float32)
    grad_up_in = (grad_hidden * s_gate_out * sigmoid_gate).astype(jnp.bfloat16)
    grad_gate_in = (
        grad_hidden * s_up_out * sigmoid_gate * (1.0 + s_gate_out * (1.0 - sigmoid_gate))
    ).astype(jnp.bfloat16)
    grad_gate_part = jnp.einsum(
        "rc,rk->ck", student_normed, grad_gate_in, preferred_element_type=jnp.float32
    )
    grad_up_part = jnp.einsum(
        "rc,rk->ck", student_normed, grad_up_in, preferred_element_type=jnp.float32
    )
    square_sum = jnp.sum(difference * difference)
    grad_gate, grad_up, grad_down, square_total = (
        lax.psum(grad_gate_part.astype(jnp.bfloat16), "dp").astype(jnp.float32),
        lax.psum(grad_up_part.astype(jnp.bfloat16), "dp").astype(jnp.float32),
        lax.psum(grad_down_part.astype(jnp.bfloat16), "dp").astype(jnp.float32),
        lax.psum(square_sum.astype(jnp.bfloat16), "dp").astype(jnp.float32),
    )
    error = square_total / (total_rows * difference.shape[1])
    return (teacher_out, grad_gate, grad_up, grad_down, error)


def dot(a, b):
    return jnp.dot(a, b, preferred_element_type=F32)


def dot_over(a, b, dims):
    return lax.dot_general(a, b, ((dims[:1], dims[1:]), ((), ())), preferred_element_type=F32)


def params(limit):
    return pltpu.CompilerParams(vmem_limit_bytes=limit * MIB)


def whole(shape):
    return pl.BlockSpec(shape, lambda *_: (0,) * len(shape))


def cost(flops, moved, transcendentals=0):
    return pl.CostEstimate(
        flops=int(flops), bytes_accessed=int(moved), transcendentals=int(transcendentals)
    )


def qkv_kernel(info_ref, *refs, ring, heads, factor):
    blocks = [refs[:ring], refs[ring : 2 * ring]]
    gain_ref, cos_ref, sin_ref, *sources = refs[2 * ring : 2 * ring + 6]
    outs = refs[2 * ring + 6 : 2 * ring + 6 + heads]
    tok_ref, stamp_ref, normed, made, weights, sems = refs[2 * ring + 6 + heads :]
    half, width = blocks[0][0].shape
    depth = gain_ref.shape[1]
    copies = [
        pltpu.make_async_copy(source, weights.at[k], sems.at[k])
        for k, source in enumerate(sources)
    ]
    for copy in copies:
        copy.start()
    for k in range(2):
        mine = slice(k * half, (k + 1) * half)
        total = jnp.zeros((half, 1), F32)
        for block in blocks[k]:
            part = block[...].astype(F32)
            total += jnp.sum(part * part, axis=1, keepdims=True)
        scale = lax.rsqrt(total / depth + 1e-05)
        for s, block in enumerate(blocks[k]):
            at = pl.ds(pl.multiple_of(info_ref[s] * width, 128), width)
            part = block[...]
            tok_ref[mine, at] = part
            normed[mine, at] = (part.astype(F32) * scale * gain_ref[:, at]).astype(BF16)
    for kind, copy in enumerate(copies):
        copy.wait()
        result = dot(normed[...], weights[kind])
        for h in range(heads):
            head = result[:, h * HD : (h + 1) * HD]
            if kind < 2:
                head = head * cos_ref[...] + pltpu.roll(head, HD // 2, 1) * sin_ref[...]
            if kind == 0:
                head = head * factor
            made[h, kind] = head.astype(BF16)
    for f in range(heads):
        outs[f][...] = made[info_ref[ring] ^ f]
    stamp_ref[...] = jnp.zeros_like(stamp_ref)


def qkv_call(info, blocks, gain, cosine, sine, *weights):
    half, width = blocks[0][0].shape
    rows, ring = 2 * half, len(blocks[0])
    depth, out_cols = weights[0].shape
    heads = out_cols // HD
    result = pl.pallas_call(
        functools.partial(
            qkv_kernel, ring=ring, heads=heads, factor=HD ** (-0.5) * math.log2(math.e)
        ),
        out_shape=[jax.ShapeDtypeStruct((3, rows, HD), BF16)] * heads
        + [jax.ShapeDtypeStruct((rows, depth), BF16), jax.ShapeDtypeStruct((8, HD), F32)],
        grid_spec=pltpu.PrefetchScalarGridSpec(
            num_scalar_prefetch=1,
            grid=(1,),
            in_specs=[whole((half, width))] * (2 * ring)
            + [whole((1, depth)), whole((rows, HD)), whole((rows, HD))]
            + [pl.BlockSpec(memory_space=pl.ANY)] * 3,
            out_specs=[whole((3, rows, HD))] * heads + [whole((rows, depth)), whole((8, HD))],
            scratch_shapes=[
                pltpu.VMEM((rows, depth), BF16),
                pltpu.VMEM((heads, 3, rows, HD), BF16),
                pltpu.VMEM((3, depth, out_cols), BF16),
                pltpu.SemaphoreType.DMA((3,)),
            ],
        ),
        compiler_params=params(42),
        cost_estimate=cost(6 * rows * depth * out_cols, 6 * depth * out_cols),
        name="qkv",
    )(info, *blocks[0], *blocks[1], gain, cosine, sine, *weights)
    return result[:heads], result[heads], result[heads + 1]


def attention_kernel(info_ref, *refs, chips):
    own, other = refs[:chips], refs[chips : 2 * chips]
    outs = refs[2 * chips : 3 * chips]
    keys_all, values_all = refs[3 * chips :]
    chip, core = info_ref[SERIES], info_ref[SERIES + 1]
    half = outs[0].shape[1]
    span = 2 * half
    for f in range(chips):
        for source, side in ((own[f], core), (other[f], 1 - core)):
            at = pl.ds(pl.multiple_of(side * half, half), half)
            for odd, index in ((0, side), (1, 1 - side)):
                block = 2 * (chip ^ f) + odd
                keys_all[block, at, :] = source[1, index]
                values_all[block, :, at] = source[2, index].T

    def first_of(row):
        found = jnp.int32(0)
        for s in range(SERIES):
            edge = info_ref[s]
            found = jnp.where(edge <= row, jnp.maximum(found, edge), found)
        return found

    for f in range(chips):
        even = 2 * (chip ^ f)
        first_row = even * span + core * half
        last_row = first_row + span + half - 1
        query = jnp.concatenate([own[f][0, core], own[f][0, 1 - core]], axis=0)
        place = lax.broadcasted_iota(jnp.int32, (1, span), 1)
        row = first_row + place + jnp.where(place < half, 0, half)
        start = jnp.zeros((1, span), jnp.int32)
        for s in range(SERIES):
            edge = info_ref[s]
            start = jnp.where(edge <= row, jnp.maximum(start, edge), start)
        lane = lax.broadcasted_iota(jnp.int32, (span, 1), 0)

        def body(at, carry, masked, query=query, row=row, start=start, lane=lane):
            peak, denom, accum = carry
            scores = dot_over(keys_all[at], query, (1, 1))
            if masked:
                column = lane + at * span
                allowed = (column >= start) & (column <= row)
                scores = jnp.where(allowed, scores, -1e30)
            new_peak = jnp.maximum(peak, jnp.max(scores, axis=0, keepdims=True))
            weights = jnp.exp2(scores - new_peak)
            if masked:
                weights = jnp.where(allowed, weights, 0.0)
            keep = jnp.exp2(peak - new_peak)
            denom = denom * keep + jnp.sum(weights, axis=0, keepdims=True)
            accum = accum * keep + dot(values_all[at], weights.astype(BF16))
            return new_peak, denom, accum

        begin = first_of(first_row) // span
        full = jnp.minimum(even, (first_of(last_row) + span - 1) // span)
        carry = (
            jnp.full((1, span), -1e30, F32),
            jnp.zeros((1, span), F32),
            jnp.zeros((HD, span), F32),
        )
        carry = lax.fori_loop(begin, full, functools.partial(body, masked=True), carry)
        carry = lax.fori_loop(full, even, functools.partial(body, masked=False), carry)
        peak, denom, accum = body(even, carry, masked=True)
        outs[f][core] = (accum[:, :half] / denom[:, :half]).T.astype(BF16)
        carry = (peak[:, half:], denom[:, half:], accum[:, half:])
        _, denom, accum = body(
            even + 1, carry, True, query[half:], row[:, half:], start[:, half:], lane
        )
        outs[f][1 - core] = (accum / denom).T.astype(BF16)


def attention_call(info, own, other):
    chips = len(own)
    _, _, half, _ = own[0].shape
    return pl.pallas_call(
        functools.partial(attention_kernel, chips=chips),
        out_shape=[jax.ShapeDtypeStruct((2, half, HD), BF16)] * chips,
        grid_spec=pltpu.PrefetchScalarGridSpec(
            num_scalar_prefetch=1,
            grid=(1,),
            in_specs=[whole((3, 2, half, HD))] * (2 * chips),
            out_specs=[whole((2, half, HD))] * chips,
            scratch_shapes=[
                pltpu.VMEM((2 * chips, 2 * half, HD), BF16),
                pltpu.VMEM((2 * chips, HD, 2 * half), BF16),
            ],
        ),
        compiler_params=params(24),
        cost_estimate=cost(
            4 * chips * half * 4 * chips * half * HD,
            12 * chips * half * HD * 2,
            2 * chips * half * 4 * chips * half // 2,
        ),
        name="attention",
    )(info, *own, *other)


def middle_kernel(info_ref, *refs, ring, chips):
    parts = [refs[:ring], refs[ring : 2 * ring]]
    refs = refs[2 * ring :]
    tok_ref, w_own_ref = refs[:2]
    near_first, near_rest = refs[2 : 2 + chips], refs[2 + chips : 2 + 2 * chips]
    far_first, far_rest = refs[2 + 2 * chips], refs[3 + 2 * chips : 3 + 3 * chips]
    refs = refs[3 + 3 * chips :]
    gain_ref, gate_ref, up_ref, wp_ref, proj_ref, student_ref = refs[:6]
    hidden_ref, own_ref = refs[6:8]
    pieces = refs[8 : 8 + ring]
    attended, mixed, total, near, far, gates, ups, wp, proj, sems = refs[8 + ring :]
    step = pl.program_id(0)
    level, chip, core = info_ref[0], info_ref[1], info_ref[2]
    rows, depth = mixed.shape
    half = rows // 2
    width = own_ref.shape[1]
    blocks, _, wide = gates.shape

    used = iter(range(sems.shape[0]))
    copy = lambda source, target: pltpu.make_async_copy(source, target, sems.at[next(used)])
    heads = []
    for k in range(2):
        for s, part in enumerate(parts[k]):
            count = part.shape[0]
            for i in range(count):
                at = s * width + (chip ^ (k * count + i)) * HD
                at = pl.ds(pl.multiple_of(at, HD), HD)
                for side in range(2):
                    rows_at = pl.ds(side * half, half)
                    heads.append(copy(part.at[i, side], attended.at[rows_at, at]))
    slices = [
        [
            copy(near_first[f], near.at[f, 0]),
            copy(near_rest[f], near.at[f, pl.ds(1, ring - 2)]),
            copy(far_first.at[f, 0], far.at[f, 0]),
            copy(far_rest[f], far.at[f, pl.ds(1, ring - 2)]),
        ]
        for f in range(chips)
    ]
    own_rows = pl.ds(pl.multiple_of(level * width, width), width)
    late = [copy(proj_ref.at[own_rows], proj), copy(student_ref, total)]
    columns = [pl.ds(i * wide, wide) for i in range(blocks)]
    units = [
        [
            copy(gate_ref.at[:, columns[i]], gates.at[i]),
            copy(up_ref.at[:, columns[i]], ups.at[i]),
            copy(wp_ref.at[columns[i]], wp.at[i]),
        ]
        for i in range(blocks)
    ]

    @pl.when(step == 0)
    def _():
        for c in heads + slices[0]:
            c.start()
        for c in sum(slices[1:], []) + late + sum(units, []):
            c.start()
        for c in heads:
            c.wait()

    for f in range(chips):

        @pl.when(step == f)
        def _(f=f):
            for c in slices[f]:
                c.wait()

    @pl.when(step < chips)
    def _():
        for gathered, side in ((near, core), (far, 1 - core)):
            here = pl.ds(pl.multiple_of(side * COLS, COLS), COLS)
            result = tok_ref[:, here].astype(F32) + dot(attended[:, :width], w_own_ref[:, here])
            weight = gathered[step].reshape(depth - width, COLS)
            result += dot(attended[:, width:], weight)
            at = pl.ds(pl.multiple_of((2 * (step ^ chip) + side) * COLS, COLS), COLS)
            mixed[:, at] = result.astype(BF16)

    @pl.when(step == chips)
    def _():
        for c in late:
            c.wait()
        values = mixed[...].astype(F32)
        attended[...] = (rms_scale(values) * gain_ref[...]).astype(BF16)
        own = mixed[:, pl.ds(pl.multiple_of(level * width, 128), width)]
        own_ref[...] = own
        total[...] -= dot(own, proj[...])

    for i in range(blocks):

        @pl.when(step == chips + i)
        def _(i=i):
            for c in units[i]:
                c.wait()

    @pl.when(step >= chips)
    def _():
        index = step - chips
        gate = dot(attended[...], gates[index])
        up = dot(attended[...], ups[index])
        hidden = (gate * jax.nn.sigmoid(gate) * up).astype(BF16)
        hidden_ref[...] = hidden
        total[...] -= dot(hidden, wp[index])

    @pl.when(step == pl.num_programs(0) - 1)
    def _():
        size = rows // ring
        for s in range(ring):
            at = pl.ds(pl.multiple_of((level + s) % ring * size, size), size)
            pieces[s][...] = total[at, :].astype(BF16)


def middle_call(info, parts, tok, w_out, near, far, gain, w_gate, w_up, wp, projector, student):
    rows, depth = tok.shape
    ring, chips = len(parts[0]), len(near[0])
    units = w_gate.shape[1]
    wide = 2 * COLS
    width = depth // ring
    sd = projector.shape[1]
    blocks = units // wide
    tile = lambda j, info: (0, jnp.minimum(j, chips - 1) ^ info[1])
    late = lambda j, info: (0, jnp.maximum(j - chips, 0))
    anywhere = pl.BlockSpec(memory_space=pl.ANY)
    count = 2 * ring * parts[0][0].shape[0] * 2 + 4 * chips + 2 + 3 * blocks
    result = pl.pallas_call(
        functools.partial(middle_kernel, ring=ring, chips=chips),
        out_shape=[
            jax.ShapeDtypeStruct((rows, units), BF16),
            jax.ShapeDtypeStruct((rows, width), BF16),
        ]
        + [jax.ShapeDtypeStruct((rows // ring, sd), BF16)] * ring,
        grid_spec=pltpu.PrefetchScalarGridSpec(
            num_scalar_prefetch=1,
            grid=(chips + blocks,),
            in_specs=[anywhere] * (2 * ring)
            + [pl.BlockSpec((rows, wide), tile), pl.BlockSpec((width, wide), tile)]
            + [anywhere] * (3 * chips + 1)
            + [whole((1, depth))]
            + [anywhere] * 5,
            out_specs=[
                pl.BlockSpec((rows, wide), late),
                whole((rows, width)),
            ]
            + [whole((rows // ring, sd))] * ring,
            scratch_shapes=[
                pltpu.VMEM((rows, depth), BF16),
                pltpu.VMEM((rows, depth), BF16),
                pltpu.VMEM((rows, sd), F32),
                pltpu.VMEM((chips, ring - 1, width, COLS), BF16),
                pltpu.VMEM((chips, ring - 1, width, COLS), BF16),
                pltpu.VMEM((blocks, depth, wide), BF16),
                pltpu.VMEM((blocks, depth, wide), BF16),
                pltpu.VMEM((blocks, wide, sd), BF16),
                pltpu.VMEM((width, sd), BF16),
                pltpu.SemaphoreType.DMA((count,)),
            ],
        ),
        compiler_params=params(42),
        cost_estimate=cost(
            2 * rows * depth * (depth + 2 * units) + 2 * rows * sd * (units + width),
            2 * depth * (depth + 2 * units),
            rows * units,
        ),
        name="middle",
    )(
        info,
        *parts[0],
        *parts[1],
        tok,
        w_out,
        *near[0],
        *near[1],
        far[0],
        *far[1],
        gain,
        w_gate,
        w_up,
        wp,
        projector,
        student,
    )
    return result[0], result[1], result[2:]


def down_kernel(level_ref, hidden_ref, weight_ref, *outs):
    result = dot(hidden_ref[...], weight_ref[...]).astype(BF16)
    for j, out in enumerate(outs):

        @pl.when(pl.program_id(0) == j)
        def _(out=out):
            out[...] = result


def down_call(level, hidden, w_down, ring):
    rows, units = hidden.shape
    depth = w_down.shape[1]
    width = depth // ring
    return pl.pallas_call(
        down_kernel,
        out_shape=[jax.ShapeDtypeStruct((rows, width), BF16)] * ring,
        grid_spec=pltpu.PrefetchScalarGridSpec(
            num_scalar_prefetch=1,
            grid=(ring,),
            in_specs=[
                whole((rows, units)),
                pl.BlockSpec((units, width), lambda j, level: (0, level[0] ^ (ring - 1 - j))),
            ],
            out_specs=[whole((rows, width))] * ring,
        ),
        compiler_params=params(24),
        cost_estimate=cost(2 * rows * units * depth, 2 * units * depth),
        name="down",
    )(level, hidden, w_down)


def grads_kernel(info_ref, *refs, ring, chips):
    pieces = refs[:ring]
    normed_ref, hidden_ref, s_down_ref, up_ref, gate_ref = refs[ring : ring + 5]
    keep_ref, give_ref, scaled, grads = refs[ring + 5 :]
    chip, core = info_ref[ring], info_ref[ring + 1]
    size, sd = pieces[0].shape
    for s in range(ring):
        scaled[pl.ds(pl.multiple_of(info_ref[s] * size, size), size), :] = pieces[s][...]
    value = scaled[...]
    wide = value.astype(F32)
    error = jnp.sum(wide * wide)
    grad_hidden = dot_over(value, s_down_ref[...], (1, 1))
    grads[0] = dot_over(normed_ref[...], (grad_hidden * gate_ref[...].astype(F32)).astype(BF16), (0, 0))
    grads[1] = dot_over(normed_ref[...], (grad_hidden * up_ref[...].astype(F32)).astype(BF16), (0, 0))
    grads[2] = dot_over(hidden_ref[...], value, (0, 0))
    share = grads.shape[1] // (2 * chips)
    for f in range(chips):
        for k in range(3):
            for part, ref in ((core, keep_ref), (1 - core, give_ref)):
                at = pl.multiple_of((part * chips + (chip ^ f)) * share, share)
                ref[f, k * share : (k + 1) * share] = grads[k, pl.ds(at, share), :].astype(
                    ref.dtype
                )
        for ref in (keep_ref, give_ref):
            ref[f, 3 * share :] = jnp.full((NOTE, sd), error, F32).astype(ref.dtype)


def grads_call(info, pieces, normed, hidden, s_down, up, gate, chips):
    ring = len(pieces)
    rows, sd = normed.shape
    units = hidden.shape[1]
    share = 3 * sd // (2 * chips) + NOTE
    operands = [*pieces, normed, hidden, s_down, up, gate]
    return pl.pallas_call(
        functools.partial(grads_kernel, ring=ring, chips=chips),
        out_shape=(
            jax.ShapeDtypeStruct((chips, share, units), F32),
            jax.ShapeDtypeStruct((chips, share, units), BF16),
        ),
        grid_spec=pltpu.PrefetchScalarGridSpec(
            num_scalar_prefetch=1,
            grid=(1,),
            in_specs=[whole(a.shape) for a in operands],
            out_specs=(whole((chips, share, units)), whole((chips, share, units))),
            scratch_shapes=[pltpu.VMEM((rows, sd), BF16), pltpu.VMEM((3, sd, units), F32)],
        ),
        compiler_params=params(22),
        cost_estimate=cost(8 * rows * sd * units, 20 * sd * units),
        name="grads",
    )(info, *operands)


def pair_kernel(keep_ref, theirs_ref, *outs):
    for f, out in enumerate(outs):
        out[...] = (keep_ref[f] + theirs_ref[f].astype(F32)).astype(out.dtype)


def pair_call(keep, theirs):
    chips, share, sd = keep.shape
    return pl.pallas_call(
        pair_kernel,
        out_shape=[jax.ShapeDtypeStruct((share, sd), BF16)] * chips,
        compiler_params=params(10),
        cost_estimate=cost(keep.size, 8 * keep.size),
        name="pair",
    )(keep, theirs)


def finish_kernel(info_ref, *refs, chips):
    mine, others = refs[:chips], refs[chips : 2 * chips]
    outs = refs[2 * chips : 2 * chips + 3]
    notes = refs[2 * chips + 3]
    chip, core = info_ref[0], info_ref[1]
    share = (mine[0].shape[0] - NOTE) // 3
    for f in range(chips):
        for part, ref in ((core, mine[f]), (1 - core, others[f])):
            index = part * chips + (chip ^ f)
            at = pl.ds(pl.multiple_of(index * share, share), share)
            for k in range(3):
                outs[k][at, :] = ref[k * share : (k + 1) * share].astype(F32)
            notes[index] = ref[3 * share :, :HD].astype(F32)


def finish_call(info, mine, others):
    chips = len(mine)
    share, sd = mine[0].shape
    rows = (share - NOTE) // 3 * 2 * chips
    return pl.pallas_call(
        functools.partial(finish_kernel, chips=chips),
        out_shape=[jax.ShapeDtypeStruct((rows, sd), F32)] * 3
        + [jax.ShapeDtypeStruct((2 * chips, NOTE, HD), F32)],
        grid_spec=pltpu.PrefetchScalarGridSpec(
            num_scalar_prefetch=1,
            grid=(1,),
            in_specs=[whole((share, sd))] * (2 * chips),
            out_specs=[whole((rows, sd))] * 3 + [whole((2 * chips, NOTE, HD))],
        ),
        compiler_params=params(14),
        cost_estimate=cost(rows * sd, 12 * rows * sd),
        name="finish",
    )(info, *mine, *others)


def step_on(block, axis):
    size = lax.axis_size(axis)
    return lax.ppermute(block, axis, [(i, (i + 1) % size) for i in range(size)])


def ring_gather(block, axis, steps=None):
    blocks = [block]
    for _ in range(lax.axis_size(axis) - 1 if steps is None else steps):
        blocks.append(step_on(blocks[-1], axis))
    return blocks


def shifted(pieces, axis):
    size = lax.axis_size(axis)
    moved = [
        lax.ppermute(pieces[s], axis, [(i, (i + s) % size) for i in range(size)])
        for s in range(1, size)
    ]
    return [pieces[0], *moved]


def flipped(pieces):
    size = lax.axis_size("dp")
    moved = [
        lax.ppermute(pieces[f], "dp", [(i, i ^ (2 * f)) for i in range(size)])
        for f in range(1, len(pieces))
    ]
    return [pieces[0], *moved]


def swapped(value):
    size = lax.axis_size("dp")
    return lax.ppermute(value, "dp", [(i, i ^ 1) for i in range(size)])


def after(value, *others):
    return lax.optimization_barrier((value, *others))[0]


def paired(
    tokens,
    series_ids,
    offsets,
    norm_gain,
    mlp_gain,
    w_query,
    w_key,
    w_value,
    w_out,
    w_gate,
    w_up,
    w_down,
    projector,
    student_in,
    s_gate,
    s_up,
    s_down,
):
    rows = tokens.shape[0]
    depth, sd = w_query.shape[0], student_in.shape[1]
    dp, ring = lax.axis_size("dp"), lax.axis_size("tensor")
    here, level = lax.axis_index("dp"), lax.axis_index("tensor")
    chips, half = dp // 2, rows // 2
    chip, core = here // 2, here % 2
    total_rows = rows * dp
    number = lambda *values: jnp.stack([jnp.asarray(v, jnp.int32) for v in values])
    source = [(level - s) % ring for s in range(ring)]

    def deal(value):
        parts = value.reshape((2, half) + value.shape[1:])
        kept = lax.dynamic_index_in_dim(parts, core, 0, False)
        return kept, swapped(lax.dynamic_index_in_dim(parts, 1 - core, 0, False))

    token_chunks = deal(tokens)
    token_rings = [ring_gather(chunk, "tensor") for chunk in token_chunks]
    student_chunks = deal(student_in)
    offset_chunks = deal(offsets.astype(F32))

    angles = jnp.concatenate(offset_chunks)[:, None] * frequencies(HD)[None, :]
    cosine, sine = jnp.cos(angles), jnp.sin(angles)
    cosine = jnp.concatenate([cosine, cosine], axis=1)
    sine = jnp.concatenate([-sine, sine], axis=1)
    student_full = jnp.concatenate(student_chunks, axis=0).astype(F32)
    student_normed = rms_scale(student_full).astype(BF16)
    below = jnp.sum(
        series_ids[None, :] < jnp.arange(SERIES, dtype=jnp.int32)[:, None], axis=1, dtype=jnp.int32
    )

    info = number(*source, chip)
    made, tok_full, stamp = qkv_call(
        info, token_rings, norm_gain[None, :], cosine, sine, w_query, w_key, w_value
    )

    held = lax.optimization_barrier((student_normed, projector, stamp))
    student_normed = held[0]
    s_gate_out = dot(student_normed, s_gate)
    s_up_out = dot(student_normed, s_up)
    sigmoid_gate = jax.nn.sigmoid(s_gate_out)
    up_slope = s_gate_out * sigmoid_gate
    gate_slope = s_up_out * sigmoid_gate * (1.0 + s_gate_out * (1.0 - sigmoid_gate))
    s_hidden = (up_slope * s_up_out).astype(BF16)
    up_slope, gate_slope = up_slope.astype(BF16), gate_slope.astype(BF16)
    student_part = dot(s_hidden, s_down)
    projected = dot(w_down, held[1]).astype(BF16)
    early = (projected, student_part, s_hidden, up_slope, gate_slope, student_normed)

    slice_cols = depth // dp
    w_slice = lax.dynamic_slice_in_dim(w_out, here * slice_cols, slice_cols, 1)
    w_slice = after(w_slice, stamp)
    w_others = shifted([w_slice] * ring, "tensor")[1:]

    own = flipped(made)
    held = lax.optimization_barrier((*own, *w_others[:2], *early))
    own, w_others[:2] = held[:chips], held[chips : chips + 2]
    other = [swapped(a) for a in own]
    near_first = flipped([w_others[0]] * chips)
    pairs = lambda a: a.reshape(3, 2, half, HD)
    made = attention_call(
        jnp.concatenate([below, number(chip, core)]),
        [pairs(a) for a in own],
        [pairs(a) for a in other],
    )
    held = lax.optimization_barrier((*made, *w_others[1:], *near_first))
    made, w_rest = held[:chips], jnp.stack(held[chips : chips + ring - 2])
    attended = lax.optimization_barrier(tuple(flipped(made)))
    parts = [
        ring_gather(jnp.stack(attended[k : k + chips // 2]), "tensor") for k in (0, chips // 2)
    ]
    w_rest = after(w_rest, *attended)
    near_rest = flipped([w_rest] * chips)
    far_first = swapped(after(jnp.stack(near_first)[:, None], *attended))
    far_rest = [swapped(after(a, parts[1][1])) for a in near_rest]

    hidden, mixed_own, pieces = middle_call(
        number(level, chip, core),
        parts,
        tok_full,
        w_out,
        (near_first, near_rest),
        (far_first, far_rest),
        mlp_gain[None, :],
        w_gate,
        w_up,
        projected,
        projector,
        student_part,
    )

    size = rows // ring
    own = lax.dynamic_slice_in_dim(student_full, level * size, size, 0)
    moved = shifted(pieces, "tensor")
    difference = own + sum(piece.astype(F32) for piece in moved)
    own = (difference * total_rows ** (-0.5)).astype(BF16)
    scaled = shifted([own] * ring, "tensor")

    far_theirs, far_mine, near_theirs, kept = down_call(
        level.astype(jnp.int32)[None], after(hidden, *moved[1:]), w_down, ring
    )
    over = lambda value, bit: lax.ppermute(value, "tensor", [(i, i ^ bit) for i in range(ring)])
    far_sum = over(after(far_theirs, *scaled), 1)

    keep, give = grads_call(
        after(number(*source, chip, core), kept),
        scaled,
        student_normed,
        s_hidden,
        s_down,
        up_slope,
        gate_slope,
        chips,
    )
    shares = pair_call(keep, swapped(give))
    far_sum = after(far_sum, shares[0]).astype(F32) + far_mine.astype(F32)
    far_sum = far_sum.astype(BF16)
    shares = flipped(shares)
    own = sum(share.astype(F32) for share in shares).astype(BF16)
    own = after(own, far_sum)
    mine = flipped([own] * chips)
    others = [swapped(share) for share in mine]

    mlp_own = over(after(near_theirs, far_sum), 1).astype(F32) + over(far_sum, 2).astype(F32)
    teacher = mixed_own.astype(F32) + (kept.astype(F32) + mlp_own)
    teacher = teacher.astype(BF16)
    back = swapped(teacher[half:])
    teacher_out = jnp.where(
        core == 0,
        jnp.concatenate([teacher[:half], back], axis=0),
        jnp.concatenate([back, teacher[:half]], axis=0),
    )
    grad_gate, grad_up, grad_down, notes = finish_call(number(chip, core), mine, others)
    return teacher_out, grad_gate, grad_up, grad_down, notes[0, 0, 0] / sd


def local(*args):
    rows, w_query, s_gate = args[0].shape[0], args[5], args[14]
    dp, ring = lax.axis_size("dp"), lax.axis_size("tensor")
    heads = w_query.shape[1] // HD
    fits = (
        dp == 2 * heads
        and heads > 1
        and ring == 4
        and heads & (heads - 1) == 0
        and w_query.shape[0] == dp * COLS
        and s_gate.shape[0] == s_gate.shape[1]
        and rows % (32 * ring) == 0
    )
    return paired(*args) if fits else general(*args)


def solution(mesh):
    in_specs = (
        P("dp", "tensor"),
        P(),
        P("dp"),
        P(),
        P(),
        P(None, "tensor"),
        P(None, "tensor"),
        P(None, "tensor"),
        P("tensor", None),
        P(None, "tensor"),
        P(None, "tensor"),
        P("tensor", None),
        P(),
        P("dp", None),
        P(None, "tensor"),
        P(None, "tensor"),
        P("tensor", None),
    )
    out_specs = (P("dp", "tensor"), P(None, "tensor"), P(None, "tensor"), P("tensor", None), P())
    return jax.shard_map(local, mesh=mesh, in_specs=in_specs, out_specs=out_specs, check_vma=False)
```

```python
import functools
import math

import jax
import jax.numpy as jnp
from jax import lax
from jax.experimental import pallas as pl
from jax.experimental.pallas import tpu as pltpu
from jax.sharding import PartitionSpec as P

HD = 128
COLS = 256
NOTE = 16
SERIES = 8
F32 = jnp.float32
BF16 = jnp.bfloat16
MIB = 1024 * 1024


def rms_scale(values):
    return values * lax.rsqrt(jnp.mean(values * values, axis=-1, keepdims=True) + 1e-05)


def frequencies(head_dim):
    indices = jnp.arange(head_dim // 2).astype(jnp.float32)
    return jnp.exp(-jnp.log(500000.0) * 2.0 * indices / head_dim)


def rotary(inputs, angles):
    half_dim = inputs.shape[-1] // 2
    cosine = jnp.cos(angles)
    sine = jnp.sin(angles)
    first_half = inputs[..., :half_dim]
    second_half = inputs[..., half_dim:]
    return jnp.concatenate(
        [first_half * cosine - second_half * sine, first_half * sine + second_half * cosine],
        axis=-1,
    )


def general(
    tokens,
    series_ids,
    offsets,
    norm_gain,
    mlp_gain,
    w_query,
    w_key,
    w_value,
    w_out,
    w_gate,
    w_up,
    w_down,
    projector,
    student_in,
    s_gate,
    s_up,
    s_down,
):
    row_count = tokens.shape[0]
    heads_dev = w_query.shape[1] // HD
    first_row = lax.axis_index("dp") * row_count
    tokens_full = lax.all_gather(tokens, "tensor", axis=1, tiled=True).astype(jnp.float32)
    normed = (rms_scale(tokens_full) * norm_gain).astype(jnp.bfloat16)
    angles = offsets.astype(jnp.float32)[:, None, None] * frequencies(HD)[None, None, :]
    queries = rotary(
        jnp.dot(normed, w_query, preferred_element_type=jnp.float32).reshape(
            row_count, heads_dev, HD
        ),
        angles,
    ).astype(jnp.bfloat16)
    keys_rot = rotary(
        jnp.dot(normed, w_key, preferred_element_type=jnp.float32).reshape(
            row_count, heads_dev, HD
        ),
        angles,
    ).astype(jnp.bfloat16)
    values_mine = jnp.dot(normed, w_value, preferred_element_type=jnp.float32).astype(jnp.bfloat16)
    keys_flat = keys_rot.reshape(row_count, heads_dev * HD)
    query_pos = first_row + jnp.arange(row_count, dtype=jnp.int32)
    query_series = lax.dynamic_slice_in_dim(series_ids, first_row, row_count, 0)
    factor = HD ** (-0.5)
    peak = jnp.full((row_count, heads_dev), -1e30, jnp.float32)
    key_block = lax.all_gather(keys_flat, "dp", axis=0, tiled=True)
    value_block = lax.all_gather(values_mine, "dp", axis=0, tiled=True)
    count = key_block.shape[0]
    key_pos = jnp.arange(count, dtype=jnp.int32)
    allowed = (
        (key_pos[None, :] >= 0)
        & (key_pos[None, :] <= query_pos[:, None])
        & (series_ids[None, :] == query_series[:, None])
    )
    scores = (
        jnp.einsum(
            "qhd,khd->qhk",
            queries,
            key_block.reshape(count, heads_dev, HD),
            preferred_element_type=jnp.float32,
        )
        * factor
    )
    scores = jnp.where(allowed[:, None, :], scores, -1e30)
    new_peak = jnp.maximum(peak, jnp.max(scores, axis=2))
    weights = jnp.where(allowed[:, None, :], jnp.exp(scores - new_peak[:, :, None]), 0.0)
    denom = jnp.sum(weights, axis=2)
    accum = jnp.einsum(
        "qhk,khd->qhd",
        weights.astype(jnp.bfloat16),
        value_block.reshape(count, heads_dev, HD),
        preferred_element_type=jnp.float32,
    )
    peak, denom, accum = (new_peak, denom, accum)
    attended = (accum / denom[:, :, None]).astype(jnp.bfloat16).reshape(row_count, heads_dev * HD)
    partial_out = jnp.dot(attended, w_out, preferred_element_type=jnp.float32)
    own_sum = lax.psum_scatter(
        partial_out.astype(jnp.bfloat16), "tensor", scatter_dimension=1, tiled=True
    ).astype(jnp.float32)
    mixed_own = (tokens.astype(jnp.float32) + own_sum).astype(jnp.bfloat16)
    mixed = lax.all_gather(mixed_own, "tensor", axis=1, tiled=True)
    normed_two = (rms_scale(mixed.astype(jnp.float32)) * mlp_gain).astype(jnp.bfloat16)
    gate_out = jnp.dot(normed_two, w_gate, preferred_element_type=jnp.float32)
    up_out = jnp.dot(normed_two, w_up, preferred_element_type=jnp.float32)
    hidden = (jax.nn.silu(gate_out) * up_out).astype(jnp.bfloat16)
    mlp_part = jnp.dot(hidden, w_down, preferred_element_type=jnp.float32)
    mlp_own = lax.psum_scatter(
        mlp_part.astype(jnp.bfloat16), "tensor", scatter_dimension=1, tiled=True
    ).astype(jnp.float32)
    teacher_out = (mixed_own.astype(jnp.float32) + mlp_own).astype(jnp.bfloat16)
    student_full = student_in.astype(jnp.float32)
    student_normed = rms_scale(student_full).astype(jnp.bfloat16)
    s_gate_out = jnp.dot(student_normed, s_gate, preferred_element_type=jnp.float32)
    s_up_out = jnp.dot(student_normed, s_up, preferred_element_type=jnp.float32)
    sigmoid_gate = jax.nn.sigmoid(s_gate_out)
    s_hidden = (s_gate_out * sigmoid_gate * s_up_out).astype(jnp.bfloat16)
    student_part = jnp.dot(s_hidden, s_down, preferred_element_type=jnp.float32)
    teacher_full = lax.all_gather(teacher_out, "tensor", axis=1, tiled=True)
    target = jnp.dot(teacher_full, projector, preferred_element_type=jnp.float32)
    student_summed = lax.psum(student_part.astype(jnp.bfloat16), "tensor").astype(jnp.float32)
    difference = student_full + student_summed - target
    total_rows = row_count * lax.axis_size("dp")
    scaled = (difference * total_rows ** (-0.5)).astype(jnp.bfloat16)
    grad_down_part = jnp.einsum("rk,rc->kc", s_hidden, scaled, preferred_element_type=jnp.float32)
    grad_hidden = jnp.einsum("rc,kc->rk", scaled, s_down, preferred_element_type=jnp.float32)
    grad_up_in = (grad_hidden * s_gate_out * sigmoid_gate).astype(jnp.bfloat16)
    grad_gate_in = (
        grad_hidden * s_up_out * sigmoid_gate * (1.0 + s_gate_out * (1.0 - sigmoid_gate))
    ).astype(jnp.bfloat16)
    grad_gate_part = jnp.einsum(
        "rc,rk->ck", student_normed, grad_gate_in, preferred_element_type=jnp.float32
    )
    grad_up_part = jnp.einsum(
        "rc,rk->ck", student_normed, grad_up_in, preferred_element_type=jnp.float32
    )
    square_sum = jnp.sum(difference * difference)
    grad_gate, grad_up, grad_down, square_total = (
        lax.psum(grad_gate_part.astype(jnp.bfloat16), "dp").astype(jnp.float32),
        lax.psum(grad_up_part.astype(jnp.bfloat16), "dp").astype(jnp.float32),
        lax.psum(grad_down_part.astype(jnp.bfloat16), "dp").astype(jnp.float32),
        lax.psum(square_sum.astype(jnp.bfloat16), "dp").astype(jnp.float32),
    )
    error = square_total / (total_rows * difference.shape[1])
    return (teacher_out, grad_gate, grad_up, grad_down, error)


def dot(a, b):
    return jnp.dot(a, b, preferred_element_type=F32)


def dot_over(a, b, dims):
    return lax.dot_general(a, b, ((dims[:1], dims[1:]), ((), ())), preferred_element_type=F32)


def params(limit):
    return pltpu.CompilerParams(vmem_limit_bytes=limit * MIB)


def whole(shape):
    return pl.BlockSpec(shape, lambda *_: (0,) * len(shape))


def cost(flops, moved, transcendentals=0):
    return pl.CostEstimate(
        flops=int(flops), bytes_accessed=int(moved), transcendentals=int(transcendentals)
    )


def qkv_kernel(info_ref, *refs, ring, heads, factor):
    blocks = [refs[:ring], refs[ring : 2 * ring]]
    gain_ref, cos_ref, sin_ref, *sources = refs[2 * ring : 2 * ring + 6]
    outs = refs[2 * ring + 6 : 2 * ring + 6 + heads]
    tok_ref, stamp_ref, normed, made, weights, sems = refs[2 * ring + 6 + heads :]
    half, width = blocks[0][0].shape
    depth = gain_ref.shape[1]
    copies = [
        pltpu.make_async_copy(source, weights.at[k], sems.at[k])
        for k, source in enumerate(sources)
    ]
    for copy in copies:
        copy.start()
    for k in range(2):
        mine = slice(k * half, (k + 1) * half)
        total = jnp.zeros((half, 1), F32)
        for block in blocks[k]:
            part = block[...].astype(F32)
            total += jnp.sum(part * part, axis=1, keepdims=True)
        scale = lax.rsqrt(total / depth + 1e-05)
        for s, block in enumerate(blocks[k]):
            at = pl.ds(pl.multiple_of(info_ref[s] * width, 128), width)
            part = block[...]
            tok_ref[mine, at] = part
            normed[mine, at] = (part.astype(F32) * scale * gain_ref[:, at]).astype(BF16)
    for kind, copy in enumerate(copies):
        copy.wait()
        result = dot(normed[...], weights[kind])
        for h in range(heads):
            head = result[:, h * HD : (h + 1) * HD]
            if kind < 2:
                head = head * cos_ref[...] + pltpu.roll(head, HD // 2, 1) * sin_ref[...]
            if kind == 0:
                head = head * factor
            made[h, kind] = head.astype(BF16)
    for f in range(heads):
        outs[f][...] = made[info_ref[ring + 1] ^ f]
    stamp_ref[...] = jnp.zeros_like(stamp_ref)


def qkv_call(info, blocks, gain, cosine, sine, *weights):
    half, width = blocks[0][0].shape
    rows, ring = 2 * half, len(blocks[0])
    depth, out_cols = weights[0].shape
    heads = out_cols // HD
    result = pl.pallas_call(
        functools.partial(
            qkv_kernel, ring=ring, heads=heads, factor=HD ** (-0.5) * math.log2(math.e)
        ),
        out_shape=[jax.ShapeDtypeStruct((3, rows, HD), BF16)] * heads
        + [jax.ShapeDtypeStruct((rows, depth), BF16), jax.ShapeDtypeStruct((8, HD), F32)],
        grid_spec=pltpu.PrefetchScalarGridSpec(
            num_scalar_prefetch=1,
            grid=(1,),
            in_specs=[whole((half, width))] * (2 * ring)
            + [whole((1, depth)), whole((rows, HD)), whole((rows, HD))]
            + [pl.BlockSpec(memory_space=pl.ANY)] * 3,
            out_specs=[whole((3, rows, HD))] * heads + [whole((rows, depth)), whole((8, HD))],
            scratch_shapes=[
                pltpu.VMEM((rows, depth), BF16),
                pltpu.VMEM((heads, 3, rows, HD), BF16),
                pltpu.VMEM((3, depth, out_cols), BF16),
                pltpu.SemaphoreType.DMA((3,)),
            ],
        ),
        compiler_params=params(42),
        cost_estimate=cost(6 * rows * depth * out_cols, 6 * depth * out_cols),
        name="qkv",
    )(info, *blocks[0], *blocks[1], gain, cosine, sine, *weights)
    return result[:heads], result[heads], result[heads + 1]


def attention_kernel(first_ref, info_ref, *refs, chips, ring):
    own, other = refs[:chips], refs[chips : 2 * chips]
    outs = refs[2 * chips : 3 * chips]
    keys_all, values_all = refs[3 * chips :]
    chip, core = info_ref[ring + 1], info_ref[ring + 2]
    half = outs[0].shape[1]
    span = 2 * half
    for f in range(chips):
        for source, side in ((own[f], core), (other[f], 1 - core)):
            at = pl.ds(pl.multiple_of(side * half, half), half)
            for odd, index in ((0, side), (1, 1 - side)):
                block = 2 * (chip ^ f) + odd
                keys_all[block, at, :] = source[1, index]
                values_all[block, :, at] = source[2, index].T

    def first_of(row):
        found = jnp.int32(0)
        for s in range(SERIES):
            edge = first_ref[s]
            found = jnp.where(edge <= row, jnp.maximum(found, edge), found)
        return found

    for f in range(chips):
        even = 2 * (chip ^ f)
        first_row = even * span + core * half
        last_row = first_row + span + half - 1
        query = jnp.concatenate([own[f][0, core], own[f][0, 1 - core]], axis=0)
        place = lax.broadcasted_iota(jnp.int32, (1, span), 1)
        row = first_row + place + jnp.where(place < half, 0, half)
        start = jnp.zeros((1, span), jnp.int32)
        for s in range(SERIES):
            edge = first_ref[s]
            start = jnp.where(edge <= row, jnp.maximum(start, edge), start)
        lane = lax.broadcasted_iota(jnp.int32, (span, 1), 0)

        def body(at, carry, masked, query=query, row=row, start=start, lane=lane):
            peak, denom, accum = carry
            scores = dot_over(keys_all[at], query, (1, 1))
            if masked:
                column = lane + at * span
                allowed = (column >= start) & (column <= row)
                scores = jnp.where(allowed, scores, -1e30)
            new_peak = jnp.maximum(peak, jnp.max(scores, axis=0, keepdims=True))
            weights = jnp.exp2(scores - new_peak)
            if masked:
                weights = jnp.where(allowed, weights, 0.0)
            keep = jnp.exp2(peak - new_peak)
            denom = denom * keep + jnp.sum(weights, axis=0, keepdims=True)
            accum = accum * keep + dot(values_all[at], weights.astype(BF16))
            return new_peak, denom, accum

        begin = first_of(first_row) // span
        full = jnp.minimum(even, (first_of(last_row) + span - 1) // span)
        carry = (
            jnp.full((1, span), -1e30, F32),
            jnp.zeros((1, span), F32),
            jnp.zeros((HD, span), F32),
        )
        carry = lax.fori_loop(begin, full, functools.partial(body, masked=True), carry)
        carry = lax.fori_loop(full, even, functools.partial(body, masked=False), carry)
        peak, denom, accum = body(even, carry, masked=True)
        outs[f][core] = (accum[:, :half] / denom[:, :half]).T.astype(BF16)
        carry = (peak[:, half:], denom[:, half:], accum[:, half:])
        _, denom, accum = body(
            even + 1, carry, True, query[half:], row[:, half:], start[:, half:], lane
        )
        outs[f][1 - core] = (accum / denom).T.astype(BF16)


def attention_call(first, info, own, other, ring):
    chips = len(own)
    _, _, half, _ = own[0].shape
    return pl.pallas_call(
        functools.partial(attention_kernel, chips=chips, ring=ring),
        out_shape=[jax.ShapeDtypeStruct((2, half, HD), BF16)] * chips,
        grid_spec=pltpu.PrefetchScalarGridSpec(
            num_scalar_prefetch=2,
            grid=(1,),
            in_specs=[whole((3, 2, half, HD))] * (2 * chips),
            out_specs=[whole((2, half, HD))] * chips,
            scratch_shapes=[
                pltpu.VMEM((2 * chips, 2 * half, HD), BF16),
                pltpu.VMEM((2 * chips, HD, 2 * half), BF16),
            ],
        ),
        compiler_params=params(24),
        cost_estimate=cost(
            4 * chips * half * 4 * chips * half * HD,
            12 * chips * half * HD * 2,
            2 * chips * half * 4 * chips * half // 2,
        ),
        name="attention",
    )(first, info, *own, *other)


def middle_kernel(info_ref, *refs, ring, chips):
    parts = [refs[:ring], refs[ring : 2 * ring]]
    refs = refs[2 * ring :]
    tok_ref, w_own_ref = refs[:2]
    near_first, near_rest = refs[2 : 2 + chips], refs[2 + chips : 2 + 2 * chips]
    far_first, far_rest = refs[2 + 2 * chips], refs[3 + 2 * chips : 3 + 3 * chips]
    refs = refs[3 + 3 * chips :]
    gain_ref, gate_ref, up_ref, wp_ref, proj_ref, student_ref = refs[:6]
    hidden_ref, own_ref = refs[6:8]
    pieces = refs[8 : 8 + ring]
    attended, mixed, total, near, far, gates, ups, wp, proj, sems = refs[8 + ring :]
    step = pl.program_id(0)
    level, chip, core = info_ref[ring], info_ref[ring + 1], info_ref[ring + 2]
    rows, depth = mixed.shape
    half = rows // 2
    width = own_ref.shape[1]
    blocks, _, wide = gates.shape

    used = iter(range(sems.shape[0]))
    copy = lambda source, target: pltpu.make_async_copy(source, target, sems.at[next(used)])
    heads = []
    for k in range(2):
        for s, part in enumerate(parts[k]):
            count = part.shape[0]
            for i in range(count):
                at = s * width + (chip ^ (k * count + i)) * HD
                at = pl.ds(pl.multiple_of(at, HD), HD)
                for side in range(2):
                    rows_at = pl.ds(side * half, half)
                    heads.append(copy(part.at[i, side], attended.at[rows_at, at]))
    slices = [
        [
            copy(near_first[f], near.at[f, 0]),
            copy(near_rest[f], near.at[f, pl.ds(1, ring - 2)]),
            copy(far_first.at[f, 0], far.at[f, 0]),
            copy(far_rest[f], far.at[f, pl.ds(1, ring - 2)]),
        ]
        for f in range(chips)
    ]
    own_rows = pl.ds(pl.multiple_of(level * width, width), width)
    late = [copy(proj_ref.at[own_rows], proj), copy(student_ref, total)]
    columns = [pl.ds(i * wide, wide) for i in range(blocks)]
    units = [
        [
            copy(gate_ref.at[:, columns[i]], gates.at[i]),
            copy(up_ref.at[:, columns[i]], ups.at[i]),
            copy(wp_ref.at[columns[i]], wp.at[i]),
        ]
        for i in range(blocks)
    ]

    @pl.when(step == 0)
    def _():
        for c in heads + slices[0]:
            c.start()
        for c in sum(slices[1:], []) + late:
            c.start()
        for c in heads:
            c.wait()

    for f in range(chips):

        @pl.when(step == f)
        def _(f=f):
            for c in slices[f]:
                c.wait()
            for c in sum(units[f::chips], []):
                c.start()

    @pl.when(step < chips)
    def _():
        for gathered, side in ((near, core), (far, 1 - core)):
            here = pl.ds(pl.multiple_of(side * COLS, COLS), COLS)
            result = tok_ref[:, here].astype(F32) + dot(attended[:, :width], w_own_ref[:, here])
            weight = gathered[step].reshape(depth - width, COLS)
            result += dot(attended[:, width:], weight)
            at = pl.ds(pl.multiple_of((2 * (step ^ chip) + side) * COLS, COLS), COLS)
            mixed[:, at] = result.astype(BF16)

    @pl.when(step == chips)
    def _():
        for c in late:
            c.wait()
        values = mixed[...].astype(F32)
        attended[...] = (rms_scale(values) * gain_ref[...]).astype(BF16)
        own = mixed[:, pl.ds(pl.multiple_of(level * width, 128), width)]
        own_ref[...] = own
        total[...] -= dot(own, proj[...])

    for i in range(blocks):

        @pl.when(step == chips + i)
        def _(i=i):
            for c in units[i]:
                c.wait()

    @pl.when(step >= chips)
    def _():
        index = step - chips
        gate = dot(attended[...], gates[index])
        up = dot(attended[...], ups[index])
        hidden = (gate * jax.nn.sigmoid(gate) * up).astype(BF16)
        hidden_ref[...] = hidden
        total[...] -= dot(hidden, wp[index])

    @pl.when(step == pl.num_programs(0) - 1)
    def _():
        size = rows // ring
        for s in range(ring):
            at = pl.ds(pl.multiple_of(((level + s) & (ring - 1)) * size, size), size)
            pieces[s][...] = total[at, :].astype(BF16)


def middle_call(info, parts, tok, w_out, near, far, gain, w_gate, w_up, wp, projector, student):
    rows, depth = tok.shape
    ring, chips = len(parts[0]), len(near[0])
    units = w_gate.shape[1]
    wide = 2 * COLS
    width = depth // ring
    sd = projector.shape[1]
    blocks = units // wide
    tile = lambda j, info: (0, jnp.minimum(j, chips - 1) ^ info[ring + 1])
    late = lambda j, info: (0, jnp.maximum(j - chips, 0))
    anywhere = pl.BlockSpec(memory_space=pl.ANY)
    count = 2 * ring * parts[0][0].shape[0] * 2 + 4 * chips + 2 + 3 * blocks
    result = pl.pallas_call(
        functools.partial(middle_kernel, ring=ring, chips=chips),
        out_shape=[
            jax.ShapeDtypeStruct((rows, units), BF16),
            jax.ShapeDtypeStruct((rows, width), BF16),
        ]
        + [jax.ShapeDtypeStruct((rows // ring, sd), BF16)] * ring,
        grid_spec=pltpu.PrefetchScalarGridSpec(
            num_scalar_prefetch=1,
            grid=(chips + blocks,),
            in_specs=[anywhere] * (2 * ring)
            + [pl.BlockSpec((rows, wide), tile), pl.BlockSpec((width, wide), tile)]
            + [anywhere] * (3 * chips + 1)
            + [whole((1, depth))]
            + [anywhere] * 5,
            out_specs=[
                pl.BlockSpec((rows, wide), late),
                whole((rows, width)),
            ]
            + [whole((rows // ring, sd))] * ring,
            scratch_shapes=[
                pltpu.VMEM((rows, depth), BF16),
                pltpu.VMEM((rows, depth), BF16),
                pltpu.VMEM((rows, sd), F32),
                pltpu.VMEM((chips, ring - 1, width, COLS), BF16),
                pltpu.VMEM((chips, ring - 1, width, COLS), BF16),
                pltpu.VMEM((blocks, depth, wide), BF16),
                pltpu.VMEM((blocks, depth, wide), BF16),
                pltpu.VMEM((blocks, wide, sd), BF16),
                pltpu.VMEM((width, sd), BF16),
                pltpu.SemaphoreType.DMA((count,)),
            ],
        ),
        compiler_params=params(42),
        cost_estimate=cost(
            2 * rows * depth * (depth + 2 * units) + 2 * rows * sd * (units + width),
            2 * depth * (depth + 2 * units),
            rows * units,
        ),
        name="middle",
    )(
        info,
        *parts[0],
        *parts[1],
        tok,
        w_out,
        *near[0],
        *near[1],
        far[0],
        *far[1],
        gain,
        w_gate,
        w_up,
        wp,
        projector,
        student,
    )
    return result[0], result[1], result[2:]


def down_kernel(info_ref, hidden_ref, weight_ref, *outs):
    result = dot(hidden_ref[...], weight_ref[...]).astype(BF16)
    for j, out in enumerate(outs):

        @pl.when(pl.program_id(0) == j)
        def _(out=out):
            out[...] = result


def down_call(info, hidden, w_down, ring):
    rows, units = hidden.shape
    depth = w_down.shape[1]
    width = depth // ring
    return pl.pallas_call(
        down_kernel,
        out_shape=[jax.ShapeDtypeStruct((rows, width), BF16)] * ring,
        grid_spec=pltpu.PrefetchScalarGridSpec(
            num_scalar_prefetch=1,
            grid=(ring,),
            in_specs=[
                whole((rows, units)),
                pl.BlockSpec((units, width), lambda j, info: (0, info[ring] ^ (ring - 1 - j))),
            ],
            out_specs=[whole((rows, width))] * ring,
        ),
        compiler_params=params(24),
        cost_estimate=cost(2 * rows * units * depth, 2 * units * depth),
        name="down",
    )(info, hidden, w_down)


def grads_kernel(info_ref, *refs, ring, chips):
    pieces = refs[:ring]
    normed_ref, hidden_ref, s_down_ref, up_ref, gate_ref = refs[ring : ring + 5]
    keep_ref, give_ref, scaled, grads = refs[ring + 5 :]
    chip, core = info_ref[ring + 1], info_ref[ring + 2]
    size, sd = pieces[0].shape
    for s in range(ring):
        scaled[pl.ds(pl.multiple_of(info_ref[s] * size, size), size), :] = pieces[s][...]
    value = scaled[...]
    wide = value.astype(F32)
    error = jnp.sum(wide * wide)
    grad_hidden = dot_over(value, s_down_ref[...], (1, 1))
    grads[0] = dot_over(normed_ref[...], (grad_hidden * gate_ref[...].astype(F32)).astype(BF16), (0, 0))
    grads[1] = dot_over(normed_ref[...], (grad_hidden * up_ref[...].astype(F32)).astype(BF16), (0, 0))
    grads[2] = dot_over(hidden_ref[...], value, (0, 0))
    share = grads.shape[1] // (2 * chips)
    for f in range(chips):
        for k in range(3):
            for part, ref in ((core, keep_ref), (1 - core, give_ref)):
                at = pl.multiple_of((part * chips + (chip ^ f)) * share, share)
                ref[f, k * share : (k + 1) * share] = grads[k, pl.ds(at, share), :].astype(
                    ref.dtype
                )
        for ref in (keep_ref, give_ref):
            ref[f, 3 * share :] = jnp.full((NOTE, sd), error, F32).astype(ref.dtype)


def grads_call(info, pieces, normed, hidden, s_down, up, gate, chips):
    ring = len(pieces)
    rows, sd = normed.shape
    units = hidden.shape[1]
    share = 3 * sd // (2 * chips) + NOTE
    operands = [*pieces, normed, hidden, s_down, up, gate]
    return pl.pallas_call(
        functools.partial(grads_kernel, ring=ring, chips=chips),
        out_shape=(
            jax.ShapeDtypeStruct((chips, share, units), F32),
            jax.ShapeDtypeStruct((chips, share, units), BF16),
        ),
        grid_spec=pltpu.PrefetchScalarGridSpec(
            num_scalar_prefetch=1,
            grid=(1,),
            in_specs=[whole(a.shape) for a in operands],
            out_specs=(whole((chips, share, units)), whole((chips, share, units))),
            scratch_shapes=[pltpu.VMEM((rows, sd), BF16), pltpu.VMEM((3, sd, units), F32)],
        ),
        compiler_params=params(22),
        cost_estimate=cost(8 * rows * sd * units, 20 * sd * units),
        name="grads",
    )(info, *operands)


def pair_kernel(keep_ref, theirs_ref, *outs):
    for f, out in enumerate(outs):
        out[...] = (keep_ref[f] + theirs_ref[f].astype(F32)).astype(out.dtype)


def pair_call(keep, theirs):
    chips, share, sd = keep.shape
    return pl.pallas_call(
        pair_kernel,
        out_shape=[jax.ShapeDtypeStruct((share, sd), BF16)] * chips,
        compiler_params=params(10),
        cost_estimate=cost(keep.size, 8 * keep.size),
        name="pair",
    )(keep, theirs)


def finish_kernel(info_ref, *refs, chips, ring):
    mine, others = refs[:chips], refs[chips : 2 * chips]
    outs = refs[2 * chips : 2 * chips + 3]
    notes = refs[2 * chips + 3]
    chip, core = info_ref[ring + 1], info_ref[ring + 2]
    share = (mine[0].shape[0] - NOTE) // 3
    for f in range(chips):
        for part, ref in ((core, mine[f]), (1 - core, others[f])):
            index = part * chips + (chip ^ f)
            at = pl.ds(pl.multiple_of(index * share, share), share)
            for k in range(3):
                outs[k][at, :] = ref[k * share : (k + 1) * share].astype(F32)
            notes[index] = ref[3 * share :, :HD].astype(F32)


def finish_call(info, mine, others, ring):
    chips = len(mine)
    share, sd = mine[0].shape
    rows = (share - NOTE) // 3 * 2 * chips
    return pl.pallas_call(
        functools.partial(finish_kernel, chips=chips, ring=ring),
        out_shape=[jax.ShapeDtypeStruct((rows, sd), F32)] * 3
        + [jax.ShapeDtypeStruct((2 * chips, NOTE, HD), F32)],
        grid_spec=pltpu.PrefetchScalarGridSpec(
            num_scalar_prefetch=1,
            grid=(1,),
            in_specs=[whole((share, sd))] * (2 * chips),
            out_specs=[whole((rows, sd))] * 3 + [whole((2 * chips, NOTE, HD))],
        ),
        compiler_params=params(14),
        cost_estimate=cost(rows * sd, 12 * rows * sd),
        name="finish",
    )(info, *mine, *others)


def step_on(block, axis):
    size = lax.axis_size(axis)
    return lax.ppermute(block, axis, [(i, (i + 1) % size) for i in range(size)])


def ring_gather(block, axis, steps=None):
    blocks = [block]
    for _ in range(lax.axis_size(axis) - 1 if steps is None else steps):
        blocks.append(step_on(blocks[-1], axis))
    return blocks


def shifted(pieces, axis):
    size = lax.axis_size(axis)
    moved = [
        lax.ppermute(pieces[s], axis, [(i, (i + s) % size) for i in range(size)])
        for s in range(1, size)
    ]
    return [pieces[0], *moved]


def flipped(pieces):
    size = lax.axis_size("dp")
    moved = [
        lax.ppermute(pieces[f], "dp", [(i, i ^ (2 * f)) for i in range(size)])
        for f in range(1, len(pieces))
    ]
    return [pieces[0], *moved]


def swapped(value):
    size = lax.axis_size("dp")
    return lax.ppermute(value, "dp", [(i, i ^ 1) for i in range(size)])


def after(value, *others):
    return lax.optimization_barrier((value, *others))[0]


def paired(
    tokens,
    series_ids,
    offsets,
    norm_gain,
    mlp_gain,
    w_query,
    w_key,
    w_value,
    w_out,
    w_gate,
    w_up,
    w_down,
    projector,
    student_in,
    s_gate,
    s_up,
    s_down,
):
    rows = tokens.shape[0]
    depth, sd = w_query.shape[0], student_in.shape[1]
    dp, ring = lax.axis_size("dp"), lax.axis_size("tensor")
    here, level = lax.axis_index("dp"), lax.axis_index("tensor")
    chips, half = dp // 2, rows // 2
    total_rows = rows * dp
    size = rows // ring
    slice_cols = depth // dp

    places = [(level - s) & (ring - 1) for s in range(ring)] + [level, here >> 1, here & 1]
    slots = lax.broadcasted_iota(jnp.int32, (16,), 0)
    info = sum(jnp.where(slots == k, place, 0) for k, place in enumerate(places))
    starts = jnp.stack([here & 1, (here & 1) ^ 1, level * size, here * slice_cols])
    *starts, zero = [starts[k].astype(jnp.uint32) for k in range(4)] + [jnp.uint32(0)]
    first_core = (here & 1) == 0
    tokens, info, first_core, *starts = lax.optimization_barrier(
        (tokens, info, first_core, *starts)
    )

    def deal(value):
        parts = value.reshape((2, half) + value.shape[1:])
        shape = (1,) + parts.shape[1:]
        rest = [zero] * (parts.ndim - 1)
        kept, given = [lax.dynamic_slice(parts, [k, *rest], shape)[0] for k in starts[:2]]
        return kept, swapped(given)

    token_chunks = deal(tokens)
    token_rings = [ring_gather(chunk, "tensor") for chunk in token_chunks]
    student_chunks = deal(student_in)
    offset_chunks = deal(offsets.astype(F32))

    angles = jnp.concatenate(offset_chunks)[:, None] * frequencies(HD)[None, :]
    cosine, sine = jnp.cos(angles), jnp.sin(angles)
    cosine = jnp.concatenate([cosine, cosine], axis=1)
    sine = jnp.concatenate([-sine, sine], axis=1)
    student_full = jnp.concatenate(student_chunks, axis=0).astype(F32)
    student_normed = rms_scale(student_full).astype(BF16)
    below = jnp.sum(
        series_ids[None, :] < jnp.arange(SERIES, dtype=jnp.int32)[:, None], axis=1, dtype=jnp.int32
    )

    made, tok_full, stamp = qkv_call(
        info, token_rings, norm_gain[None, :], cosine, sine, w_query, w_key, w_value
    )

    held = lax.optimization_barrier((student_normed, projector, stamp))
    student_normed = held[0]
    s_gate_out = dot(student_normed, s_gate)
    s_up_out = dot(student_normed, s_up)
    sigmoid_gate = jax.nn.sigmoid(s_gate_out)
    up_slope = s_gate_out * sigmoid_gate
    gate_slope = s_up_out * sigmoid_gate * (1.0 + s_gate_out * (1.0 - sigmoid_gate))
    s_hidden = (up_slope * s_up_out).astype(BF16)
    up_slope, gate_slope = up_slope.astype(BF16), gate_slope.astype(BF16)
    student_part = dot(s_hidden, s_down)
    projected = dot(w_down, held[1]).astype(BF16)
    student_own = lax.dynamic_slice(student_full, [starts[2], zero], (size, sd))
    early = (projected, student_part, s_hidden, up_slope, gate_slope, student_normed, student_own)

    w_slice = lax.dynamic_slice(w_out, [zero, starts[3]], (w_out.shape[0], slice_cols))
    w_slice = after(w_slice, stamp)
    w_others = shifted([w_slice] * ring, "tensor")[1:]

    own = flipped(made)
    held = lax.optimization_barrier((*own, *w_others[:2], *early))
    own, w_others[:2] = held[:chips], held[chips : chips + 2]
    other = [swapped(a) for a in own]
    near_first = flipped([w_others[0]] * chips)
    pairs = lambda a: a.reshape(3, 2, half, HD)
    made = attention_call(
        below, info, [pairs(a) for a in own], [pairs(a) for a in other], ring
    )
    held = lax.optimization_barrier((*made, *w_others[1:], *near_first))
    made, w_rest = held[:chips], jnp.stack(held[chips : chips + ring - 2])
    attended = lax.optimization_barrier(tuple(flipped(made)))
    parts = [
        ring_gather(jnp.stack(attended[k : k + chips // 2]), "tensor") for k in (0, chips // 2)
    ]
    w_rest = after(w_rest, *attended)
    near_rest = flipped([w_rest] * chips)
    far_first = swapped(after(jnp.stack(near_first)[:, None], *attended))
    far_rest = [swapped(after(a, parts[1][1])) for a in near_rest]

    hidden, mixed_own, pieces = middle_call(
        info,
        parts,
        tok_full,
        w_out,
        (near_first, near_rest),
        (far_first, far_rest),
        mlp_gain[None, :],
        w_gate,
        w_up,
        projected,
        projector,
        student_part,
    )

    own = student_own
    moved = shifted(pieces, "tensor")
    difference = own + sum(piece.astype(F32) for piece in moved)
    own = (difference * total_rows ** (-0.5)).astype(BF16)
    scaled = shifted([own] * ring, "tensor")

    far_theirs, far_mine, near_theirs, kept = down_call(
        info, after(hidden, *moved[1:]), w_down, ring
    )
    over = lambda value, bit: lax.ppermute(value, "tensor", [(i, i ^ bit) for i in range(ring)])
    far_sum = over(after(far_theirs, *scaled), 1)

    keep, give = grads_call(
        after(info, kept),
        scaled,
        student_normed,
        s_hidden,
        s_down,
        up_slope,
        gate_slope,
        chips,
    )
    far_sum = (after(far_sum, keep).astype(F32) + far_mine.astype(F32)).astype(BF16)
    shares = flipped(pair_call(keep, after(swapped(give), far_sum)))
    own = sum(share.astype(F32) for share in shares).astype(BF16)
    mine = flipped([own] * chips)
    others = [swapped(share) for share in mine]

    level_sums = [over(after(near_theirs, far_sum), 1), over(far_sum, 2)]
    mlp_own = sum(after(value, mine[-1]).astype(F32) for value in level_sums)
    teacher = mixed_own.astype(F32) + (kept.astype(F32) + mlp_own)
    teacher = teacher.astype(BF16)
    back = swapped(teacher[half:])
    teacher_out = jnp.where(
        first_core,
        jnp.concatenate([teacher[:half], back], axis=0),
        jnp.concatenate([back, teacher[:half]], axis=0),
    )
    grad_gate, grad_up, grad_down, notes = finish_call(info, mine, others, ring)
    return teacher_out, grad_gate, grad_up, grad_down, notes[0, 0, 0] / sd


def local(*args):
    rows, w_query, s_gate = args[0].shape[0], args[5], args[14]
    dp, ring = lax.axis_size("dp"), lax.axis_size("tensor")
    heads = w_query.shape[1] // HD
    fits = (
        dp == 2 * heads
        and heads > 1
        and ring == 4
        and heads & (heads - 1) == 0
        and w_query.shape[0] == dp * COLS
        and s_gate.shape[0] == s_gate.shape[1]
        and rows % (32 * ring) == 0
    )
    return paired(*args) if fits else general(*args)


def solution(mesh):
    in_specs = (
        P("dp", "tensor"),
        P(),
        P("dp"),
        P(),
        P(),
        P(None, "tensor"),
        P(None, "tensor"),
        P(None, "tensor"),
        P("tensor", None),
        P(None, "tensor"),
        P(None, "tensor"),
        P("tensor", None),
        P(),
        P("dp", None),
        P(None, "tensor"),
        P(None, "tensor"),
        P("tensor", None),
    )
    out_specs = (P("dp", "tensor"), P(None, "tensor"), P(None, "tensor"), P("tensor", None), P())
    return jax.shard_map(local, mesh=mesh, in_specs=in_specs, out_specs=out_specs, check_vma=False)
```

```python
import functools
import math

import jax
import jax.numpy as jnp
from jax import lax
from jax.experimental import pallas as pl
from jax.experimental.pallas import tpu as pltpu
from jax.sharding import PartitionSpec as P

HD = 128
COLS = 256
NOTE = 16
SERIES = 8
F32 = jnp.float32
BF16 = jnp.bfloat16
MIB = 1024 * 1024


def rms_scale(values):
    return values * lax.rsqrt(jnp.mean(values * values, axis=-1, keepdims=True) + 1e-05)


def frequencies(head_dim):
    indices = jnp.arange(head_dim // 2).astype(jnp.float32)
    return jnp.exp(-jnp.log(500000.0) * 2.0 * indices / head_dim)


def rotary(inputs, angles):
    half_dim = inputs.shape[-1] // 2
    cosine = jnp.cos(angles)
    sine = jnp.sin(angles)
    first_half = inputs[..., :half_dim]
    second_half = inputs[..., half_dim:]
    return jnp.concatenate(
        [first_half * cosine - second_half * sine, first_half * sine + second_half * cosine],
        axis=-1,
    )


def general(
    tokens,
    series_ids,
    offsets,
    norm_gain,
    mlp_gain,
    w_query,
    w_key,
    w_value,
    w_out,
    w_gate,
    w_up,
    w_down,
    projector,
    student_in,
    s_gate,
    s_up,
    s_down,
):
    row_count = tokens.shape[0]
    heads_dev = w_query.shape[1] // HD
    first_row = lax.axis_index("dp") * row_count
    tokens_full = lax.all_gather(tokens, "tensor", axis=1, tiled=True).astype(jnp.float32)
    normed = (rms_scale(tokens_full) * norm_gain).astype(jnp.bfloat16)
    angles = offsets.astype(jnp.float32)[:, None, None] * frequencies(HD)[None, None, :]
    queries = rotary(
        jnp.dot(normed, w_query, preferred_element_type=jnp.float32).reshape(
            row_count, heads_dev, HD
        ),
        angles,
    ).astype(jnp.bfloat16)
    keys_rot = rotary(
        jnp.dot(normed, w_key, preferred_element_type=jnp.float32).reshape(
            row_count, heads_dev, HD
        ),
        angles,
    ).astype(jnp.bfloat16)
    values_mine = jnp.dot(normed, w_value, preferred_element_type=jnp.float32).astype(jnp.bfloat16)
    keys_flat = keys_rot.reshape(row_count, heads_dev * HD)
    query_pos = first_row + jnp.arange(row_count, dtype=jnp.int32)
    query_series = lax.dynamic_slice_in_dim(series_ids, first_row, row_count, 0)
    factor = HD ** (-0.5)
    peak = jnp.full((row_count, heads_dev), -1e30, jnp.float32)
    key_block = lax.all_gather(keys_flat, "dp", axis=0, tiled=True)
    value_block = lax.all_gather(values_mine, "dp", axis=0, tiled=True)
    count = key_block.shape[0]
    key_pos = jnp.arange(count, dtype=jnp.int32)
    allowed = (
        (key_pos[None, :] >= 0)
        & (key_pos[None, :] <= query_pos[:, None])
        & (series_ids[None, :] == query_series[:, None])
    )
    scores = (
        jnp.einsum(
            "qhd,khd->qhk",
            queries,
            key_block.reshape(count, heads_dev, HD),
            preferred_element_type=jnp.float32,
        )
        * factor
    )
    scores = jnp.where(allowed[:, None, :], scores, -1e30)
    new_peak = jnp.maximum(peak, jnp.max(scores, axis=2))
    weights = jnp.where(allowed[:, None, :], jnp.exp(scores - new_peak[:, :, None]), 0.0)
    denom = jnp.sum(weights, axis=2)
    accum = jnp.einsum(
        "qhk,khd->qhd",
        weights.astype(jnp.bfloat16),
        value_block.reshape(count, heads_dev, HD),
        preferred_element_type=jnp.float32,
    )
    peak, denom, accum = (new_peak, denom, accum)
    attended = (accum / denom[:, :, None]).astype(jnp.bfloat16).reshape(row_count, heads_dev * HD)
    partial_out = jnp.dot(attended, w_out, preferred_element_type=jnp.float32)
    own_sum = lax.psum_scatter(
        partial_out.astype(jnp.bfloat16), "tensor", scatter_dimension=1, tiled=True
    ).astype(jnp.float32)
    mixed_own = (tokens.astype(jnp.float32) + own_sum).astype(jnp.bfloat16)
    mixed = lax.all_gather(mixed_own, "tensor", axis=1, tiled=True)
    normed_two = (rms_scale(mixed.astype(jnp.float32)) * mlp_gain).astype(jnp.bfloat16)
    gate_out = jnp.dot(normed_two, w_gate, preferred_element_type=jnp.float32)
    up_out = jnp.dot(normed_two, w_up, preferred_element_type=jnp.float32)
    hidden = (jax.nn.silu(gate_out) * up_out).astype(jnp.bfloat16)
    mlp_part = jnp.dot(hidden, w_down, preferred_element_type=jnp.float32)
    mlp_own = lax.psum_scatter(
        mlp_part.astype(jnp.bfloat16), "tensor", scatter_dimension=1, tiled=True
    ).astype(jnp.float32)
    teacher_out = (mixed_own.astype(jnp.float32) + mlp_own).astype(jnp.bfloat16)
    student_full = student_in.astype(jnp.float32)
    student_normed = rms_scale(student_full).astype(jnp.bfloat16)
    s_gate_out = jnp.dot(student_normed, s_gate, preferred_element_type=jnp.float32)
    s_up_out = jnp.dot(student_normed, s_up, preferred_element_type=jnp.float32)
    sigmoid_gate = jax.nn.sigmoid(s_gate_out)
    s_hidden = (s_gate_out * sigmoid_gate * s_up_out).astype(jnp.bfloat16)
    student_part = jnp.dot(s_hidden, s_down, preferred_element_type=jnp.float32)
    teacher_full = lax.all_gather(teacher_out, "tensor", axis=1, tiled=True)
    target = jnp.dot(teacher_full, projector, preferred_element_type=jnp.float32)
    student_summed = lax.psum(student_part.astype(jnp.bfloat16), "tensor").astype(jnp.float32)
    difference = student_full + student_summed - target
    total_rows = row_count * lax.axis_size("dp")
    scaled = (difference * total_rows ** (-0.5)).astype(jnp.bfloat16)
    grad_down_part = jnp.einsum("rk,rc->kc", s_hidden, scaled, preferred_element_type=jnp.float32)
    grad_hidden = jnp.einsum("rc,kc->rk", scaled, s_down, preferred_element_type=jnp.float32)
    grad_up_in = (grad_hidden * s_gate_out * sigmoid_gate).astype(jnp.bfloat16)
    grad_gate_in = (
        grad_hidden * s_up_out * sigmoid_gate * (1.0 + s_gate_out * (1.0 - sigmoid_gate))
    ).astype(jnp.bfloat16)
    grad_gate_part = jnp.einsum(
        "rc,rk->ck", student_normed, grad_gate_in, preferred_element_type=jnp.float32
    )
    grad_up_part = jnp.einsum(
        "rc,rk->ck", student_normed, grad_up_in, preferred_element_type=jnp.float32
    )
    square_sum = jnp.sum(difference * difference)
    grad_gate, grad_up, grad_down, square_total = (
        lax.psum(grad_gate_part.astype(jnp.bfloat16), "dp").astype(jnp.float32),
        lax.psum(grad_up_part.astype(jnp.bfloat16), "dp").astype(jnp.float32),
        lax.psum(grad_down_part.astype(jnp.bfloat16), "dp").astype(jnp.float32),
        lax.psum(square_sum.astype(jnp.bfloat16), "dp").astype(jnp.float32),
    )
    error = square_total / (total_rows * difference.shape[1])
    return (teacher_out, grad_gate, grad_up, grad_down, error)


def dot(a, b):
    return jnp.dot(a, b, preferred_element_type=F32)


def dot_over(a, b, dims):
    return lax.dot_general(a, b, ((dims[:1], dims[1:]), ((), ())), preferred_element_type=F32)


def params(limit):
    return pltpu.CompilerParams(vmem_limit_bytes=limit * MIB)


def whole(shape):
    return pl.BlockSpec(shape, lambda *_: (0,) * len(shape))


def cost(flops, moved, transcendentals=0):
    return pl.CostEstimate(
        flops=int(flops), bytes_accessed=int(moved), transcendentals=int(transcendentals)
    )


def qkv_kernel(info_ref, *refs, ring, heads, factor):
    blocks = [refs[:ring], refs[ring : 2 * ring]]
    gain_ref, cos_ref, sin_ref, *sources = refs[2 * ring : 2 * ring + 6]
    outs = refs[2 * ring + 6 : 2 * ring + 6 + heads]
    tok_ref, normed, made, weights, sems = refs[2 * ring + 6 + heads :]
    half, width = blocks[0][0].shape
    depth = gain_ref.shape[1]
    copies = [
        pltpu.make_async_copy(source, weights.at[k], sems.at[k])
        for k, source in enumerate(sources)
    ]
    for copy in copies:
        copy.start()
    for k in range(2):
        mine = slice(k * half, (k + 1) * half)
        total = jnp.zeros((half, 1), F32)
        for block in blocks[k]:
            part = block[...].astype(F32)
            total += jnp.sum(part * part, axis=1, keepdims=True)
        scale = lax.rsqrt(total / depth + 1e-05)
        for s, block in enumerate(blocks[k]):
            at = pl.ds(pl.multiple_of(info_ref[s] * width, 128), width)
            part = block[...]
            tok_ref[mine, at] = part
            normed[mine, at] = (part.astype(F32) * scale * gain_ref[:, at]).astype(BF16)
    for kind, copy in enumerate(copies):
        copy.wait()
        result = dot(normed[...], weights[kind])
        for h in range(heads):
            head = result[:, h * HD : (h + 1) * HD]
            if kind < 2:
                head = head * cos_ref[...] + pltpu.roll(head, HD // 2, 1) * sin_ref[...]
            if kind == 0:
                head = head * factor
            made[h, kind] = head.astype(BF16)
    for f in range(heads):
        outs[f][...] = made[info_ref[ring + 1] ^ f]


def qkv_call(info, blocks, gain, cosine, sine, *weights):
    half, width = blocks[0][0].shape
    rows, ring = 2 * half, len(blocks[0])
    depth, out_cols = weights[0].shape
    heads = out_cols // HD
    result = pl.pallas_call(
        functools.partial(
            qkv_kernel, ring=ring, heads=heads, factor=HD ** (-0.5) * math.log2(math.e)
        ),
        out_shape=[jax.ShapeDtypeStruct((3, rows, HD), BF16)] * heads
        + [jax.ShapeDtypeStruct((rows, depth), BF16)],
        grid_spec=pltpu.PrefetchScalarGridSpec(
            num_scalar_prefetch=1,
            grid=(1,),
            in_specs=[whole((half, width))] * (2 * ring)
            + [whole((1, depth)), whole((rows, HD)), whole((rows, HD))]
            + [pl.BlockSpec(memory_space=pl.ANY)] * 3,
            out_specs=[whole((3, rows, HD))] * heads + [whole((rows, depth))],
            scratch_shapes=[
                pltpu.VMEM((rows, depth), BF16),
                pltpu.VMEM((heads, 3, rows, HD), BF16),
                pltpu.VMEM((3, depth, out_cols), BF16),
                pltpu.SemaphoreType.DMA((3,)),
            ],
        ),
        compiler_params=params(42),
        cost_estimate=cost(6 * rows * depth * out_cols, 6 * depth * out_cols),
        name="qkv",
    )(info, *blocks[0], *blocks[1], gain, cosine, sine, *weights)
    return result[:heads], result[heads]


def attention_kernel(first_ref, info_ref, *refs, chips, ring):
    own, other = refs[:chips], refs[chips : 2 * chips]
    outs = refs[2 * chips : 3 * chips]
    keys_all, values_all = refs[3 * chips :]
    chip, core = info_ref[ring + 1], info_ref[ring + 2]
    span = outs[0].shape[0]
    for f in range(chips):
        for source, side in ((own[f], core), (other[f], 1 - core)):
            block = 2 * (chip ^ f) + side
            keys_all[block] = source[1]
            values_all[block] = source[2].T

    def first_of(row):
        found = jnp.int32(0)
        for s in range(SERIES):
            edge = first_ref[s]
            found = jnp.where(edge <= row, jnp.maximum(found, edge), found)
        return found

    for f in range(chips):
        last = 2 * (chip ^ f) + core
        query = own[f][0]
        row = last * span + lax.broadcasted_iota(jnp.int32, (1, span), 1)
        start = jnp.zeros((1, span), jnp.int32)
        for s in range(SERIES):
            edge = first_ref[s]
            start = jnp.where(edge <= row, jnp.maximum(start, edge), start)
        lane = lax.broadcasted_iota(jnp.int32, (span, 1), 0)

        def body(at, carry, masked, query=query, row=row, start=start, lane=lane):
            peak, denom, accum = carry
            scores = dot_over(keys_all[at], query, (1, 1))
            if masked:
                column = lane + at * span
                allowed = (column >= start) & (column <= row)
                scores = jnp.where(allowed, scores, -1e30)
            new_peak = jnp.maximum(peak, jnp.max(scores, axis=0, keepdims=True))
            weights = jnp.exp2(scores - new_peak)
            if masked:
                weights = jnp.where(allowed, weights, 0.0)
            keep = jnp.exp2(peak - new_peak)
            denom = denom * keep + jnp.sum(weights, axis=0, keepdims=True)
            accum = accum * keep + dot(values_all[at], weights.astype(BF16))
            return new_peak, denom, accum

        begin = first_of(last * span) // span
        full = jnp.minimum(last, (first_of(last * span + span - 1) + span - 1) // span)
        carry = (
            jnp.full((1, span), -1e30, F32),
            jnp.zeros((1, span), F32),
            jnp.zeros((HD, span), F32),
        )
        carry = lax.fori_loop(begin, full, functools.partial(body, masked=True), carry)
        carry = lax.fori_loop(full, last, functools.partial(body, masked=False), carry)
        _, denom, accum = body(last, carry, masked=True)
        outs[f][...] = (accum / denom).T.astype(BF16)


def attention_call(first, info, own, other, ring):
    chips = len(own)
    _, rows, _ = own[0].shape
    return pl.pallas_call(
        functools.partial(attention_kernel, chips=chips, ring=ring),
        out_shape=[jax.ShapeDtypeStruct((rows, HD), BF16)] * chips,
        grid_spec=pltpu.PrefetchScalarGridSpec(
            num_scalar_prefetch=2,
            grid=(1,),
            in_specs=[whole((3, rows, HD))] * (2 * chips),
            out_specs=[whole((rows, HD))] * chips,
            scratch_shapes=[
                pltpu.VMEM((2 * chips, rows, HD), BF16),
                pltpu.VMEM((2 * chips, HD, rows), BF16),
            ],
        ),
        compiler_params=params(24),
        cost_estimate=cost(
            4 * chips * rows * chips * rows * HD,
            16 * chips * rows * HD,
            chips * rows * chips * rows,
        ),
        name="attention",
    )(first, info, *own, *other)


def middle_kernel(info_ref, *refs, ring, chips):
    parts = [refs[:ring], refs[ring : 2 * ring]]
    refs = refs[2 * ring :]
    tok_ref, w_own_ref = refs[:2]
    near_first, near_rest = refs[2 : 2 + chips], refs[2 + chips : 2 + 2 * chips]
    far_first, far_rest = refs[2 + 2 * chips], refs[3 + 2 * chips : 3 + 3 * chips]
    refs = refs[3 + 3 * chips :]
    gain_ref, gate_ref, up_ref, wp_ref, proj_ref, student_ref = refs[:6]
    hidden_ref, own_ref = refs[6:8]
    pieces = refs[8 : 8 + ring]
    attended, mixed, total, near, far, gates, ups, wp, proj, sems = refs[8 + ring :]
    step = pl.program_id(0)
    level, chip, core = info_ref[ring], info_ref[ring + 1], info_ref[ring + 2]
    rows, depth = mixed.shape
    width = own_ref.shape[1]
    blocks, _, wide = gates.shape

    used = iter(range(sems.shape[0]))
    copy = lambda source, target: pltpu.make_async_copy(source, target, sems.at[next(used)])
    heads = []
    for k in range(2):
        for s, part in enumerate(parts[k]):
            count = part.shape[0]
            for i in range(count):
                at = (level ^ info_ref[s]) * width + (chip ^ (k * count + i)) * HD
                heads.append(copy(part.at[i], attended.at[:, pl.ds(pl.multiple_of(at, HD), HD)]))
    slices = [
        [
            copy(near_first[f], near.at[f, 0]),
            copy(near_rest[f], near.at[f, pl.ds(1, ring - 2)]),
            copy(far_first.at[f, 0], far.at[f, 0]),
            copy(far_rest[f], far.at[f, pl.ds(1, ring - 2)]),
        ]
        for f in range(chips)
    ]
    own_rows = pl.ds(pl.multiple_of(level * width, width), width)
    late = [copy(proj_ref.at[own_rows], proj), copy(student_ref, total)]
    columns = [pl.ds(i * wide, wide) for i in range(blocks)]
    units = [
        [
            copy(gate_ref.at[:, columns[i]], gates.at[i]),
            copy(up_ref.at[:, columns[i]], ups.at[i]),
            copy(wp_ref.at[columns[i]], wp.at[i]),
        ]
        for i in range(blocks)
    ]

    @pl.when(step == 0)
    def _():
        for c in heads + slices[0]:
            c.start()
        for c in sum(slices[1:], []) + late:
            c.start()
        for c in heads:
            c.wait()

    for f in range(chips):

        @pl.when(step == f)
        def _(f=f):
            for c in slices[f]:
                c.wait()
            for c in sum(units[f::chips], []):
                c.start()

    @pl.when(step < chips)
    def _():
        for gathered, side in ((near, core), (far, 1 - core)):
            here = pl.ds(pl.multiple_of(side * COLS, COLS), COLS)
            result = tok_ref[:, here].astype(F32) + dot(attended[:, :width], w_own_ref[:, here])
            weight = gathered[step].reshape(depth - width, COLS)
            result += dot(attended[:, width:], weight)
            at = pl.ds(pl.multiple_of((2 * (step ^ chip) + side) * COLS, COLS), COLS)
            mixed[:, at] = result.astype(BF16)

    @pl.when(step == chips)
    def _():
        for c in late:
            c.wait()
        values = mixed[...].astype(F32)
        attended[...] = (rms_scale(values) * gain_ref[...]).astype(BF16)
        own = mixed[:, pl.ds(pl.multiple_of(level * width, 128), width)]
        own_ref[...] = own
        total[...] -= dot(own, proj[...])

    for i in range(blocks):

        @pl.when(step == chips + i)
        def _(i=i):
            for c in units[i]:
                c.wait()

    @pl.when(step >= chips)
    def _():
        index = step - chips
        gate = dot(attended[...], gates[index])
        up = dot(attended[...], ups[index])
        hidden = (gate * jax.nn.sigmoid(gate) * up).astype(BF16)
        hidden_ref[...] = hidden
        total[...] -= dot(hidden, wp[index])

    @pl.when(step == pl.num_programs(0) - 1)
    def _():
        size = rows // ring
        for s in range(ring):
            at = pl.ds(pl.multiple_of(((level + s) & (ring - 1)) * size, size), size)
            pieces[s][...] = total[at, :].astype(BF16)


def middle_call(info, parts, tok, w_out, near, far, gain, w_gate, w_up, wp, projector, student):
    rows, depth = tok.shape
    ring, chips = len(parts[0]), len(near[0])
    units = w_gate.shape[1]
    wide = 2 * COLS
    width = depth // ring
    sd = projector.shape[1]
    blocks = units // wide
    tile = lambda j, info: (0, jnp.minimum(j, chips - 1) ^ info[ring + 1])
    late = lambda j, info: (0, jnp.maximum(j - chips, 0))
    anywhere = pl.BlockSpec(memory_space=pl.ANY)
    count = 2 * ring * parts[0][0].shape[0] + 4 * chips + 2 + 3 * blocks
    result = pl.pallas_call(
        functools.partial(middle_kernel, ring=ring, chips=chips),
        out_shape=[
            jax.ShapeDtypeStruct((rows, units), BF16),
            jax.ShapeDtypeStruct((rows, width), BF16),
        ]
        + [jax.ShapeDtypeStruct((rows // ring, sd), BF16)] * ring,
        grid_spec=pltpu.PrefetchScalarGridSpec(
            num_scalar_prefetch=1,
            grid=(chips + blocks,),
            in_specs=[anywhere] * (2 * ring)
            + [pl.BlockSpec((rows, wide), tile), pl.BlockSpec((width, wide), tile)]
            + [anywhere] * (3 * chips + 1)
            + [whole((1, depth))]
            + [anywhere] * 5,
            out_specs=[
                pl.BlockSpec((rows, wide), late),
                whole((rows, width)),
            ]
            + [whole((rows // ring, sd))] * ring,
            scratch_shapes=[
                pltpu.VMEM((rows, depth), BF16),
                pltpu.VMEM((rows, depth), BF16),
                pltpu.VMEM((rows, sd), F32),
                pltpu.VMEM((chips, ring - 1, width, COLS), BF16),
                pltpu.VMEM((chips, ring - 1, width, COLS), BF16),
                pltpu.VMEM((blocks, depth, wide), BF16),
                pltpu.VMEM((blocks, depth, wide), BF16),
                pltpu.VMEM((blocks, wide, sd), BF16),
                pltpu.VMEM((width, sd), BF16),
                pltpu.SemaphoreType.DMA((count,)),
            ],
        ),
        compiler_params=params(42),
        cost_estimate=cost(
            2 * rows * depth * (depth + 2 * units) + 2 * rows * sd * (units + width),
            2 * depth * (depth + 2 * units),
            rows * units,
        ),
        name="middle",
    )(
        info,
        *parts[0],
        *parts[1],
        tok,
        w_out,
        *near[0],
        *near[1],
        far[0],
        *far[1],
        gain,
        w_gate,
        w_up,
        wp,
        projector,
        student,
    )
    return result[0], result[1], result[2:]


def down_kernel(info_ref, hidden_ref, weight_ref, *outs):
    result = dot(hidden_ref[...], weight_ref[...]).astype(BF16)
    for j, out in enumerate(outs):

        @pl.when(pl.program_id(0) == j)
        def _(out=out):
            out[...] = result


def down_call(info, hidden, w_down, ring):
    rows, units = hidden.shape
    depth = w_down.shape[1]
    width = depth // ring
    return pl.pallas_call(
        down_kernel,
        out_shape=[jax.ShapeDtypeStruct((rows, width), BF16)] * ring,
        grid_spec=pltpu.PrefetchScalarGridSpec(
            num_scalar_prefetch=1,
            grid=(ring,),
            in_specs=[
                whole((rows, units)),
                pl.BlockSpec((units, width), lambda j, info: (0, info[ring] ^ (ring - 1 - j))),
            ],
            out_specs=[whole((rows, width))] * ring,
        ),
        compiler_params=params(24),
        cost_estimate=cost(2 * rows * units * depth, 2 * units * depth),
        name="down",
    )(info, hidden, w_down)


def grads_kernel(info_ref, *refs, ring, chips):
    pieces = refs[:ring]
    normed_ref, hidden_ref, s_down_ref, up_ref, gate_ref = refs[ring : ring + 5]
    keep_ref, give_ref, scaled, grads = refs[ring + 5 :]
    chip, core = info_ref[ring + 1], info_ref[ring + 2]
    size, sd = pieces[0].shape
    for s in range(ring):
        scaled[pl.ds(pl.multiple_of(info_ref[s] * size, size), size), :] = pieces[s][...]
    value = scaled[...]
    wide = value.astype(F32)
    error = jnp.sum(wide * wide)
    grad_hidden = dot_over(value, s_down_ref[...], (1, 1))
    grads[0] = dot_over(normed_ref[...], (grad_hidden * gate_ref[...].astype(F32)).astype(BF16), (0, 0))
    grads[1] = dot_over(normed_ref[...], (grad_hidden * up_ref[...].astype(F32)).astype(BF16), (0, 0))
    grads[2] = dot_over(hidden_ref[...], value, (0, 0))
    share = grads.shape[1] // (2 * chips)
    for f in range(chips):
        for k in range(3):
            for part, ref in ((core, keep_ref), (1 - core, give_ref)):
                at = pl.multiple_of((part * chips + (chip ^ f)) * share, share)
                ref[f, k * share : (k + 1) * share] = grads[k, pl.ds(at, share), :].astype(
                    ref.dtype
                )
        for ref in (keep_ref, give_ref):
            ref[f, 3 * share :] = jnp.full((NOTE, sd), error, F32).astype(ref.dtype)


def grads_call(info, pieces, normed, hidden, s_down, up, gate, chips):
    ring = len(pieces)
    rows, sd = normed.shape
    units = hidden.shape[1]
    share = 3 * sd // (2 * chips) + NOTE
    operands = [*pieces, normed, hidden, s_down, up, gate]
    return pl.pallas_call(
        functools.partial(grads_kernel, ring=ring, chips=chips),
        out_shape=(
            jax.ShapeDtypeStruct((chips, share, units), F32),
            jax.ShapeDtypeStruct((chips, share, units), BF16),
        ),
        grid_spec=pltpu.PrefetchScalarGridSpec(
            num_scalar_prefetch=1,
            grid=(1,),
            in_specs=[whole(a.shape) for a in operands],
            out_specs=(whole((chips, share, units)), whole((chips, share, units))),
            scratch_shapes=[pltpu.VMEM((rows, sd), BF16), pltpu.VMEM((3, sd, units), F32)],
        ),
        compiler_params=params(22),
        cost_estimate=cost(8 * rows * sd * units, 20 * sd * units),
        name="grads",
    )(info, *operands)


def pair_kernel(keep_ref, theirs_ref, *outs):
    for f, out in enumerate(outs):
        out[...] = (keep_ref[f] + theirs_ref[f].astype(F32)).astype(out.dtype)


def pair_call(keep, theirs):
    chips, share, sd = keep.shape
    return pl.pallas_call(
        pair_kernel,
        out_shape=[jax.ShapeDtypeStruct((share, sd), BF16)] * chips,
        compiler_params=params(10),
        cost_estimate=cost(keep.size, 8 * keep.size),
        name="pair",
    )(keep, theirs)


def finish_kernel(info_ref, *refs, chips, ring):
    mine, others = refs[:chips], refs[chips : 2 * chips]
    outs = refs[2 * chips : 2 * chips + 3]
    notes = refs[2 * chips + 3]
    chip, core = info_ref[ring + 1], info_ref[ring + 2]
    share = (mine[0].shape[0] - NOTE) // 3
    for f in range(chips):
        for part, ref in ((core, mine[f]), (1 - core, others[f])):
            index = part * chips + (chip ^ f)
            at = pl.ds(pl.multiple_of(index * share, share), share)
            for k in range(3):
                outs[k][at, :] = ref[k * share : (k + 1) * share].astype(F32)
            notes[index] = ref[3 * share :, :HD].astype(F32)


def finish_call(info, mine, others, ring):
    chips = len(mine)
    share, sd = mine[0].shape
    rows = (share - NOTE) // 3 * 2 * chips
    return pl.pallas_call(
        functools.partial(finish_kernel, chips=chips, ring=ring),
        out_shape=[jax.ShapeDtypeStruct((rows, sd), F32)] * 3
        + [jax.ShapeDtypeStruct((2 * chips, NOTE, HD), F32)],
        grid_spec=pltpu.PrefetchScalarGridSpec(
            num_scalar_prefetch=1,
            grid=(1,),
            in_specs=[whole((share, sd))] * (2 * chips),
            out_specs=[whole((rows, sd))] * 3 + [whole((2 * chips, NOTE, HD))],
        ),
        compiler_params=params(14),
        cost_estimate=cost(rows * sd, 12 * rows * sd),
        name="finish",
    )(info, *mine, *others)


def step_on(block, axis):
    size = lax.axis_size(axis)
    return lax.ppermute(block, axis, [(i, (i + 1) % size) for i in range(size)])


def ring_gather(block, axis, steps=None):
    blocks = [block]
    for _ in range(lax.axis_size(axis) - 1 if steps is None else steps):
        blocks.append(step_on(blocks[-1], axis))
    return blocks


def shifted(pieces, axis):
    size = lax.axis_size(axis)
    moved = [
        lax.ppermute(pieces[s], axis, [(i, (i + s) % size) for i in range(size)])
        for s in range(1, size)
    ]
    return [pieces[0], *moved]


def flipped(pieces):
    size = lax.axis_size("dp")
    moved = [
        lax.ppermute(pieces[f], "dp", [(i, i ^ (2 * f)) for i in range(size)])
        for f in range(1, len(pieces))
    ]
    return [pieces[0], *moved]


def swapped(value):
    size = lax.axis_size("dp")
    return lax.ppermute(value, "dp", [(i, i ^ 1) for i in range(size)])


def after(value, *others):
    return lax.optimization_barrier((value, *others))[0]


def paired(
    tokens,
    series_ids,
    offsets,
    norm_gain,
    mlp_gain,
    w_query,
    w_key,
    w_value,
    w_out,
    w_gate,
    w_up,
    w_down,
    projector,
    student_in,
    s_gate,
    s_up,
    s_down,
):
    rows = tokens.shape[0]
    depth, sd = w_query.shape[0], student_in.shape[1]
    dp, ring = lax.axis_size("dp"), lax.axis_size("tensor")
    here, level = lax.axis_index("dp"), lax.axis_index("tensor")
    chips, half = dp // 2, rows // 2
    total_rows = rows * dp
    size = rows // ring
    slice_cols = depth // dp

    places = [(level - s) & (ring - 1) for s in range(ring)] + [level, here >> 1, here & 1]
    slots = lax.broadcasted_iota(jnp.int32, (16,), 0)
    info = sum(jnp.where(slots == k, place, 0) for k, place in enumerate(places))
    starts = [level * size, here * slice_cols]
    *starts, zero = [jnp.asarray(start, jnp.uint32) for start in (*starts, 0)]
    tokens, info, *starts = lax.optimization_barrier((tokens, info, *starts))

    token_rings = [ring_gather(tokens[k : k + half], "tensor") for k in (0, half)]

    angles = offsets.astype(F32)[:, None] * frequencies(HD)[None, :]
    cosine, sine = jnp.cos(angles), jnp.sin(angles)
    cosine = jnp.concatenate([cosine, cosine], axis=1)
    sine = jnp.concatenate([-sine, sine], axis=1)
    student_full = student_in.astype(F32)
    student_normed = rms_scale(student_full).astype(BF16)
    below = jnp.sum(
        series_ids[None, :] < jnp.arange(SERIES, dtype=jnp.int32)[:, None], axis=1, dtype=jnp.int32
    )

    made, tok_full = qkv_call(
        info, token_rings, norm_gain[None, :], cosine, sine, w_query, w_key, w_value
    )

    student_normed, projected, tok_full = lax.optimization_barrier(
        (student_normed, projector, tok_full)
    )
    s_gate_out = dot(student_normed, s_gate)
    s_up_out = dot(student_normed, s_up)
    sigmoid_gate = jax.nn.sigmoid(s_gate_out)
    up_slope = s_gate_out * sigmoid_gate
    gate_slope = s_up_out * sigmoid_gate * (1.0 + s_gate_out * (1.0 - sigmoid_gate))
    s_hidden = (up_slope * s_up_out).astype(BF16)
    up_slope, gate_slope = up_slope.astype(BF16), gate_slope.astype(BF16)
    student_part = dot(s_hidden, s_down)
    projected = dot(w_down, projected).astype(BF16)
    student_own = lax.dynamic_slice(student_full, [starts[0], zero], (size, sd))
    early = (projected, student_part, s_hidden, up_slope, gate_slope, student_normed, student_own)

    over = lambda value, bit: lax.ppermute(value, "tensor", [(i, i ^ bit) for i in range(ring)])
    w_slice = lax.dynamic_slice(w_out, [zero, starts[1]], (w_out.shape[0], slice_cols))
    w_slice = after(w_slice, s_gate_out)
    w_first = over(w_slice, 1)
    w_rest = over(jnp.stack([w_slice, w_first]), 2)

    own = flipped(made)
    *own, w_first = lax.optimization_barrier((*own, w_first, *early))[: chips + 1]
    other = [swapped(a) for a in own]
    near_first = flipped([w_first] * chips)
    made = attention_call(below, info, own, other, ring)
    *made, w_rest = lax.optimization_barrier((*made, w_rest, *near_first))[: chips + 1]
    attended = lax.optimization_barrier(tuple(flipped(made)))
    parts = [
        ring_gather(jnp.stack(attended[k : k + chips // 2]), "tensor") for k in (0, chips // 2)
    ]
    w_rest = after(w_rest, *attended)
    near_rest = flipped([w_rest] * chips)
    far_first = swapped(after(jnp.stack(near_first)[:, None], *attended))
    far_rest = [swapped(after(a, parts[1][1])) for a in near_rest]

    hidden, mixed_own, pieces = middle_call(
        info,
        parts,
        tok_full,
        w_out,
        (near_first, near_rest),
        (far_first, far_rest),
        mlp_gain[None, :],
        w_gate,
        w_up,
        projected,
        projector,
        student_part,
    )

    far_theirs, far_mine, near_theirs, kept = down_call(info, hidden, w_down, ring)

    moved = lax.optimization_barrier((*shifted(pieces, "tensor"), kept))[:ring]
    difference = student_own + sum(piece.astype(F32) for piece in moved)
    own = (difference * total_rows ** (-0.5)).astype(BF16)
    scaled = shifted([own] * ring, "tensor")
    far_sum = over(after(far_theirs, own), 1)

    keep, give = grads_call(
        info,
        scaled,
        student_normed,
        s_hidden,
        s_down,
        up_slope,
        gate_slope,
        chips,
    )
    shares = pair_call(keep, swapped(give))
    far_sum = (after(far_sum, shares[0]).astype(F32) + far_mine.astype(F32)).astype(BF16)
    shares = flipped(shares)
    own = sum(share.astype(F32) for share in shares).astype(BF16)
    mine = flipped([own] * chips)
    others = [swapped(share) for share in mine]

    level_sums = [over(after(near_theirs, far_sum), 1), over(far_sum, 2)]
    mlp_own = sum(after(value, mine[-1]).astype(F32) for value in level_sums)
    teacher_out = (mixed_own.astype(F32) + (kept.astype(F32) + mlp_own)).astype(BF16)
    grad_gate, grad_up, grad_down, notes = finish_call(info, mine, others, ring)
    return teacher_out, grad_gate, grad_up, grad_down, notes[0, 0, 0] / sd


def local(*args):
    rows, w_query, s_gate = args[0].shape[0], args[5], args[14]
    dp, ring = lax.axis_size("dp"), lax.axis_size("tensor")
    heads = w_query.shape[1] // HD
    fits = (
        dp == 2 * heads
        and heads > 1
        and ring == 4
        and heads & (heads - 1) == 0
        and w_query.shape[0] == dp * COLS
        and s_gate.shape[0] == s_gate.shape[1]
        and rows % (32 * ring) == 0
    )
    return paired(*args) if fits else general(*args)


def solution(mesh):
    in_specs = (
        P("dp", "tensor"),
        P(),
        P("dp"),
        P(),
        P(),
        P(None, "tensor"),
        P(None, "tensor"),
        P(None, "tensor"),
        P("tensor", None),
        P(None, "tensor"),
        P(None, "tensor"),
        P("tensor", None),
        P(),
        P("dp", None),
        P(None, "tensor"),
        P(None, "tensor"),
        P("tensor", None),
    )
    out_specs = (P("dp", "tensor"), P(None, "tensor"), P(None, "tensor"), P("tensor", None), P())
    return jax.shard_map(local, mesh=mesh, in_specs=in_specs, out_specs=out_specs, check_vma=False)
```

```python
import functools
import math

import jax
import jax.numpy as jnp
from jax import lax
from jax.experimental import pallas as pl
from jax.experimental.pallas import tpu as pltpu
from jax.sharding import PartitionSpec as P

HD = 128
COLS = 256
NOTE = 16
SERIES = 8
F32 = jnp.float32
BF16 = jnp.bfloat16
MIB = 1024 * 1024


def rms_scale(values):
    return values * lax.rsqrt(jnp.mean(values * values, axis=-1, keepdims=True) + 1e-05)


def frequencies(head_dim):
    indices = jnp.arange(head_dim // 2).astype(jnp.float32)
    return jnp.exp(-jnp.log(500000.0) * 2.0 * indices / head_dim)


def rotary(inputs, angles):
    half_dim = inputs.shape[-1] // 2
    cosine = jnp.cos(angles)
    sine = jnp.sin(angles)
    first_half = inputs[..., :half_dim]
    second_half = inputs[..., half_dim:]
    return jnp.concatenate(
        [first_half * cosine - second_half * sine, first_half * sine + second_half * cosine],
        axis=-1,
    )


def general(
    tokens,
    series_ids,
    offsets,
    norm_gain,
    mlp_gain,
    w_query,
    w_key,
    w_value,
    w_out,
    w_gate,
    w_up,
    w_down,
    projector,
    student_in,
    s_gate,
    s_up,
    s_down,
):
    row_count = tokens.shape[0]
    heads_dev = w_query.shape[1] // HD
    first_row = lax.axis_index("dp") * row_count
    tokens_full = lax.all_gather(tokens, "tensor", axis=1, tiled=True).astype(jnp.float32)
    normed = (rms_scale(tokens_full) * norm_gain).astype(jnp.bfloat16)
    angles = offsets.astype(jnp.float32)[:, None, None] * frequencies(HD)[None, None, :]
    queries = rotary(
        jnp.dot(normed, w_query, preferred_element_type=jnp.float32).reshape(
            row_count, heads_dev, HD
        ),
        angles,
    ).astype(jnp.bfloat16)
    keys_rot = rotary(
        jnp.dot(normed, w_key, preferred_element_type=jnp.float32).reshape(
            row_count, heads_dev, HD
        ),
        angles,
    ).astype(jnp.bfloat16)
    values_mine = jnp.dot(normed, w_value, preferred_element_type=jnp.float32).astype(jnp.bfloat16)
    keys_flat = keys_rot.reshape(row_count, heads_dev * HD)
    query_pos = first_row + jnp.arange(row_count, dtype=jnp.int32)
    query_series = lax.dynamic_slice_in_dim(series_ids, first_row, row_count, 0)
    factor = HD ** (-0.5)
    peak = jnp.full((row_count, heads_dev), -1e30, jnp.float32)
    key_block = lax.all_gather(keys_flat, "dp", axis=0, tiled=True)
    value_block = lax.all_gather(values_mine, "dp", axis=0, tiled=True)
    count = key_block.shape[0]
    key_pos = jnp.arange(count, dtype=jnp.int32)
    allowed = (
        (key_pos[None, :] >= 0)
        & (key_pos[None, :] <= query_pos[:, None])
        & (series_ids[None, :] == query_series[:, None])
    )
    scores = (
        jnp.einsum(
            "qhd,khd->qhk",
            queries,
            key_block.reshape(count, heads_dev, HD),
            preferred_element_type=jnp.float32,
        )
        * factor
    )
    scores = jnp.where(allowed[:, None, :], scores, -1e30)
    new_peak = jnp.maximum(peak, jnp.max(scores, axis=2))
    weights = jnp.where(allowed[:, None, :], jnp.exp(scores - new_peak[:, :, None]), 0.0)
    denom = jnp.sum(weights, axis=2)
    accum = jnp.einsum(
        "qhk,khd->qhd",
        weights.astype(jnp.bfloat16),
        value_block.reshape(count, heads_dev, HD),
        preferred_element_type=jnp.float32,
    )
    peak, denom, accum = (new_peak, denom, accum)
    attended = (accum / denom[:, :, None]).astype(jnp.bfloat16).reshape(row_count, heads_dev * HD)
    partial_out = jnp.dot(attended, w_out, preferred_element_type=jnp.float32)
    own_sum = lax.psum_scatter(
        partial_out.astype(jnp.bfloat16), "tensor", scatter_dimension=1, tiled=True
    ).astype(jnp.float32)
    mixed_own = (tokens.astype(jnp.float32) + own_sum).astype(jnp.bfloat16)
    mixed = lax.all_gather(mixed_own, "tensor", axis=1, tiled=True)
    normed_two = (rms_scale(mixed.astype(jnp.float32)) * mlp_gain).astype(jnp.bfloat16)
    gate_out = jnp.dot(normed_two, w_gate, preferred_element_type=jnp.float32)
    up_out = jnp.dot(normed_two, w_up, preferred_element_type=jnp.float32)
    hidden = (jax.nn.silu(gate_out) * up_out).astype(jnp.bfloat16)
    mlp_part = jnp.dot(hidden, w_down, preferred_element_type=jnp.float32)
    mlp_own = lax.psum_scatter(
        mlp_part.astype(jnp.bfloat16), "tensor", scatter_dimension=1, tiled=True
    ).astype(jnp.float32)
    teacher_out = (mixed_own.astype(jnp.float32) + mlp_own).astype(jnp.bfloat16)
    student_full = student_in.astype(jnp.float32)
    student_normed = rms_scale(student_full).astype(jnp.bfloat16)
    s_gate_out = jnp.dot(student_normed, s_gate, preferred_element_type=jnp.float32)
    s_up_out = jnp.dot(student_normed, s_up, preferred_element_type=jnp.float32)
    sigmoid_gate = jax.nn.sigmoid(s_gate_out)
    s_hidden = (s_gate_out * sigmoid_gate * s_up_out).astype(jnp.bfloat16)
    student_part = jnp.dot(s_hidden, s_down, preferred_element_type=jnp.float32)
    teacher_full = lax.all_gather(teacher_out, "tensor", axis=1, tiled=True)
    target = jnp.dot(teacher_full, projector, preferred_element_type=jnp.float32)
    student_summed = lax.psum(student_part.astype(jnp.bfloat16), "tensor").astype(jnp.float32)
    difference = student_full + student_summed - target
    total_rows = row_count * lax.axis_size("dp")
    scaled = (difference * total_rows ** (-0.5)).astype(jnp.bfloat16)
    grad_down_part = jnp.einsum("rk,rc->kc", s_hidden, scaled, preferred_element_type=jnp.float32)
    grad_hidden = jnp.einsum("rc,kc->rk", scaled, s_down, preferred_element_type=jnp.float32)
    grad_up_in = (grad_hidden * s_gate_out * sigmoid_gate).astype(jnp.bfloat16)
    grad_gate_in = (
        grad_hidden * s_up_out * sigmoid_gate * (1.0 + s_gate_out * (1.0 - sigmoid_gate))
    ).astype(jnp.bfloat16)
    grad_gate_part = jnp.einsum(
        "rc,rk->ck", student_normed, grad_gate_in, preferred_element_type=jnp.float32
    )
    grad_up_part = jnp.einsum(
        "rc,rk->ck", student_normed, grad_up_in, preferred_element_type=jnp.float32
    )
    square_sum = jnp.sum(difference * difference)
    grad_gate, grad_up, grad_down, square_total = (
        lax.psum(grad_gate_part.astype(jnp.bfloat16), "dp").astype(jnp.float32),
        lax.psum(grad_up_part.astype(jnp.bfloat16), "dp").astype(jnp.float32),
        lax.psum(grad_down_part.astype(jnp.bfloat16), "dp").astype(jnp.float32),
        lax.psum(square_sum.astype(jnp.bfloat16), "dp").astype(jnp.float32),
    )
    error = square_total / (total_rows * difference.shape[1])
    return (teacher_out, grad_gate, grad_up, grad_down, error)


def dot(a, b):
    return jnp.dot(a, b, preferred_element_type=F32)


def dot_over(a, b, dims):
    return lax.dot_general(a, b, ((dims[:1], dims[1:]), ((), ())), preferred_element_type=F32)


def params(limit):
    return pltpu.CompilerParams(vmem_limit_bytes=limit * MIB)


def whole(shape):
    return pl.BlockSpec(shape, lambda *_: (0,) * len(shape))


def cost(flops, moved, transcendentals=0):
    return pl.CostEstimate(
        flops=int(flops), bytes_accessed=int(moved), transcendentals=int(transcendentals)
    )


def qkv_kernel(info_ref, *refs, ring, heads, factor):
    blocks = [refs[:ring], refs[ring : 2 * ring]]
    gain_ref, cos_ref, sin_ref, *sources = refs[2 * ring : 2 * ring + 6]
    outs = refs[2 * ring + 6 : 2 * ring + 6 + heads]
    tok_ref, normed, made, weights, sems = refs[2 * ring + 6 + heads :]
    half, width = blocks[0][0].shape
    depth = gain_ref.shape[1]
    copies = [
        pltpu.make_async_copy(source, weights.at[k], sems.at[k])
        for k, source in enumerate(sources)
    ]
    for copy in copies:
        copy.start()
    for k in range(2):
        mine = slice(k * half, (k + 1) * half)
        total = jnp.zeros((half, 1), F32)
        for block in blocks[k]:
            part = block[...].astype(F32)
            total += jnp.sum(part * part, axis=1, keepdims=True)
        scale = lax.rsqrt(total / depth + 1e-05)
        for s, block in enumerate(blocks[k]):
            at = pl.ds(pl.multiple_of(info_ref[s] * width, 128), width)
            part = block[...]
            tok_ref[mine, at] = part
            normed[mine, at] = (part.astype(F32) * scale * gain_ref[:, at]).astype(BF16)
    for kind, copy in enumerate(copies):
        copy.wait()
        result = dot(normed[...], weights[kind])
        for h in range(heads):
            head = result[:, h * HD : (h + 1) * HD]
            if kind < 2:
                head = head * cos_ref[...] + pltpu.roll(head, HD // 2, 1) * sin_ref[...]
            if kind == 0:
                head = head * factor
            made[h, kind] = head.astype(BF16)
    for f in range(heads):
        outs[f][...] = made[info_ref[ring + 1] ^ f]


def qkv_call(info, blocks, gain, cosine, sine, *weights):
    half, width = blocks[0][0].shape
    rows, ring = 2 * half, len(blocks[0])
    depth, out_cols = weights[0].shape
    heads = out_cols // HD
    result = pl.pallas_call(
        functools.partial(
            qkv_kernel, ring=ring, heads=heads, factor=HD ** (-0.5) * math.log2(math.e)
        ),
        out_shape=[jax.ShapeDtypeStruct((3, rows, HD), BF16)] * heads
        + [jax.ShapeDtypeStruct((rows, depth), BF16)],
        grid_spec=pltpu.PrefetchScalarGridSpec(
            num_scalar_prefetch=1,
            grid=(1,),
            in_specs=[whole((half, width))] * (2 * ring)
            + [whole((1, depth)), whole((rows, HD)), whole((rows, HD))]
            + [pl.BlockSpec(memory_space=pl.ANY)] * 3,
            out_specs=[whole((3, rows, HD))] * heads + [whole((rows, depth))],
            scratch_shapes=[
                pltpu.VMEM((rows, depth), BF16),
                pltpu.VMEM((heads, 3, rows, HD), BF16),
                pltpu.VMEM((3, depth, out_cols), BF16),
                pltpu.SemaphoreType.DMA((3,)),
            ],
        ),
        compiler_params=params(42),
        cost_estimate=cost(6 * rows * depth * out_cols, 6 * depth * out_cols),
        name="qkv",
    )(info, *blocks[0], *blocks[1], gain, cosine, sine, *weights)
    return result[:heads], result[heads]


def attention_kernel(first_ref, info_ref, *refs, chips, ring):
    own, other = refs[:chips], refs[chips : 2 * chips]
    outs = refs[2 * chips : 3 * chips]
    keys_all, values_all = refs[3 * chips :]
    chip, core = info_ref[ring + 1], info_ref[ring + 2]
    span = outs[0].shape[0]
    for f in range(chips):
        for source, side in ((own[f], core), (other[f], 1 - core)):
            block = 2 * (chip ^ f) + side
            keys_all[block] = source[1]
            values_all[block] = source[2].T

    def first_of(row):
        found = jnp.int32(0)
        for s in range(SERIES):
            edge = first_ref[s]
            found = jnp.where(edge <= row, jnp.maximum(found, edge), found)
        return found

    for f in range(chips):
        last = 2 * (chip ^ f) + core
        query = own[f][0]
        row = last * span + lax.broadcasted_iota(jnp.int32, (1, span), 1)
        start = jnp.zeros((1, span), jnp.int32)
        for s in range(SERIES):
            edge = first_ref[s]
            start = jnp.where(edge <= row, jnp.maximum(start, edge), start)
        lane = lax.broadcasted_iota(jnp.int32, (span, 1), 0)

        def body(at, carry, masked, query=query, row=row, start=start, lane=lane):
            peak, denom, accum = carry
            scores = dot_over(keys_all[at], query, (1, 1))
            if masked:
                column = lane + at * span
                allowed = (column >= start) & (column <= row)
                scores = jnp.where(allowed, scores, -1e30)
            new_peak = jnp.maximum(peak, jnp.max(scores, axis=0, keepdims=True))
            weights = jnp.exp2(scores - new_peak)
            if masked:
                weights = jnp.where(allowed, weights, 0.0)
            keep = jnp.exp2(peak - new_peak)
            denom = denom * keep + jnp.sum(weights, axis=0, keepdims=True)
            accum = accum * keep + dot(values_all[at], weights.astype(BF16))
            return new_peak, denom, accum

        begin = first_of(last * span) // span
        full = jnp.minimum(last, (first_of(last * span + span - 1) + span - 1) // span)
        carry = (
            jnp.full((1, span), -1e30, F32),
            jnp.zeros((1, span), F32),
            jnp.zeros((HD, span), F32),
        )
        carry = lax.fori_loop(begin, full, functools.partial(body, masked=True), carry)
        carry = lax.fori_loop(full, last, functools.partial(body, masked=False), carry)
        _, denom, accum = body(last, carry, masked=True)
        outs[f][...] = (accum / denom).T.astype(BF16)


def attention_call(first, info, own, other, ring):
    chips = len(own)
    _, rows, _ = own[0].shape
    return pl.pallas_call(
        functools.partial(attention_kernel, chips=chips, ring=ring),
        out_shape=[jax.ShapeDtypeStruct((rows, HD), BF16)] * chips,
        grid_spec=pltpu.PrefetchScalarGridSpec(
            num_scalar_prefetch=2,
            grid=(1,),
            in_specs=[whole((3, rows, HD))] * (2 * chips),
            out_specs=[whole((rows, HD))] * chips,
            scratch_shapes=[
                pltpu.VMEM((2 * chips, rows, HD), BF16),
                pltpu.VMEM((2 * chips, HD, rows), BF16),
            ],
        ),
        compiler_params=params(24),
        cost_estimate=cost(
            4 * chips * rows * chips * rows * HD,
            16 * chips * rows * HD,
            chips * rows * chips * rows,
        ),
        name="attention",
    )(first, info, *own, *other)


def middle_kernel(info_ref, *refs, ring, chips):
    parts = [refs[:ring], refs[ring : 2 * ring]]
    refs = refs[2 * ring :]
    tok_ref, w_own_ref = refs[:2]
    near_first, near_rest = refs[2 : 2 + chips], refs[2 + chips : 2 + 2 * chips]
    far_first, far_rest = refs[2 + 2 * chips], refs[3 + 2 * chips : 3 + 3 * chips]
    refs = refs[3 + 3 * chips :]
    gain_ref, gate_ref, up_ref, wp_ref, proj_ref, student_ref = refs[:6]
    hidden_ref, own_ref = refs[6:8]
    pieces = refs[8 : 8 + ring]
    attended, mixed, total, near, far, gates, ups, wp, proj, sems = refs[8 + ring :]
    step = pl.program_id(0)
    level, chip, core = info_ref[ring], info_ref[ring + 1], info_ref[ring + 2]
    rows, depth = mixed.shape
    width = own_ref.shape[1]
    blocks, _, wide = gates.shape

    used = iter(range(sems.shape[0]))
    copy = lambda source, target: pltpu.make_async_copy(source, target, sems.at[next(used)])
    heads = []
    for k in range(2):
        for s, part in enumerate(parts[k]):
            count = part.shape[0]
            for i in range(count):
                at = (level ^ info_ref[s]) * width + (chip ^ (k * count + i)) * HD
                heads.append(copy(part.at[i], attended.at[:, pl.ds(pl.multiple_of(at, HD), HD)]))
    slices = [
        [
            copy(near_first[f], near.at[f, 0]),
            copy(near_rest[f], near.at[f, pl.ds(1, ring - 2)]),
            copy(far_first.at[f, 0], far.at[f, 0]),
            copy(far_rest[f], far.at[f, pl.ds(1, ring - 2)]),
        ]
        for f in range(chips)
    ]
    own_rows = pl.ds(pl.multiple_of(level * width, width), width)
    late = [copy(proj_ref.at[own_rows], proj), copy(student_ref, total)]
    columns = [pl.ds(i * wide, wide) for i in range(blocks)]
    units = [
        [
            copy(gate_ref.at[:, columns[i]], gates.at[i]),
            copy(up_ref.at[:, columns[i]], ups.at[i]),
            copy(wp_ref.at[columns[i]], wp.at[i]),
        ]
        for i in range(blocks)
    ]

    @pl.when(step == 0)
    def _():
        for c in heads + slices[0]:
            c.start()
        for c in sum(slices[1:], []) + late:
            c.start()
        for c in heads:
            c.wait()

    for f in range(chips):

        @pl.when(step == f)
        def _(f=f):
            for c in slices[f]:
                c.wait()
            for c in sum(units[f::chips], []):
                c.start()

    @pl.when(step < chips)
    def _():
        for gathered, side in ((near, core), (far, 1 - core)):
            here = pl.ds(pl.multiple_of(side * COLS, COLS), COLS)
            result = tok_ref[:, here].astype(F32) + dot(attended[:, :width], w_own_ref[:, here])
            weight = gathered[step].reshape(depth - width, COLS)
            result += dot(attended[:, width:], weight)
            at = pl.ds(pl.multiple_of((2 * (step ^ chip) + side) * COLS, COLS), COLS)
            mixed[:, at] = result.astype(BF16)

    @pl.when(step == chips)
    def _():
        for c in late:
            c.wait()
        values = mixed[...].astype(F32)
        attended[...] = (rms_scale(values) * gain_ref[...]).astype(BF16)
        own = mixed[:, pl.ds(pl.multiple_of(level * width, 128), width)]
        own_ref[...] = own
        total[...] -= dot(own, proj[...])

    for i in range(blocks):

        @pl.when(step == chips + i)
        def _(i=i):
            for c in units[i]:
                c.wait()

    @pl.when(step >= chips)
    def _():
        index = step - chips
        gate = dot(attended[...], gates[index])
        up = dot(attended[...], ups[index])
        hidden = (gate * jax.nn.sigmoid(gate) * up).astype(BF16)
        hidden_ref[...] = hidden
        total[...] -= dot(hidden, wp[index])

    @pl.when(step == pl.num_programs(0) - 1)
    def _():
        size = rows // ring
        for s in range(ring):
            at = pl.ds(pl.multiple_of(((level + s) & (ring - 1)) * size, size), size)
            pieces[s][...] = total[at, :].astype(BF16)


def middle_call(info, parts, tok, w_out, near, far, gain, w_gate, w_up, wp, projector, student):
    rows, depth = tok.shape
    ring, chips = len(parts[0]), len(near[0])
    units = w_gate.shape[1]
    wide = 2 * COLS
    width = depth // ring
    sd = projector.shape[1]
    blocks = units // wide
    tile = lambda j, info: (0, jnp.minimum(j, chips - 1) ^ info[ring + 1])
    late = lambda j, info: (0, jnp.maximum(j - chips, 0))
    anywhere = pl.BlockSpec(memory_space=pl.ANY)
    count = 2 * ring * parts[0][0].shape[0] + 4 * chips + 2 + 3 * blocks
    result = pl.pallas_call(
        functools.partial(middle_kernel, ring=ring, chips=chips),
        out_shape=[
            jax.ShapeDtypeStruct((rows, units), BF16),
            jax.ShapeDtypeStruct((rows, width), BF16),
        ]
        + [jax.ShapeDtypeStruct((rows // ring, sd), BF16)] * ring,
        grid_spec=pltpu.PrefetchScalarGridSpec(
            num_scalar_prefetch=1,
            grid=(chips + blocks,),
            in_specs=[anywhere] * (2 * ring)
            + [pl.BlockSpec((rows, wide), tile), pl.BlockSpec((width, wide), tile)]
            + [anywhere] * (3 * chips + 1)
            + [whole((1, depth))]
            + [anywhere] * 5,
            out_specs=[
                pl.BlockSpec((rows, wide), late),
                whole((rows, width)),
            ]
            + [whole((rows // ring, sd))] * ring,
            scratch_shapes=[
                pltpu.VMEM((rows, depth), BF16),
                pltpu.VMEM((rows, depth), BF16),
                pltpu.VMEM((rows, sd), F32),
                pltpu.VMEM((chips, ring - 1, width, COLS), BF16),
                pltpu.VMEM((chips, ring - 1, width, COLS), BF16),
                pltpu.VMEM((blocks, depth, wide), BF16),
                pltpu.VMEM((blocks, depth, wide), BF16),
                pltpu.VMEM((blocks, wide, sd), BF16),
                pltpu.VMEM((width, sd), BF16),
                pltpu.SemaphoreType.DMA((count,)),
            ],
        ),
        compiler_params=params(42),
        cost_estimate=cost(
            2 * rows * depth * (depth + 2 * units) + 2 * rows * sd * (units + width),
            2 * depth * (depth + 2 * units),
            rows * units,
        ),
        name="middle",
    )(
        info,
        *parts[0],
        *parts[1],
        tok,
        w_out,
        *near[0],
        *near[1],
        far[0],
        *far[1],
        gain,
        w_gate,
        w_up,
        wp,
        projector,
        student,
    )
    return result[0], result[1], result[2:]


def down_kernel(info_ref, hidden_ref, weight_ref, *outs):
    result = dot(hidden_ref[...], weight_ref[...]).astype(BF16)
    for j, out in enumerate(outs):

        @pl.when(pl.program_id(0) == j)
        def _(out=out):
            out[...] = result


def down_call(info, hidden, w_down, ring):
    rows, units = hidden.shape
    depth = w_down.shape[1]
    width = depth // ring
    return pl.pallas_call(
        down_kernel,
        out_shape=[jax.ShapeDtypeStruct((rows, width), BF16)] * ring,
        grid_spec=pltpu.PrefetchScalarGridSpec(
            num_scalar_prefetch=1,
            grid=(ring,),
            in_specs=[
                whole((rows, units)),
                pl.BlockSpec((units, width), lambda j, info: (0, info[ring] ^ (ring - 1 - j))),
            ],
            out_specs=[whole((rows, width))] * ring,
        ),
        compiler_params=params(24),
        cost_estimate=cost(2 * rows * units * depth, 2 * units * depth),
        name="down",
    )(info, hidden, w_down)


def grads_kernel(info_ref, *refs, ring, chips):
    pieces = refs[:ring]
    normed_ref, hidden_ref, s_down_ref, up_ref, gate_ref = refs[ring : ring + 5]
    keep_ref, give_ref, scaled, grads = refs[ring + 5 :]
    chip, core = info_ref[ring + 1], info_ref[ring + 2]
    size, sd = pieces[0].shape
    for s in range(ring):
        scaled[pl.ds(pl.multiple_of(info_ref[s] * size, size), size), :] = pieces[s][...]
    value = scaled[...]
    wide = value.astype(F32)
    error = jnp.sum(wide * wide)
    grad_hidden = dot_over(value, s_down_ref[...], (1, 1))
    grads[0] = dot_over(normed_ref[...], (grad_hidden * gate_ref[...].astype(F32)).astype(BF16), (0, 0))
    grads[1] = dot_over(normed_ref[...], (grad_hidden * up_ref[...].astype(F32)).astype(BF16), (0, 0))
    grads[2] = dot_over(hidden_ref[...], value, (0, 0))
    share = grads.shape[1] // (2 * chips)
    for f in range(chips):
        for k in range(3):
            for part, ref in ((core, keep_ref), (1 - core, give_ref)):
                at = pl.multiple_of((part * chips + (chip ^ f)) * share, share)
                ref[f, k * share : (k + 1) * share] = grads[k, pl.ds(at, share), :].astype(
                    ref.dtype
                )
        for ref in (keep_ref, give_ref):
            ref[f, 3 * share :] = jnp.full((NOTE, sd), error, F32).astype(ref.dtype)


def grads_call(info, pieces, normed, hidden, s_down, up, gate, chips):
    ring = len(pieces)
    rows, sd = normed.shape
    units = hidden.shape[1]
    share = 3 * sd // (2 * chips) + NOTE
    operands = [*pieces, normed, hidden, s_down, up, gate]
    return pl.pallas_call(
        functools.partial(grads_kernel, ring=ring, chips=chips),
        out_shape=(
            jax.ShapeDtypeStruct((chips, share, units), F32),
            jax.ShapeDtypeStruct((chips, share, units), BF16),
        ),
        grid_spec=pltpu.PrefetchScalarGridSpec(
            num_scalar_prefetch=1,
            grid=(1,),
            in_specs=[whole(a.shape) for a in operands],
            out_specs=(whole((chips, share, units)), whole((chips, share, units))),
            scratch_shapes=[pltpu.VMEM((rows, sd), BF16), pltpu.VMEM((3, sd, units), F32)],
        ),
        compiler_params=params(22),
        cost_estimate=cost(8 * rows * sd * units, 20 * sd * units),
        name="grads",
    )(info, *operands)


def pair_kernel(keep_ref, theirs_ref, *outs):
    for f, out in enumerate(outs):
        out[...] = (keep_ref[f] + theirs_ref[f].astype(F32)).astype(out.dtype)


def pair_call(keep, theirs):
    chips, share, sd = keep.shape
    return pl.pallas_call(
        pair_kernel,
        out_shape=[jax.ShapeDtypeStruct((share, sd), BF16)] * chips,
        compiler_params=params(10),
        cost_estimate=cost(keep.size, 8 * keep.size),
        name="pair",
    )(keep, theirs)


def finish_kernel(info_ref, *refs, chips, ring):
    mine, others = refs[:chips], refs[chips : 2 * chips]
    outs = refs[2 * chips : 2 * chips + 3]
    notes = refs[2 * chips + 3]
    chip, core = info_ref[ring + 1], info_ref[ring + 2]
    share = (mine[0].shape[0] - NOTE) // 3
    for f in range(chips):
        for part, ref in ((core, mine[f]), (1 - core, others[f])):
            index = part * chips + (chip ^ f)
            at = pl.ds(pl.multiple_of(index * share, share), share)
            for k in range(3):
                outs[k][at, :] = ref[k * share : (k + 1) * share].astype(F32)
            notes[index] = ref[3 * share :, :HD].astype(F32)


def finish_call(info, mine, others, ring):
    chips = len(mine)
    share, sd = mine[0].shape
    rows = (share - NOTE) // 3 * 2 * chips
    return pl.pallas_call(
        functools.partial(finish_kernel, chips=chips, ring=ring),
        out_shape=[jax.ShapeDtypeStruct((rows, sd), F32)] * 3
        + [jax.ShapeDtypeStruct((2 * chips, NOTE, HD), F32)],
        grid_spec=pltpu.PrefetchScalarGridSpec(
            num_scalar_prefetch=1,
            grid=(1,),
            in_specs=[whole((share, sd))] * (2 * chips),
            out_specs=[whole((rows, sd))] * 3 + [whole((2 * chips, NOTE, HD))],
        ),
        compiler_params=params(14),
        cost_estimate=cost(rows * sd, 12 * rows * sd),
        name="finish",
    )(info, *mine, *others)


def step_on(block, axis):
    size = lax.axis_size(axis)
    return lax.ppermute(block, axis, [(i, (i + 1) % size) for i in range(size)])


def ring_gather(block, axis, steps=None):
    blocks = [block]
    for _ in range(lax.axis_size(axis) - 1 if steps is None else steps):
        blocks.append(step_on(blocks[-1], axis))
    return blocks


def shifted(pieces, axis):
    size = lax.axis_size(axis)
    moved = [
        lax.ppermute(pieces[s], axis, [(i, (i + s) % size) for i in range(size)])
        for s in range(1, size)
    ]
    return [pieces[0], *moved]


def flipped(pieces):
    size = lax.axis_size("dp")
    moved = [
        lax.ppermute(pieces[f], "dp", [(i, i ^ (2 * f)) for i in range(size)])
        for f in range(1, len(pieces))
    ]
    return [pieces[0], *moved]


def swapped(value):
    size = lax.axis_size("dp")
    return lax.ppermute(value, "dp", [(i, i ^ 1) for i in range(size)])


def after(value, *others):
    return lax.optimization_barrier((value, *others))[0]


def paired(
    tokens,
    series_ids,
    offsets,
    norm_gain,
    mlp_gain,
    w_query,
    w_key,
    w_value,
    w_out,
    w_gate,
    w_up,
    w_down,
    projector,
    student_in,
    s_gate,
    s_up,
    s_down,
):
    rows = tokens.shape[0]
    depth, sd = w_query.shape[0], student_in.shape[1]
    dp, ring = lax.axis_size("dp"), lax.axis_size("tensor")
    here, level = lax.axis_index("dp"), lax.axis_index("tensor")
    chips, half = dp // 2, rows // 2
    total_rows = rows * dp
    size = rows // ring
    slice_cols = depth // dp

    places = [(level - s) & (ring - 1) for s in range(ring)] + [level, here >> 1, here & 1]
    slots = lax.broadcasted_iota(jnp.int32, (16,), 0)
    info = sum(jnp.where(slots == k, place, 0) for k, place in enumerate(places))
    starts = [level * size, here * slice_cols]
    *starts, zero = [jnp.asarray(start, jnp.uint32) for start in (*starts, 0)]
    tokens, info, *starts = lax.optimization_barrier((tokens, info, *starts))

    token_rings = [ring_gather(tokens[k : k + half], "tensor") for k in (0, half)]

    angles = offsets.astype(F32)[:, None] * frequencies(HD)[None, :]
    cosine, sine = jnp.cos(angles), jnp.sin(angles)
    cosine = jnp.concatenate([cosine, cosine], axis=1)
    sine = jnp.concatenate([-sine, sine], axis=1)
    student_full = student_in.astype(F32)
    student_normed = rms_scale(student_full).astype(BF16)
    below = jnp.sum(
        series_ids[None, :] < jnp.arange(SERIES, dtype=jnp.int32)[:, None], axis=1, dtype=jnp.int32
    )

    made, tok_full = qkv_call(
        info, token_rings, norm_gain[None, :], cosine, sine, w_query, w_key, w_value
    )

    student_normed, projected, tok_full = lax.optimization_barrier(
        (student_normed, projector, tok_full)
    )
    s_gate_out = dot(student_normed, s_gate)
    s_up_out = dot(student_normed, s_up)
    sigmoid_gate = jax.nn.sigmoid(s_gate_out)
    up_slope = s_gate_out * sigmoid_gate
    gate_slope = s_up_out * sigmoid_gate * (1.0 + s_gate_out * (1.0 - sigmoid_gate))
    s_hidden = (up_slope * s_up_out).astype(BF16)
    up_slope, gate_slope = up_slope.astype(BF16), gate_slope.astype(BF16)
    student_part = dot(s_hidden, s_down)
    projected = dot(w_down, projected).astype(BF16)
    student_own = lax.dynamic_slice(student_full, [starts[0], zero], (size, sd))
    early = (projected, student_part, s_hidden, up_slope, gate_slope, student_normed, student_own)

    over = lambda value, bit: lax.ppermute(value, "tensor", [(i, i ^ bit) for i in range(ring)])
    w_slice = lax.dynamic_slice(w_out, [zero, starts[1]], (w_out.shape[0], slice_cols))
    w_slice = after(w_slice, s_gate_out)
    w_first, w_second = over(w_slice, 1), over(w_slice, 2)

    own = flipped(made)
    own = lax.optimization_barrier((*own, *early))[:chips]
    w_first, w_second = lax.optimization_barrier((w_first, w_second, *own))[:2]
    w_third = over(w_second, 1)
    other = [swapped(a) for a in own]
    near_first = flipped([w_first] * chips)
    made = attention_call(below, info, own, other, ring)
    *made, w_third = lax.optimization_barrier((*made, w_third, *near_first))[: chips + 1]
    w_rest = jnp.stack([w_second, w_third])
    attended = lax.optimization_barrier(tuple(flipped(made)))
    parts = [
        ring_gather(jnp.stack(attended[k : k + chips // 2]), "tensor") for k in (0, chips // 2)
    ]
    w_rest = after(w_rest, *attended)
    near_rest = flipped([w_rest] * chips)
    far_first = swapped(after(jnp.stack(near_first)[:, None], *attended))
    far_rest = [swapped(after(a, parts[1][1])) for a in near_rest]

    hidden, mixed_own, pieces = middle_call(
        info,
        parts,
        tok_full,
        w_out,
        (near_first, near_rest),
        (far_first, far_rest),
        mlp_gain[None, :],
        w_gate,
        w_up,
        projected,
        projector,
        student_part,
    )

    far_theirs, far_mine, near_theirs, kept = down_call(info, hidden, w_down, ring)

    moved = lax.optimization_barrier((*shifted(pieces, "tensor"), kept))[:ring]
    difference = student_own + sum(piece.astype(F32) for piece in moved)
    own = (difference * total_rows ** (-0.5)).astype(BF16)
    scaled = shifted([own] * ring, "tensor")
    far_sum = over(after(far_theirs, own), 1)

    keep, give = grads_call(
        after(info, far_sum),
        scaled,
        student_normed,
        s_hidden,
        s_down,
        up_slope,
        gate_slope,
        chips,
    )
    shares = pair_call(keep, swapped(give))
    far_sum = (far_sum.astype(F32) + far_mine.astype(F32)).astype(BF16)
    shares = flipped(shares)
    own = sum(share.astype(F32) for share in shares).astype(BF16)
    mine = flipped([own] * chips)
    others = [swapped(share) for share in mine]

    level_sums = [over(after(near_theirs, far_sum), 1), over(far_sum, 2)]
    mlp_own = sum(after(value, mine[-1]).astype(F32) for value in level_sums)
    teacher_out = (mixed_own.astype(F32) + (kept.astype(F32) + mlp_own)).astype(BF16)
    grad_gate, grad_up, grad_down, notes = finish_call(info, mine, others, ring)
    return teacher_out, grad_gate, grad_up, grad_down, notes[0, 0, 0] / sd


def local(*args):
    rows, w_query, s_gate = args[0].shape[0], args[5], args[14]
    dp, ring = lax.axis_size("dp"), lax.axis_size("tensor")
    heads = w_query.shape[1] // HD
    fits = (
        dp == 2 * heads
        and heads > 1
        and ring == 4
        and heads & (heads - 1) == 0
        and w_query.shape[0] == dp * COLS
        and s_gate.shape[0] == s_gate.shape[1]
        and rows % (32 * ring) == 0
    )
    return paired(*args) if fits else general(*args)


def solution(mesh):
    in_specs = (
        P("dp", "tensor"),
        P(),
        P("dp"),
        P(),
        P(),
        P(None, "tensor"),
        P(None, "tensor"),
        P(None, "tensor"),
        P("tensor", None),
        P(None, "tensor"),
        P(None, "tensor"),
        P("tensor", None),
        P(),
        P("dp", None),
        P(None, "tensor"),
        P(None, "tensor"),
        P("tensor", None),
    )
    out_specs = (P("dp", "tensor"), P(None, "tensor"), P(None, "tensor"), P("tensor", None), P())
    return jax.shard_map(local, mesh=mesh, in_specs=in_specs, out_specs=out_specs, check_vma=False)
```

```python
import functools
import math

import jax
import jax.numpy as jnp
from jax import lax
from jax.experimental import pallas as pl
from jax.experimental.pallas import tpu as pltpu
from jax.sharding import PartitionSpec as P

HD = 128
COLS = 256
NOTE = 16
SERIES = 8
F32 = jnp.float32
BF16 = jnp.bfloat16
MIB = 1024 * 1024


def rms_scale(values):
    return values * lax.rsqrt(jnp.mean(values * values, axis=-1, keepdims=True) + 1e-05)


def frequencies(head_dim):
    indices = jnp.arange(head_dim // 2).astype(jnp.float32)
    return jnp.exp(-jnp.log(500000.0) * 2.0 * indices / head_dim)


def rotary(inputs, angles):
    half_dim = inputs.shape[-1] // 2
    cosine = jnp.cos(angles)
    sine = jnp.sin(angles)
    first_half = inputs[..., :half_dim]
    second_half = inputs[..., half_dim:]
    return jnp.concatenate(
        [first_half * cosine - second_half * sine, first_half * sine + second_half * cosine],
        axis=-1,
    )


def general(
    tokens,
    series_ids,
    offsets,
    norm_gain,
    mlp_gain,
    w_query,
    w_key,
    w_value,
    w_out,
    w_gate,
    w_up,
    w_down,
    projector,
    student_in,
    s_gate,
    s_up,
    s_down,
):
    row_count = tokens.shape[0]
    heads_dev = w_query.shape[1] // HD
    first_row = lax.axis_index("dp") * row_count
    tokens_full = lax.all_gather(tokens, "tensor", axis=1, tiled=True).astype(jnp.float32)
    normed = (rms_scale(tokens_full) * norm_gain).astype(jnp.bfloat16)
    angles = offsets.astype(jnp.float32)[:, None, None] * frequencies(HD)[None, None, :]
    queries = rotary(
        jnp.dot(normed, w_query, preferred_element_type=jnp.float32).reshape(
            row_count, heads_dev, HD
        ),
        angles,
    ).astype(jnp.bfloat16)
    keys_rot = rotary(
        jnp.dot(normed, w_key, preferred_element_type=jnp.float32).reshape(
            row_count, heads_dev, HD
        ),
        angles,
    ).astype(jnp.bfloat16)
    values_mine = jnp.dot(normed, w_value, preferred_element_type=jnp.float32).astype(jnp.bfloat16)
    keys_flat = keys_rot.reshape(row_count, heads_dev * HD)
    query_pos = first_row + jnp.arange(row_count, dtype=jnp.int32)
    query_series = lax.dynamic_slice_in_dim(series_ids, first_row, row_count, 0)
    factor = HD ** (-0.5)
    peak = jnp.full((row_count, heads_dev), -1e30, jnp.float32)
    key_block = lax.all_gather(keys_flat, "dp", axis=0, tiled=True)
    value_block = lax.all_gather(values_mine, "dp", axis=0, tiled=True)
    count = key_block.shape[0]
    key_pos = jnp.arange(count, dtype=jnp.int32)
    allowed = (
        (key_pos[None, :] >= 0)
        & (key_pos[None, :] <= query_pos[:, None])
        & (series_ids[None, :] == query_series[:, None])
    )
    scores = (
        jnp.einsum(
            "qhd,khd->qhk",
            queries,
            key_block.reshape(count, heads_dev, HD),
            preferred_element_type=jnp.float32,
        )
        * factor
    )
    scores = jnp.where(allowed[:, None, :], scores, -1e30)
    new_peak = jnp.maximum(peak, jnp.max(scores, axis=2))
    weights = jnp.where(allowed[:, None, :], jnp.exp(scores - new_peak[:, :, None]), 0.0)
    denom = jnp.sum(weights, axis=2)
    accum = jnp.einsum(
        "qhk,khd->qhd",
        weights.astype(jnp.bfloat16),
        value_block.reshape(count, heads_dev, HD),
        preferred_element_type=jnp.float32,
    )
    peak, denom, accum = (new_peak, denom, accum)
    attended = (accum / denom[:, :, None]).astype(jnp.bfloat16).reshape(row_count, heads_dev * HD)
    partial_out = jnp.dot(attended, w_out, preferred_element_type=jnp.float32)
    own_sum = lax.psum_scatter(
        partial_out.astype(jnp.bfloat16), "tensor", scatter_dimension=1, tiled=True
    ).astype(jnp.float32)
    mixed_own = (tokens.astype(jnp.float32) + own_sum).astype(jnp.bfloat16)
    mixed = lax.all_gather(mixed_own, "tensor", axis=1, tiled=True)
    normed_two = (rms_scale(mixed.astype(jnp.float32)) * mlp_gain).astype(jnp.bfloat16)
    gate_out = jnp.dot(normed_two, w_gate, preferred_element_type=jnp.float32)
    up_out = jnp.dot(normed_two, w_up, preferred_element_type=jnp.float32)
    hidden = (jax.nn.silu(gate_out) * up_out).astype(jnp.bfloat16)
    mlp_part = jnp.dot(hidden, w_down, preferred_element_type=jnp.float32)
    mlp_own = lax.psum_scatter(
        mlp_part.astype(jnp.bfloat16), "tensor", scatter_dimension=1, tiled=True
    ).astype(jnp.float32)
    teacher_out = (mixed_own.astype(jnp.float32) + mlp_own).astype(jnp.bfloat16)
    student_full = student_in.astype(jnp.float32)
    student_normed = rms_scale(student_full).astype(jnp.bfloat16)
    s_gate_out = jnp.dot(student_normed, s_gate, preferred_element_type=jnp.float32)
    s_up_out = jnp.dot(student_normed, s_up, preferred_element_type=jnp.float32)
    sigmoid_gate = jax.nn.sigmoid(s_gate_out)
    s_hidden = (s_gate_out * sigmoid_gate * s_up_out).astype(jnp.bfloat16)
    student_part = jnp.dot(s_hidden, s_down, preferred_element_type=jnp.float32)
    teacher_full = lax.all_gather(teacher_out, "tensor", axis=1, tiled=True)
    target = jnp.dot(teacher_full, projector, preferred_element_type=jnp.float32)
    student_summed = lax.psum(student_part.astype(jnp.bfloat16), "tensor").astype(jnp.float32)
    difference = student_full + student_summed - target
    total_rows = row_count * lax.axis_size("dp")
    scaled = (difference * total_rows ** (-0.5)).astype(jnp.bfloat16)
    grad_down_part = jnp.einsum("rk,rc->kc", s_hidden, scaled, preferred_element_type=jnp.float32)
    grad_hidden = jnp.einsum("rc,kc->rk", scaled, s_down, preferred_element_type=jnp.float32)
    grad_up_in = (grad_hidden * s_gate_out * sigmoid_gate).astype(jnp.bfloat16)
    grad_gate_in = (
        grad_hidden * s_up_out * sigmoid_gate * (1.0 + s_gate_out * (1.0 - sigmoid_gate))
    ).astype(jnp.bfloat16)
    grad_gate_part = jnp.einsum(
        "rc,rk->ck", student_normed, grad_gate_in, preferred_element_type=jnp.float32
    )
    grad_up_part = jnp.einsum(
        "rc,rk->ck", student_normed, grad_up_in, preferred_element_type=jnp.float32
    )
    square_sum = jnp.sum(difference * difference)
    grad_gate, grad_up, grad_down, square_total = (
        lax.psum(grad_gate_part.astype(jnp.bfloat16), "dp").astype(jnp.float32),
        lax.psum(grad_up_part.astype(jnp.bfloat16), "dp").astype(jnp.float32),
        lax.psum(grad_down_part.astype(jnp.bfloat16), "dp").astype(jnp.float32),
        lax.psum(square_sum.astype(jnp.bfloat16), "dp").astype(jnp.float32),
    )
    error = square_total / (total_rows * difference.shape[1])
    return (teacher_out, grad_gate, grad_up, grad_down, error)


def dot(a, b):
    return jnp.dot(a, b, preferred_element_type=F32)


def dot_over(a, b, dims):
    return lax.dot_general(a, b, ((dims[:1], dims[1:]), ((), ())), preferred_element_type=F32)


def params(limit):
    return pltpu.CompilerParams(vmem_limit_bytes=limit * MIB)


def whole(shape):
    return pl.BlockSpec(shape, lambda *_: (0,) * len(shape))


def cost(flops, moved, transcendentals=0):
    return pl.CostEstimate(
        flops=int(flops), bytes_accessed=int(moved), transcendentals=int(transcendentals)
    )


def qkv_kernel(info_ref, *refs, ring, heads, factor):
    blocks = [refs[:ring], refs[ring : 2 * ring]]
    gain_ref, cos_ref, sin_ref, *sources = refs[2 * ring : 2 * ring + 6]
    outs = refs[2 * ring + 6 : 2 * ring + 6 + heads]
    tok_ref, normed, made, weights, sems = refs[2 * ring + 6 + heads :]
    half, width = blocks[0][0].shape
    depth = gain_ref.shape[1]
    copies = [
        pltpu.make_async_copy(source, weights.at[k], sems.at[k])
        for k, source in enumerate(sources)
    ]
    for copy in copies:
        copy.start()
    for k in range(2):
        mine = slice(k * half, (k + 1) * half)
        total = jnp.zeros((half, 1), F32)
        for block in blocks[k]:
            part = block[...].astype(F32)
            total += jnp.sum(part * part, axis=1, keepdims=True)
        scale = lax.rsqrt(total / depth + 1e-05)
        for s, block in enumerate(blocks[k]):
            at = pl.ds(pl.multiple_of(info_ref[s] * width, 128), width)
            part = block[...]
            tok_ref[mine, at] = part
            normed[mine, at] = (part.astype(F32) * scale * gain_ref[:, at]).astype(BF16)
    for kind, copy in enumerate(copies):
        copy.wait()
        result = dot(normed[...], weights[kind])
        for h in range(heads):
            head = result[:, h * HD : (h + 1) * HD]
            if kind < 2:
                head = head * cos_ref[...] + pltpu.roll(head, HD // 2, 1) * sin_ref[...]
            if kind == 0:
                head = head * factor
            made[h, kind] = head.astype(BF16)
    for f in range(heads):
        outs[f][...] = made[info_ref[ring + 1] ^ f]


def qkv_call(info, blocks, gain, cosine, sine, *weights):
    half, width = blocks[0][0].shape
    rows, ring = 2 * half, len(blocks[0])
    depth, out_cols = weights[0].shape
    heads = out_cols // HD
    result = pl.pallas_call(
        functools.partial(
            qkv_kernel, ring=ring, heads=heads, factor=HD ** (-0.5) * math.log2(math.e)
        ),
        out_shape=[jax.ShapeDtypeStruct((3, rows, HD), BF16)] * heads
        + [jax.ShapeDtypeStruct((rows, depth), BF16)],
        grid_spec=pltpu.PrefetchScalarGridSpec(
            num_scalar_prefetch=1,
            grid=(1,),
            in_specs=[whole((half, width))] * (2 * ring)
            + [whole((1, depth)), whole((rows, HD)), whole((rows, HD))]
            + [pl.BlockSpec(memory_space=pl.ANY)] * 3,
            out_specs=[whole((3, rows, HD))] * heads + [whole((rows, depth))],
            scratch_shapes=[
                pltpu.VMEM((rows, depth), BF16),
                pltpu.VMEM((heads, 3, rows, HD), BF16),
                pltpu.VMEM((3, depth, out_cols), BF16),
                pltpu.SemaphoreType.DMA((3,)),
            ],
        ),
        compiler_params=params(42),
        cost_estimate=cost(6 * rows * depth * out_cols, 6 * depth * out_cols),
        name="qkv",
    )(info, *blocks[0], *blocks[1], gain, cosine, sine, *weights)
    return result[:heads], result[heads]


def attention_kernel(first_ref, info_ref, *refs, chips, ring):
    own, other = refs[:chips], refs[chips : 2 * chips]
    outs = refs[2 * chips : 3 * chips]
    keys_all, values_all = refs[3 * chips :]
    chip, core = info_ref[ring + 1], info_ref[ring + 2]
    span = outs[0].shape[0]
    for f in range(chips):
        for source, side in ((own[f], core), (other[f], 1 - core)):
            block = 2 * (chip ^ f) + side
            keys_all[block] = source[1]
            values_all[block] = source[2].T

    def first_of(row):
        found = jnp.int32(0)
        for s in range(SERIES):
            edge = first_ref[s]
            found = jnp.where(edge <= row, jnp.maximum(found, edge), found)
        return found

    for f in range(chips):
        last = 2 * (chip ^ f) + core
        query = own[f][0]
        row = last * span + lax.broadcasted_iota(jnp.int32, (1, span), 1)
        start = jnp.zeros((1, span), jnp.int32)
        for s in range(SERIES):
            edge = first_ref[s]
            start = jnp.where(edge <= row, jnp.maximum(start, edge), start)
        lane = lax.broadcasted_iota(jnp.int32, (span, 1), 0)

        def body(at, carry, masked, query=query, row=row, start=start, lane=lane):
            peak, denom, accum = carry
            scores = dot_over(keys_all[at], query, (1, 1))
            if masked:
                column = lane + at * span
                allowed = (column >= start) & (column <= row)
                scores = jnp.where(allowed, scores, -1e30)
            new_peak = jnp.maximum(peak, jnp.max(scores, axis=0, keepdims=True))
            weights = jnp.exp2(scores - new_peak)
            if masked:
                weights = jnp.where(allowed, weights, 0.0)
            keep = jnp.exp2(peak - new_peak)
            denom = denom * keep + jnp.sum(weights, axis=0, keepdims=True)
            accum = accum * keep + dot(values_all[at], weights.astype(BF16))
            return new_peak, denom, accum

        def pair(turn, carry, query=query, full=None):
            peak, denom, accum = carry
            at = full + 2 * turn
            blocks = (at, at + 1)
            scores = [dot_over(keys_all[block], query, (1, 1)) for block in blocks]
            tops = [jnp.max(score, axis=0, keepdims=True) for score in scores]
            new_peak = jnp.maximum(peak, jnp.maximum(*tops))
            keep = jnp.exp2(peak - new_peak)
            denom, accum = denom * keep, accum * keep
            for block, score in zip(blocks, scores):
                weights = jnp.exp2(score - new_peak)
                denom += jnp.sum(weights, axis=0, keepdims=True)
                accum += dot(values_all[block], weights.astype(BF16))
            return new_peak, denom, accum

        begin = first_of(last * span) // span
        full = jnp.minimum(last, (first_of(last * span + span - 1) + span - 1) // span)
        carry = (
            jnp.full((1, span), -1e30, F32),
            jnp.zeros((1, span), F32),
            jnp.zeros((HD, span), F32),
        )
        carry = lax.fori_loop(begin, full, functools.partial(body, masked=True), carry)
        turns = (last - full) // 2
        carry = lax.fori_loop(0, turns, functools.partial(pair, full=full), carry)
        rest = full + 2 * turns
        carry = lax.fori_loop(rest, last, functools.partial(body, masked=False), carry)
        _, denom, accum = body(last, carry, masked=True)
        outs[f][...] = (accum / denom).T.astype(BF16)


def attention_call(first, info, own, other, ring):
    chips = len(own)
    _, rows, _ = own[0].shape
    return pl.pallas_call(
        functools.partial(attention_kernel, chips=chips, ring=ring),
        out_shape=[jax.ShapeDtypeStruct((rows, HD), BF16)] * chips,
        grid_spec=pltpu.PrefetchScalarGridSpec(
            num_scalar_prefetch=2,
            grid=(1,),
            in_specs=[whole((3, rows, HD))] * (2 * chips),
            out_specs=[whole((rows, HD))] * chips,
            scratch_shapes=[
                pltpu.VMEM((2 * chips, rows, HD), BF16),
                pltpu.VMEM((2 * chips, HD, rows), BF16),
            ],
        ),
        compiler_params=params(24),
        cost_estimate=cost(
            4 * chips * rows * chips * rows * HD,
            16 * chips * rows * HD,
            chips * rows * chips * rows,
        ),
        name="attention",
    )(first, info, *own, *other)


def middle_kernel(info_ref, *refs, ring, chips):
    parts = [refs[:ring], refs[ring : 2 * ring]]
    refs = refs[2 * ring :]
    tok_ref, w_own_ref = refs[:2]
    near_first, near_rest = refs[2 : 2 + chips], refs[2 + chips : 2 + 2 * chips]
    far_first, far_rest = refs[2 + 2 * chips], refs[3 + 2 * chips : 3 + 3 * chips]
    refs = refs[3 + 3 * chips :]
    gain_ref, gate_ref, up_ref, wp_ref, proj_ref, student_ref = refs[:6]
    hidden_ref, own_ref = refs[6:8]
    pieces = refs[8 : 8 + ring]
    attended, mixed, total, near, far, gates, ups, wp, proj, sems = refs[8 + ring :]
    step = pl.program_id(0)
    level, chip, core = info_ref[ring], info_ref[ring + 1], info_ref[ring + 2]
    rows, depth = mixed.shape
    width = own_ref.shape[1]
    blocks, _, wide = gates.shape

    used = iter(range(sems.shape[0]))
    copy = lambda source, target: pltpu.make_async_copy(source, target, sems.at[next(used)])
    heads = []
    for k in range(2):
        for s, part in enumerate(parts[k]):
            count = part.shape[0]
            for i in range(count):
                at = (level ^ info_ref[s]) * width + (chip ^ (k * count + i)) * HD
                heads.append(copy(part.at[i], attended.at[:, pl.ds(pl.multiple_of(at, HD), HD)]))
    slices = [
        [
            copy(near_first[f], near.at[f, 0]),
            copy(near_rest[f], near.at[f, pl.ds(1, ring - 2)]),
            copy(far_first.at[f, 0], far.at[f, 0]),
            copy(far_rest[f], far.at[f, pl.ds(1, ring - 2)]),
        ]
        for f in range(chips)
    ]
    own_rows = pl.ds(pl.multiple_of(level * width, width), width)
    late = [copy(proj_ref.at[own_rows], proj), copy(student_ref, total)]
    columns = [pl.ds(i * wide, wide) for i in range(blocks)]
    units = [
        [
            copy(gate_ref.at[:, columns[i]], gates.at[i]),
            copy(up_ref.at[:, columns[i]], ups.at[i]),
            copy(wp_ref.at[columns[i]], wp.at[i]),
        ]
        for i in range(blocks)
    ]

    @pl.when(step == 0)
    def _():
        for c in heads + slices[0]:
            c.start()
        for c in sum(slices[1:], []) + late:
            c.start()
        for c in heads:
            c.wait()

    for f in range(chips):

        @pl.when(step == f)
        def _(f=f):
            for c in slices[f]:
                c.wait()
            for c in sum(units[f::chips], []):
                c.start()

    @pl.when(step < chips)
    def _():
        for gathered, side in ((near, core), (far, 1 - core)):
            here = pl.ds(pl.multiple_of(side * COLS, COLS), COLS)
            result = tok_ref[:, here].astype(F32) + dot(attended[:, :width], w_own_ref[:, here])
            weight = gathered[step].reshape(depth - width, COLS)
            result += dot(attended[:, width:], weight)
            at = pl.ds(pl.multiple_of((2 * (step ^ chip) + side) * COLS, COLS), COLS)
            mixed[:, at] = result.astype(BF16)

    @pl.when(step == chips)
    def _():
        for c in late:
            c.wait()
        values = mixed[...].astype(F32)
        attended[...] = (rms_scale(values) * gain_ref[...]).astype(BF16)
        own = mixed[:, pl.ds(pl.multiple_of(level * width, 128), width)]
        own_ref[...] = own
        total[...] -= dot(own, proj[...])

    for i in range(blocks):

        @pl.when(step == chips + i)
        def _(i=i):
            for c in units[i]:
                c.wait()

    @pl.when(step >= chips)
    def _():
        index = step - chips
        gate = dot(attended[...], gates[index])
        up = dot(attended[...], ups[index])
        hidden = (gate * jax.nn.sigmoid(gate) * up).astype(BF16)
        hidden_ref[...] = hidden
        total[...] -= dot(hidden, wp[index])

    @pl.when(step == pl.num_programs(0) - 1)
    def _():
        size = rows // ring
        for s in range(ring):
            at = pl.ds(pl.multiple_of(((level + s) & (ring - 1)) * size, size), size)
            pieces[s][...] = total[at, :].astype(BF16)


def middle_call(info, parts, tok, w_out, near, far, gain, w_gate, w_up, wp, projector, student):
    rows, depth = tok.shape
    ring, chips = len(parts[0]), len(near[0])
    units = w_gate.shape[1]
    wide = 2 * COLS
    width = depth // ring
    sd = projector.shape[1]
    blocks = units // wide
    tile = lambda j, info: (0, jnp.minimum(j, chips - 1) ^ info[ring + 1])
    late = lambda j, info: (0, jnp.maximum(j - chips, 0))
    anywhere = pl.BlockSpec(memory_space=pl.ANY)
    count = 2 * ring * parts[0][0].shape[0] + 4 * chips + 2 + 3 * blocks
    result = pl.pallas_call(
        functools.partial(middle_kernel, ring=ring, chips=chips),
        out_shape=[
            jax.ShapeDtypeStruct((rows, units), BF16),
            jax.ShapeDtypeStruct((rows, width), BF16),
        ]
        + [jax.ShapeDtypeStruct((rows // ring, sd), BF16)] * ring,
        grid_spec=pltpu.PrefetchScalarGridSpec(
            num_scalar_prefetch=1,
            grid=(chips + blocks,),
            in_specs=[anywhere] * (2 * ring)
            + [pl.BlockSpec((rows, wide), tile), pl.BlockSpec((width, wide), tile)]
            + [anywhere] * (3 * chips + 1)
            + [whole((1, depth))]
            + [anywhere] * 5,
            out_specs=[
                pl.BlockSpec((rows, wide), late),
                whole((rows, width)),
            ]
            + [whole((rows // ring, sd))] * ring,
            scratch_shapes=[
                pltpu.VMEM((rows, depth), BF16),
                pltpu.VMEM((rows, depth), BF16),
                pltpu.VMEM((rows, sd), F32),
                pltpu.VMEM((chips, ring - 1, width, COLS), BF16),
                pltpu.VMEM((chips, ring - 1, width, COLS), BF16),
                pltpu.VMEM((blocks, depth, wide), BF16),
                pltpu.VMEM((blocks, depth, wide), BF16),
                pltpu.VMEM((blocks, wide, sd), BF16),
                pltpu.VMEM((width, sd), BF16),
                pltpu.SemaphoreType.DMA((count,)),
            ],
        ),
        compiler_params=params(42),
        cost_estimate=cost(
            2 * rows * depth * (depth + 2 * units) + 2 * rows * sd * (units + width),
            2 * depth * (depth + 2 * units),
            rows * units,
        ),
        name="middle",
    )(
        info,
        *parts[0],
        *parts[1],
        tok,
        w_out,
        *near[0],
        *near[1],
        far[0],
        *far[1],
        gain,
        w_gate,
        w_up,
        wp,
        projector,
        student,
    )
    return result[0], result[1], result[2:]


def down_kernel(info_ref, hidden_ref, weight_ref, *outs):
    result = dot(hidden_ref[...], weight_ref[...]).astype(BF16)
    for j, out in enumerate(outs):

        @pl.when(pl.program_id(0) == j)
        def _(out=out):
            out[...] = result


def down_call(info, hidden, w_down, ring):
    rows, units = hidden.shape
    depth = w_down.shape[1]
    width = depth // ring
    return pl.pallas_call(
        down_kernel,
        out_shape=[jax.ShapeDtypeStruct((rows, width), BF16)] * ring,
        grid_spec=pltpu.PrefetchScalarGridSpec(
            num_scalar_prefetch=1,
            grid=(ring,),
            in_specs=[
                whole((rows, units)),
                pl.BlockSpec((units, width), lambda j, info: (0, info[ring] ^ (ring - 1 - j))),
            ],
            out_specs=[whole((rows, width))] * ring,
        ),
        compiler_params=params(24),
        cost_estimate=cost(2 * rows * units * depth, 2 * units * depth),
        name="down",
    )(info, hidden, w_down)


def grads_kernel(info_ref, *refs, ring, chips):
    pieces = refs[:ring]
    normed_ref, hidden_ref, s_down_ref, up_ref, gate_ref = refs[ring : ring + 5]
    keep_ref, give_ref, scaled, grads = refs[ring + 5 :]
    chip, core = info_ref[ring + 1], info_ref[ring + 2]
    size, sd = pieces[0].shape
    for s in range(ring):
        scaled[pl.ds(pl.multiple_of(info_ref[s] * size, size), size), :] = pieces[s][...]
    value = scaled[...]
    wide = value.astype(F32)
    error = jnp.sum(wide * wide)
    grad_hidden = dot_over(value, s_down_ref[...], (1, 1))
    grads[0] = dot_over(normed_ref[...], (grad_hidden * gate_ref[...].astype(F32)).astype(BF16), (0, 0))
    grads[1] = dot_over(normed_ref[...], (grad_hidden * up_ref[...].astype(F32)).astype(BF16), (0, 0))
    grads[2] = dot_over(hidden_ref[...], value, (0, 0))
    share = grads.shape[1] // (2 * chips)
    for f in range(chips):
        for k in range(3):
            for part, ref in ((core, keep_ref), (1 - core, give_ref)):
                at = pl.multiple_of((part * chips + (chip ^ f)) * share, share)
                ref[f, k * share : (k + 1) * share] = grads[k, pl.ds(at, share), :].astype(
                    ref.dtype
                )
        for ref in (keep_ref, give_ref):
            ref[f, 3 * share :] = jnp.full((NOTE, sd), error, F32).astype(ref.dtype)


def grads_call(info, pieces, normed, hidden, s_down, up, gate, chips):
    ring = len(pieces)
    rows, sd = normed.shape
    units = hidden.shape[1]
    share = 3 * sd // (2 * chips) + NOTE
    operands = [*pieces, normed, hidden, s_down, up, gate]
    return pl.pallas_call(
        functools.partial(grads_kernel, ring=ring, chips=chips),
        out_shape=(
            jax.ShapeDtypeStruct((chips, share, units), F32),
            jax.ShapeDtypeStruct((chips, share, units), BF16),
        ),
        grid_spec=pltpu.PrefetchScalarGridSpec(
            num_scalar_prefetch=1,
            grid=(1,),
            in_specs=[whole(a.shape) for a in operands],
            out_specs=(whole((chips, share, units)), whole((chips, share, units))),
            scratch_shapes=[pltpu.VMEM((rows, sd), BF16), pltpu.VMEM((3, sd, units), F32)],
        ),
        compiler_params=params(22),
        cost_estimate=cost(8 * rows * sd * units, 20 * sd * units),
        name="grads",
    )(info, *operands)


def pair_kernel(keep_ref, theirs_ref, *outs):
    for f, out in enumerate(outs):
        out[...] = (keep_ref[f] + theirs_ref[f].astype(F32)).astype(out.dtype)


def pair_call(keep, theirs):
    chips, share, sd = keep.shape
    return pl.pallas_call(
        pair_kernel,
        out_shape=[jax.ShapeDtypeStruct((share, sd), BF16)] * chips,
        compiler_params=params(10),
        cost_estimate=cost(keep.size, 8 * keep.size),
        name="pair",
    )(keep, theirs)


def finish_kernel(info_ref, *refs, chips, ring):
    mine, others = refs[:chips], refs[chips : 2 * chips]
    outs = refs[2 * chips : 2 * chips + 3]
    notes = refs[2 * chips + 3]
    chip, core = info_ref[ring + 1], info_ref[ring + 2]
    share = (mine[0].shape[0] - NOTE) // 3
    for f in range(chips):
        for part, ref in ((core, mine[f]), (1 - core, others[f])):
            index = part * chips + (chip ^ f)
            at = pl.ds(pl.multiple_of(index * share, share), share)
            for k in range(3):
                outs[k][at, :] = ref[k * share : (k + 1) * share].astype(F32)
            notes[index] = ref[3 * share :, :HD].astype(F32)


def finish_call(info, mine, others, ring):
    chips = len(mine)
    share, sd = mine[0].shape
    rows = (share - NOTE) // 3 * 2 * chips
    return pl.pallas_call(
        functools.partial(finish_kernel, chips=chips, ring=ring),
        out_shape=[jax.ShapeDtypeStruct((rows, sd), F32)] * 3
        + [jax.ShapeDtypeStruct((2 * chips, NOTE, HD), F32)],
        grid_spec=pltpu.PrefetchScalarGridSpec(
            num_scalar_prefetch=1,
            grid=(1,),
            in_specs=[whole((share, sd))] * (2 * chips),
            out_specs=[whole((rows, sd))] * 3 + [whole((2 * chips, NOTE, HD))],
        ),
        compiler_params=params(14),
        cost_estimate=cost(rows * sd, 12 * rows * sd),
        name="finish",
    )(info, *mine, *others)


def step_on(block, axis):
    size = lax.axis_size(axis)
    return lax.ppermute(block, axis, [(i, (i + 1) % size) for i in range(size)])


def ring_gather(block, axis, steps=None):
    blocks = [block]
    for _ in range(lax.axis_size(axis) - 1 if steps is None else steps):
        blocks.append(step_on(blocks[-1], axis))
    return blocks


def shifted(pieces, axis):
    size = lax.axis_size(axis)
    moved = [
        lax.ppermute(pieces[s], axis, [(i, (i + s) % size) for i in range(size)])
        for s in range(1, size)
    ]
    return [pieces[0], *moved]


def flipped(pieces):
    size = lax.axis_size("dp")
    moved = [
        lax.ppermute(pieces[f], "dp", [(i, i ^ (2 * f)) for i in range(size)])
        for f in range(1, len(pieces))
    ]
    return [pieces[0], *moved]


def swapped(value):
    size = lax.axis_size("dp")
    return lax.ppermute(value, "dp", [(i, i ^ 1) for i in range(size)])


def after(value, *others):
    return lax.optimization_barrier((value, *others))[0]


def paired(
    tokens,
    series_ids,
    offsets,
    norm_gain,
    mlp_gain,
    w_query,
    w_key,
    w_value,
    w_out,
    w_gate,
    w_up,
    w_down,
    projector,
    student_in,
    s_gate,
    s_up,
    s_down,
):
    rows = tokens.shape[0]
    depth, sd = w_query.shape[0], student_in.shape[1]
    dp, ring = lax.axis_size("dp"), lax.axis_size("tensor")
    here, level = lax.axis_index("dp"), lax.axis_index("tensor")
    chips, half = dp // 2, rows // 2
    total_rows = rows * dp
    size = rows // ring
    slice_cols = depth // dp

    places = [(level - s) & (ring - 1) for s in range(ring)] + [level, here >> 1, here & 1]
    slots = lax.broadcasted_iota(jnp.int32, (16,), 0)
    info = sum(jnp.where(slots == k, place, 0) for k, place in enumerate(places))
    starts = [level * size, here * slice_cols]
    *starts, zero = [jnp.asarray(start, jnp.uint32) for start in (*starts, 0)]
    tokens, info, *starts = lax.optimization_barrier((tokens, info, *starts))

    token_rings = [ring_gather(tokens[k : k + half], "tensor") for k in (0, half)]

    angles = offsets.astype(F32)[:, None] * frequencies(HD)[None, :]
    cosine, sine = jnp.cos(angles), jnp.sin(angles)
    cosine = jnp.concatenate([cosine, cosine], axis=1)
    sine = jnp.concatenate([-sine, sine], axis=1)
    student_full = student_in.astype(F32)
    student_normed = rms_scale(student_full).astype(BF16)
    below = jnp.sum(
        series_ids[None, :] < jnp.arange(SERIES, dtype=jnp.int32)[:, None], axis=1, dtype=jnp.int32
    )

    made, tok_full = qkv_call(
        info, token_rings, norm_gain[None, :], cosine, sine, w_query, w_key, w_value
    )

    student_normed, projected, tok_full = lax.optimization_barrier(
        (student_normed, projector, tok_full)
    )
    s_gate_out = dot(student_normed, s_gate)
    s_up_out = dot(student_normed, s_up)
    sigmoid_gate = jax.nn.sigmoid(s_gate_out)
    up_slope = s_gate_out * sigmoid_gate
    gate_slope = s_up_out * sigmoid_gate * (1.0 + s_gate_out * (1.0 - sigmoid_gate))
    s_hidden = (up_slope * s_up_out).astype(BF16)
    up_slope, gate_slope = up_slope.astype(BF16), gate_slope.astype(BF16)
    student_part = dot(s_hidden, s_down)
    projected = dot(w_down, projected).astype(BF16)
    student_own = lax.dynamic_slice(student_full, [starts[0], zero], (size, sd))
    early = (projected, student_part, s_hidden, up_slope, gate_slope, student_normed, student_own)

    over = lambda value, bit: lax.ppermute(value, "tensor", [(i, i ^ bit) for i in range(ring)])
    w_slice = lax.dynamic_slice(w_out, [zero, starts[1]], (w_out.shape[0], slice_cols))
    w_slice, tok_full = lax.optimization_barrier((w_slice, tok_full))
    w_first, w_second = over(w_slice, 1), over(w_slice, 2)

    own = flipped(made)
    held = lax.optimization_barrier((*own, w_first, w_second, *early))
    own, (w_first, w_second) = held[:chips], held[chips : chips + 2]
    w_third = over(w_second, 1)
    other = [swapped(a) for a in own]
    near_first = flipped([w_first] * chips)
    made = attention_call(below, info, own, other, ring)
    *made, w_third = lax.optimization_barrier((*made, w_third, *near_first))[: chips + 1]
    w_rest = jnp.stack([w_second, w_third])
    attended = lax.optimization_barrier(tuple(flipped(made)))
    parts = [
        ring_gather(jnp.stack(attended[k : k + chips // 2]), "tensor") for k in (0, chips // 2)
    ]
    w_rest = after(w_rest, *attended)
    near_rest = flipped([w_rest] * chips)
    far_first = swapped(after(jnp.stack(near_first)[:, None], *attended))
    far_rest = [swapped(after(a, parts[1][1])) for a in near_rest]

    hidden, mixed_own, pieces = middle_call(
        info,
        parts,
        tok_full,
        w_out,
        (near_first, near_rest),
        (far_first, far_rest),
        mlp_gain[None, :],
        w_gate,
        w_up,
        projected,
        projector,
        student_part,
    )

    far_theirs, far_mine, near_theirs, kept = down_call(info, hidden, w_down, ring)

    moved = lax.optimization_barrier((*shifted(pieces, "tensor"), kept))[:ring]
    difference = student_own + sum(piece.astype(F32) for piece in moved)
    own = (difference * total_rows ** (-0.5)).astype(BF16)
    scaled = shifted([own] * ring, "tensor")
    far_sum = over(after(far_theirs, own), 1)

    keep, give = grads_call(
        after(info, far_sum),
        scaled,
        student_normed,
        s_hidden,
        s_down,
        up_slope,
        gate_slope,
        chips,
    )
    shares = pair_call(keep, swapped(give))
    far_sum = (far_sum.astype(F32) + far_mine.astype(F32)).astype(BF16)
    shares = flipped(shares)
    own = sum(share.astype(F32) for share in shares).astype(BF16)
    mine = flipped([own] * chips)
    others = [swapped(share) for share in mine]

    level_sums = [over(after(near_theirs, far_sum), 1), over(far_sum, 2)]
    mlp_own = sum(after(value, mine[-1]).astype(F32) for value in level_sums)
    teacher_out = (mixed_own.astype(F32) + (kept.astype(F32) + mlp_own)).astype(BF16)
    grad_gate, grad_up, grad_down, notes = finish_call(info, mine, others, ring)
    return teacher_out, grad_gate, grad_up, grad_down, notes[0, 0, 0] / sd


def local(*args):
    rows, w_query, s_gate = args[0].shape[0], args[5], args[14]
    dp, ring = lax.axis_size("dp"), lax.axis_size("tensor")
    heads = w_query.shape[1] // HD
    fits = (
        dp == 2 * heads
        and heads > 1
        and ring == 4
        and heads & (heads - 1) == 0
        and w_query.shape[0] == dp * COLS
        and s_gate.shape[0] == s_gate.shape[1]
        and rows % (32 * ring) == 0
    )
    return paired(*args) if fits else general(*args)


def solution(mesh):
    in_specs = (
        P("dp", "tensor"),
        P(),
        P("dp"),
        P(),
        P(),
        P(None, "tensor"),
        P(None, "tensor"),
        P(None, "tensor"),
        P("tensor", None),
        P(None, "tensor"),
        P(None, "tensor"),
        P("tensor", None),
        P(),
        P("dp", None),
        P(None, "tensor"),
        P(None, "tensor"),
        P("tensor", None),
    )
    out_specs = (P("dp", "tensor"), P(None, "tensor"), P(None, "tensor"), P("tensor", None), P())
    return jax.shard_map(local, mesh=mesh, in_specs=in_specs, out_specs=out_specs, check_vma=False)
```

```python
import functools
import math

import jax
import jax.numpy as jnp
from jax import lax
from jax.experimental import pallas as pl
from jax.experimental.pallas import tpu as pltpu
from jax.sharding import PartitionSpec as P

HD = 128
COLS = 256
NOTE = 16
SERIES = 8
F32 = jnp.float32
BF16 = jnp.bfloat16
MIB = 1024 * 1024


def rms_scale(values):
    return values * lax.rsqrt(jnp.mean(values * values, axis=-1, keepdims=True) + 1e-05)


def frequencies(head_dim):
    indices = jnp.arange(head_dim // 2).astype(jnp.float32)
    return jnp.exp(-jnp.log(500000.0) * 2.0 * indices / head_dim)


def rotary(inputs, angles):
    half_dim = inputs.shape[-1] // 2
    cosine = jnp.cos(angles)
    sine = jnp.sin(angles)
    first_half = inputs[..., :half_dim]
    second_half = inputs[..., half_dim:]
    return jnp.concatenate(
        [first_half * cosine - second_half * sine, first_half * sine + second_half * cosine],
        axis=-1,
    )


def general(
    tokens,
    series_ids,
    offsets,
    norm_gain,
    mlp_gain,
    w_query,
    w_key,
    w_value,
    w_out,
    w_gate,
    w_up,
    w_down,
    projector,
    student_in,
    s_gate,
    s_up,
    s_down,
):
    row_count = tokens.shape[0]
    heads_dev = w_query.shape[1] // HD
    first_row = lax.axis_index("dp") * row_count
    tokens_full = lax.all_gather(tokens, "tensor", axis=1, tiled=True).astype(jnp.float32)
    normed = (rms_scale(tokens_full) * norm_gain).astype(jnp.bfloat16)
    angles = offsets.astype(jnp.float32)[:, None, None] * frequencies(HD)[None, None, :]
    queries = rotary(
        jnp.dot(normed, w_query, preferred_element_type=jnp.float32).reshape(
            row_count, heads_dev, HD
        ),
        angles,
    ).astype(jnp.bfloat16)
    keys_rot = rotary(
        jnp.dot(normed, w_key, preferred_element_type=jnp.float32).reshape(
            row_count, heads_dev, HD
        ),
        angles,
    ).astype(jnp.bfloat16)
    values_mine = jnp.dot(normed, w_value, preferred_element_type=jnp.float32).astype(jnp.bfloat16)
    keys_flat = keys_rot.reshape(row_count, heads_dev * HD)
    query_pos = first_row + jnp.arange(row_count, dtype=jnp.int32)
    query_series = lax.dynamic_slice_in_dim(series_ids, first_row, row_count, 0)
    factor = HD ** (-0.5)
    peak = jnp.full((row_count, heads_dev), -1e30, jnp.float32)
    key_block = lax.all_gather(keys_flat, "dp", axis=0, tiled=True)
    value_block = lax.all_gather(values_mine, "dp", axis=0, tiled=True)
    count = key_block.shape[0]
    key_pos = jnp.arange(count, dtype=jnp.int32)
    allowed = (
        (key_pos[None, :] >= 0)
        & (key_pos[None, :] <= query_pos[:, None])
        & (series_ids[None, :] == query_series[:, None])
    )
    scores = (
        jnp.einsum(
            "qhd,khd->qhk",
            queries,
            key_block.reshape(count, heads_dev, HD),
            preferred_element_type=jnp.float32,
        )
        * factor
    )
    scores = jnp.where(allowed[:, None, :], scores, -1e30)
    new_peak = jnp.maximum(peak, jnp.max(scores, axis=2))
    weights = jnp.where(allowed[:, None, :], jnp.exp(scores - new_peak[:, :, None]), 0.0)
    denom = jnp.sum(weights, axis=2)
    accum = jnp.einsum(
        "qhk,khd->qhd",
        weights.astype(jnp.bfloat16),
        value_block.reshape(count, heads_dev, HD),
        preferred_element_type=jnp.float32,
    )
    peak, denom, accum = (new_peak, denom, accum)
    attended = (accum / denom[:, :, None]).astype(jnp.bfloat16).reshape(row_count, heads_dev * HD)
    partial_out = jnp.dot(attended, w_out, preferred_element_type=jnp.float32)
    own_sum = lax.psum_scatter(
        partial_out.astype(jnp.bfloat16), "tensor", scatter_dimension=1, tiled=True
    ).astype(jnp.float32)
    mixed_own = (tokens.astype(jnp.float32) + own_sum).astype(jnp.bfloat16)
    mixed = lax.all_gather(mixed_own, "tensor", axis=1, tiled=True)
    normed_two = (rms_scale(mixed.astype(jnp.float32)) * mlp_gain).astype(jnp.bfloat16)
    gate_out = jnp.dot(normed_two, w_gate, preferred_element_type=jnp.float32)
    up_out = jnp.dot(normed_two, w_up, preferred_element_type=jnp.float32)
    hidden = (jax.nn.silu(gate_out) * up_out).astype(jnp.bfloat16)
    mlp_part = jnp.dot(hidden, w_down, preferred_element_type=jnp.float32)
    mlp_own = lax.psum_scatter(
        mlp_part.astype(jnp.bfloat16), "tensor", scatter_dimension=1, tiled=True
    ).astype(jnp.float32)
    teacher_out = (mixed_own.astype(jnp.float32) + mlp_own).astype(jnp.bfloat16)
    student_full = student_in.astype(jnp.float32)
    student_normed = rms_scale(student_full).astype(jnp.bfloat16)
    s_gate_out = jnp.dot(student_normed, s_gate, preferred_element_type=jnp.float32)
    s_up_out = jnp.dot(student_normed, s_up, preferred_element_type=jnp.float32)
    sigmoid_gate = jax.nn.sigmoid(s_gate_out)
    s_hidden = (s_gate_out * sigmoid_gate * s_up_out).astype(jnp.bfloat16)
    student_part = jnp.dot(s_hidden, s_down, preferred_element_type=jnp.float32)
    teacher_full = lax.all_gather(teacher_out, "tensor", axis=1, tiled=True)
    target = jnp.dot(teacher_full, projector, preferred_element_type=jnp.float32)
    student_summed = lax.psum(student_part.astype(jnp.bfloat16), "tensor").astype(jnp.float32)
    difference = student_full + student_summed - target
    total_rows = row_count * lax.axis_size("dp")
    scaled = (difference * total_rows ** (-0.5)).astype(jnp.bfloat16)
    grad_down_part = jnp.einsum("rk,rc->kc", s_hidden, scaled, preferred_element_type=jnp.float32)
    grad_hidden = jnp.einsum("rc,kc->rk", scaled, s_down, preferred_element_type=jnp.float32)
    grad_up_in = (grad_hidden * s_gate_out * sigmoid_gate).astype(jnp.bfloat16)
    grad_gate_in = (
        grad_hidden * s_up_out * sigmoid_gate * (1.0 + s_gate_out * (1.0 - sigmoid_gate))
    ).astype(jnp.bfloat16)
    grad_gate_part = jnp.einsum(
        "rc,rk->ck", student_normed, grad_gate_in, preferred_element_type=jnp.float32
    )
    grad_up_part = jnp.einsum(
        "rc,rk->ck", student_normed, grad_up_in, preferred_element_type=jnp.float32
    )
    square_sum = jnp.sum(difference * difference)
    grad_gate, grad_up, grad_down, square_total = (
        lax.psum(grad_gate_part.astype(jnp.bfloat16), "dp").astype(jnp.float32),
        lax.psum(grad_up_part.astype(jnp.bfloat16), "dp").astype(jnp.float32),
        lax.psum(grad_down_part.astype(jnp.bfloat16), "dp").astype(jnp.float32),
        lax.psum(square_sum.astype(jnp.bfloat16), "dp").astype(jnp.float32),
    )
    error = square_total / (total_rows * difference.shape[1])
    return (teacher_out, grad_gate, grad_up, grad_down, error)


def dot(a, b):
    return jnp.dot(a, b, preferred_element_type=F32)


def dot_over(a, b, dims):
    return lax.dot_general(a, b, ((dims[:1], dims[1:]), ((), ())), preferred_element_type=F32)


def params(limit):
    return pltpu.CompilerParams(vmem_limit_bytes=limit * MIB)


def whole(shape):
    return pl.BlockSpec(shape, lambda *_: (0,) * len(shape))


def cost(flops, moved, transcendentals=0):
    return pl.CostEstimate(
        flops=int(flops), bytes_accessed=int(moved), transcendentals=int(transcendentals)
    )


def qkv_kernel(info_ref, *refs, ring, heads, factor):
    blocks = [refs[:ring], refs[ring : 2 * ring]]
    gain_ref, cos_ref, sin_ref, *sources = refs[2 * ring : 2 * ring + 6]
    outs = refs[2 * ring + 6 : 2 * ring + 6 + heads]
    tok_ref, normed, made, weights, sems = refs[2 * ring + 6 + heads :]
    half, width = blocks[0][0].shape
    depth = gain_ref.shape[1]
    copies = [
        pltpu.make_async_copy(source, weights.at[k], sems.at[k])
        for k, source in enumerate(sources)
    ]
    for copy in copies:
        copy.start()
    for k in range(2):
        mine = slice(k * half, (k + 1) * half)
        total = jnp.zeros((half, 1), F32)
        for block in blocks[k]:
            part = block[...].astype(F32)
            total += jnp.sum(part * part, axis=1, keepdims=True)
        scale = lax.rsqrt(total / depth + 1e-05)
        for s, block in enumerate(blocks[k]):
            at = pl.ds(pl.multiple_of(info_ref[s] * width, 128), width)
            part = block[...]
            tok_ref[mine, at] = part
            normed[mine, at] = (part.astype(F32) * scale * gain_ref[:, at]).astype(BF16)
    for kind, copy in enumerate(copies):
        copy.wait()
        result = dot(normed[...], weights[kind])
        for h in range(heads):
            head = result[:, h * HD : (h + 1) * HD]
            if kind < 2:
                head = head * cos_ref[...] + pltpu.roll(head, HD // 2, 1) * sin_ref[...]
            if kind == 0:
                head = head * factor
            made[h, kind] = head.astype(BF16)
    for f in range(heads):
        outs[f][...] = made[info_ref[ring + 1] ^ f]


def qkv_call(info, blocks, gain, cosine, sine, *weights):
    half, width = blocks[0][0].shape
    rows, ring = 2 * half, len(blocks[0])
    depth, out_cols = weights[0].shape
    heads = out_cols // HD
    result = pl.pallas_call(
        functools.partial(
            qkv_kernel, ring=ring, heads=heads, factor=HD ** (-0.5) * math.log2(math.e)
        ),
        out_shape=[jax.ShapeDtypeStruct((3, rows, HD), BF16)] * heads
        + [jax.ShapeDtypeStruct((rows, depth), BF16)],
        grid_spec=pltpu.PrefetchScalarGridSpec(
            num_scalar_prefetch=1,
            grid=(1,),
            in_specs=[whole((half, width))] * (2 * ring)
            + [whole((1, depth)), whole((rows, HD)), whole((rows, HD))]
            + [pl.BlockSpec(memory_space=pl.ANY)] * 3,
            out_specs=[whole((3, rows, HD))] * heads + [whole((rows, depth))],
            scratch_shapes=[
                pltpu.VMEM((rows, depth), BF16),
                pltpu.VMEM((heads, 3, rows, HD), BF16),
                pltpu.VMEM((3, depth, out_cols), BF16),
                pltpu.SemaphoreType.DMA((3,)),
            ],
        ),
        compiler_params=params(42),
        cost_estimate=cost(6 * rows * depth * out_cols, 6 * depth * out_cols),
        name="qkv",
    )(info, *blocks[0], *blocks[1], gain, cosine, sine, *weights)
    return result[:heads], result[heads]


def attention_kernel(first_ref, info_ref, *refs, chips, ring):
    own, other = refs[:chips], refs[chips : 2 * chips]
    outs = refs[2 * chips : 3 * chips]
    keys_all, values_all = refs[3 * chips :]
    chip, core = info_ref[ring + 1], info_ref[ring + 2]
    span = outs[0].shape[0]
    for f in range(chips):
        for source, side in ((own[f], core), (other[f], 1 - core)):
            block = 2 * (chip ^ f) + side
            keys_all[block] = source[1]
            values_all[block] = source[2].T

    def first_of(row):
        found = jnp.int32(0)
        for s in range(SERIES):
            edge = first_ref[s]
            found = jnp.where(edge <= row, jnp.maximum(found, edge), found)
        return found

    for f in range(chips):
        last = 2 * (chip ^ f) + core
        query = own[f][0]
        row = last * span + lax.broadcasted_iota(jnp.int32, (1, span), 1)
        start = jnp.zeros((1, span), jnp.int32)
        for s in range(SERIES):
            edge = first_ref[s]
            start = jnp.where(edge <= row, jnp.maximum(start, edge), start)
        lane = lax.broadcasted_iota(jnp.int32, (span, 1), 0)

        def body(at, carry, masked, query=query, row=row, start=start, lane=lane):
            peak, denom, accum = carry
            scores = dot_over(keys_all[at], query, (1, 1))
            if masked:
                column = lane + at * span
                allowed = (column >= start) & (column <= row)
                scores = jnp.where(allowed, scores, -1e30)
            new_peak = jnp.maximum(peak, jnp.max(scores, axis=0, keepdims=True))
            weights = jnp.exp2(scores - new_peak)
            if masked:
                weights = jnp.where(allowed, weights, 0.0)
            keep = jnp.exp2(peak - new_peak)
            denom = denom * keep + jnp.sum(weights, axis=0, keepdims=True)
            accum = accum * keep + dot(values_all[at], weights.astype(BF16))
            return new_peak, denom, accum

        def pair(turn, carry, query=query, full=None):
            peak, denom, accum = carry
            at = full + 2 * turn
            blocks = (at, at + 1)
            scores = [dot_over(keys_all[block], query, (1, 1)) for block in blocks]
            tops = [jnp.max(score, axis=0, keepdims=True) for score in scores]
            new_peak = jnp.maximum(peak, jnp.maximum(*tops))
            keep = jnp.exp2(peak - new_peak)
            denom, accum = denom * keep, accum * keep
            for block, score in zip(blocks, scores):
                weights = jnp.exp2(score - new_peak)
                denom += jnp.sum(weights, axis=0, keepdims=True)
                accum += dot(values_all[block], weights.astype(BF16))
            return new_peak, denom, accum

        begin = first_of(last * span) // span
        full = jnp.minimum(last, (first_of(last * span + span - 1) + span - 1) // span)
        carry = (
            jnp.full((1, span), -1e30, F32),
            jnp.zeros((1, span), F32),
            jnp.zeros((HD, span), F32),
        )
        carry = lax.fori_loop(begin, full, functools.partial(body, masked=True), carry)
        turns = (last - full) // 2
        carry = lax.fori_loop(0, turns, functools.partial(pair, full=full), carry)
        rest = full + 2 * turns
        carry = lax.fori_loop(rest, last, functools.partial(body, masked=False), carry)
        _, denom, accum = body(last, carry, masked=True)
        outs[f][...] = (accum / denom).T.astype(BF16)


def attention_call(first, info, own, other, ring):
    chips = len(own)
    _, rows, _ = own[0].shape
    return pl.pallas_call(
        functools.partial(attention_kernel, chips=chips, ring=ring),
        out_shape=[jax.ShapeDtypeStruct((rows, HD), BF16)] * chips,
        grid_spec=pltpu.PrefetchScalarGridSpec(
            num_scalar_prefetch=2,
            grid=(1,),
            in_specs=[whole((3, rows, HD))] * (2 * chips),
            out_specs=[whole((rows, HD))] * chips,
            scratch_shapes=[
                pltpu.VMEM((2 * chips, rows, HD), BF16),
                pltpu.VMEM((2 * chips, HD, rows), BF16),
            ],
        ),
        compiler_params=params(24),
        cost_estimate=cost(
            4 * chips * rows * chips * rows * HD,
            16 * chips * rows * HD,
            chips * rows * chips * rows,
        ),
        name="attention",
    )(first, info, *own, *other)


def middle_kernel(info_ref, *refs, ring, chips):
    parts = [refs[:ring], refs[ring : 2 * ring]]
    refs = refs[2 * ring :]
    tok_ref, w_own_ref = refs[:2]
    near_first, near_rest = refs[2 : 2 + chips], refs[2 + chips : 2 + 2 * chips]
    far_first, far_rest = refs[2 + 2 * chips], refs[3 + 2 * chips : 3 + 3 * chips]
    refs = refs[3 + 3 * chips :]
    gain_ref, gate_ref, up_ref, wp_ref, proj_ref, student_ref = refs[:6]
    hidden_ref, own_ref = refs[6:8]
    pieces = refs[8 : 8 + ring]
    attended, mixed, total, near, far, gates, ups, wp, proj, sems = refs[8 + ring :]
    step = pl.program_id(0)
    level, chip, core = info_ref[ring], info_ref[ring + 1], info_ref[ring + 2]
    rows, depth = mixed.shape
    width = own_ref.shape[1]
    blocks, _, wide = gates.shape

    used = iter(range(sems.shape[0]))
    copy = lambda source, target: pltpu.make_async_copy(source, target, sems.at[next(used)])
    heads = []
    for k in range(2):
        for s, part in enumerate(parts[k]):
            count = part.shape[0]
            for i in range(count):
                at = (level ^ info_ref[s]) * width + (chip ^ (k * count + i)) * HD
                heads.append(copy(part.at[i], attended.at[:, pl.ds(pl.multiple_of(at, HD), HD)]))
    slices = [
        [
            copy(near_first[f], near.at[f, 0]),
            copy(near_rest[f], near.at[f, pl.ds(1, ring - 2)]),
            copy(far_first.at[f, 0], far.at[f, 0]),
            copy(far_rest[f], far.at[f, pl.ds(1, ring - 2)]),
        ]
        for f in range(chips)
    ]
    own_rows = pl.ds(pl.multiple_of(level * width, width), width)
    late = [copy(proj_ref.at[own_rows], proj), copy(student_ref, total)]
    columns = [pl.ds(i * wide, wide) for i in range(blocks)]
    units = [
        [
            copy(gate_ref.at[:, columns[i]], gates.at[i]),
            copy(up_ref.at[:, columns[i]], ups.at[i]),
            copy(wp_ref.at[columns[i]], wp.at[i]),
        ]
        for i in range(blocks)
    ]

    @pl.when(step == 0)
    def _():
        for c in heads + slices[0]:
            c.start()
        for c in sum(slices[1:], []) + late:
            c.start()
        for c in heads:
            c.wait()

    for f in range(chips):

        @pl.when(step == f)
        def _(f=f):
            for c in slices[f]:
                c.wait()
            for c in sum(units[f::chips], []):
                c.start()

    @pl.when(step < chips)
    def _():
        for gathered, side in ((near, core), (far, 1 - core)):
            here = pl.ds(pl.multiple_of(side * COLS, COLS), COLS)
            result = tok_ref[:, here].astype(F32) + dot(attended[:, :width], w_own_ref[:, here])
            weight = gathered[step].reshape(depth - width, COLS)
            result += dot(attended[:, width:], weight)
            at = pl.ds(pl.multiple_of((2 * (step ^ chip) + side) * COLS, COLS), COLS)
            mixed[:, at] = result.astype(BF16)

    @pl.when(step == chips)
    def _():
        for c in late:
            c.wait()
        values = mixed[...].astype(F32)
        attended[...] = (rms_scale(values) * gain_ref[...]).astype(BF16)
        own = mixed[:, pl.ds(pl.multiple_of(level * width, 128), width)]
        own_ref[...] = own
        total[...] -= dot(own, proj[...])

    for i in range(blocks):

        @pl.when(step == chips + i)
        def _(i=i):
            for c in units[i]:
                c.wait()

    @pl.when(step >= chips)
    def _():
        index = step - chips
        gate = dot(attended[...], gates[index])
        up = dot(attended[...], ups[index])
        hidden = (gate * jax.nn.sigmoid(gate) * up).astype(BF16)
        hidden_ref[...] = hidden
        total[...] -= dot(hidden, wp[index])

    @pl.when(step == pl.num_programs(0) - 1)
    def _():
        size = rows // ring
        for s in range(ring):
            at = pl.ds(pl.multiple_of(((level + s) & (ring - 1)) * size, size), size)
            pieces[s][...] = total[at, :].astype(BF16)


def middle_call(info, parts, tok, w_out, near, far, gain, w_gate, w_up, wp, projector, student):
    rows, depth = tok.shape
    ring, chips = len(parts[0]), len(near[0])
    units = w_gate.shape[1]
    wide = 2 * COLS
    width = depth // ring
    sd = projector.shape[1]
    blocks = units // wide
    tile = lambda j, info: (0, jnp.minimum(j, chips - 1) ^ info[ring + 1])
    late = lambda j, info: (0, jnp.maximum(j - chips, 0))
    anywhere = pl.BlockSpec(memory_space=pl.ANY)
    count = 2 * ring * parts[0][0].shape[0] + 4 * chips + 2 + 3 * blocks
    result = pl.pallas_call(
        functools.partial(middle_kernel, ring=ring, chips=chips),
        out_shape=[
            jax.ShapeDtypeStruct((rows, units), BF16),
            jax.ShapeDtypeStruct((rows, width), BF16),
        ]
        + [jax.ShapeDtypeStruct((rows // ring, sd), BF16)] * ring,
        grid_spec=pltpu.PrefetchScalarGridSpec(
            num_scalar_prefetch=1,
            grid=(chips + blocks,),
            in_specs=[anywhere] * (2 * ring)
            + [pl.BlockSpec((rows, wide), tile), pl.BlockSpec((width, wide), tile)]
            + [anywhere] * (3 * chips + 1)
            + [whole((1, depth))]
            + [anywhere] * 5,
            out_specs=[
                pl.BlockSpec((rows, wide), late),
                whole((rows, width)),
            ]
            + [whole((rows // ring, sd))] * ring,
            scratch_shapes=[
                pltpu.VMEM((rows, depth), BF16),
                pltpu.VMEM((rows, depth), BF16),
                pltpu.VMEM((rows, sd), F32),
                pltpu.VMEM((chips, ring - 1, width, COLS), BF16),
                pltpu.VMEM((chips, ring - 1, width, COLS), BF16),
                pltpu.VMEM((blocks, depth, wide), BF16),
                pltpu.VMEM((blocks, depth, wide), BF16),
                pltpu.VMEM((blocks, wide, sd), BF16),
                pltpu.VMEM((width, sd), BF16),
                pltpu.SemaphoreType.DMA((count,)),
            ],
        ),
        compiler_params=params(42),
        cost_estimate=cost(
            2 * rows * depth * (depth + 2 * units) + 2 * rows * sd * (units + width),
            2 * depth * (depth + 2 * units),
            rows * units,
        ),
        name="middle",
    )(
        info,
        *parts[0],
        *parts[1],
        tok,
        w_out,
        *near[0],
        *near[1],
        far[0],
        *far[1],
        gain,
        w_gate,
        w_up,
        wp,
        projector,
        student,
    )
    return result[0], result[1], result[2:]


def down_kernel(info_ref, hidden_ref, weight_ref, *outs):
    result = dot(hidden_ref[...], weight_ref[...]).astype(BF16)
    for j, out in enumerate(outs):

        @pl.when(pl.program_id(0) == j)
        def _(out=out):
            out[...] = result


def down_call(info, hidden, w_down, ring, first_flip, last_flip):
    rows, units = hidden.shape
    depth = w_down.shape[1]
    width = depth // ring
    count = first_flip - last_flip + 1
    return pl.pallas_call(
        down_kernel,
        out_shape=[jax.ShapeDtypeStruct((rows, width), BF16)] * count,
        grid_spec=pltpu.PrefetchScalarGridSpec(
            num_scalar_prefetch=1,
            grid=(count,),
            in_specs=[
                whole((rows, units)),
                pl.BlockSpec((units, width), lambda j, info: (0, info[ring] ^ (first_flip - j))),
            ],
            out_specs=[whole((rows, width))] * count,
        ),
        compiler_params=params(24),
        cost_estimate=cost(2 * rows * units * width * count, 2 * units * width * count),
        name="down",
    )(info, hidden, w_down)


def grads_kernel(info_ref, *refs, ring, chips):
    pieces = refs[:ring]
    normed_ref, hidden_ref, s_down_ref, up_ref, gate_ref = refs[ring : ring + 5]
    keep_ref, give_ref, scaled, grads = refs[ring + 5 :]
    chip, core = info_ref[ring + 1], info_ref[ring + 2]
    size, sd = pieces[0].shape
    for s in range(ring):
        scaled[pl.ds(pl.multiple_of(info_ref[s] * size, size), size), :] = pieces[s][...]
    value = scaled[...]
    wide = value.astype(F32)
    error = jnp.sum(wide * wide)
    grad_hidden = dot_over(value, s_down_ref[...], (1, 1))
    grads[0] = dot_over(normed_ref[...], (grad_hidden * gate_ref[...].astype(F32)).astype(BF16), (0, 0))
    grads[1] = dot_over(normed_ref[...], (grad_hidden * up_ref[...].astype(F32)).astype(BF16), (0, 0))
    grads[2] = dot_over(hidden_ref[...], value, (0, 0))
    share = grads.shape[1] // (2 * chips)
    for f in range(chips):
        for k in range(3):
            for part, ref in ((core, keep_ref), (1 - core, give_ref)):
                at = pl.multiple_of((part * chips + (chip ^ f)) * share, share)
                ref[f, k * share : (k + 1) * share] = grads[k, pl.ds(at, share), :].astype(
                    ref.dtype
                )
        for ref in (keep_ref, give_ref):
            ref[f, 3 * share :] = jnp.full((NOTE, sd), error, F32).astype(ref.dtype)


def grads_call(info, pieces, normed, hidden, s_down, up, gate, chips):
    ring = len(pieces)
    rows, sd = normed.shape
    units = hidden.shape[1]
    share = 3 * sd // (2 * chips) + NOTE
    operands = [*pieces, normed, hidden, s_down, up, gate]
    return pl.pallas_call(
        functools.partial(grads_kernel, ring=ring, chips=chips),
        out_shape=(
            jax.ShapeDtypeStruct((chips, share, units), F32),
            jax.ShapeDtypeStruct((chips, share, units), BF16),
        ),
        grid_spec=pltpu.PrefetchScalarGridSpec(
            num_scalar_prefetch=1,
            grid=(1,),
            in_specs=[whole(a.shape) for a in operands],
            out_specs=(whole((chips, share, units)), whole((chips, share, units))),
            scratch_shapes=[pltpu.VMEM((rows, sd), BF16), pltpu.VMEM((3, sd, units), F32)],
        ),
        compiler_params=params(22),
        cost_estimate=cost(8 * rows * sd * units, 20 * sd * units),
        name="grads",
    )(info, *operands)


def pair_kernel(keep_ref, theirs_ref, *outs):
    for f, out in enumerate(outs):
        out[...] = (keep_ref[f] + theirs_ref[f].astype(F32)).astype(out.dtype)


def pair_call(keep, theirs):
    chips, share, sd = keep.shape
    return pl.pallas_call(
        pair_kernel,
        out_shape=[jax.ShapeDtypeStruct((share, sd), BF16)] * chips,
        compiler_params=params(10),
        cost_estimate=cost(keep.size, 8 * keep.size),
        name="pair",
    )(keep, theirs)


def finish_kernel(info_ref, *refs, chips, ring):
    mine, others = refs[:chips], refs[chips : 2 * chips]
    outs = refs[2 * chips : 2 * chips + 3]
    notes = refs[2 * chips + 3]
    chip, core = info_ref[ring + 1], info_ref[ring + 2]
    share = (mine[0].shape[0] - NOTE) // 3
    for f in range(chips):
        for part, ref in ((core, mine[f]), (1 - core, others[f])):
            index = part * chips + (chip ^ f)
            at = pl.ds(pl.multiple_of(index * share, share), share)
            for k in range(3):
                outs[k][at, :] = ref[k * share : (k + 1) * share].astype(F32)
            notes[index] = ref[3 * share :, :HD].astype(F32)


def finish_call(info, mine, others, ring):
    chips = len(mine)
    share, sd = mine[0].shape
    rows = (share - NOTE) // 3 * 2 * chips
    return pl.pallas_call(
        functools.partial(finish_kernel, chips=chips, ring=ring),
        out_shape=[jax.ShapeDtypeStruct((rows, sd), F32)] * 3
        + [jax.ShapeDtypeStruct((2 * chips, NOTE, HD), F32)],
        grid_spec=pltpu.PrefetchScalarGridSpec(
            num_scalar_prefetch=1,
            grid=(1,),
            in_specs=[whole((share, sd))] * (2 * chips),
            out_specs=[whole((rows, sd))] * 3 + [whole((2 * chips, NOTE, HD))],
        ),
        compiler_params=params(14),
        cost_estimate=cost(rows * sd, 12 * rows * sd),
        name="finish",
    )(info, *mine, *others)


def step_on(block, axis):
    size = lax.axis_size(axis)
    return lax.ppermute(block, axis, [(i, (i + 1) % size) for i in range(size)])


def ring_gather(block, axis, steps=None):
    blocks = [block]
    for _ in range(lax.axis_size(axis) - 1 if steps is None else steps):
        blocks.append(step_on(blocks[-1], axis))
    return blocks


def shifted(pieces, axis):
    size = lax.axis_size(axis)
    moved = [
        lax.ppermute(pieces[s], axis, [(i, (i + s) % size) for i in range(size)])
        for s in range(1, size)
    ]
    return [pieces[0], *moved]


def flipped(pieces):
    size = lax.axis_size("dp")
    moved = [
        lax.ppermute(pieces[f], "dp", [(i, i ^ (2 * f)) for i in range(size)])
        for f in range(1, len(pieces))
    ]
    return [pieces[0], *moved]


def swapped(value):
    size = lax.axis_size("dp")
    return lax.ppermute(value, "dp", [(i, i ^ 1) for i in range(size)])


def after(value, *others):
    return lax.optimization_barrier((value, *others))[0]


def paired(
    tokens,
    series_ids,
    offsets,
    norm_gain,
    mlp_gain,
    w_query,
    w_key,
    w_value,
    w_out,
    w_gate,
    w_up,
    w_down,
    projector,
    student_in,
    s_gate,
    s_up,
    s_down,
):
    rows = tokens.shape[0]
    depth, sd = w_query.shape[0], student_in.shape[1]
    dp, ring = lax.axis_size("dp"), lax.axis_size("tensor")
    here, level = lax.axis_index("dp"), lax.axis_index("tensor")
    chips, half = dp // 2, rows // 2
    total_rows = rows * dp
    size = rows // ring
    slice_cols = depth // dp

    places = [(level - s) & (ring - 1) for s in range(ring)] + [level, here >> 1, here & 1]
    slots = lax.broadcasted_iota(jnp.int32, (16,), 0)
    info = sum(jnp.where(slots == k, place, 0) for k, place in enumerate(places))
    starts = [level * size, here * slice_cols]
    *starts, zero = [jnp.asarray(start, jnp.uint32) for start in (*starts, 0)]
    tokens, info, *starts = lax.optimization_barrier((tokens, info, *starts))

    token_rings = [ring_gather(tokens[k : k + half], "tensor") for k in (0, half)]

    angles = offsets.astype(F32)[:, None] * frequencies(HD)[None, :]
    cosine, sine = jnp.cos(angles), jnp.sin(angles)
    cosine = jnp.concatenate([cosine, cosine], axis=1)
    sine = jnp.concatenate([-sine, sine], axis=1)
    student_full = student_in.astype(F32)
    student_normed = rms_scale(student_full).astype(BF16)
    below = jnp.sum(
        series_ids[None, :] < jnp.arange(SERIES, dtype=jnp.int32)[:, None], axis=1, dtype=jnp.int32
    )

    made, tok_full = qkv_call(
        info, token_rings, norm_gain[None, :], cosine, sine, w_query, w_key, w_value
    )

    student_normed, projected, tok_full = lax.optimization_barrier(
        (student_normed, projector, tok_full)
    )
    s_gate_out = dot(student_normed, s_gate)
    s_up_out = dot(student_normed, s_up)
    sigmoid_gate = jax.nn.sigmoid(s_gate_out)
    up_slope = s_gate_out * sigmoid_gate
    gate_slope = s_up_out * sigmoid_gate * (1.0 + s_gate_out * (1.0 - sigmoid_gate))
    s_hidden = (up_slope * s_up_out).astype(BF16)
    up_slope, gate_slope = up_slope.astype(BF16), gate_slope.astype(BF16)
    student_part = dot(s_hidden, s_down)
    projected = dot(w_down, projected).astype(BF16)
    student_own = lax.dynamic_slice(student_full, [starts[0], zero], (size, sd))
    early = (projected, student_part, s_hidden, up_slope, gate_slope, student_normed, student_own)

    over = lambda value, bit: lax.ppermute(value, "tensor", [(i, i ^ bit) for i in range(ring)])
    w_slice = lax.dynamic_slice(w_out, [zero, starts[1]], (w_out.shape[0], slice_cols))
    w_slice, tok_full = lax.optimization_barrier((w_slice, tok_full))
    w_first, w_second = over(w_slice, 1), over(w_slice, 2)

    own = flipped(made)
    held = lax.optimization_barrier((*own, w_first, w_second, *early))
    own, (w_first, w_second) = held[:chips], held[chips : chips + 2]
    w_third = over(w_second, 1)
    other = [swapped(a) for a in own]
    near_first = flipped([w_first] * chips)
    made = attention_call(below, info, own, other, ring)
    *made, w_third = lax.optimization_barrier((*made, w_third, *near_first))[: chips + 1]
    w_rest = jnp.stack([w_second, w_third])
    attended = lax.optimization_barrier(tuple(flipped(made)))
    parts = [
        ring_gather(jnp.stack(attended[k : k + chips // 2]), "tensor") for k in (0, chips // 2)
    ]
    w_rest = after(w_rest, *attended)
    near_rest = flipped([w_rest] * chips)
    far_first = swapped(after(jnp.stack(near_first)[:, None], *attended))
    far_rest = [swapped(after(a, parts[1][1])) for a in near_rest]

    hidden, mixed_own, pieces = middle_call(
        info,
        parts,
        tok_full,
        w_out,
        (near_first, near_rest),
        (far_first, far_rest),
        mlp_gain[None, :],
        w_gate,
        w_up,
        projected,
        projector,
        student_part,
    )

    far_sum = over(down_call(info, hidden, w_down, ring, 3, 3)[0], 1)
    far_mine, near_theirs, kept = down_call(info, hidden, w_down, ring, 2, 0)

    moved = lax.optimization_barrier((*shifted(pieces, "tensor"), kept))[:ring]
    difference = student_own + sum(piece.astype(F32) for piece in moved)
    own = (difference * total_rows ** (-0.5)).astype(BF16)
    scaled = shifted([own] * ring, "tensor")

    keep, give = grads_call(
        after(info, far_sum),
        scaled,
        student_normed,
        s_hidden,
        s_down,
        up_slope,
        gate_slope,
        chips,
    )
    shares = pair_call(keep, swapped(give))
    far_sum = (far_sum.astype(F32) + far_mine.astype(F32)).astype(BF16)
    shares = flipped(shares)
    own = sum(share.astype(F32) for share in shares).astype(BF16)
    mine = flipped([own] * chips)
    others = [swapped(share) for share in mine]

    level_sums = [over(after(near_theirs, far_sum), 1), over(far_sum, 2)]
    mlp_own = sum(after(value, mine[-1]).astype(F32) for value in level_sums)
    teacher_out = (mixed_own.astype(F32) + (kept.astype(F32) + mlp_own)).astype(BF16)
    grad_gate, grad_up, grad_down, notes = finish_call(info, mine, others, ring)
    return teacher_out, grad_gate, grad_up, grad_down, notes[0, 0, 0] / sd


def local(*args):
    rows, w_query, s_gate = args[0].shape[0], args[5], args[14]
    dp, ring = lax.axis_size("dp"), lax.axis_size("tensor")
    heads = w_query.shape[1] // HD
    fits = (
        dp == 2 * heads
        and heads > 1
        and ring == 4
        and heads & (heads - 1) == 0
        and w_query.shape[0] == dp * COLS
        and s_gate.shape[0] == s_gate.shape[1]
        and rows % (32 * ring) == 0
    )
    return paired(*args) if fits else general(*args)


def solution(mesh):
    in_specs = (
        P("dp", "tensor"),
        P(),
        P("dp"),
        P(),
        P(),
        P(None, "tensor"),
        P(None, "tensor"),
        P(None, "tensor"),
        P("tensor", None),
        P(None, "tensor"),
        P(None, "tensor"),
        P("tensor", None),
        P(),
        P("dp", None),
        P(None, "tensor"),
        P(None, "tensor"),
        P("tensor", None),
    )
    out_specs = (P("dp", "tensor"), P(None, "tensor"), P(None, "tensor"), P("tensor", None), P())
    return jax.shard_map(local, mesh=mesh, in_specs=in_specs, out_specs=out_specs, check_vma=False)
```

```python
import functools
import math

import jax
import jax.numpy as jnp
from jax import lax
from jax.experimental import pallas as pl
from jax.experimental.pallas import tpu as pltpu
from jax.sharding import PartitionSpec as P

HD = 128
COLS = 256
NOTE = 16
SERIES = 8
F32 = jnp.float32
BF16 = jnp.bfloat16
MIB = 1024 * 1024


def rms_scale(values):
    return values * lax.rsqrt(jnp.mean(values * values, axis=-1, keepdims=True) + 1e-05)


def frequencies(head_dim):
    indices = jnp.arange(head_dim // 2).astype(jnp.float32)
    return jnp.exp(-jnp.log(500000.0) * 2.0 * indices / head_dim)


def rotary(inputs, angles):
    half_dim = inputs.shape[-1] // 2
    cosine = jnp.cos(angles)
    sine = jnp.sin(angles)
    first_half = inputs[..., :half_dim]
    second_half = inputs[..., half_dim:]
    return jnp.concatenate(
        [first_half * cosine - second_half * sine, first_half * sine + second_half * cosine],
        axis=-1,
    )


def general(
    tokens,
    series_ids,
    offsets,
    norm_gain,
    mlp_gain,
    w_query,
    w_key,
    w_value,
    w_out,
    w_gate,
    w_up,
    w_down,
    projector,
    student_in,
    s_gate,
    s_up,
    s_down,
):
    row_count = tokens.shape[0]
    heads_dev = w_query.shape[1] // HD
    first_row = lax.axis_index("dp") * row_count
    tokens_full = lax.all_gather(tokens, "tensor", axis=1, tiled=True).astype(jnp.float32)
    normed = (rms_scale(tokens_full) * norm_gain).astype(jnp.bfloat16)
    angles = offsets.astype(jnp.float32)[:, None, None] * frequencies(HD)[None, None, :]
    queries = rotary(
        jnp.dot(normed, w_query, preferred_element_type=jnp.float32).reshape(
            row_count, heads_dev, HD
        ),
        angles,
    ).astype(jnp.bfloat16)
    keys_rot = rotary(
        jnp.dot(normed, w_key, preferred_element_type=jnp.float32).reshape(
            row_count, heads_dev, HD
        ),
        angles,
    ).astype(jnp.bfloat16)
    values_mine = jnp.dot(normed, w_value, preferred_element_type=jnp.float32).astype(jnp.bfloat16)
    keys_flat = keys_rot.reshape(row_count, heads_dev * HD)
    query_pos = first_row + jnp.arange(row_count, dtype=jnp.int32)
    query_series = lax.dynamic_slice_in_dim(series_ids, first_row, row_count, 0)
    factor = HD ** (-0.5)
    peak = jnp.full((row_count, heads_dev), -1e30, jnp.float32)
    key_block = lax.all_gather(keys_flat, "dp", axis=0, tiled=True)
    value_block = lax.all_gather(values_mine, "dp", axis=0, tiled=True)
    count = key_block.shape[0]
    key_pos = jnp.arange(count, dtype=jnp.int32)
    allowed = (
        (key_pos[None, :] >= 0)
        & (key_pos[None, :] <= query_pos[:, None])
        & (series_ids[None, :] == query_series[:, None])
    )
    scores = (
        jnp.einsum(
            "qhd,khd->qhk",
            queries,
            key_block.reshape(count, heads_dev, HD),
            preferred_element_type=jnp.float32,
        )
        * factor
    )
    scores = jnp.where(allowed[:, None, :], scores, -1e30)
    new_peak = jnp.maximum(peak, jnp.max(scores, axis=2))
    weights = jnp.where(allowed[:, None, :], jnp.exp(scores - new_peak[:, :, None]), 0.0)
    denom = jnp.sum(weights, axis=2)
    accum = jnp.einsum(
        "qhk,khd->qhd",
        weights.astype(jnp.bfloat16),
        value_block.reshape(count, heads_dev, HD),
        preferred_element_type=jnp.float32,
    )
    peak, denom, accum = (new_peak, denom, accum)
    attended = (accum / denom[:, :, None]).astype(jnp.bfloat16).reshape(row_count, heads_dev * HD)
    partial_out = jnp.dot(attended, w_out, preferred_element_type=jnp.float32)
    own_sum = lax.psum_scatter(
        partial_out.astype(jnp.bfloat16), "tensor", scatter_dimension=1, tiled=True
    ).astype(jnp.float32)
    mixed_own = (tokens.astype(jnp.float32) + own_sum).astype(jnp.bfloat16)
    mixed = lax.all_gather(mixed_own, "tensor", axis=1, tiled=True)
    normed_two = (rms_scale(mixed.astype(jnp.float32)) * mlp_gain).astype(jnp.bfloat16)
    gate_out = jnp.dot(normed_two, w_gate, preferred_element_type=jnp.float32)
    up_out = jnp.dot(normed_two, w_up, preferred_element_type=jnp.float32)
    hidden = (jax.nn.silu(gate_out) * up_out).astype(jnp.bfloat16)
    mlp_part = jnp.dot(hidden, w_down, preferred_element_type=jnp.float32)
    mlp_own = lax.psum_scatter(
        mlp_part.astype(jnp.bfloat16), "tensor", scatter_dimension=1, tiled=True
    ).astype(jnp.float32)
    teacher_out = (mixed_own.astype(jnp.float32) + mlp_own).astype(jnp.bfloat16)
    student_full = student_in.astype(jnp.float32)
    student_normed = rms_scale(student_full).astype(jnp.bfloat16)
    s_gate_out = jnp.dot(student_normed, s_gate, preferred_element_type=jnp.float32)
    s_up_out = jnp.dot(student_normed, s_up, preferred_element_type=jnp.float32)
    sigmoid_gate = jax.nn.sigmoid(s_gate_out)
    s_hidden = (s_gate_out * sigmoid_gate * s_up_out).astype(jnp.bfloat16)
    student_part = jnp.dot(s_hidden, s_down, preferred_element_type=jnp.float32)
    teacher_full = lax.all_gather(teacher_out, "tensor", axis=1, tiled=True)
    target = jnp.dot(teacher_full, projector, preferred_element_type=jnp.float32)
    student_summed = lax.psum(student_part.astype(jnp.bfloat16), "tensor").astype(jnp.float32)
    difference = student_full + student_summed - target
    total_rows = row_count * lax.axis_size("dp")
    scaled = (difference * total_rows ** (-0.5)).astype(jnp.bfloat16)
    grad_down_part = jnp.einsum("rk,rc->kc", s_hidden, scaled, preferred_element_type=jnp.float32)
    grad_hidden = jnp.einsum("rc,kc->rk", scaled, s_down, preferred_element_type=jnp.float32)
    grad_up_in = (grad_hidden * s_gate_out * sigmoid_gate).astype(jnp.bfloat16)
    grad_gate_in = (
        grad_hidden * s_up_out * sigmoid_gate * (1.0 + s_gate_out * (1.0 - sigmoid_gate))
    ).astype(jnp.bfloat16)
    grad_gate_part = jnp.einsum(
        "rc,rk->ck", student_normed, grad_gate_in, preferred_element_type=jnp.float32
    )
    grad_up_part = jnp.einsum(
        "rc,rk->ck", student_normed, grad_up_in, preferred_element_type=jnp.float32
    )
    square_sum = jnp.sum(difference * difference)
    grad_gate, grad_up, grad_down, square_total = (
        lax.psum(grad_gate_part.astype(jnp.bfloat16), "dp").astype(jnp.float32),
        lax.psum(grad_up_part.astype(jnp.bfloat16), "dp").astype(jnp.float32),
        lax.psum(grad_down_part.astype(jnp.bfloat16), "dp").astype(jnp.float32),
        lax.psum(square_sum.astype(jnp.bfloat16), "dp").astype(jnp.float32),
    )
    error = square_total / (total_rows * difference.shape[1])
    return (teacher_out, grad_gate, grad_up, grad_down, error)


def dot(a, b):
    return jnp.dot(a, b, preferred_element_type=F32)


def dot_over(a, b, dims):
    return lax.dot_general(a, b, ((dims[:1], dims[1:]), ((), ())), preferred_element_type=F32)


def params(limit):
    return pltpu.CompilerParams(vmem_limit_bytes=limit * MIB)


def whole(shape):
    return pl.BlockSpec(shape, lambda *_: (0,) * len(shape))


def cost(flops, moved, transcendentals=0):
    return pl.CostEstimate(
        flops=int(flops), bytes_accessed=int(moved), transcendentals=int(transcendentals)
    )


def qkv_kernel(info_ref, *refs, ring, heads, factor):
    blocks = [refs[:ring], refs[ring : 2 * ring]]
    gain_ref, cos_ref, sin_ref, *sources = refs[2 * ring : 2 * ring + 6]
    outs = refs[2 * ring + 6 : 2 * ring + 6 + heads]
    tok_ref, normed, made, weights, sems = refs[2 * ring + 6 + heads :]
    half, width = blocks[0][0].shape
    depth = gain_ref.shape[1]
    copies = [
        pltpu.make_async_copy(source, weights.at[k], sems.at[k])
        for k, source in enumerate(sources)
    ]
    for copy in copies:
        copy.start()
    for k in range(2):
        mine = slice(k * half, (k + 1) * half)
        total = jnp.zeros((half, 1), F32)
        for block in blocks[k]:
            part = block[...].astype(F32)
            total += jnp.sum(part * part, axis=1, keepdims=True)
        scale = lax.rsqrt(total / depth + 1e-05)
        for s, block in enumerate(blocks[k]):
            at = pl.ds(pl.multiple_of(info_ref[s] * width, 128), width)
            part = block[...]
            tok_ref[mine, at] = part
            normed[mine, at] = (part.astype(F32) * scale * gain_ref[:, at]).astype(BF16)
    for kind, copy in enumerate(copies):
        copy.wait()
        result = dot(normed[...], weights[kind])
        for h in range(heads):
            head = result[:, h * HD : (h + 1) * HD]
            if kind < 2:
                head = head * cos_ref[...] + pltpu.roll(head, HD // 2, 1) * sin_ref[...]
            if kind == 0:
                head = head * factor
            made[h, kind] = head.astype(BF16)
    for f in range(heads):
        outs[f][...] = made[info_ref[ring + 1] ^ f]


def qkv_call(info, blocks, gain, cosine, sine, *weights):
    half, width = blocks[0][0].shape
    rows, ring = 2 * half, len(blocks[0])
    depth, out_cols = weights[0].shape
    heads = out_cols // HD
    result = pl.pallas_call(
        functools.partial(
            qkv_kernel, ring=ring, heads=heads, factor=HD ** (-0.5) * math.log2(math.e)
        ),
        out_shape=[jax.ShapeDtypeStruct((3, rows, HD), BF16)] * heads
        + [jax.ShapeDtypeStruct((rows, depth), BF16)],
        grid_spec=pltpu.PrefetchScalarGridSpec(
            num_scalar_prefetch=1,
            grid=(1,),
            in_specs=[whole((half, width))] * (2 * ring)
            + [whole((1, depth)), whole((rows, HD)), whole((rows, HD))]
            + [pl.BlockSpec(memory_space=pl.ANY)] * 3,
            out_specs=[whole((3, rows, HD))] * heads + [whole((rows, depth))],
            scratch_shapes=[
                pltpu.VMEM((rows, depth), BF16),
                pltpu.VMEM((heads, 3, rows, HD), BF16),
                pltpu.VMEM((3, depth, out_cols), BF16),
                pltpu.SemaphoreType.DMA((3,)),
            ],
        ),
        compiler_params=params(42),
        cost_estimate=cost(6 * rows * depth * out_cols, 6 * depth * out_cols),
        name="qkv",
    )(info, *blocks[0], *blocks[1], gain, cosine, sine, *weights)
    return result[:heads], result[heads]


def attention_kernel(first_ref, info_ref, *refs, chips, ring):
    own, other = refs[:chips], refs[chips : 2 * chips]
    outs = refs[2 * chips : 3 * chips]
    keys_all, values_all = refs[3 * chips :]
    chip, core = info_ref[ring + 1], info_ref[ring + 2]
    span = outs[0].shape[0]
    for f in range(chips):
        for source, side in ((own[f], core), (other[f], 1 - core)):
            block = 2 * (chip ^ f) + side
            keys_all[block] = source[1]
            values_all[block] = source[2].T

    def first_of(row):
        found = jnp.int32(0)
        for s in range(SERIES):
            edge = first_ref[s]
            found = jnp.where(edge <= row, jnp.maximum(found, edge), found)
        return found

    for f in range(chips):
        last = 2 * (chip ^ f) + core
        query = own[f][0]
        row = last * span + lax.broadcasted_iota(jnp.int32, (1, span), 1)
        start = jnp.zeros((1, span), jnp.int32)
        for s in range(SERIES):
            edge = first_ref[s]
            start = jnp.where(edge <= row, jnp.maximum(start, edge), start)
        lane = lax.broadcasted_iota(jnp.int32, (span, 1), 0)

        def body(at, carry, masked, query=query, row=row, start=start, lane=lane):
            peak, denom, accum = carry
            scores = dot_over(keys_all[at], query, (1, 1))
            if masked:
                column = lane + at * span
                allowed = (column >= start) & (column <= row)
                scores = jnp.where(allowed, scores, -1e30)
            new_peak = jnp.maximum(peak, jnp.max(scores, axis=0, keepdims=True))
            weights = jnp.exp2(scores - new_peak)
            if masked:
                weights = jnp.where(allowed, weights, 0.0)
            keep = jnp.exp2(peak - new_peak)
            denom = denom * keep + jnp.sum(weights, axis=0, keepdims=True)
            accum = accum * keep + dot(values_all[at], weights.astype(BF16))
            return new_peak, denom, accum

        def pair(turn, carry, query=query, full=None):
            peak, denom, accum = carry
            at = full + 2 * turn
            blocks = (at, at + 1)
            scores = [dot_over(keys_all[block], query, (1, 1)) for block in blocks]
            tops = [jnp.max(score, axis=0, keepdims=True) for score in scores]
            new_peak = jnp.maximum(peak, jnp.maximum(*tops))
            keep = jnp.exp2(peak - new_peak)
            denom, accum = denom * keep, accum * keep
            for block, score in zip(blocks, scores):
                weights = jnp.exp2(score - new_peak)
                denom += jnp.sum(weights, axis=0, keepdims=True)
                accum += dot(values_all[block], weights.astype(BF16))
            return new_peak, denom, accum

        begin = first_of(last * span) // span
        full = jnp.minimum(last, (first_of(last * span + span - 1) + span - 1) // span)
        carry = (
            jnp.full((1, span), -1e30, F32),
            jnp.zeros((1, span), F32),
            jnp.zeros((HD, span), F32),
        )
        carry = lax.fori_loop(begin, full, functools.partial(body, masked=True), carry)
        turns = (last - full) // 2
        carry = lax.fori_loop(0, turns, functools.partial(pair, full=full), carry)
        rest = full + 2 * turns
        carry = lax.fori_loop(rest, last, functools.partial(body, masked=False), carry)
        _, denom, accum = body(last, carry, masked=True)
        outs[f][...] = (accum / denom).T.astype(BF16)


def attention_call(first, info, own, other, ring):
    chips = len(own)
    _, rows, _ = own[0].shape
    return pl.pallas_call(
        functools.partial(attention_kernel, chips=chips, ring=ring),
        out_shape=[jax.ShapeDtypeStruct((rows, HD), BF16)] * chips,
        grid_spec=pltpu.PrefetchScalarGridSpec(
            num_scalar_prefetch=2,
            grid=(1,),
            in_specs=[whole((3, rows, HD))] * (2 * chips),
            out_specs=[whole((rows, HD))] * chips,
            scratch_shapes=[
                pltpu.VMEM((2 * chips, rows, HD), BF16),
                pltpu.VMEM((2 * chips, HD, rows), BF16),
            ],
        ),
        compiler_params=params(24),
        cost_estimate=cost(
            4 * chips * rows * chips * rows * HD,
            16 * chips * rows * HD,
            chips * rows * chips * rows,
        ),
        name="attention",
    )(first, info, *own, *other)


def middle_kernel(info_ref, *refs, ring, chips):
    parts = [refs[:ring], refs[ring : 2 * ring]]
    refs = refs[2 * ring :]
    tok_ref, w_own_ref = refs[:2]
    near_first, near_rest = refs[2 : 2 + chips], refs[2 + chips : 2 + 2 * chips]
    far_first, far_rest = refs[2 + 2 * chips], refs[3 + 2 * chips : 3 + 3 * chips]
    refs = refs[3 + 3 * chips :]
    gain_ref, gate_ref, up_ref, wp_ref, proj_ref, student_ref = refs[:6]
    hidden_ref, own_ref = refs[6:8]
    pieces = refs[8 : 8 + ring]
    attended, mixed, total, near, far, gates, ups, wp, proj, sems = refs[8 + ring :]
    step = pl.program_id(0)
    level, chip, core = info_ref[ring], info_ref[ring + 1], info_ref[ring + 2]
    rows, depth = mixed.shape
    width = own_ref.shape[1]
    blocks, _, wide = gates.shape

    used = iter(range(sems.shape[0]))
    copy = lambda source, target: pltpu.make_async_copy(source, target, sems.at[next(used)])
    heads = []
    for k in range(2):
        for s, part in enumerate(parts[k]):
            count = part.shape[0]
            for i in range(count):
                flip = level ^ info_ref[s]
                at = ((flip & 1) * 2 + (flip >> 1)) * width + (chip ^ (k * count + i)) * HD
                heads.append(copy(part.at[i], attended.at[:, pl.ds(pl.multiple_of(at, HD), HD)]))
    slices = [
        [
            copy(near_first[f], near.at[f, 0]),
            copy(near_rest[f], near.at[f, pl.ds(1, ring - 2)]),
            copy(far_first.at[f, 0], far.at[f, 0]),
            copy(far_rest[f], far.at[f, pl.ds(1, ring - 2)]),
        ]
        for f in range(chips)
    ]
    own_rows = pl.ds(pl.multiple_of(level * width, width), width)
    late = [copy(proj_ref.at[own_rows], proj), copy(student_ref, total)]
    columns = [pl.ds(i * wide, wide) for i in range(blocks)]
    units = [
        [
            copy(gate_ref.at[:, columns[i]], gates.at[i]),
            copy(up_ref.at[:, columns[i]], ups.at[i]),
            copy(wp_ref.at[columns[i]], wp.at[i]),
        ]
        for i in range(blocks)
    ]

    @pl.when(step == 0)
    def _():
        for c in heads + slices[0]:
            c.start()
        for c in sum(slices[1:], []) + late:
            c.start()
        for c in heads:
            c.wait()

    for f in range(chips):

        @pl.when(step == f)
        def _(f=f):
            for c in slices[f]:
                c.wait()
            for c in sum(units[f::chips], []):
                c.start()

    @pl.when(step < chips)
    def _():
        for gathered, side in ((near, core), (far, 1 - core)):
            here = pl.ds(pl.multiple_of(side * COLS, COLS), COLS)
            result = tok_ref[:, here].astype(F32) + dot(attended[:, :width], w_own_ref[:, here])
            weight = gathered[step].reshape(depth - width, COLS)
            result += dot(attended[:, width:], weight)
            at = pl.ds(pl.multiple_of((2 * (step ^ chip) + side) * COLS, COLS), COLS)
            mixed[:, at] = result.astype(BF16)

    @pl.when(step == chips)
    def _():
        for c in late:
            c.wait()
        values = mixed[...].astype(F32)
        attended[...] = (rms_scale(values) * gain_ref[...]).astype(BF16)
        own = mixed[:, pl.ds(pl.multiple_of(level * width, 128), width)]
        own_ref[...] = own
        total[...] -= dot(own, proj[...])

    for i in range(blocks):

        @pl.when(step == chips + i)
        def _(i=i):
            for c in units[i]:
                c.wait()

    @pl.when(step >= chips)
    def _():
        index = step - chips
        gate = dot(attended[...], gates[index])
        up = dot(attended[...], ups[index])
        hidden = (gate * jax.nn.sigmoid(gate) * up).astype(BF16)
        hidden_ref[...] = hidden
        total[...] -= dot(hidden, wp[index])

    @pl.when(step == pl.num_programs(0) - 1)
    def _():
        size = rows // ring
        for s in range(ring):
            at = pl.ds(pl.multiple_of(((level + s) & (ring - 1)) * size, size), size)
            pieces[s][...] = total[at, :].astype(BF16)


def middle_call(info, parts, tok, w_out, near, far, gain, w_gate, w_up, wp, projector, student):
    rows, depth = tok.shape
    ring, chips = len(parts[0]), len(near[0])
    units = w_gate.shape[1]
    wide = 2 * COLS
    width = depth // ring
    sd = projector.shape[1]
    blocks = units // wide
    tile = lambda j, info: (0, jnp.minimum(j, chips - 1) ^ info[ring + 1])
    late = lambda j, info: (0, jnp.maximum(j - chips, 0))
    anywhere = pl.BlockSpec(memory_space=pl.ANY)
    count = 2 * ring * parts[0][0].shape[0] + 4 * chips + 2 + 3 * blocks
    result = pl.pallas_call(
        functools.partial(middle_kernel, ring=ring, chips=chips),
        out_shape=[
            jax.ShapeDtypeStruct((rows, units), BF16),
            jax.ShapeDtypeStruct((rows, width), BF16),
        ]
        + [jax.ShapeDtypeStruct((rows // ring, sd), BF16)] * ring,
        grid_spec=pltpu.PrefetchScalarGridSpec(
            num_scalar_prefetch=1,
            grid=(chips + blocks,),
            in_specs=[anywhere] * (2 * ring)
            + [pl.BlockSpec((rows, wide), tile), pl.BlockSpec((width, wide), tile)]
            + [anywhere] * (3 * chips + 1)
            + [whole((1, depth))]
            + [anywhere] * 5,
            out_specs=[
                pl.BlockSpec((rows, wide), late),
                whole((rows, width)),
            ]
            + [whole((rows // ring, sd))] * ring,
            scratch_shapes=[
                pltpu.VMEM((rows, depth), BF16),
                pltpu.VMEM((rows, depth), BF16),
                pltpu.VMEM((rows, sd), F32),
                pltpu.VMEM((chips, ring - 1, width, COLS), BF16),
                pltpu.VMEM((chips, ring - 1, width, COLS), BF16),
                pltpu.VMEM((blocks, depth, wide), BF16),
                pltpu.VMEM((blocks, depth, wide), BF16),
                pltpu.VMEM((blocks, wide, sd), BF16),
                pltpu.VMEM((width, sd), BF16),
                pltpu.SemaphoreType.DMA((count,)),
            ],
        ),
        compiler_params=params(42),
        cost_estimate=cost(
            2 * rows * depth * (depth + 2 * units) + 2 * rows * sd * (units + width),
            2 * depth * (depth + 2 * units),
            rows * units,
        ),
        name="middle",
    )(
        info,
        *parts[0],
        *parts[1],
        tok,
        w_out,
        *near[0],
        *near[1],
        far[0],
        *far[1],
        gain,
        w_gate,
        w_up,
        wp,
        projector,
        student,
    )
    return result[0], result[1], result[2:]


def down_kernel(info_ref, hidden_ref, weight_ref, *outs):
    result = dot(hidden_ref[...], weight_ref[...]).astype(BF16)
    for j, out in enumerate(outs):

        @pl.when(pl.program_id(0) == j)
        def _(out=out):
            out[...] = result


def down_call(info, hidden, w_down, ring, first_flip, last_flip):
    rows, units = hidden.shape
    depth = w_down.shape[1]
    width = depth // ring
    count = first_flip - last_flip + 1
    return pl.pallas_call(
        down_kernel,
        out_shape=[jax.ShapeDtypeStruct((rows, width), BF16)] * count,
        grid_spec=pltpu.PrefetchScalarGridSpec(
            num_scalar_prefetch=1,
            grid=(count,),
            in_specs=[
                whole((rows, units)),
                pl.BlockSpec((units, width), lambda j, info: (0, info[ring] ^ (first_flip - j))),
            ],
            out_specs=[whole((rows, width))] * count,
        ),
        compiler_params=params(24),
        cost_estimate=cost(2 * rows * units * width * count, 2 * units * width * count),
        name="down",
    )(info, hidden, w_down)


def grads_kernel(info_ref, *refs, ring, chips):
    pieces = refs[:ring]
    normed_ref, hidden_ref, s_down_ref, up_ref, gate_ref = refs[ring : ring + 5]
    keep_ref, give_ref, scaled, grads = refs[ring + 5 :]
    chip, core = info_ref[ring + 1], info_ref[ring + 2]
    size, sd = pieces[0].shape
    for s in range(ring):
        scaled[pl.ds(pl.multiple_of(info_ref[s] * size, size), size), :] = pieces[s][...]
    value = scaled[...]
    wide = value.astype(F32)
    error = jnp.sum(wide * wide)
    grad_hidden = dot_over(value, s_down_ref[...], (1, 1))
    grads[0] = dot_over(normed_ref[...], (grad_hidden * gate_ref[...].astype(F32)).astype(BF16), (0, 0))
    grads[1] = dot_over(normed_ref[...], (grad_hidden * up_ref[...].astype(F32)).astype(BF16), (0, 0))
    grads[2] = dot_over(hidden_ref[...], value, (0, 0))
    share = grads.shape[1] // (2 * chips)
    for f in range(chips):
        for k in range(3):
            for part, ref in ((core, keep_ref), (1 - core, give_ref)):
                at = pl.multiple_of((part * chips + (chip ^ f)) * share, share)
                ref[f, k * share : (k + 1) * share] = grads[k, pl.ds(at, share), :].astype(
                    ref.dtype
                )
        for ref in (keep_ref, give_ref):
            ref[f, 3 * share :] = jnp.full((NOTE, sd), error, F32).astype(ref.dtype)


def grads_call(info, pieces, normed, hidden, s_down, up, gate, chips):
    ring = len(pieces)
    rows, sd = normed.shape
    units = hidden.shape[1]
    share = 3 * sd // (2 * chips) + NOTE
    operands = [*pieces, normed, hidden, s_down, up, gate]
    return pl.pallas_call(
        functools.partial(grads_kernel, ring=ring, chips=chips),
        out_shape=(
            jax.ShapeDtypeStruct((chips, share, units), F32),
            jax.ShapeDtypeStruct((chips, share, units), BF16),
        ),
        grid_spec=pltpu.PrefetchScalarGridSpec(
            num_scalar_prefetch=1,
            grid=(1,),
            in_specs=[whole(a.shape) for a in operands],
            out_specs=(whole((chips, share, units)), whole((chips, share, units))),
            scratch_shapes=[pltpu.VMEM((rows, sd), BF16), pltpu.VMEM((3, sd, units), F32)],
        ),
        compiler_params=params(22),
        cost_estimate=cost(8 * rows * sd * units, 20 * sd * units),
        name="grads",
    )(info, *operands)


def pair_kernel(keep_ref, theirs_ref, *outs):
    for f, out in enumerate(outs):
        out[...] = (keep_ref[f] + theirs_ref[f].astype(F32)).astype(out.dtype)


def pair_call(keep, theirs):
    chips, share, sd = keep.shape
    return pl.pallas_call(
        pair_kernel,
        out_shape=[jax.ShapeDtypeStruct((share, sd), BF16)] * chips,
        compiler_params=params(10),
        cost_estimate=cost(keep.size, 8 * keep.size),
        name="pair",
    )(keep, theirs)


def finish_kernel(info_ref, *refs, chips, ring):
    mine, others = refs[:chips], refs[chips : 2 * chips]
    outs = refs[2 * chips : 2 * chips + 3]
    notes = refs[2 * chips + 3]
    chip, core = info_ref[ring + 1], info_ref[ring + 2]
    share = (mine[0].shape[0] - NOTE) // 3
    for f in range(chips):
        for part, ref in ((core, mine[f]), (1 - core, others[f])):
            index = part * chips + (chip ^ f)
            at = pl.ds(pl.multiple_of(index * share, share), share)
            for k in range(3):
                outs[k][at, :] = ref[k * share : (k + 1) * share].astype(F32)
            notes[index] = ref[3 * share :, :HD].astype(F32)


def finish_call(info, mine, others, ring):
    chips = len(mine)
    share, sd = mine[0].shape
    rows = (share - NOTE) // 3 * 2 * chips
    return pl.pallas_call(
        functools.partial(finish_kernel, chips=chips, ring=ring),
        out_shape=[jax.ShapeDtypeStruct((rows, sd), F32)] * 3
        + [jax.ShapeDtypeStruct((2 * chips, NOTE, HD), F32)],
        grid_spec=pltpu.PrefetchScalarGridSpec(
            num_scalar_prefetch=1,
            grid=(1,),
            in_specs=[whole((share, sd))] * (2 * chips),
            out_specs=[whole((rows, sd))] * 3 + [whole((2 * chips, NOTE, HD))],
        ),
        compiler_params=params(14),
        cost_estimate=cost(rows * sd, 12 * rows * sd),
        name="finish",
    )(info, *mine, *others)


def step_on(block, axis):
    size = lax.axis_size(axis)
    return lax.ppermute(block, axis, [(i, (i + 1) % size) for i in range(size)])


def ring_gather(block, axis, steps=None):
    blocks = [block]
    for _ in range(lax.axis_size(axis) - 1 if steps is None else steps):
        blocks.append(step_on(blocks[-1], axis))
    return blocks


def shifted(pieces, axis):
    size = lax.axis_size(axis)
    moved = [
        lax.ppermute(pieces[s], axis, [(i, (i + s) % size) for i in range(size)])
        for s in range(1, size)
    ]
    return [pieces[0], *moved]


def flipped(pieces):
    size = lax.axis_size("dp")
    moved = [
        lax.ppermute(pieces[f], "dp", [(i, i ^ (2 * f)) for i in range(size)])
        for f in range(1, len(pieces))
    ]
    return [pieces[0], *moved]


def swapped(value):
    size = lax.axis_size("dp")
    return lax.ppermute(value, "dp", [(i, i ^ 1) for i in range(size)])


def after(value, *others):
    return lax.optimization_barrier((value, *others))[0]


def paired(
    tokens,
    series_ids,
    offsets,
    norm_gain,
    mlp_gain,
    w_query,
    w_key,
    w_value,
    w_out,
    w_gate,
    w_up,
    w_down,
    projector,
    student_in,
    s_gate,
    s_up,
    s_down,
):
    rows = tokens.shape[0]
    depth, sd = w_query.shape[0], student_in.shape[1]
    dp, ring = lax.axis_size("dp"), lax.axis_size("tensor")
    here, level = lax.axis_index("dp"), lax.axis_index("tensor")
    chips, half = dp // 2, rows // 2
    total_rows = rows * dp
    size = rows // ring
    slice_cols = depth // dp

    places = [(level - s) & (ring - 1) for s in range(ring)] + [level, here >> 1, here & 1]
    slots = lax.broadcasted_iota(jnp.int32, (16,), 0)
    info = sum(jnp.where(slots == k, place, 0) for k, place in enumerate(places))
    starts = [level * size, here * slice_cols]
    *starts, zero = [jnp.asarray(start, jnp.uint32) for start in (*starts, 0)]
    tokens, info, *starts = lax.optimization_barrier((tokens, info, *starts))

    token_rings = [ring_gather(tokens[k : k + half], "tensor") for k in (0, half)]

    angles = offsets.astype(F32)[:, None] * frequencies(HD)[None, :]
    cosine, sine = jnp.cos(angles), jnp.sin(angles)
    cosine = jnp.concatenate([cosine, cosine], axis=1)
    sine = jnp.concatenate([-sine, sine], axis=1)
    student_full = student_in.astype(F32)
    student_normed = rms_scale(student_full).astype(BF16)
    below = jnp.sum(
        series_ids[None, :] < jnp.arange(SERIES, dtype=jnp.int32)[:, None], axis=1, dtype=jnp.int32
    )

    made, tok_full = qkv_call(
        info, token_rings, norm_gain[None, :], cosine, sine, w_query, w_key, w_value
    )

    student_normed, projected, tok_full = lax.optimization_barrier(
        (student_normed, projector, tok_full)
    )
    s_gate_out = dot(student_normed, s_gate)
    s_up_out = dot(student_normed, s_up)
    sigmoid_gate = jax.nn.sigmoid(s_gate_out)
    up_slope = s_gate_out * sigmoid_gate
    gate_slope = s_up_out * sigmoid_gate * (1.0 + s_gate_out * (1.0 - sigmoid_gate))
    s_hidden = (up_slope * s_up_out).astype(BF16)
    up_slope, gate_slope = up_slope.astype(BF16), gate_slope.astype(BF16)
    student_part = dot(s_hidden, s_down)
    projected = dot(w_down, projected).astype(BF16)
    student_own = lax.dynamic_slice(student_full, [starts[0], zero], (size, sd))
    early = (projected, student_part, s_hidden, up_slope, gate_slope, student_normed, student_own)

    over = lambda value, bit: lax.ppermute(value, "tensor", [(i, i ^ bit) for i in range(ring)])
    w_slice = lax.dynamic_slice(w_out, [zero, starts[1]], (w_out.shape[0], slice_cols))
    w_slice, tok_full, _ = lax.optimization_barrier((w_slice, tok_full, s_gate_out))
    w_first = over(w_slice, 2)

    own = flipped(made)
    *own, w_first = lax.optimization_barrier((*own, w_first, *early))[: chips + 1]
    w_rest = over(jnp.stack([w_slice, w_first]), 1)
    other = [swapped(a) for a in own]
    near_first = flipped([w_first] * chips)
    made = attention_call(below, info, own, other, ring)
    *made, w_rest = lax.optimization_barrier((*made, w_rest, *near_first))[: chips + 1]
    attended = lax.optimization_barrier(tuple(flipped(made)))
    parts = [
        ring_gather(jnp.stack(attended[k : k + chips // 2]), "tensor") for k in (0, chips // 2)
    ]
    w_rest = after(w_rest, *attended)
    near_rest = flipped([w_rest] * chips)
    far_first = swapped(after(jnp.stack(near_first)[:, None], *attended))
    far_rest = [swapped(after(a, parts[1][1])) for a in near_rest]

    hidden, mixed_own, pieces = middle_call(
        info,
        parts,
        tok_full,
        w_out,
        (near_first, near_rest),
        (far_first, far_rest),
        mlp_gain[None, :],
        w_gate,
        w_up,
        projected,
        projector,
        student_part,
    )

    far_sum = over(down_call(info, hidden, w_down, ring, 3, 3)[0], 1)
    far_mine, near_theirs, kept = down_call(info, hidden, w_down, ring, 2, 0)

    moved = lax.optimization_barrier((*shifted(pieces, "tensor"), kept))[:ring]
    difference = student_own + sum(piece.astype(F32) for piece in moved)
    own = (difference * total_rows ** (-0.5)).astype(BF16)
    scaled = shifted([own] * ring, "tensor")

    keep, give = grads_call(
        after(info, far_sum),
        scaled,
        student_normed,
        s_hidden,
        s_down,
        up_slope,
        gate_slope,
        chips,
    )
    shares = pair_call(keep, swapped(give))
    far_sum = (far_sum.astype(F32) + far_mine.astype(F32)).astype(BF16)
    shares = flipped(shares)
    own = sum(share.astype(F32) for share in shares).astype(BF16)
    mine = flipped([own] * chips)
    others = [swapped(share) for share in mine]

    level_sums = [over(after(near_theirs, far_sum), 1), over(far_sum, 2)]
    mlp_own = sum(after(value, mine[-1]).astype(F32) for value in level_sums)
    teacher_out = (mixed_own.astype(F32) + (kept.astype(F32) + mlp_own)).astype(BF16)
    grad_gate, grad_up, grad_down, notes = finish_call(info, mine, others, ring)
    return teacher_out, grad_gate, grad_up, grad_down, notes[0, 0, 0] / sd


def local(*args):
    rows, w_query, s_gate = args[0].shape[0], args[5], args[14]
    dp, ring = lax.axis_size("dp"), lax.axis_size("tensor")
    heads = w_query.shape[1] // HD
    fits = (
        dp == 2 * heads
        and heads > 1
        and ring == 4
        and heads & (heads - 1) == 0
        and w_query.shape[0] == dp * COLS
        and s_gate.shape[0] == s_gate.shape[1]
        and rows % (32 * ring) == 0
    )
    return paired(*args) if fits else general(*args)


def solution(mesh):
    in_specs = (
        P("dp", "tensor"),
        P(),
        P("dp"),
        P(),
        P(),
        P(None, "tensor"),
        P(None, "tensor"),
        P(None, "tensor"),
        P("tensor", None),
        P(None, "tensor"),
        P(None, "tensor"),
        P("tensor", None),
        P(),
        P("dp", None),
        P(None, "tensor"),
        P(None, "tensor"),
        P("tensor", None),
    )
    out_specs = (P("dp", "tensor"), P(None, "tensor"), P(None, "tensor"), P("tensor", None), P())
    return jax.shard_map(local, mesh=mesh, in_specs=in_specs, out_specs=out_specs, check_vma=False)
```

```python
import functools
import math

import jax
import jax.numpy as jnp
from jax import lax
from jax.experimental import pallas as pl
from jax.experimental.pallas import tpu as pltpu
from jax.sharding import PartitionSpec as P

HD = 128
COLS = 256
NOTE = 16
SERIES = 8
F32 = jnp.float32
BF16 = jnp.bfloat16
MIB = 1024 * 1024


def rms_scale(values):
    return values * lax.rsqrt(jnp.mean(values * values, axis=-1, keepdims=True) + 1e-05)


def frequencies(head_dim):
    indices = jnp.arange(head_dim // 2).astype(jnp.float32)
    return jnp.exp(-jnp.log(500000.0) * 2.0 * indices / head_dim)


def rotary(inputs, angles):
    half_dim = inputs.shape[-1] // 2
    cosine = jnp.cos(angles)
    sine = jnp.sin(angles)
    first_half = inputs[..., :half_dim]
    second_half = inputs[..., half_dim:]
    return jnp.concatenate(
        [first_half * cosine - second_half * sine, first_half * sine + second_half * cosine],
        axis=-1,
    )


def general(
    tokens,
    series_ids,
    offsets,
    norm_gain,
    mlp_gain,
    w_query,
    w_key,
    w_value,
    w_out,
    w_gate,
    w_up,
    w_down,
    projector,
    student_in,
    s_gate,
    s_up,
    s_down,
):
    row_count = tokens.shape[0]
    heads_dev = w_query.shape[1] // HD
    first_row = lax.axis_index("dp") * row_count
    tokens_full = lax.all_gather(tokens, "tensor", axis=1, tiled=True).astype(jnp.float32)
    normed = (rms_scale(tokens_full) * norm_gain).astype(jnp.bfloat16)
    angles = offsets.astype(jnp.float32)[:, None, None] * frequencies(HD)[None, None, :]
    queries = rotary(
        jnp.dot(normed, w_query, preferred_element_type=jnp.float32).reshape(
            row_count, heads_dev, HD
        ),
        angles,
    ).astype(jnp.bfloat16)
    keys_rot = rotary(
        jnp.dot(normed, w_key, preferred_element_type=jnp.float32).reshape(
            row_count, heads_dev, HD
        ),
        angles,
    ).astype(jnp.bfloat16)
    values_mine = jnp.dot(normed, w_value, preferred_element_type=jnp.float32).astype(jnp.bfloat16)
    keys_flat = keys_rot.reshape(row_count, heads_dev * HD)
    query_pos = first_row + jnp.arange(row_count, dtype=jnp.int32)
    query_series = lax.dynamic_slice_in_dim(series_ids, first_row, row_count, 0)
    factor = HD ** (-0.5)
    peak = jnp.full((row_count, heads_dev), -1e30, jnp.float32)
    key_block = lax.all_gather(keys_flat, "dp", axis=0, tiled=True)
    value_block = lax.all_gather(values_mine, "dp", axis=0, tiled=True)
    count = key_block.shape[0]
    key_pos = jnp.arange(count, dtype=jnp.int32)
    allowed = (
        (key_pos[None, :] >= 0)
        & (key_pos[None, :] <= query_pos[:, None])
        & (series_ids[None, :] == query_series[:, None])
    )
    scores = (
        jnp.einsum(
            "qhd,khd->qhk",
            queries,
            key_block.reshape(count, heads_dev, HD),
            preferred_element_type=jnp.float32,
        )
        * factor
    )
    scores = jnp.where(allowed[:, None, :], scores, -1e30)
    new_peak = jnp.maximum(peak, jnp.max(scores, axis=2))
    weights = jnp.where(allowed[:, None, :], jnp.exp(scores - new_peak[:, :, None]), 0.0)
    denom = jnp.sum(weights, axis=2)
    accum = jnp.einsum(
        "qhk,khd->qhd",
        weights.astype(jnp.bfloat16),
        value_block.reshape(count, heads_dev, HD),
        preferred_element_type=jnp.float32,
    )
    peak, denom, accum = (new_peak, denom, accum)
    attended = (accum / denom[:, :, None]).astype(jnp.bfloat16).reshape(row_count, heads_dev * HD)
    partial_out = jnp.dot(attended, w_out, preferred_element_type=jnp.float32)
    own_sum = lax.psum_scatter(
        partial_out.astype(jnp.bfloat16), "tensor", scatter_dimension=1, tiled=True
    ).astype(jnp.float32)
    mixed_own = (tokens.astype(jnp.float32) + own_sum).astype(jnp.bfloat16)
    mixed = lax.all_gather(mixed_own, "tensor", axis=1, tiled=True)
    normed_two = (rms_scale(mixed.astype(jnp.float32)) * mlp_gain).astype(jnp.bfloat16)
    gate_out = jnp.dot(normed_two, w_gate, preferred_element_type=jnp.float32)
    up_out = jnp.dot(normed_two, w_up, preferred_element_type=jnp.float32)
    hidden = (jax.nn.silu(gate_out) * up_out).astype(jnp.bfloat16)
    mlp_part = jnp.dot(hidden, w_down, preferred_element_type=jnp.float32)
    mlp_own = lax.psum_scatter(
        mlp_part.astype(jnp.bfloat16), "tensor", scatter_dimension=1, tiled=True
    ).astype(jnp.float32)
    teacher_out = (mixed_own.astype(jnp.float32) + mlp_own).astype(jnp.bfloat16)
    student_full = student_in.astype(jnp.float32)
    student_normed = rms_scale(student_full).astype(jnp.bfloat16)
    s_gate_out = jnp.dot(student_normed, s_gate, preferred_element_type=jnp.float32)
    s_up_out = jnp.dot(student_normed, s_up, preferred_element_type=jnp.float32)
    sigmoid_gate = jax.nn.sigmoid(s_gate_out)
    s_hidden = (s_gate_out * sigmoid_gate * s_up_out).astype(jnp.bfloat16)
    student_part = jnp.dot(s_hidden, s_down, preferred_element_type=jnp.float32)
    teacher_full = lax.all_gather(teacher_out, "tensor", axis=1, tiled=True)
    target = jnp.dot(teacher_full, projector, preferred_element_type=jnp.float32)
    student_summed = lax.psum(student_part.astype(jnp.bfloat16), "tensor").astype(jnp.float32)
    difference = student_full + student_summed - target
    total_rows = row_count * lax.axis_size("dp")
    scaled = (difference * total_rows ** (-0.5)).astype(jnp.bfloat16)
    grad_down_part = jnp.einsum("rk,rc->kc", s_hidden, scaled, preferred_element_type=jnp.float32)
    grad_hidden = jnp.einsum("rc,kc->rk", scaled, s_down, preferred_element_type=jnp.float32)
    grad_up_in = (grad_hidden * s_gate_out * sigmoid_gate).astype(jnp.bfloat16)
    grad_gate_in = (
        grad_hidden * s_up_out * sigmoid_gate * (1.0 + s_gate_out * (1.0 - sigmoid_gate))
    ).astype(jnp.bfloat16)
    grad_gate_part = jnp.einsum(
        "rc,rk->ck", student_normed, grad_gate_in, preferred_element_type=jnp.float32
    )
    grad_up_part = jnp.einsum(
        "rc,rk->ck", student_normed, grad_up_in, preferred_element_type=jnp.float32
    )
    square_sum = jnp.sum(difference * difference)
    grad_gate, grad_up, grad_down, square_total = (
        lax.psum(grad_gate_part.astype(jnp.bfloat16), "dp").astype(jnp.float32),
        lax.psum(grad_up_part.astype(jnp.bfloat16), "dp").astype(jnp.float32),
        lax.psum(grad_down_part.astype(jnp.bfloat16), "dp").astype(jnp.float32),
        lax.psum(square_sum.astype(jnp.bfloat16), "dp").astype(jnp.float32),
    )
    error = square_total / (total_rows * difference.shape[1])
    return (teacher_out, grad_gate, grad_up, grad_down, error)


def dot(a, b):
    return jnp.dot(a, b, preferred_element_type=F32)


def dot_over(a, b, dims):
    return lax.dot_general(a, b, ((dims[:1], dims[1:]), ((), ())), preferred_element_type=F32)


def params(limit):
    return pltpu.CompilerParams(vmem_limit_bytes=limit * MIB)


def whole(shape):
    return pl.BlockSpec(shape, lambda *_: (0,) * len(shape))


def cost(flops, moved, transcendentals=0):
    return pl.CostEstimate(
        flops=int(flops), bytes_accessed=int(moved), transcendentals=int(transcendentals)
    )


def qkv_kernel(info_ref, *refs, ring, heads, factor):
    blocks = [refs[:ring], refs[ring : 2 * ring]]
    gain_ref, cos_ref, sin_ref, *sources = refs[2 * ring : 2 * ring + 6]
    outs = refs[2 * ring + 6 : 2 * ring + 6 + heads]
    tok_ref, stamp_ref, normed, made, weights, sems = refs[2 * ring + 6 + heads :]
    half, width = blocks[0][0].shape
    depth = gain_ref.shape[1]
    copies = [
        pltpu.make_async_copy(source, weights.at[k], sems.at[k])
        for k, source in enumerate(sources)
    ]
    for copy in copies:
        copy.start()
    for k in range(2):
        mine = slice(k * half, (k + 1) * half)
        total = jnp.zeros((half, 1), F32)
        for block in blocks[k]:
            part = block[...].astype(F32)
            total += jnp.sum(part * part, axis=1, keepdims=True)
        scale = lax.rsqrt(total / depth + 1e-05)
        for s, block in enumerate(blocks[k]):
            at = pl.ds(pl.multiple_of(info_ref[s] * width, 128), width)
            part = block[...]
            tok_ref[mine, at] = part
            normed[mine, at] = (part.astype(F32) * scale * gain_ref[:, at]).astype(BF16)
    for kind, copy in enumerate(copies):
        copy.wait()
        result = dot(normed[...], weights[kind])
        for h in range(heads):
            head = result[:, h * HD : (h + 1) * HD]
            if kind < 2:
                head = head * cos_ref[...] + pltpu.roll(head, HD // 2, 1) * sin_ref[...]
            if kind == 0:
                head = head * factor
            made[h, kind] = head.astype(BF16)
    for f in range(heads):
        outs[f][...] = made[info_ref[ring + 1] ^ f]
    stamp_ref[...] = jnp.zeros_like(stamp_ref)


def qkv_call(info, blocks, gain, cosine, sine, *weights):
    half, width = blocks[0][0].shape
    rows, ring = 2 * half, len(blocks[0])
    depth, out_cols = weights[0].shape
    heads = out_cols // HD
    result = pl.pallas_call(
        functools.partial(
            qkv_kernel, ring=ring, heads=heads, factor=HD ** (-0.5) * math.log2(math.e)
        ),
        out_shape=[jax.ShapeDtypeStruct((3, rows, HD), BF16)] * heads
        + [jax.ShapeDtypeStruct((rows, depth), BF16), jax.ShapeDtypeStruct((8, HD), F32)],
        grid_spec=pltpu.PrefetchScalarGridSpec(
            num_scalar_prefetch=1,
            grid=(1,),
            in_specs=[whole((half, width))] * (2 * ring)
            + [whole((1, depth)), whole((rows, HD)), whole((rows, HD))]
            + [pl.BlockSpec(memory_space=pl.ANY)] * 3,
            out_specs=[whole((3, rows, HD))] * heads + [whole((rows, depth)), whole((8, HD))],
            scratch_shapes=[
                pltpu.VMEM((rows, depth), BF16),
                pltpu.VMEM((heads, 3, rows, HD), BF16),
                pltpu.VMEM((3, depth, out_cols), BF16),
                pltpu.SemaphoreType.DMA((3,)),
            ],
        ),
        compiler_params=params(42),
        cost_estimate=cost(6 * rows * depth * out_cols, 6 * depth * out_cols),
        name="qkv",
    )(info, *blocks[0], *blocks[1], gain, cosine, sine, *weights)
    return result[:heads], result[heads], result[heads + 1]


def attention_kernel(first_ref, info_ref, *refs, chips, ring):
    own, other = refs[:chips], refs[chips : 2 * chips]
    outs = refs[2 * chips + 1 : 3 * chips + 1]
    keys_all, values_all = refs[3 * chips + 1 :]
    chip, core = info_ref[ring + 1], info_ref[ring + 2]
    span = outs[0].shape[0]
    for f in range(chips):
        for source, side in ((own[f], core), (other[f], 1 - core)):
            block = 2 * (chip ^ f) + side
            keys_all[block] = source[1]
            values_all[block] = source[2].T

    def first_of(row):
        found = jnp.int32(0)
        for s in range(SERIES):
            edge = first_ref[s]
            found = jnp.where(edge <= row, jnp.maximum(found, edge), found)
        return found

    for f in range(chips):
        last = 2 * (chip ^ f) + core
        query = own[f][0]
        row = last * span + lax.broadcasted_iota(jnp.int32, (1, span), 1)
        start = jnp.zeros((1, span), jnp.int32)
        for s in range(SERIES):
            edge = first_ref[s]
            start = jnp.where(edge <= row, jnp.maximum(start, edge), start)
        lane = lax.broadcasted_iota(jnp.int32, (span, 1), 0)

        def body(at, carry, masked, query=query, row=row, start=start, lane=lane):
            peak, denom, accum = carry
            count = lane.shape[0]
            scores = dot_over(keys_all[at, :count], query, (1, 1))
            if masked:
                column = lane + at * span
                allowed = (column >= start) & (column <= row)
                scores = jnp.where(allowed, scores, -1e30)
            new_peak = jnp.maximum(peak, jnp.max(scores, axis=0, keepdims=True))
            weights = jnp.exp2(scores - new_peak)
            if masked:
                weights = jnp.where(allowed, weights, 0.0)
            keep = jnp.exp2(peak - new_peak)
            denom = denom * keep + jnp.sum(weights, axis=0, keepdims=True)
            accum = accum * keep + dot(values_all[at, :, :count], weights.astype(BF16))
            return new_peak, denom, accum

        def pair(turn, carry, query=query, full=None):
            peak, denom, accum = carry
            at = full + 2 * turn
            blocks = (at, at + 1)
            scores = [dot_over(keys_all[block], query, (1, 1)) for block in blocks]
            tops = [jnp.max(score, axis=0, keepdims=True) for score in scores]
            new_peak = jnp.maximum(peak, jnp.maximum(*tops))
            keep = jnp.exp2(peak - new_peak)
            denom, accum = denom * keep, accum * keep
            for block, score in zip(blocks, scores):
                weights = jnp.exp2(score - new_peak)
                denom += jnp.sum(weights, axis=0, keepdims=True)
                accum += dot(values_all[block], weights.astype(BF16))
            return new_peak, denom, accum

        begin = first_of(last * span) // span
        full = jnp.minimum(last, (first_of(last * span + span - 1) + span - 1) // span)
        carry = (
            jnp.full((1, span), -1e30, F32),
            jnp.zeros((1, span), F32),
            jnp.zeros((HD, span), F32),
        )
        carry = lax.fori_loop(begin, full, functools.partial(body, masked=True), carry)
        turns = (last - full) // 2
        carry = lax.fori_loop(0, turns, functools.partial(pair, full=full), carry)
        rest = full + 2 * turns
        carry = lax.fori_loop(rest, last, functools.partial(body, masked=False), carry)
        half = span // 2
        for at in (slice(0, half), slice(half, span)):
            part = tuple(value[:, at] for value in carry)
            _, denom, accum = body(
                last, part, True, query[at], row[:, at], start[:, at], lane[: at.stop]
            )
            outs[f][at] = (accum / denom).T.astype(BF16)


def attention_call(first, info, own, other, stamp, ring):
    chips = len(own)
    _, rows, _ = own[0].shape
    return pl.pallas_call(
        functools.partial(attention_kernel, chips=chips, ring=ring),
        out_shape=[jax.ShapeDtypeStruct((rows, HD), BF16)] * chips,
        grid_spec=pltpu.PrefetchScalarGridSpec(
            num_scalar_prefetch=2,
            grid=(1,),
            in_specs=[whole((3, rows, HD))] * (2 * chips) + [whole(stamp.shape)],
            out_specs=[whole((rows, HD))] * chips,
            scratch_shapes=[
                pltpu.VMEM((2 * chips, rows, HD), BF16),
                pltpu.VMEM((2 * chips, HD, rows), BF16),
            ],
        ),
        compiler_params=params(24),
        cost_estimate=cost(
            4 * chips * rows * chips * rows * HD,
            16 * chips * rows * HD,
            chips * rows * chips * rows,
        ),
        name="attention",
    )(first, info, *own, *other, stamp)


def middle_kernel(info_ref, *refs, ring, chips):
    parts = [refs[:ring], refs[ring : 2 * ring]]
    refs = refs[2 * ring :]
    tok_ref, w_own_ref = refs[:2]
    near_first, near_rest = refs[2 : 2 + chips], refs[2 + chips : 2 + 2 * chips]
    far_first, far_rest = refs[2 + 2 * chips], refs[3 + 2 * chips : 3 + 3 * chips]
    refs = refs[3 + 3 * chips :]
    gain_ref, gate_ref, up_ref, wp_ref, proj_ref, student_ref = refs[:6]
    hidden_ref, own_ref = refs[6:8]
    pieces = refs[8 : 8 + ring]
    attended, mixed, total, near, far, gates, ups, wp, proj, sems = refs[8 + ring :]
    step = pl.program_id(0)
    level, chip, core = info_ref[ring], info_ref[ring + 1], info_ref[ring + 2]
    rows, depth = mixed.shape
    width = own_ref.shape[1]
    blocks, _, wide = gates.shape

    used = iter(range(sems.shape[0]))
    copy = lambda source, target: pltpu.make_async_copy(source, target, sems.at[next(used)])
    heads = []
    for k in range(2):
        for s, part in enumerate(parts[k]):
            count = part.shape[0]
            for i in range(count):
                flip = level ^ info_ref[s]
                at = ((flip & 1) * 2 + (flip >> 1)) * width + (chip ^ (k * count + i)) * HD
                heads.append(copy(part.at[i], attended.at[:, pl.ds(pl.multiple_of(at, HD), HD)]))
    slices = [
        [
            copy(near_first[f], near.at[f, 0]),
            copy(near_rest[f], near.at[f, pl.ds(1, ring - 2)]),
            copy(far_first.at[f, 0], far.at[f, 0]),
            copy(far_rest[f], far.at[f, pl.ds(1, ring - 2)]),
        ]
        for f in range(chips)
    ]
    own_rows = pl.ds(pl.multiple_of(level * width, width), width)
    late = [copy(proj_ref.at[own_rows], proj), copy(student_ref, total)]
    columns = [pl.ds(i * wide, wide) for i in range(blocks)]
    units = [
        [
            copy(gate_ref.at[:, columns[i]], gates.at[i]),
            copy(up_ref.at[:, columns[i]], ups.at[i]),
            copy(wp_ref.at[columns[i]], wp.at[i]),
        ]
        for i in range(blocks)
    ]

    @pl.when(step == 0)
    def _():
        for c in heads + slices[0]:
            c.start()
        for c in sum(slices[1:], []) + late:
            c.start()
        for c in heads:
            c.wait()

    for f in range(chips):

        @pl.when(step == f)
        def _(f=f):
            for c in slices[f]:
                c.wait()
            for c in sum(units[f::chips], []):
                c.start()

    @pl.when(step < chips)
    def _():
        for gathered, side in ((near, core), (far, 1 - core)):
            here = pl.ds(pl.multiple_of(side * COLS, COLS), COLS)
            result = tok_ref[:, here].astype(F32) + dot(attended[:, :width], w_own_ref[:, here])
            weight = gathered[step].reshape(depth - width, COLS)
            result += dot(attended[:, width:], weight)
            at = pl.ds(pl.multiple_of((2 * (step ^ chip) + side) * COLS, COLS), COLS)
            mixed[:, at] = result.astype(BF16)

    @pl.when(step == chips)
    def _():
        for c in late:
            c.wait()
        values = mixed[...].astype(F32)
        attended[...] = (rms_scale(values) * gain_ref[...]).astype(BF16)
        own = mixed[:, pl.ds(pl.multiple_of(level * width, 128), width)]
        own_ref[...] = own
        total[...] -= dot(own, proj[...])

    for i in range(blocks):

        @pl.when(step == chips + i)
        def _(i=i):
            for c in units[i]:
                c.wait()

    @pl.when(step >= chips)
    def _():
        index = step - chips
        gate = dot(attended[...], gates[index])
        up = dot(attended[...], ups[index])
        hidden = (gate * jax.nn.sigmoid(gate) * up).astype(BF16)
        hidden_ref[...] = hidden
        total[...] -= dot(hidden, wp[index])

    @pl.when(step == pl.num_programs(0) - 1)
    def _():
        size = rows // ring
        for s in range(ring):
            at = pl.ds(pl.multiple_of(((level + s) & (ring - 1)) * size, size), size)
            pieces[s][...] = total[at, :].astype(BF16)


def middle_call(info, parts, tok, w_out, near, far, gain, w_gate, w_up, wp, projector, student):
    rows, depth = tok.shape
    ring, chips = len(parts[0]), len(near[0])
    units = w_gate.shape[1]
    wide = 2 * COLS
    width = depth // ring
    sd = projector.shape[1]
    blocks = units // wide
    tile = lambda j, info: (0, jnp.minimum(j, chips - 1) ^ info[ring + 1])
    late = lambda j, info: (0, jnp.maximum(j - chips, 0))
    anywhere = pl.BlockSpec(memory_space=pl.ANY)
    count = 2 * ring * parts[0][0].shape[0] + 4 * chips + 2 + 3 * blocks
    result = pl.pallas_call(
        functools.partial(middle_kernel, ring=ring, chips=chips),
        out_shape=[
            jax.ShapeDtypeStruct((rows, units), BF16),
            jax.ShapeDtypeStruct((rows, width), BF16),
        ]
        + [jax.ShapeDtypeStruct((rows // ring, sd), BF16)] * ring,
        grid_spec=pltpu.PrefetchScalarGridSpec(
            num_scalar_prefetch=1,
            grid=(chips + blocks,),
            in_specs=[anywhere] * (2 * ring)
            + [pl.BlockSpec((rows, wide), tile), pl.BlockSpec((width, wide), tile)]
            + [anywhere] * (3 * chips + 1)
            + [whole((1, depth))]
            + [anywhere] * 5,
            out_specs=[
                pl.BlockSpec((rows, wide), late),
                whole((rows, width)),
            ]
            + [whole((rows // ring, sd))] * ring,
            scratch_shapes=[
                pltpu.VMEM((rows, depth), BF16),
                pltpu.VMEM((rows, depth), BF16),
                pltpu.VMEM((rows, sd), F32),
                pltpu.VMEM((chips, ring - 1, width, COLS), BF16),
                pltpu.VMEM((chips, ring - 1, width, COLS), BF16),
                pltpu.VMEM((blocks, depth, wide), BF16),
                pltpu.VMEM((blocks, depth, wide), BF16),
                pltpu.VMEM((blocks, wide, sd), BF16),
                pltpu.VMEM((width, sd), BF16),
                pltpu.SemaphoreType.DMA((count,)),
            ],
        ),
        compiler_params=params(42),
        cost_estimate=cost(
            2 * rows * depth * (depth + 2 * units) + 2 * rows * sd * (units + width),
            2 * depth * (depth + 2 * units),
            rows * units,
        ),
        name="middle",
    )(
        info,
        *parts[0],
        *parts[1],
        tok,
        w_out,
        *near[0],
        *near[1],
        far[0],
        *far[1],
        gain,
        w_gate,
        w_up,
        wp,
        projector,
        student,
    )
    return result[0], result[1], result[2:]


def down_kernel(info_ref, hidden_ref, weight_ref, *outs):
    result = dot(hidden_ref[...], weight_ref[...]).astype(BF16)
    for j, out in enumerate(outs):

        @pl.when(pl.program_id(0) == j)
        def _(out=out):
            out[...] = result


def down_call(info, hidden, w_down, ring, first_flip, last_flip):
    rows, units = hidden.shape
    depth = w_down.shape[1]
    width = depth // ring
    count = first_flip - last_flip + 1
    return pl.pallas_call(
        down_kernel,
        out_shape=[jax.ShapeDtypeStruct((rows, width), BF16)] * count,
        grid_spec=pltpu.PrefetchScalarGridSpec(
            num_scalar_prefetch=1,
            grid=(count,),
            in_specs=[
                whole((rows, units)),
                pl.BlockSpec((units, width), lambda j, info: (0, info[ring] ^ (first_flip - j))),
            ],
            out_specs=[whole((rows, width))] * count,
        ),
        compiler_params=params(24),
        cost_estimate=cost(2 * rows * units * width * count, 2 * units * width * count),
        name="down",
    )(info, hidden, w_down)


def grads_kernel(info_ref, *refs, ring, chips):
    pieces = refs[:ring]
    normed_ref, hidden_ref, s_down_ref, up_ref, gate_ref = refs[ring : ring + 5]
    keep_ref, give_ref, scaled, grads = refs[ring + 5 :]
    chip, core = info_ref[ring + 1], info_ref[ring + 2]
    size, sd = pieces[0].shape
    for s in range(ring):
        scaled[pl.ds(pl.multiple_of(info_ref[s] * size, size), size), :] = pieces[s][...]
    value = scaled[...]
    wide = value.astype(F32)
    error = jnp.sum(wide * wide)
    grad_hidden = dot_over(value, s_down_ref[...], (1, 1))
    grads[0] = dot_over(normed_ref[...], (grad_hidden * gate_ref[...].astype(F32)).astype(BF16), (0, 0))
    grads[1] = dot_over(normed_ref[...], (grad_hidden * up_ref[...].astype(F32)).astype(BF16), (0, 0))
    grads[2] = dot_over(hidden_ref[...], value, (0, 0))
    share = grads.shape[1] // (2 * chips)
    for f in range(chips):
        for k in range(3):
            for part, ref in ((core, keep_ref), (1 - core, give_ref)):
                at = pl.multiple_of((part * chips + (chip ^ f)) * share, share)
                ref[f, k * share : (k + 1) * share] = grads[k, pl.ds(at, share), :].astype(
                    ref.dtype
                )
        for ref in (keep_ref, give_ref):
            ref[f, 3 * share :] = jnp.full((NOTE, sd), error, F32).astype(ref.dtype)


def grads_call(info, pieces, normed, hidden, s_down, up, gate, chips):
    ring = len(pieces)
    rows, sd = normed.shape
    units = hidden.shape[1]
    share = 3 * sd // (2 * chips) + NOTE
    operands = [*pieces, normed, hidden, s_down, up, gate]
    return pl.pallas_call(
        functools.partial(grads_kernel, ring=ring, chips=chips),
        out_shape=(
            jax.ShapeDtypeStruct((chips, share, units), F32),
            jax.ShapeDtypeStruct((chips, share, units), BF16),
        ),
        grid_spec=pltpu.PrefetchScalarGridSpec(
            num_scalar_prefetch=1,
            grid=(1,),
            in_specs=[whole(a.shape) for a in operands],
            out_specs=(whole((chips, share, units)), whole((chips, share, units))),
            scratch_shapes=[pltpu.VMEM((rows, sd), BF16), pltpu.VMEM((3, sd, units), F32)],
        ),
        compiler_params=params(22),
        cost_estimate=cost(8 * rows * sd * units, 20 * sd * units),
        name="grads",
    )(info, *operands)


def pair_kernel(keep_ref, theirs_ref, *outs):
    for f, out in enumerate(outs):
        out[...] = (keep_ref[f] + theirs_ref[f].astype(F32)).astype(out.dtype)


def pair_call(keep, theirs):
    chips, share, sd = keep.shape
    return pl.pallas_call(
        pair_kernel,
        out_shape=[jax.ShapeDtypeStruct((share, sd), BF16)] * chips,
        compiler_params=params(10),
        cost_estimate=cost(keep.size, 8 * keep.size),
        name="pair",
    )(keep, theirs)


def finish_kernel(info_ref, *refs, chips, ring):
    mine, others = refs[:chips], refs[chips : 2 * chips]
    outs = refs[2 * chips : 2 * chips + 3]
    notes = refs[2 * chips + 3]
    chip, core = info_ref[ring + 1], info_ref[ring + 2]
    share = (mine[0].shape[0] - NOTE) // 3
    for f in range(chips):
        for part, ref in ((core, mine[f]), (1 - core, others[f])):
            index = part * chips + (chip ^ f)
            at = pl.ds(pl.multiple_of(index * share, share), share)
            for k in range(3):
                outs[k][at, :] = ref[k * share : (k + 1) * share].astype(F32)
            notes[index] = ref[3 * share :, :HD].astype(F32)


def finish_call(info, mine, others, ring):
    chips = len(mine)
    share, sd = mine[0].shape
    rows = (share - NOTE) // 3 * 2 * chips
    return pl.pallas_call(
        functools.partial(finish_kernel, chips=chips, ring=ring),
        out_shape=[jax.ShapeDtypeStruct((rows, sd), F32)] * 3
        + [jax.ShapeDtypeStruct((2 * chips, NOTE, HD), F32)],
        grid_spec=pltpu.PrefetchScalarGridSpec(
            num_scalar_prefetch=1,
            grid=(1,),
            in_specs=[whole((share, sd))] * (2 * chips),
            out_specs=[whole((rows, sd))] * 3 + [whole((2 * chips, NOTE, HD))],
        ),
        compiler_params=params(14),
        cost_estimate=cost(rows * sd, 12 * rows * sd),
        name="finish",
    )(info, *mine, *others)


def step_on(block, axis):
    size = lax.axis_size(axis)
    return lax.ppermute(block, axis, [(i, (i + 1) % size) for i in range(size)])


def ring_gather(block, axis, steps=None):
    blocks = [block]
    for _ in range(lax.axis_size(axis) - 1 if steps is None else steps):
        blocks.append(step_on(blocks[-1], axis))
    return blocks


def shifted(pieces, axis):
    size = lax.axis_size(axis)
    moved = [
        lax.ppermute(pieces[s], axis, [(i, (i + s) % size) for i in range(size)])
        for s in range(1, size)
    ]
    return [pieces[0], *moved]


def flipped(pieces):
    size = lax.axis_size("dp")
    moved = [
        lax.ppermute(pieces[f], "dp", [(i, i ^ (2 * f)) for i in range(size)])
        for f in range(1, len(pieces))
    ]
    return [pieces[0], *moved]


def swapped(value):
    size = lax.axis_size("dp")
    return lax.ppermute(value, "dp", [(i, i ^ 1) for i in range(size)])


def after(value, *others):
    return lax.optimization_barrier((value, *others))[0]


def paired(
    tokens,
    series_ids,
    offsets,
    norm_gain,
    mlp_gain,
    w_query,
    w_key,
    w_value,
    w_out,
    w_gate,
    w_up,
    w_down,
    projector,
    student_in,
    s_gate,
    s_up,
    s_down,
):
    rows = tokens.shape[0]
    depth, sd = w_query.shape[0], student_in.shape[1]
    dp, ring = lax.axis_size("dp"), lax.axis_size("tensor")
    here, level = lax.axis_index("dp"), lax.axis_index("tensor")
    chips, half = dp // 2, rows // 2
    total_rows = rows * dp
    size = rows // ring
    slice_cols = depth // dp

    places = [(level - s) & (ring - 1) for s in range(ring)] + [level, here >> 1, here & 1]
    slots = lax.broadcasted_iota(jnp.int32, (16,), 0)
    info = sum(jnp.where(slots == k, place, 0) for k, place in enumerate(places))
    starts = [level * size, here * slice_cols]
    *starts, zero = [jnp.asarray(start, jnp.uint32) for start in (*starts, 0)]
    tokens, info, *starts = lax.optimization_barrier((tokens, info, *starts))

    token_rings = [ring_gather(tokens[k : k + half], "tensor") for k in (0, half)]

    angles = offsets.astype(F32)[:, None] * frequencies(HD)[None, :]
    cosine, sine = jnp.cos(angles), jnp.sin(angles)
    cosine = jnp.concatenate([cosine, cosine], axis=1)
    sine = jnp.concatenate([-sine, sine], axis=1)
    student_full = student_in.astype(F32)
    student_normed = rms_scale(student_full).astype(BF16)
    below = jnp.sum(
        series_ids[None, :] < jnp.arange(SERIES, dtype=jnp.int32)[:, None], axis=1, dtype=jnp.int32
    )

    made, tok_full, stamp = qkv_call(
        info, token_rings, norm_gain[None, :], cosine, sine, w_query, w_key, w_value
    )

    student_normed, projected, stamp = lax.optimization_barrier((student_normed, projector, stamp))
    s_gate_out = dot(student_normed, s_gate)
    s_up_out = dot(student_normed, s_up)
    sigmoid_gate = jax.nn.sigmoid(s_gate_out)
    up_slope = s_gate_out * sigmoid_gate
    gate_slope = s_up_out * sigmoid_gate * (1.0 + s_gate_out * (1.0 - sigmoid_gate))
    s_hidden = (up_slope * s_up_out).astype(BF16)
    up_slope, gate_slope = up_slope.astype(BF16), gate_slope.astype(BF16)
    student_part = dot(s_hidden, s_down)
    projected = dot(w_down, projected).astype(BF16)
    student_own = lax.dynamic_slice(student_full, [starts[0], zero], (size, sd))
    early = (projected, student_part, s_hidden, up_slope, gate_slope, student_normed, student_own)

    over = lambda value, bit: lax.ppermute(value, "tensor", [(i, i ^ bit) for i in range(ring)])
    w_slice = lax.dynamic_slice(w_out, [zero, starts[1]], (w_out.shape[0], slice_cols))
    w_slice, stamp, _ = lax.optimization_barrier((w_slice, stamp, s_gate_out))
    w_first = over(w_slice, 2)

    own = flipped(made)
    *own, w_first = lax.optimization_barrier((*own, w_first, *early))[: chips + 1]
    w_rest = over(jnp.stack([w_slice, w_first]), 1)
    other = [swapped(a) for a in own]
    near_first = flipped([w_first] * chips)
    made = attention_call(below, info, own, other, stamp, ring)
    attended = lax.optimization_barrier((*flipped(made), w_rest, *near_first))
    w_rest, near_first, attended = attended[chips], attended[chips + 1 :], attended[:chips]
    parts = [
        ring_gather(jnp.stack(attended[k : k + chips // 2]), "tensor") for k in (0, chips // 2)
    ]
    w_rest = after(w_rest, *attended)
    near_rest = flipped([w_rest] * chips)
    far_first = swapped(after(jnp.stack(near_first)[:, None], *attended))
    far_rest = [swapped(after(a, parts[1][1])) for a in near_rest]

    hidden, mixed_own, pieces = middle_call(
        info,
        parts,
        tok_full,
        w_out,
        (near_first, near_rest),
        (far_first, far_rest),
        mlp_gain[None, :],
        w_gate,
        w_up,
        projected,
        projector,
        student_part,
    )

    far_sum = over(down_call(info, hidden, w_down, ring, 3, 3)[0], 1)
    far_mine, near_theirs, kept = down_call(info, hidden, w_down, ring, 2, 0)

    moved = lax.optimization_barrier((*shifted(pieces, "tensor"), kept))[:ring]
    difference = student_own + sum(piece.astype(F32) for piece in moved)
    own = (difference * total_rows ** (-0.5)).astype(BF16)
    scaled = shifted([own] * ring, "tensor")

    keep, give = grads_call(
        after(info, far_sum),
        scaled,
        student_normed,
        s_hidden,
        s_down,
        up_slope,
        gate_slope,
        chips,
    )
    shares = pair_call(keep, swapped(give))
    far_sum = (far_sum.astype(F32) + far_mine.astype(F32)).astype(BF16)
    shares = flipped(shares)
    own = sum(share.astype(F32) for share in shares).astype(BF16)
    mine = flipped([own] * chips)
    others = [swapped(share) for share in mine]

    level_sums = [over(after(near_theirs, far_sum), 1), over(far_sum, 2)]
    mlp_own = sum(after(value, mine[-1]).astype(F32) for value in level_sums)
    teacher_out = (mixed_own.astype(F32) + (kept.astype(F32) + mlp_own)).astype(BF16)
    grad_gate, grad_up, grad_down, notes = finish_call(info, mine, others, ring)
    return teacher_out, grad_gate, grad_up, grad_down, notes[0, 0, 0] / sd


def local(*args):
    rows, w_query, s_gate = args[0].shape[0], args[5], args[14]
    dp, ring = lax.axis_size("dp"), lax.axis_size("tensor")
    heads = w_query.shape[1] // HD
    fits = (
        dp == 2 * heads
        and heads > 1
        and ring == 4
        and heads & (heads - 1) == 0
        and w_query.shape[0] == dp * COLS
        and s_gate.shape[0] == s_gate.shape[1]
        and rows % (32 * ring) == 0
    )
    return paired(*args) if fits else general(*args)


def solution(mesh):
    in_specs = (
        P("dp", "tensor"),
        P(),
        P("dp"),
        P(),
        P(),
        P(None, "tensor"),
        P(None, "tensor"),
        P(None, "tensor"),
        P("tensor", None),
        P(None, "tensor"),
        P(None, "tensor"),
        P("tensor", None),
        P(),
        P("dp", None),
        P(None, "tensor"),
        P(None, "tensor"),
        P("tensor", None),
    )
    out_specs = (P("dp", "tensor"), P(None, "tensor"), P(None, "tensor"), P("tensor", None), P())
    return jax.shard_map(local, mesh=mesh, in_specs=in_specs, out_specs=out_specs, check_vma=False)
```

```python
import functools
import math

import jax
import jax.numpy as jnp
from jax import lax
from jax.experimental import pallas as pl
from jax.experimental.pallas import tpu as pltpu
from jax.sharding import PartitionSpec as P

HD = 128
COLS = 256
NOTE = 16
SERIES = 8
F32 = jnp.float32
BF16 = jnp.bfloat16
MIB = 1024 * 1024


def rms_scale(values):
    return values * lax.rsqrt(jnp.mean(values * values, axis=-1, keepdims=True) + 1e-05)


def frequencies(head_dim):
    indices = jnp.arange(head_dim // 2).astype(jnp.float32)
    return jnp.exp(-jnp.log(500000.0) * 2.0 * indices / head_dim)


def rotary(inputs, angles):
    half_dim = inputs.shape[-1] // 2
    cosine = jnp.cos(angles)
    sine = jnp.sin(angles)
    first_half = inputs[..., :half_dim]
    second_half = inputs[..., half_dim:]
    return jnp.concatenate(
        [first_half * cosine - second_half * sine, first_half * sine + second_half * cosine],
        axis=-1,
    )


def general(
    tokens,
    series_ids,
    offsets,
    norm_gain,
    mlp_gain,
    w_query,
    w_key,
    w_value,
    w_out,
    w_gate,
    w_up,
    w_down,
    projector,
    student_in,
    s_gate,
    s_up,
    s_down,
):
    row_count = tokens.shape[0]
    heads_dev = w_query.shape[1] // HD
    first_row = lax.axis_index("dp") * row_count
    tokens_full = lax.all_gather(tokens, "tensor", axis=1, tiled=True).astype(jnp.float32)
    normed = (rms_scale(tokens_full) * norm_gain).astype(jnp.bfloat16)
    angles = offsets.astype(jnp.float32)[:, None, None] * frequencies(HD)[None, None, :]
    queries = rotary(
        jnp.dot(normed, w_query, preferred_element_type=jnp.float32).reshape(
            row_count, heads_dev, HD
        ),
        angles,
    ).astype(jnp.bfloat16)
    keys_rot = rotary(
        jnp.dot(normed, w_key, preferred_element_type=jnp.float32).reshape(
            row_count, heads_dev, HD
        ),
        angles,
    ).astype(jnp.bfloat16)
    values_mine = jnp.dot(normed, w_value, preferred_element_type=jnp.float32).astype(jnp.bfloat16)
    keys_flat = keys_rot.reshape(row_count, heads_dev * HD)
    query_pos = first_row + jnp.arange(row_count, dtype=jnp.int32)
    query_series = lax.dynamic_slice_in_dim(series_ids, first_row, row_count, 0)
    factor = HD ** (-0.5)
    peak = jnp.full((row_count, heads_dev), -1e30, jnp.float32)
    key_block = lax.all_gather(keys_flat, "dp", axis=0, tiled=True)
    value_block = lax.all_gather(values_mine, "dp", axis=0, tiled=True)
    count = key_block.shape[0]
    key_pos = jnp.arange(count, dtype=jnp.int32)
    allowed = (
        (key_pos[None, :] >= 0)
        & (key_pos[None, :] <= query_pos[:, None])
        & (series_ids[None, :] == query_series[:, None])
    )
    scores = (
        jnp.einsum(
            "qhd,khd->qhk",
            queries,
            key_block.reshape(count, heads_dev, HD),
            preferred_element_type=jnp.float32,
        )
        * factor
    )
    scores = jnp.where(allowed[:, None, :], scores, -1e30)
    new_peak = jnp.maximum(peak, jnp.max(scores, axis=2))
    weights = jnp.where(allowed[:, None, :], jnp.exp(scores - new_peak[:, :, None]), 0.0)
    denom = jnp.sum(weights, axis=2)
    accum = jnp.einsum(
        "qhk,khd->qhd",
        weights.astype(jnp.bfloat16),
        value_block.reshape(count, heads_dev, HD),
        preferred_element_type=jnp.float32,
    )
    peak, denom, accum = (new_peak, denom, accum)
    attended = (accum / denom[:, :, None]).astype(jnp.bfloat16).reshape(row_count, heads_dev * HD)
    partial_out = jnp.dot(attended, w_out, preferred_element_type=jnp.float32)
    own_sum = lax.psum_scatter(
        partial_out.astype(jnp.bfloat16), "tensor", scatter_dimension=1, tiled=True
    ).astype(jnp.float32)
    mixed_own = (tokens.astype(jnp.float32) + own_sum).astype(jnp.bfloat16)
    mixed = lax.all_gather(mixed_own, "tensor", axis=1, tiled=True)
    normed_two = (rms_scale(mixed.astype(jnp.float32)) * mlp_gain).astype(jnp.bfloat16)
    gate_out = jnp.dot(normed_two, w_gate, preferred_element_type=jnp.float32)
    up_out = jnp.dot(normed_two, w_up, preferred_element_type=jnp.float32)
    hidden = (jax.nn.silu(gate_out) * up_out).astype(jnp.bfloat16)
    mlp_part = jnp.dot(hidden, w_down, preferred_element_type=jnp.float32)
    mlp_own = lax.psum_scatter(
        mlp_part.astype(jnp.bfloat16), "tensor", scatter_dimension=1, tiled=True
    ).astype(jnp.float32)
    teacher_out = (mixed_own.astype(jnp.float32) + mlp_own).astype(jnp.bfloat16)
    student_full = student_in.astype(jnp.float32)
    student_normed = rms_scale(student_full).astype(jnp.bfloat16)
    s_gate_out = jnp.dot(student_normed, s_gate, preferred_element_type=jnp.float32)
    s_up_out = jnp.dot(student_normed, s_up, preferred_element_type=jnp.float32)
    sigmoid_gate = jax.nn.sigmoid(s_gate_out)
    s_hidden = (s_gate_out * sigmoid_gate * s_up_out).astype(jnp.bfloat16)
    student_part = jnp.dot(s_hidden, s_down, preferred_element_type=jnp.float32)
    teacher_full = lax.all_gather(teacher_out, "tensor", axis=1, tiled=True)
    target = jnp.dot(teacher_full, projector, preferred_element_type=jnp.float32)
    student_summed = lax.psum(student_part.astype(jnp.bfloat16), "tensor").astype(jnp.float32)
    difference = student_full + student_summed - target
    total_rows = row_count * lax.axis_size("dp")
    scaled = (difference * total_rows ** (-0.5)).astype(jnp.bfloat16)
    grad_down_part = jnp.einsum("rk,rc->kc", s_hidden, scaled, preferred_element_type=jnp.float32)
    grad_hidden = jnp.einsum("rc,kc->rk", scaled, s_down, preferred_element_type=jnp.float32)
    grad_up_in = (grad_hidden * s_gate_out * sigmoid_gate).astype(jnp.bfloat16)
    grad_gate_in = (
        grad_hidden * s_up_out * sigmoid_gate * (1.0 + s_gate_out * (1.0 - sigmoid_gate))
    ).astype(jnp.bfloat16)
    grad_gate_part = jnp.einsum(
        "rc,rk->ck", student_normed, grad_gate_in, preferred_element_type=jnp.float32
    )
    grad_up_part = jnp.einsum(
        "rc,rk->ck", student_normed, grad_up_in, preferred_element_type=jnp.float32
    )
    square_sum = jnp.sum(difference * difference)
    grad_gate, grad_up, grad_down, square_total = (
        lax.psum(grad_gate_part.astype(jnp.bfloat16), "dp").astype(jnp.float32),
        lax.psum(grad_up_part.astype(jnp.bfloat16), "dp").astype(jnp.float32),
        lax.psum(grad_down_part.astype(jnp.bfloat16), "dp").astype(jnp.float32),
        lax.psum(square_sum.astype(jnp.bfloat16), "dp").astype(jnp.float32),
    )
    error = square_total / (total_rows * difference.shape[1])
    return (teacher_out, grad_gate, grad_up, grad_down, error)


def dot(a, b):
    return jnp.dot(a, b, preferred_element_type=F32)


def dot_over(a, b, dims):
    return lax.dot_general(a, b, ((dims[:1], dims[1:]), ((), ())), preferred_element_type=F32)


def params(limit):
    return pltpu.CompilerParams(vmem_limit_bytes=limit * MIB)


def whole(shape):
    return pl.BlockSpec(shape, lambda *_: (0,) * len(shape))


def cost(flops, moved, transcendentals=0):
    return pl.CostEstimate(
        flops=int(flops), bytes_accessed=int(moved), transcendentals=int(transcendentals)
    )


def qkv_kernel(info_ref, *refs, ring, heads, factor):
    blocks = [refs[:ring], refs[ring : 2 * ring]]
    gain_ref, cos_ref, sin_ref, *sources = refs[2 * ring : 2 * ring + 6]
    outs = refs[2 * ring + 6 : 2 * ring + 6 + heads]
    tok_ref, stamp_ref, normed, made, weights, tokens, sems = refs[2 * ring + 6 + heads :]
    half, width = blocks[0][0].shape
    depth = gain_ref.shape[1]
    copies = [
        pltpu.make_async_copy(source, weights.at[k], sems.at[k])
        for k, source in enumerate(sources)
    ]
    for copy in copies:
        copy.start()
    for k in range(2):
        mine = slice(k * half, (k + 1) * half)
        total = jnp.zeros((half, 1), F32)
        for block in blocks[k]:
            part = block[...].astype(F32)
            total += jnp.sum(part * part, axis=1, keepdims=True)
        scale = lax.rsqrt(total / depth + 1e-05)
        for s, block in enumerate(blocks[k]):
            at = pl.ds(pl.multiple_of(info_ref[s] * width, 128), width)
            part = block[...]
            tokens[mine, at] = part
            normed[mine, at] = (part.astype(F32) * scale * gain_ref[:, at]).astype(BF16)
    keep = pltpu.make_async_copy(tokens, tok_ref, sems.at[3])
    keep.start()
    for kind, copy in enumerate(copies):
        copy.wait()
        result = dot(normed[...], weights[kind])
        for h in range(heads):
            head = result[:, h * HD : (h + 1) * HD]
            if kind < 2:
                head = head * cos_ref[...] + pltpu.roll(head, HD // 2, 1) * sin_ref[...]
            if kind == 0:
                head = head * factor
            made[h, kind] = head.astype(BF16)
    for f in range(heads):
        outs[f][...] = made[info_ref[ring + 1] ^ f]
    stamp_ref[...] = jnp.zeros_like(stamp_ref)
    keep.wait()


def qkv_call(info, blocks, gain, cosine, sine, *weights):
    half, width = blocks[0][0].shape
    rows, ring = 2 * half, len(blocks[0])
    depth, out_cols = weights[0].shape
    heads = out_cols // HD
    result = pl.pallas_call(
        functools.partial(
            qkv_kernel, ring=ring, heads=heads, factor=HD ** (-0.5) * math.log2(math.e)
        ),
        out_shape=[jax.ShapeDtypeStruct((3, rows, HD), BF16)] * heads
        + [jax.ShapeDtypeStruct((rows, depth), BF16), jax.ShapeDtypeStruct((8, HD), F32)],
        grid_spec=pltpu.PrefetchScalarGridSpec(
            num_scalar_prefetch=1,
            grid=(1,),
            in_specs=[whole((half, width))] * (2 * ring)
            + [whole((1, depth)), whole((rows, HD)), whole((rows, HD))]
            + [pl.BlockSpec(memory_space=pl.ANY)] * 3,
            out_specs=[whole((3, rows, HD))] * heads
            + [pl.BlockSpec(memory_space=pltpu.HBM), whole((8, HD))],
            scratch_shapes=[
                pltpu.VMEM((rows, depth), BF16),
                pltpu.VMEM((heads, 3, rows, HD), BF16),
                pltpu.VMEM((3, depth, out_cols), BF16),
                pltpu.VMEM((rows, depth), BF16),
                pltpu.SemaphoreType.DMA((4,)),
            ],
        ),
        compiler_params=params(42),
        cost_estimate=cost(6 * rows * depth * out_cols, 6 * depth * out_cols),
        name="qkv",
    )(info, *blocks[0], *blocks[1], gain, cosine, sine, *weights)
    return result[:heads], result[heads], result[heads + 1]


def attention_kernel(first_ref, info_ref, *refs, chips, ring):
    own, other = refs[:chips], refs[chips : 2 * chips]
    outs = refs[2 * chips + 1 : 3 * chips + 1]
    keys_all, values_all = refs[3 * chips + 1 :]
    chip, core = info_ref[ring + 1], info_ref[ring + 2]
    span = outs[0].shape[0]
    for f in range(chips):
        for source, side in ((own[f], core), (other[f], 1 - core)):
            block = 2 * (chip ^ f) + side
            keys_all[block] = source[1]
            values_all[block] = source[2].T

    def first_of(row):
        found = jnp.int32(0)
        for s in range(SERIES):
            edge = first_ref[s]
            found = jnp.where(edge <= row, jnp.maximum(found, edge), found)
        return found

    for f in range(chips):
        last = 2 * (chip ^ f) + core
        query = own[f][0]
        row = last * span + lax.broadcasted_iota(jnp.int32, (1, span), 1)
        start = jnp.zeros((1, span), jnp.int32)
        for s in range(SERIES):
            edge = first_ref[s]
            start = jnp.where(edge <= row, jnp.maximum(start, edge), start)
        lane = lax.broadcasted_iota(jnp.int32, (span, 1), 0)

        def body(at, carry, masked, query=query, row=row, start=start, lane=lane):
            peak, denom, accum = carry
            scores = dot_over(keys_all[at], query, (1, 1))
            if masked:
                column = lane + at * span
                allowed = (column >= start) & (column <= row)
                scores = jnp.where(allowed, scores, -1e30)
            new_peak = jnp.maximum(peak, jnp.max(scores, axis=0, keepdims=True))
            weights = jnp.exp2(scores - new_peak)
            if masked:
                weights = jnp.where(allowed, weights, 0.0)
            keep = jnp.exp2(peak - new_peak)
            denom = denom * keep + jnp.sum(weights, axis=0, keepdims=True)
            accum = accum * keep + dot(values_all[at], weights.astype(BF16))
            return new_peak, denom, accum

        def pair(turn, carry, query=query, full=None):
            peak, denom, accum = carry
            at = full + 2 * turn
            blocks = (at, at + 1)
            scores = [dot_over(keys_all[block], query, (1, 1)) for block in blocks]
            tops = [jnp.max(score, axis=0, keepdims=True) for score in scores]
            new_peak = jnp.maximum(peak, jnp.maximum(*tops))
            keep = jnp.exp2(peak - new_peak)
            denom, accum = denom * keep, accum * keep
            for block, score in zip(blocks, scores):
                weights = jnp.exp2(score - new_peak)
                denom += jnp.sum(weights, axis=0, keepdims=True)
                accum += dot(values_all[block], weights.astype(BF16))
            return new_peak, denom, accum

        begin = first_of(last * span) // span
        full = jnp.minimum(last, (first_of(last * span + span - 1) + span - 1) // span)
        carry = (
            jnp.full((1, span), -1e30, F32),
            jnp.zeros((1, span), F32),
            jnp.zeros((HD, span), F32),
        )
        carry = lax.fori_loop(begin, full, functools.partial(body, masked=True), carry)
        turns = (last - full) // 2
        carry = lax.fori_loop(0, turns, functools.partial(pair, full=full), carry)
        rest = full + 2 * turns
        carry = lax.fori_loop(rest, last, functools.partial(body, masked=False), carry)
        _, denom, accum = body(last, carry, masked=True)
        outs[f][...] = (accum / denom).T.astype(BF16)


def attention_call(first, info, own, other, stamp, ring):
    chips = len(own)
    _, rows, _ = own[0].shape
    return pl.pallas_call(
        functools.partial(attention_kernel, chips=chips, ring=ring),
        out_shape=[jax.ShapeDtypeStruct((rows, HD), BF16)] * chips,
        grid_spec=pltpu.PrefetchScalarGridSpec(
            num_scalar_prefetch=2,
            grid=(1,),
            in_specs=[whole((3, rows, HD))] * (2 * chips) + [whole(stamp.shape)],
            out_specs=[whole((rows, HD))] * chips,
            scratch_shapes=[
                pltpu.VMEM((2 * chips, rows, HD), BF16),
                pltpu.VMEM((2 * chips, HD, rows), BF16),
            ],
        ),
        compiler_params=params(24),
        cost_estimate=cost(
            4 * chips * rows * chips * rows * HD,
            16 * chips * rows * HD,
            chips * rows * chips * rows,
        ),
        name="attention",
    )(first, info, *own, *other, stamp)


def middle_kernel(info_ref, *refs, ring, chips):
    parts = [refs[:ring], refs[ring : 2 * ring]]
    refs = refs[2 * ring :]
    tok_ref, w_own_ref = refs[:2]
    near_first, near_rest = refs[2 : 2 + chips], refs[2 + chips : 2 + 2 * chips]
    far_first, far_rest = refs[2 + 2 * chips], refs[3 + 2 * chips : 3 + 3 * chips]
    refs = refs[3 + 3 * chips :]
    gain_ref, gate_ref, up_ref, wp_ref, proj_ref, student_ref = refs[:6]
    hidden_ref, own_ref = refs[6:8]
    pieces = refs[8 : 8 + ring]
    attended, mixed, total, near, far, gates, ups, wp, proj, sems = refs[8 + ring :]
    step = pl.program_id(0)
    level, chip, core = info_ref[ring], info_ref[ring + 1], info_ref[ring + 2]
    rows, depth = mixed.shape
    width = own_ref.shape[1]
    blocks, _, wide = gates.shape

    used = iter(range(sems.shape[0]))
    copy = lambda source, target: pltpu.make_async_copy(source, target, sems.at[next(used)])
    heads = []
    for k in range(2):
        for s, part in enumerate(parts[k]):
            count = part.shape[0]
            for i in range(count):
                flip = level ^ info_ref[s]
                at = ((flip & 1) * 2 + (flip >> 1)) * width + (chip ^ (k * count + i)) * HD
                heads.append(copy(part.at[i], attended.at[:, pl.ds(pl.multiple_of(at, HD), HD)]))
    slices = [
        [
            copy(near_first[f], near.at[f, 0]),
            copy(near_rest[f], near.at[f, pl.ds(1, ring - 2)]),
            copy(far_first.at[f, 0], far.at[f, 0]),
            copy(far_rest[f], far.at[f, pl.ds(1, ring - 2)]),
        ]
        for f in range(chips)
    ]
    own_rows = pl.ds(pl.multiple_of(level * width, width), width)
    late = [copy(proj_ref.at[own_rows], proj), copy(student_ref, total)]
    columns = [pl.ds(i * wide, wide) for i in range(blocks)]
    units = [
        [
            copy(gate_ref.at[:, columns[i]], gates.at[i]),
            copy(up_ref.at[:, columns[i]], ups.at[i]),
            copy(wp_ref.at[columns[i]], wp.at[i]),
        ]
        for i in range(blocks)
    ]

    @pl.when(step == 0)
    def _():
        for c in heads + slices[0]:
            c.start()
        for c in sum(slices[1:], []) + late:
            c.start()
        for c in heads:
            c.wait()

    for f in range(chips):

        @pl.when(step == f)
        def _(f=f):
            for c in slices[f]:
                c.wait()
            for c in sum(units[f::chips], []):
                c.start()

    @pl.when(step < chips)
    def _():
        for gathered, side in ((near, core), (far, 1 - core)):
            here = pl.ds(pl.multiple_of(side * COLS, COLS), COLS)
            result = tok_ref[:, here].astype(F32) + dot(attended[:, :width], w_own_ref[:, here])
            weight = gathered[step].reshape(depth - width, COLS)
            result += dot(attended[:, width:], weight)
            at = pl.ds(pl.multiple_of((2 * (step ^ chip) + side) * COLS, COLS), COLS)
            mixed[:, at] = result.astype(BF16)

    @pl.when(step == chips)
    def _():
        for c in late:
            c.wait()
        values = mixed[...].astype(F32)
        attended[...] = (rms_scale(values) * gain_ref[...]).astype(BF16)
        own = mixed[:, pl.ds(pl.multiple_of(level * width, 128), width)]
        own_ref[...] = own
        total[...] -= dot(own, proj[...])

    for i in range(blocks):

        @pl.when(step == chips + i)
        def _(i=i):
            for c in units[i]:
                c.wait()

    @pl.when(step >= chips)
    def _():
        index = step - chips
        gate = dot(attended[...], gates[index])
        up = dot(attended[...], ups[index])
        hidden = (gate * jax.nn.sigmoid(gate) * up).astype(BF16)
        hidden_ref[...] = hidden
        total[...] -= dot(hidden, wp[index])

    @pl.when(step == pl.num_programs(0) - 1)
    def _():
        size = rows // ring
        for s in range(ring):
            at = pl.ds(pl.multiple_of(((level + s) & (ring - 1)) * size, size), size)
            pieces[s][...] = total[at, :].astype(BF16)


def middle_call(info, parts, tok, w_out, near, far, gain, w_gate, w_up, wp, projector, student):
    rows, depth = tok.shape
    ring, chips = len(parts[0]), len(near[0])
    units = w_gate.shape[1]
    wide = 2 * COLS
    width = depth // ring
    sd = projector.shape[1]
    blocks = units // wide
    tile = lambda j, info: (0, jnp.minimum(j, chips - 1) ^ info[ring + 1])
    late = lambda j, info: (0, jnp.maximum(j - chips, 0))
    anywhere = pl.BlockSpec(memory_space=pl.ANY)
    count = 2 * ring * parts[0][0].shape[0] + 4 * chips + 2 + 3 * blocks
    result = pl.pallas_call(
        functools.partial(middle_kernel, ring=ring, chips=chips),
        out_shape=[
            jax.ShapeDtypeStruct((rows, units), BF16),
            jax.ShapeDtypeStruct((rows, width), BF16),
        ]
        + [jax.ShapeDtypeStruct((rows // ring, sd), BF16)] * ring,
        grid_spec=pltpu.PrefetchScalarGridSpec(
            num_scalar_prefetch=1,
            grid=(chips + blocks,),
            in_specs=[anywhere] * (2 * ring)
            + [pl.BlockSpec((rows, wide), tile), pl.BlockSpec((width, wide), tile)]
            + [anywhere] * (3 * chips + 1)
            + [whole((1, depth))]
            + [anywhere] * 5,
            out_specs=[
                pl.BlockSpec((rows, wide), late),
                whole((rows, width)),
            ]
            + [whole((rows // ring, sd))] * ring,
            scratch_shapes=[
                pltpu.VMEM((rows, depth), BF16),
                pltpu.VMEM((rows, depth), BF16),
                pltpu.VMEM((rows, sd), F32),
                pltpu.VMEM((chips, ring - 1, width, COLS), BF16),
                pltpu.VMEM((chips, ring - 1, width, COLS), BF16),
                pltpu.VMEM((blocks, depth, wide), BF16),
                pltpu.VMEM((blocks, depth, wide), BF16),
                pltpu.VMEM((blocks, wide, sd), BF16),
                pltpu.VMEM((width, sd), BF16),
                pltpu.SemaphoreType.DMA((count,)),
            ],
        ),
        compiler_params=params(42),
        cost_estimate=cost(
            2 * rows * depth * (depth + 2 * units) + 2 * rows * sd * (units + width),
            2 * depth * (depth + 2 * units),
            rows * units,
        ),
        name="middle",
    )(
        info,
        *parts[0],
        *parts[1],
        tok,
        w_out,
        *near[0],
        *near[1],
        far[0],
        *far[1],
        gain,
        w_gate,
        w_up,
        wp,
        projector,
        student,
    )
    return result[0], result[1], result[2:]


def down_kernel(info_ref, hidden_ref, weight_ref, *outs):
    result = dot(hidden_ref[...], weight_ref[...]).astype(BF16)
    for j, out in enumerate(outs):

        @pl.when(pl.program_id(0) == j)
        def _(out=out):
            out[...] = result


def down_call(info, hidden, w_down, ring, first_flip, last_flip):
    rows, units = hidden.shape
    depth = w_down.shape[1]
    width = depth // ring
    count = first_flip - last_flip + 1
    return pl.pallas_call(
        down_kernel,
        out_shape=[jax.ShapeDtypeStruct((rows, width), BF16)] * count,
        grid_spec=pltpu.PrefetchScalarGridSpec(
            num_scalar_prefetch=1,
            grid=(count,),
            in_specs=[
                whole((rows, units)),
                pl.BlockSpec((units, width), lambda j, info: (0, info[ring] ^ (first_flip - j))),
            ],
            out_specs=[whole((rows, width))] * count,
        ),
        compiler_params=params(24),
        cost_estimate=cost(2 * rows * units * width * count, 2 * units * width * count),
        name="down",
    )(info, hidden, w_down)


def grads_kernel(info_ref, *refs, ring, chips):
    pieces = refs[:ring]
    normed_ref, hidden_ref, s_down_ref, up_ref, gate_ref = refs[ring : ring + 5]
    keep_ref, give_ref, scaled, grads = refs[ring + 5 :]
    chip, core = info_ref[ring + 1], info_ref[ring + 2]
    size, sd = pieces[0].shape
    for s in range(ring):
        scaled[pl.ds(pl.multiple_of(info_ref[s] * size, size), size), :] = pieces[s][...]
    value = scaled[...]
    wide = value.astype(F32)
    error = jnp.sum(wide * wide)
    grad_hidden = dot_over(value, s_down_ref[...], (1, 1))
    grads[0] = dot_over(normed_ref[...], (grad_hidden * gate_ref[...].astype(F32)).astype(BF16), (0, 0))
    grads[1] = dot_over(normed_ref[...], (grad_hidden * up_ref[...].astype(F32)).astype(BF16), (0, 0))
    grads[2] = dot_over(hidden_ref[...], value, (0, 0))
    share = grads.shape[1] // (2 * chips)
    for f in range(chips):
        for k in range(3):
            for part, ref in ((core, keep_ref), (1 - core, give_ref)):
                at = pl.multiple_of((part * chips + (chip ^ f)) * share, share)
                ref[f, k * share : (k + 1) * share] = grads[k, pl.ds(at, share), :].astype(
                    ref.dtype
                )
        for ref in (keep_ref, give_ref):
            ref[f, 3 * share :] = jnp.full((NOTE, sd), error, F32).astype(ref.dtype)


def grads_call(info, pieces, normed, hidden, s_down, up, gate, chips):
    ring = len(pieces)
    rows, sd = normed.shape
    units = hidden.shape[1]
    share = 3 * sd // (2 * chips) + NOTE
    operands = [*pieces, normed, hidden, s_down, up, gate]
    return pl.pallas_call(
        functools.partial(grads_kernel, ring=ring, chips=chips),
        out_shape=(
            jax.ShapeDtypeStruct((chips, share, units), F32),
            jax.ShapeDtypeStruct((chips, share, units), BF16),
        ),
        grid_spec=pltpu.PrefetchScalarGridSpec(
            num_scalar_prefetch=1,
            grid=(1,),
            in_specs=[whole(a.shape) for a in operands],
            out_specs=(whole((chips, share, units)), whole((chips, share, units))),
            scratch_shapes=[pltpu.VMEM((rows, sd), BF16), pltpu.VMEM((3, sd, units), F32)],
        ),
        compiler_params=params(22),
        cost_estimate=cost(8 * rows * sd * units, 20 * sd * units),
        name="grads",
    )(info, *operands)


def pair_kernel(keep_ref, theirs_ref, *outs):
    for f, out in enumerate(outs):
        out[...] = (keep_ref[f] + theirs_ref[f].astype(F32)).astype(out.dtype)


def pair_call(keep, theirs):
    chips, share, sd = keep.shape
    return pl.pallas_call(
        pair_kernel,
        out_shape=[jax.ShapeDtypeStruct((share, sd), BF16)] * chips,
        compiler_params=params(10),
        cost_estimate=cost(keep.size, 8 * keep.size),
        name="pair",
    )(keep, theirs)


def finish_kernel(info_ref, *refs, chips, ring):
    mine, others = refs[:chips], refs[chips : 2 * chips]
    outs = refs[2 * chips : 2 * chips + 3]
    error_ref, notes = refs[2 * chips + 3 :]
    chip, core = info_ref[ring + 1], info_ref[ring + 2]
    share = (mine[0].shape[0] - NOTE) // 3
    for f in range(chips):
        for part, ref in ((core, mine[f]), (1 - core, others[f])):
            index = part * chips + (chip ^ f)
            at = pl.ds(pl.multiple_of(index * share, share), share)
            for k in range(3):
                outs[k][at, :] = ref[k * share : (k + 1) * share].astype(F32)
            notes[index] = ref[3 * share :, :HD].astype(F32)
    error_ref[0, 0] = jnp.max(notes[0]) / mine[0].shape[1]


def finish_call(info, mine, others, ring):
    chips = len(mine)
    share, sd = mine[0].shape
    rows = (share - NOTE) // 3 * 2 * chips
    return pl.pallas_call(
        functools.partial(finish_kernel, chips=chips, ring=ring),
        out_shape=[jax.ShapeDtypeStruct((rows, sd), F32)] * 3
        + [jax.ShapeDtypeStruct((1, 1), F32)],
        grid_spec=pltpu.PrefetchScalarGridSpec(
            num_scalar_prefetch=1,
            grid=(1,),
            in_specs=[whole((share, sd))] * (2 * chips),
            out_specs=[whole((rows, sd))] * 3 + [pl.BlockSpec(memory_space=pltpu.SMEM)],
            scratch_shapes=[pltpu.VMEM((2 * chips, NOTE, HD), F32)],
        ),
        compiler_params=params(14),
        cost_estimate=cost(rows * sd, 12 * rows * sd),
        name="finish",
    )(info, *mine, *others)


def step_on(block, axis):
    size = lax.axis_size(axis)
    return lax.ppermute(block, axis, [(i, (i + 1) % size) for i in range(size)])


def ring_gather(block, axis, steps=None):
    blocks = [block]
    for _ in range(lax.axis_size(axis) - 1 if steps is None else steps):
        blocks.append(step_on(blocks[-1], axis))
    return blocks


def shifted(pieces, axis):
    size = lax.axis_size(axis)
    moved = [
        lax.ppermute(pieces[s], axis, [(i, (i + s) % size) for i in range(size)])
        for s in range(1, size)
    ]
    return [pieces[0], *moved]


def flipped(pieces):
    size = lax.axis_size("dp")
    moved = [
        lax.ppermute(pieces[f], "dp", [(i, i ^ (2 * f)) for i in range(size)])
        for f in range(1, len(pieces))
    ]
    return [pieces[0], *moved]


def swapped(value):
    size = lax.axis_size("dp")
    return lax.ppermute(value, "dp", [(i, i ^ 1) for i in range(size)])


def after(value, *others):
    return lax.optimization_barrier((value, *others))[0]


def paired(
    tokens,
    series_ids,
    offsets,
    norm_gain,
    mlp_gain,
    w_query,
    w_key,
    w_value,
    w_out,
    w_gate,
    w_up,
    w_down,
    projector,
    student_in,
    s_gate,
    s_up,
    s_down,
):
    rows = tokens.shape[0]
    depth, sd = w_query.shape[0], student_in.shape[1]
    dp, ring = lax.axis_size("dp"), lax.axis_size("tensor")
    here, level = lax.axis_index("dp"), lax.axis_index("tensor")
    chips, half = dp // 2, rows // 2
    total_rows = rows * dp
    size = rows // ring
    slice_cols = depth // dp

    places = [(level - s) & (ring - 1) for s in range(ring)] + [level, here >> 1, here & 1]
    slots = lax.broadcasted_iota(jnp.int32, (16,), 0)
    info = sum(jnp.where(slots == k, place, 0) for k, place in enumerate(places))
    starts = [level * size, here * slice_cols]
    *starts, zero = [jnp.asarray(start, jnp.uint32) for start in (*starts, 0)]
    tokens, info, *starts = lax.optimization_barrier((tokens, info, *starts))

    token_rings = [ring_gather(tokens[k : k + half], "tensor") for k in (0, half)]

    angles = offsets.astype(F32)[:, None] * frequencies(HD)[None, :]
    cosine, sine = jnp.cos(angles), jnp.sin(angles)
    cosine = jnp.concatenate([cosine, cosine], axis=1)
    sine = jnp.concatenate([-sine, sine], axis=1)
    student_full = student_in.astype(F32)
    student_normed = rms_scale(student_full).astype(BF16)
    below = jnp.sum(
        series_ids[None, :] < jnp.arange(SERIES, dtype=jnp.int32)[:, None], axis=1, dtype=jnp.int32
    )

    made, tok_full, stamp = qkv_call(
        info, token_rings, norm_gain[None, :], cosine, sine, w_query, w_key, w_value
    )

    student_normed, projected, stamp = lax.optimization_barrier((student_normed, projector, stamp))
    s_gate_out = dot(student_normed, s_gate)
    s_up_out = dot(student_normed, s_up)
    sigmoid_gate = jax.nn.sigmoid(s_gate_out)
    up_slope = s_gate_out * sigmoid_gate
    gate_slope = s_up_out * sigmoid_gate * (1.0 + s_gate_out * (1.0 - sigmoid_gate))
    s_hidden = (up_slope * s_up_out).astype(BF16)
    up_slope, gate_slope = up_slope.astype(BF16), gate_slope.astype(BF16)
    student_part = dot(s_hidden, s_down)
    projected = dot(w_down, projected).astype(BF16)
    student_own = lax.dynamic_slice(student_full, [starts[0], zero], (size, sd))
    early = (projected, student_part, s_hidden, up_slope, gate_slope, student_normed, student_own)

    over = lambda value, bit: lax.ppermute(value, "tensor", [(i, i ^ bit) for i in range(ring)])
    w_slice = lax.dynamic_slice(w_out, [zero, starts[1]], (w_out.shape[0], slice_cols))
    w_slice, stamp, _ = lax.optimization_barrier((w_slice, stamp, s_gate_out))
    w_first = over(w_slice, 2)

    own = flipped(made)
    *own, w_first = lax.optimization_barrier((*own, w_first, *early))[: chips + 1]
    w_rest = over(jnp.stack([w_slice, w_first]), 1)
    other = [swapped(a) for a in own]
    near_first = flipped([w_first] * chips)
    made = attention_call(below, info, own, other, stamp, ring)
    attended = lax.optimization_barrier((*flipped(made), w_rest, *near_first))
    w_rest, near_first, attended = attended[chips], attended[chips + 1 :], attended[:chips]
    parts = [
        ring_gather(jnp.stack(attended[k : k + chips // 2]), "tensor") for k in (0, chips // 2)
    ]
    w_rest = after(w_rest, *attended)
    near_rest = flipped([w_rest] * chips)
    far_first = swapped(after(jnp.stack(near_first)[:, None], *attended))
    far_rest = [swapped(after(a, parts[1][1])) for a in near_rest]

    hidden, mixed_own, pieces = middle_call(
        info,
        parts,
        tok_full,
        w_out,
        (near_first, near_rest),
        (far_first, far_rest),
        mlp_gain[None, :],
        w_gate,
        w_up,
        projected,
        projector,
        student_part,
    )

    far_sum = over(down_call(info, hidden, w_down, ring, 3, 3)[0], 1)
    far_mine, near_theirs, kept = down_call(info, hidden, w_down, ring, 2, 0)

    moved = lax.optimization_barrier((*shifted(pieces, "tensor"), kept))[:ring]
    difference = student_own + sum(piece.astype(F32) for piece in moved)
    own = (difference * total_rows ** (-0.5)).astype(BF16)
    scaled = shifted([own] * ring, "tensor")

    keep, give = grads_call(
        after(info, far_sum),
        scaled,
        student_normed,
        s_hidden,
        s_down,
        up_slope,
        gate_slope,
        chips,
    )
    shares = pair_call(keep, swapped(give))
    far_sum = (far_sum.astype(F32) + far_mine.astype(F32)).astype(BF16)
    shares = flipped(shares)
    own = sum(share.astype(F32) for share in shares).astype(BF16)
    mine = flipped([own] * chips)
    others = [swapped(share) for share in mine]

    level_sums = [over(after(near_theirs, far_sum), 1), over(far_sum, 2)]
    mlp_own = sum(after(value, mine[-1]).astype(F32) for value in level_sums)
    teacher_out = (mixed_own.astype(F32) + (kept.astype(F32) + mlp_own)).astype(BF16)
    grad_gate, grad_up, grad_down, error = finish_call(info, mine, others, ring)
    return teacher_out, grad_gate, grad_up, grad_down, error.reshape(())


def local(*args):
    rows, w_query, s_gate = args[0].shape[0], args[5], args[14]
    dp, ring = lax.axis_size("dp"), lax.axis_size("tensor")
    heads = w_query.shape[1] // HD
    fits = (
        dp == 2 * heads
        and heads > 1
        and ring == 4
        and heads & (heads - 1) == 0
        and w_query.shape[0] == dp * COLS
        and s_gate.shape[0] == s_gate.shape[1]
        and rows % (32 * ring) == 0
    )
    return paired(*args) if fits else general(*args)


def solution(mesh):
    in_specs = (
        P("dp", "tensor"),
        P(),
        P("dp"),
        P(),
        P(),
        P(None, "tensor"),
        P(None, "tensor"),
        P(None, "tensor"),
        P("tensor", None),
        P(None, "tensor"),
        P(None, "tensor"),
        P("tensor", None),
        P(),
        P("dp", None),
        P(None, "tensor"),
        P(None, "tensor"),
        P("tensor", None),
    )
    out_specs = (P("dp", "tensor"), P(None, "tensor"), P(None, "tensor"), P("tensor", None), P())
    return jax.shard_map(local, mesh=mesh, in_specs=in_specs, out_specs=out_specs, check_vma=False)
```

```python
import functools
import math

import jax
import jax.numpy as jnp
from jax import lax
from jax.experimental import pallas as pl
from jax.experimental.pallas import tpu as pltpu
from jax.sharding import PartitionSpec as P

HD = 128
COLS = 256
NOTE = 16
SERIES = 8
F32 = jnp.float32
BF16 = jnp.bfloat16
MIB = 1024 * 1024


def rms_scale(values):
    return values * lax.rsqrt(jnp.mean(values * values, axis=-1, keepdims=True) + 1e-05)


def frequencies(head_dim):
    indices = jnp.arange(head_dim // 2).astype(jnp.float32)
    return jnp.exp(-jnp.log(500000.0) * 2.0 * indices / head_dim)


def rotary(inputs, angles):
    half_dim = inputs.shape[-1] // 2
    cosine = jnp.cos(angles)
    sine = jnp.sin(angles)
    first_half = inputs[..., :half_dim]
    second_half = inputs[..., half_dim:]
    return jnp.concatenate(
        [first_half * cosine - second_half * sine, first_half * sine + second_half * cosine],
        axis=-1,
    )


def general(
    tokens,
    series_ids,
    offsets,
    norm_gain,
    mlp_gain,
    w_query,
    w_key,
    w_value,
    w_out,
    w_gate,
    w_up,
    w_down,
    projector,
    student_in,
    s_gate,
    s_up,
    s_down,
):
    row_count = tokens.shape[0]
    heads_dev = w_query.shape[1] // HD
    first_row = lax.axis_index("dp") * row_count
    tokens_full = lax.all_gather(tokens, "tensor", axis=1, tiled=True).astype(jnp.float32)
    normed = (rms_scale(tokens_full) * norm_gain).astype(jnp.bfloat16)
    angles = offsets.astype(jnp.float32)[:, None, None] * frequencies(HD)[None, None, :]
    queries = rotary(
        jnp.dot(normed, w_query, preferred_element_type=jnp.float32).reshape(
            row_count, heads_dev, HD
        ),
        angles,
    ).astype(jnp.bfloat16)
    keys_rot = rotary(
        jnp.dot(normed, w_key, preferred_element_type=jnp.float32).reshape(
            row_count, heads_dev, HD
        ),
        angles,
    ).astype(jnp.bfloat16)
    values_mine = jnp.dot(normed, w_value, preferred_element_type=jnp.float32).astype(jnp.bfloat16)
    keys_flat = keys_rot.reshape(row_count, heads_dev * HD)
    query_pos = first_row + jnp.arange(row_count, dtype=jnp.int32)
    query_series = lax.dynamic_slice_in_dim(series_ids, first_row, row_count, 0)
    factor = HD ** (-0.5)
    peak = jnp.full((row_count, heads_dev), -1e30, jnp.float32)
    key_block = lax.all_gather(keys_flat, "dp", axis=0, tiled=True)
    value_block = lax.all_gather(values_mine, "dp", axis=0, tiled=True)
    count = key_block.shape[0]
    key_pos = jnp.arange(count, dtype=jnp.int32)
    allowed = (
        (key_pos[None, :] >= 0)
        & (key_pos[None, :] <= query_pos[:, None])
        & (series_ids[None, :] == query_series[:, None])
    )
    scores = (
        jnp.einsum(
            "qhd,khd->qhk",
            queries,
            key_block.reshape(count, heads_dev, HD),
            preferred_element_type=jnp.float32,
        )
        * factor
    )
    scores = jnp.where(allowed[:, None, :], scores, -1e30)
    new_peak = jnp.maximum(peak, jnp.max(scores, axis=2))
    weights = jnp.where(allowed[:, None, :], jnp.exp(scores - new_peak[:, :, None]), 0.0)
    denom = jnp.sum(weights, axis=2)
    accum = jnp.einsum(
        "qhk,khd->qhd",
        weights.astype(jnp.bfloat16),
        value_block.reshape(count, heads_dev, HD),
        preferred_element_type=jnp.float32,
    )
    peak, denom, accum = (new_peak, denom, accum)
    attended = (accum / denom[:, :, None]).astype(jnp.bfloat16).reshape(row_count, heads_dev * HD)
    partial_out = jnp.dot(attended, w_out, preferred_element_type=jnp.float32)
    own_sum = lax.psum_scatter(
        partial_out.astype(jnp.bfloat16), "tensor", scatter_dimension=1, tiled=True
    ).astype(jnp.float32)
    mixed_own = (tokens.astype(jnp.float32) + own_sum).astype(jnp.bfloat16)
    mixed = lax.all_gather(mixed_own, "tensor", axis=1, tiled=True)
    normed_two = (rms_scale(mixed.astype(jnp.float32)) * mlp_gain).astype(jnp.bfloat16)
    gate_out = jnp.dot(normed_two, w_gate, preferred_element_type=jnp.float32)
    up_out = jnp.dot(normed_two, w_up, preferred_element_type=jnp.float32)
    hidden = (jax.nn.silu(gate_out) * up_out).astype(jnp.bfloat16)
    mlp_part = jnp.dot(hidden, w_down, preferred_element_type=jnp.float32)
    mlp_own = lax.psum_scatter(
        mlp_part.astype(jnp.bfloat16), "tensor", scatter_dimension=1, tiled=True
    ).astype(jnp.float32)
    teacher_out = (mixed_own.astype(jnp.float32) + mlp_own).astype(jnp.bfloat16)
    student_full = student_in.astype(jnp.float32)
    student_normed = rms_scale(student_full).astype(jnp.bfloat16)
    s_gate_out = jnp.dot(student_normed, s_gate, preferred_element_type=jnp.float32)
    s_up_out = jnp.dot(student_normed, s_up, preferred_element_type=jnp.float32)
    sigmoid_gate = jax.nn.sigmoid(s_gate_out)
    s_hidden = (s_gate_out * sigmoid_gate * s_up_out).astype(jnp.bfloat16)
    student_part = jnp.dot(s_hidden, s_down, preferred_element_type=jnp.float32)
    teacher_full = lax.all_gather(teacher_out, "tensor", axis=1, tiled=True)
    target = jnp.dot(teacher_full, projector, preferred_element_type=jnp.float32)
    student_summed = lax.psum(student_part.astype(jnp.bfloat16), "tensor").astype(jnp.float32)
    difference = student_full + student_summed - target
    total_rows = row_count * lax.axis_size("dp")
    scaled = (difference * total_rows ** (-0.5)).astype(jnp.bfloat16)
    grad_down_part = jnp.einsum("rk,rc->kc", s_hidden, scaled, preferred_element_type=jnp.float32)
    grad_hidden = jnp.einsum("rc,kc->rk", scaled, s_down, preferred_element_type=jnp.float32)
    grad_up_in = (grad_hidden * s_gate_out * sigmoid_gate).astype(jnp.bfloat16)
    grad_gate_in = (
        grad_hidden * s_up_out * sigmoid_gate * (1.0 + s_gate_out * (1.0 - sigmoid_gate))
    ).astype(jnp.bfloat16)
    grad_gate_part = jnp.einsum(
        "rc,rk->ck", student_normed, grad_gate_in, preferred_element_type=jnp.float32
    )
    grad_up_part = jnp.einsum(
        "rc,rk->ck", student_normed, grad_up_in, preferred_element_type=jnp.float32
    )
    square_sum = jnp.sum(difference * difference)
    grad_gate, grad_up, grad_down, square_total = (
        lax.psum(grad_gate_part.astype(jnp.bfloat16), "dp").astype(jnp.float32),
        lax.psum(grad_up_part.astype(jnp.bfloat16), "dp").astype(jnp.float32),
        lax.psum(grad_down_part.astype(jnp.bfloat16), "dp").astype(jnp.float32),
        lax.psum(square_sum.astype(jnp.bfloat16), "dp").astype(jnp.float32),
    )
    error = square_total / (total_rows * difference.shape[1])
    return (teacher_out, grad_gate, grad_up, grad_down, error)


def dot(a, b):
    return jnp.dot(a, b, preferred_element_type=F32)


def dot_over(a, b, dims):
    return lax.dot_general(a, b, ((dims[:1], dims[1:]), ((), ())), preferred_element_type=F32)


def params(limit):
    return pltpu.CompilerParams(vmem_limit_bytes=limit * MIB)


def whole(shape):
    return pl.BlockSpec(shape, lambda *_: (0,) * len(shape))


def cost(flops, moved, transcendentals=0):
    return pl.CostEstimate(
        flops=int(flops), bytes_accessed=int(moved), transcendentals=int(transcendentals)
    )


def qkv_kernel(info_ref, *refs, ring, heads, factor):
    blocks = [refs[:ring], refs[ring : 2 * ring]]
    gain_ref, cos_ref, sin_ref, *sources = refs[2 * ring : 2 * ring + 6]
    outs = refs[2 * ring + 6 : 2 * ring + 6 + heads]
    tok_ref, stamp_ref, normed, made, weights, tokens, sems = refs[2 * ring + 6 + heads :]
    half, width = blocks[0][0].shape
    depth = gain_ref.shape[1]
    copies = [
        pltpu.make_async_copy(source, weights.at[k], sems.at[k])
        for k, source in enumerate(sources)
    ]
    for copy in copies:
        copy.start()
    for k in range(2):
        mine = slice(k * half, (k + 1) * half)
        total = jnp.zeros((half, 1), F32)
        for block in blocks[k]:
            part = block[...].astype(F32)
            total += jnp.sum(part * part, axis=1, keepdims=True)
        scale = lax.rsqrt(total / depth + 1e-05)
        for s, block in enumerate(blocks[k]):
            at = pl.ds(pl.multiple_of(info_ref[s] * width, 128), width)
            part = block[...]
            tokens[mine, at] = part
            normed[mine, at] = (part.astype(F32) * scale * gain_ref[:, at]).astype(BF16)
    keep = pltpu.make_async_copy(tokens, tok_ref, sems.at[3])
    keep.start()
    for kind, copy in enumerate(copies):
        copy.wait()
        result = dot(normed[...], weights[kind])
        for h in range(heads):
            head = result[:, h * HD : (h + 1) * HD]
            if kind < 2:
                head = head * cos_ref[...] + pltpu.roll(head, HD // 2, 1) * sin_ref[...]
            if kind == 0:
                head = head * factor
            made[h, kind] = head.astype(BF16)
    for f in range(heads):
        outs[f][...] = made[info_ref[ring + 1] ^ f]
    stamp_ref[...] = jnp.zeros_like(stamp_ref)
    keep.wait()


def qkv_call(info, blocks, gain, cosine, sine, *weights):
    half, width = blocks[0][0].shape
    rows, ring = 2 * half, len(blocks[0])
    depth, out_cols = weights[0].shape
    heads = out_cols // HD
    result = pl.pallas_call(
        functools.partial(
            qkv_kernel, ring=ring, heads=heads, factor=HD ** (-0.5) * math.log2(math.e)
        ),
        out_shape=[jax.ShapeDtypeStruct((3, rows, HD), BF16)] * heads
        + [jax.ShapeDtypeStruct((rows, depth), BF16), jax.ShapeDtypeStruct((8, HD), F32)],
        grid_spec=pltpu.PrefetchScalarGridSpec(
            num_scalar_prefetch=1,
            grid=(1,),
            in_specs=[whole((half, width))] * (2 * ring)
            + [whole((1, depth)), whole((rows, HD)), whole((rows, HD))]
            + [pl.BlockSpec(memory_space=pl.ANY)] * 3,
            out_specs=[whole((3, rows, HD))] * heads
            + [pl.BlockSpec(memory_space=pltpu.HBM), whole((8, HD))],
            scratch_shapes=[
                pltpu.VMEM((rows, depth), BF16),
                pltpu.VMEM((heads, 3, rows, HD), BF16),
                pltpu.VMEM((3, depth, out_cols), BF16),
                pltpu.VMEM((rows, depth), BF16),
                pltpu.SemaphoreType.DMA((4,)),
            ],
        ),
        compiler_params=params(30),
        cost_estimate=cost(6 * rows * depth * out_cols, 6 * depth * out_cols),
        name="qkv",
    )(info, *blocks[0], *blocks[1], gain, cosine, sine, *weights)
    return result[:heads], result[heads], result[heads + 1]


def attention_kernel(first_ref, info_ref, *refs, chips, ring):
    own, other = refs[:chips], refs[chips : 2 * chips]
    outs = refs[2 * chips + 1 : 3 * chips + 1]
    keys_all, values_all = refs[3 * chips + 1 :]
    chip, core = info_ref[ring + 1], info_ref[ring + 2]
    span = outs[0].shape[0]
    for f in range(chips):
        for source, side in ((own[f], core), (other[f], 1 - core)):
            block = 2 * (chip ^ f) + side
            keys_all[block] = source[1]
            values_all[block] = source[2].T

    def first_of(row):
        found = jnp.int32(0)
        for s in range(SERIES):
            edge = first_ref[s]
            found = jnp.where(edge <= row, jnp.maximum(found, edge), found)
        return found

    for f in range(chips):
        last = 2 * (chip ^ f) + core
        query = own[f][0]
        row = last * span + lax.broadcasted_iota(jnp.int32, (1, span), 1)
        start = jnp.zeros((1, span), jnp.int32)
        for s in range(SERIES):
            edge = first_ref[s]
            start = jnp.where(edge <= row, jnp.maximum(start, edge), start)
        lane = lax.broadcasted_iota(jnp.int32, (span, 1), 0)

        def body(at, carry, masked, query=query, row=row, start=start, lane=lane):
            peak, denom, accum = carry
            scores = dot_over(keys_all[at], query, (1, 1))
            if masked:
                column = lane + at * span
                allowed = (column >= start) & (column <= row)
                scores = jnp.where(allowed, scores, -1e30)
            new_peak = jnp.maximum(peak, jnp.max(scores, axis=0, keepdims=True))
            weights = jnp.exp2(scores - new_peak)
            if masked:
                weights = jnp.where(allowed, weights, 0.0)
            keep = jnp.exp2(peak - new_peak)
            denom = denom * keep + jnp.sum(weights, axis=0, keepdims=True)
            accum = accum * keep + dot(values_all[at], weights.astype(BF16))
            return new_peak, denom, accum

        def pair(turn, carry, query=query, full=None):
            peak, denom, accum = carry
            at = full + 2 * turn
            blocks = (at, at + 1)
            scores = [dot_over(keys_all[block], query, (1, 1)) for block in blocks]
            tops = [jnp.max(score, axis=0, keepdims=True) for score in scores]
            new_peak = jnp.maximum(peak, jnp.maximum(*tops))
            keep = jnp.exp2(peak - new_peak)
            denom, accum = denom * keep, accum * keep
            for block, score in zip(blocks, scores):
                weights = jnp.exp2(score - new_peak)
                denom += jnp.sum(weights, axis=0, keepdims=True)
                accum += dot(values_all[block], weights.astype(BF16))
            return new_peak, denom, accum

        begin = first_of(last * span) // span
        full = jnp.minimum(last, (first_of(last * span + span - 1) + span - 1) // span)
        carry = (
            jnp.full((1, span), -1e30, F32),
            jnp.zeros((1, span), F32),
            jnp.zeros((HD, span), F32),
        )
        carry = lax.fori_loop(begin, full, functools.partial(body, masked=True), carry)
        turns = (last - full) // 2
        carry = lax.fori_loop(0, turns, functools.partial(pair, full=full), carry)
        rest = full + 2 * turns
        carry = lax.fori_loop(rest, last, functools.partial(body, masked=False), carry)
        _, denom, accum = body(last, carry, masked=True)
        outs[f][...] = (accum / denom).T.astype(BF16)


def attention_call(first, info, own, other, stamp, ring):
    chips = len(own)
    _, rows, _ = own[0].shape
    return pl.pallas_call(
        functools.partial(attention_kernel, chips=chips, ring=ring),
        out_shape=[jax.ShapeDtypeStruct((rows, HD), BF16)] * chips,
        grid_spec=pltpu.PrefetchScalarGridSpec(
            num_scalar_prefetch=2,
            grid=(1,),
            in_specs=[whole((3, rows, HD))] * (2 * chips) + [whole(stamp.shape)],
            out_specs=[whole((rows, HD))] * chips,
            scratch_shapes=[
                pltpu.VMEM((2 * chips, rows, HD), BF16),
                pltpu.VMEM((2 * chips, HD, rows), BF16),
            ],
        ),
        compiler_params=params(24),
        cost_estimate=cost(
            4 * chips * rows * chips * rows * HD,
            16 * chips * rows * HD,
            chips * rows * chips * rows,
        ),
        name="attention",
    )(first, info, *own, *other, stamp)


def middle_kernel(info_ref, *refs, ring, chips):
    parts = [refs[:ring], refs[ring : 2 * ring]]
    refs = refs[2 * ring :]
    tok_ref, w_own_ref = refs[:2]
    near_first, near_rest = refs[2 : 2 + chips], refs[2 + chips : 2 + 2 * chips]
    far_first, far_rest = refs[2 + 2 * chips], refs[3 + 2 * chips : 3 + 3 * chips]
    refs = refs[3 + 3 * chips :]
    gain_ref, gate_ref, up_ref, wp_ref, proj_ref, student_ref = refs[:6]
    hidden_ref, own_ref = refs[6:8]
    pieces = refs[8 : 8 + ring]
    attended, mixed, total, near, far, gates, ups, wp, proj, sems = refs[8 + ring :]
    step = pl.program_id(0)
    level, chip, core = info_ref[ring], info_ref[ring + 1], info_ref[ring + 2]
    rows, depth = mixed.shape
    width = own_ref.shape[1]
    blocks, _, wide = gates.shape

    used = iter(range(sems.shape[0]))
    copy = lambda source, target: pltpu.make_async_copy(source, target, sems.at[next(used)])
    heads = []
    for k in range(2):
        for s, part in enumerate(parts[k]):
            count = part.shape[0]
            for i in range(count):
                flip = level ^ info_ref[s]
                at = ((flip & 1) * 2 + (flip >> 1)) * width + (chip ^ (k * count + i)) * HD
                heads.append(copy(part.at[i], attended.at[:, pl.ds(pl.multiple_of(at, HD), HD)]))
    slices = [
        [
            copy(near_first[f], near.at[f, 0]),
            copy(near_rest[f], near.at[f, pl.ds(1, ring - 2)]),
            copy(far_first.at[f, 0], far.at[f, 0]),
            copy(far_rest[f], far.at[f, pl.ds(1, ring - 2)]),
        ]
        for f in range(chips)
    ]
    own_rows = pl.ds(pl.multiple_of(level * width, width), width)
    late = [copy(proj_ref.at[own_rows], proj), copy(student_ref, total)]
    columns = [pl.ds(i * wide, wide) for i in range(blocks)]
    units = [
        [
            copy(gate_ref.at[:, columns[i]], gates.at[i]),
            copy(up_ref.at[:, columns[i]], ups.at[i]),
            copy(wp_ref.at[columns[i]], wp.at[i]),
        ]
        for i in range(blocks)
    ]

    @pl.when(step == 0)
    def _():
        for c in heads + slices[0]:
            c.start()
        for c in sum(slices[1:], []) + late:
            c.start()
        for c in heads:
            c.wait()

    for f in range(chips):

        @pl.when(step == f)
        def _(f=f):
            for c in slices[f]:
                c.wait()
            for c in sum(units[f::chips], []):
                c.start()

    @pl.when(step < chips)
    def _():
        for gathered, side in ((near, core), (far, 1 - core)):
            here = pl.ds(pl.multiple_of(side * COLS, COLS), COLS)
            result = tok_ref[:, here].astype(F32) + dot(attended[:, :width], w_own_ref[:, here])
            weight = gathered[step].reshape(depth - width, COLS)
            result += dot(attended[:, width:], weight)
            at = pl.ds(pl.multiple_of((2 * (step ^ chip) + side) * COLS, COLS), COLS)
            mixed[:, at] = result.astype(BF16)

    @pl.when(step == chips)
    def _():
        for c in late:
            c.wait()
        values = mixed[...].astype(F32)
        attended[...] = (rms_scale(values) * gain_ref[...]).astype(BF16)
        own = mixed[:, pl.ds(pl.multiple_of(level * width, 128), width)]
        own_ref[...] = own
        total[...] -= dot(own, proj[...])

    for i in range(blocks):

        @pl.when(step == chips + i)
        def _(i=i):
            for c in units[i]:
                c.wait()

    @pl.when(step >= chips)
    def _():
        index = step - chips
        gate = dot(attended[...], gates[index])
        up = dot(attended[...], ups[index])
        hidden = (gate * jax.nn.sigmoid(gate) * up).astype(BF16)
        hidden_ref[...] = hidden
        total[...] -= dot(hidden, wp[index])

    @pl.when(step == pl.num_programs(0) - 1)
    def _():
        size = rows // ring
        for s in range(ring):
            at = pl.ds(pl.multiple_of(((level + s) & (ring - 1)) * size, size), size)
            pieces[s][...] = total[at, :].astype(BF16)


def middle_call(info, parts, tok, w_out, near, far, gain, w_gate, w_up, wp, projector, student):
    rows, depth = tok.shape
    ring, chips = len(parts[0]), len(near[0])
    units = w_gate.shape[1]
    wide = 2 * COLS
    width = depth // ring
    sd = projector.shape[1]
    blocks = units // wide
    tile = lambda j, info: (0, jnp.minimum(j, chips - 1) ^ info[ring + 1])
    late = lambda j, info: (0, jnp.maximum(j - chips, 0))
    anywhere = pl.BlockSpec(memory_space=pl.ANY)
    count = 2 * ring * parts[0][0].shape[0] + 4 * chips + 2 + 3 * blocks
    result = pl.pallas_call(
        functools.partial(middle_kernel, ring=ring, chips=chips),
        out_shape=[
            jax.ShapeDtypeStruct((rows, units), BF16),
            jax.ShapeDtypeStruct((rows, width), BF16),
        ]
        + [jax.ShapeDtypeStruct((rows // ring, sd), BF16)] * ring,
        grid_spec=pltpu.PrefetchScalarGridSpec(
            num_scalar_prefetch=1,
            grid=(chips + blocks,),
            in_specs=[anywhere] * (2 * ring)
            + [pl.BlockSpec((rows, wide), tile), pl.BlockSpec((width, wide), tile)]
            + [anywhere] * (3 * chips + 1)
            + [whole((1, depth))]
            + [anywhere] * 5,
            out_specs=[
                pl.BlockSpec((rows, wide), late),
                whole((rows, width)),
            ]
            + [whole((rows // ring, sd))] * ring,
            scratch_shapes=[
                pltpu.VMEM((rows, depth), BF16),
                pltpu.VMEM((rows, depth), BF16),
                pltpu.VMEM((rows, sd), F32),
                pltpu.VMEM((chips, ring - 1, width, COLS), BF16),
                pltpu.VMEM((chips, ring - 1, width, COLS), BF16),
                pltpu.VMEM((blocks, depth, wide), BF16),
                pltpu.VMEM((blocks, depth, wide), BF16),
                pltpu.VMEM((blocks, wide, sd), BF16),
                pltpu.VMEM((width, sd), BF16),
                pltpu.SemaphoreType.DMA((count,)),
            ],
        ),
        compiler_params=params(42),
        cost_estimate=cost(
            2 * rows * depth * (depth + 2 * units) + 2 * rows * sd * (units + width),
            2 * depth * (depth + 2 * units),
            rows * units,
        ),
        name="middle",
    )(
        info,
        *parts[0],
        *parts[1],
        tok,
        w_out,
        *near[0],
        *near[1],
        far[0],
        *far[1],
        gain,
        w_gate,
        w_up,
        wp,
        projector,
        student,
    )
    return result[0], result[1], result[2:]


def down_kernel(info_ref, hidden_ref, weight_ref, *outs):
    result = dot(hidden_ref[...], weight_ref[...]).astype(BF16)
    for j, out in enumerate(outs):

        @pl.when(pl.program_id(0) == j)
        def _(out=out):
            out[...] = result


def down_call(info, hidden, w_down, ring, first_flip, last_flip):
    rows, units = hidden.shape
    depth = w_down.shape[1]
    width = depth // ring
    count = first_flip - last_flip + 1
    return pl.pallas_call(
        down_kernel,
        out_shape=[jax.ShapeDtypeStruct((rows, width), BF16)] * count,
        grid_spec=pltpu.PrefetchScalarGridSpec(
            num_scalar_prefetch=1,
            grid=(count,),
            in_specs=[
                whole((rows, units)),
                pl.BlockSpec((units, width), lambda j, info: (0, info[ring] ^ (first_flip - j))),
            ],
            out_specs=[whole((rows, width))] * count,
        ),
        compiler_params=params(24),
        cost_estimate=cost(2 * rows * units * width * count, 2 * units * width * count),
        name="down",
    )(info, hidden, w_down)


def grads_kernel(info_ref, *refs, ring, chips):
    pieces = refs[:ring]
    normed_ref, hidden_ref, s_down_ref, up_ref, gate_ref = refs[ring : ring + 5]
    keep_ref, give_ref, scaled, grads = refs[ring + 5 :]
    chip, core = info_ref[ring + 1], info_ref[ring + 2]
    size, sd = pieces[0].shape
    for s in range(ring):
        scaled[pl.ds(pl.multiple_of(info_ref[s] * size, size), size), :] = pieces[s][...]
    value = scaled[...]
    wide = value.astype(F32)
    error = jnp.sum(wide * wide)
    grad_hidden = dot_over(value, s_down_ref[...], (1, 1))
    grads[0] = dot_over(normed_ref[...], (grad_hidden * gate_ref[...].astype(F32)).astype(BF16), (0, 0))
    grads[1] = dot_over(normed_ref[...], (grad_hidden * up_ref[...].astype(F32)).astype(BF16), (0, 0))
    grads[2] = dot_over(hidden_ref[...], value, (0, 0))
    share = grads.shape[1] // (2 * chips)
    for f in range(chips):
        for k in range(3):
            for part, ref in ((core, keep_ref), (1 - core, give_ref)):
                at = pl.multiple_of((part * chips + (chip ^ f)) * share, share)
                ref[f, k * share : (k + 1) * share] = grads[k, pl.ds(at, share), :].astype(
                    ref.dtype
                )
        for ref in (keep_ref, give_ref):
            ref[f, 3 * share :] = jnp.full((NOTE, sd), error, F32).astype(ref.dtype)


def grads_call(info, pieces, normed, hidden, s_down, up, gate, chips):
    ring = len(pieces)
    rows, sd = normed.shape
    units = hidden.shape[1]
    share = 3 * sd // (2 * chips) + NOTE
    operands = [*pieces, normed, hidden, s_down, up, gate]
    return pl.pallas_call(
        functools.partial(grads_kernel, ring=ring, chips=chips),
        out_shape=(
            jax.ShapeDtypeStruct((chips, share, units), F32),
            jax.ShapeDtypeStruct((chips, share, units), BF16),
        ),
        grid_spec=pltpu.PrefetchScalarGridSpec(
            num_scalar_prefetch=1,
            grid=(1,),
            in_specs=[whole(a.shape) for a in operands],
            out_specs=(whole((chips, share, units)), whole((chips, share, units))),
            scratch_shapes=[pltpu.VMEM((rows, sd), BF16), pltpu.VMEM((3, sd, units), F32)],
        ),
        compiler_params=params(22),
        cost_estimate=cost(8 * rows * sd * units, 20 * sd * units),
        name="grads",
    )(info, *operands)


def pair_kernel(keep_ref, theirs_ref, *outs):
    for f, out in enumerate(outs):
        out[...] = (keep_ref[f] + theirs_ref[f].astype(F32)).astype(out.dtype)


def pair_call(keep, theirs):
    chips, share, sd = keep.shape
    return pl.pallas_call(
        pair_kernel,
        out_shape=[jax.ShapeDtypeStruct((share, sd), BF16)] * chips,
        compiler_params=params(10),
        cost_estimate=cost(keep.size, 8 * keep.size),
        name="pair",
    )(keep, theirs)


def finish_kernel(info_ref, *refs, chips, ring):
    mine, others = refs[:chips], refs[chips : 2 * chips]
    outs = refs[2 * chips : 2 * chips + 3]
    error_ref, notes = refs[2 * chips + 3 :]
    chip, core = info_ref[ring + 1], info_ref[ring + 2]
    share = (mine[0].shape[0] - NOTE) // 3
    for f in range(chips):
        for part, ref in ((core, mine[f]), (1 - core, others[f])):
            index = part * chips + (chip ^ f)
            at = pl.ds(pl.multiple_of(index * share, share), share)
            for k in range(3):
                outs[k][at, :] = ref[k * share : (k + 1) * share].astype(F32)
            notes[index] = ref[3 * share :, :HD].astype(F32)
    error_ref[0, 0] = jnp.max(notes[0]) / mine[0].shape[1]


def finish_call(info, mine, others, ring):
    chips = len(mine)
    share, sd = mine[0].shape
    rows = (share - NOTE) // 3 * 2 * chips
    return pl.pallas_call(
        functools.partial(finish_kernel, chips=chips, ring=ring),
        out_shape=[jax.ShapeDtypeStruct((rows, sd), F32)] * 3
        + [jax.ShapeDtypeStruct((1, 1), F32)],
        grid_spec=pltpu.PrefetchScalarGridSpec(
            num_scalar_prefetch=1,
            grid=(1,),
            in_specs=[whole((share, sd))] * (2 * chips),
            out_specs=[whole((rows, sd))] * 3 + [pl.BlockSpec(memory_space=pltpu.SMEM)],
            scratch_shapes=[pltpu.VMEM((2 * chips, NOTE, HD), F32)],
        ),
        compiler_params=params(14),
        cost_estimate=cost(rows * sd, 12 * rows * sd),
        name="finish",
    )(info, *mine, *others)


def step_on(block, axis):
    size = lax.axis_size(axis)
    return lax.ppermute(block, axis, [(i, (i + 1) % size) for i in range(size)])


def ring_gather(block, axis, steps=None):
    blocks = [block]
    for _ in range(lax.axis_size(axis) - 1 if steps is None else steps):
        blocks.append(step_on(blocks[-1], axis))
    return blocks


def shifted(pieces, axis):
    size = lax.axis_size(axis)
    moved = [
        lax.ppermute(pieces[s], axis, [(i, (i + s) % size) for i in range(size)])
        for s in range(1, size)
    ]
    return [pieces[0], *moved]


def flipped(pieces):
    size = lax.axis_size("dp")
    moved = [
        lax.ppermute(pieces[f], "dp", [(i, i ^ (2 * f)) for i in range(size)])
        for f in range(1, len(pieces))
    ]
    return [pieces[0], *moved]


def swapped(value):
    size = lax.axis_size("dp")
    return lax.ppermute(value, "dp", [(i, i ^ 1) for i in range(size)])


def after(value, *others):
    return lax.optimization_barrier((value, *others))[0]


def paired(
    tokens,
    series_ids,
    offsets,
    norm_gain,
    mlp_gain,
    w_query,
    w_key,
    w_value,
    w_out,
    w_gate,
    w_up,
    w_down,
    projector,
    student_in,
    s_gate,
    s_up,
    s_down,
):
    rows = tokens.shape[0]
    depth, sd = w_query.shape[0], student_in.shape[1]
    dp, ring = lax.axis_size("dp"), lax.axis_size("tensor")
    here, level = lax.axis_index("dp"), lax.axis_index("tensor")
    chips, half = dp // 2, rows // 2
    total_rows = rows * dp
    size = rows // ring
    slice_cols = depth // dp

    places = [(level - s) & (ring - 1) for s in range(ring)] + [level, here >> 1, here & 1]
    slots = lax.broadcasted_iota(jnp.int32, (16,), 0)
    info = sum(jnp.where(slots == k, place, 0) for k, place in enumerate(places))
    starts = [level * size, here * slice_cols]
    *starts, zero = [jnp.asarray(start, jnp.uint32) for start in (*starts, 0)]
    tokens, info, *starts = lax.optimization_barrier((tokens, info, *starts))

    token_rings = [ring_gather(tokens[k : k + half], "tensor") for k in (0, half)]

    angles = offsets.astype(F32)[:, None] * frequencies(HD)[None, :]
    cosine, sine = jnp.cos(angles), jnp.sin(angles)
    cosine = jnp.concatenate([cosine, cosine], axis=1)
    sine = jnp.concatenate([-sine, sine], axis=1)
    student_full = student_in.astype(F32)
    student_normed = rms_scale(student_full).astype(BF16)
    below = jnp.sum(
        series_ids[None, :] < jnp.arange(SERIES, dtype=jnp.int32)[:, None], axis=1, dtype=jnp.int32
    )

    made, tok_full, stamp = qkv_call(
        info, token_rings, norm_gain[None, :], cosine, sine, w_query, w_key, w_value
    )

    student_normed, projected, stamp = lax.optimization_barrier((student_normed, projector, stamp))
    s_gate_out = dot(student_normed, s_gate)
    s_up_out = dot(student_normed, s_up)
    sigmoid_gate = jax.nn.sigmoid(s_gate_out)
    up_slope = s_gate_out * sigmoid_gate
    gate_slope = s_up_out * sigmoid_gate * (1.0 + s_gate_out * (1.0 - sigmoid_gate))
    s_hidden = (up_slope * s_up_out).astype(BF16)
    up_slope, gate_slope = up_slope.astype(BF16), gate_slope.astype(BF16)
    student_part = dot(s_hidden, s_down)
    projected = dot(w_down, projected).astype(BF16)
    student_own = lax.dynamic_slice(student_full, [starts[0], zero], (size, sd))
    early = (projected, student_part, s_hidden, up_slope, gate_slope, student_normed, student_own)

    over = lambda value, bit: lax.ppermute(value, "tensor", [(i, i ^ bit) for i in range(ring)])
    w_slice = lax.dynamic_slice(w_out, [zero, starts[1]], (w_out.shape[0], slice_cols))
    w_slice, stamp, _ = lax.optimization_barrier((w_slice, stamp, s_gate_out))
    w_first = over(w_slice, 2)

    own = flipped(made)
    *own, w_first = lax.optimization_barrier((*own, w_first, *early))[: chips + 1]
    w_rest = over(jnp.stack([w_slice, w_first]), 1)
    other = [swapped(a) for a in own]
    near_first = flipped([w_first] * chips)
    made = attention_call(below, info, own, other, stamp, ring)
    attended = lax.optimization_barrier((*flipped(made), w_rest, *near_first))
    w_rest, near_first, attended = attended[chips], attended[chips + 1 :], attended[:chips]
    parts = [
        ring_gather(jnp.stack(attended[k : k + chips // 2]), "tensor") for k in (0, chips // 2)
    ]
    w_rest = after(w_rest, *attended)
    near_rest = flipped([w_rest] * chips)
    far_first = swapped(after(jnp.stack(near_first)[:, None], *attended))
    far_rest = [swapped(after(a, parts[1][1])) for a in near_rest]

    hidden, mixed_own, pieces = middle_call(
        info,
        parts,
        tok_full,
        w_out,
        (near_first, near_rest),
        (far_first, far_rest),
        mlp_gain[None, :],
        w_gate,
        w_up,
        projected,
        projector,
        student_part,
    )

    far_sum = over(down_call(info, hidden, w_down, ring, 3, 3)[0], 1)
    far_mine, near_theirs, kept = down_call(info, hidden, w_down, ring, 2, 0)

    moved = lax.optimization_barrier((*shifted(pieces, "tensor"), kept))[:ring]
    difference = student_own + sum(piece.astype(F32) for piece in moved)
    own = (difference * total_rows ** (-0.5)).astype(BF16)
    scaled = shifted([own] * ring, "tensor")

    keep, give = grads_call(
        after(info, far_sum),
        scaled,
        student_normed,
        s_hidden,
        s_down,
        up_slope,
        gate_slope,
        chips,
    )
    shares = pair_call(keep, swapped(give))
    far_sum = (far_sum.astype(F32) + far_mine.astype(F32)).astype(BF16)
    shares = flipped(shares)
    own = sum(share.astype(F32) for share in shares).astype(BF16)
    mine = flipped([own] * chips)
    others = [swapped(share) for share in mine]

    level_sums = [over(after(near_theirs, far_sum), 1), over(far_sum, 2)]
    mlp_own = sum(after(value, mine[-1]).astype(F32) for value in level_sums)
    teacher_out = (mixed_own.astype(F32) + (kept.astype(F32) + mlp_own)).astype(BF16)
    grad_gate, grad_up, grad_down, error = finish_call(info, mine, others, ring)
    return teacher_out, grad_gate, grad_up, grad_down, error.reshape(())


def local(*args):
    rows, w_query, s_gate = args[0].shape[0], args[5], args[14]
    dp, ring = lax.axis_size("dp"), lax.axis_size("tensor")
    heads = w_query.shape[1] // HD
    fits = (
        dp == 2 * heads
        and heads > 1
        and ring == 4
        and heads & (heads - 1) == 0
        and w_query.shape[0] == dp * COLS
        and s_gate.shape[0] == s_gate.shape[1]
        and rows % (32 * ring) == 0
    )
    return paired(*args) if fits else general(*args)


def solution(mesh):
    in_specs = (
        P("dp", "tensor"),
        P(),
        P("dp"),
        P(),
        P(),
        P(None, "tensor"),
        P(None, "tensor"),
        P(None, "tensor"),
        P("tensor", None),
        P(None, "tensor"),
        P(None, "tensor"),
        P("tensor", None),
        P(),
        P("dp", None),
        P(None, "tensor"),
        P(None, "tensor"),
        P("tensor", None),
    )
    out_specs = (P("dp", "tensor"), P(None, "tensor"), P(None, "tensor"), P("tensor", None), P())
    return jax.shard_map(local, mesh=mesh, in_specs=in_specs, out_specs=out_specs, check_vma=False)
```
